32 devices in a mesh: ka: 4 (over y, x), pts: 8 (over z, core).
Axes of the slice: x: 2, y: 2, z: 4, core: 2. Of those that a mesh axis runs over, the one named last changes fastest.
Arguments:
- orbitals: bfloat16 [32, 2, 512, 2048], P('ka', None, None, 'pts'), may hold values from -1.078125 to 1.078125
- coulomb: bfloat16 [32, 32, 2048], P('ka', None, 'pts'), may hold values from -6 to 6
Outputs:
- exchange: bfloat16 [512, 32, 2, 512], P('pts', 'ka')
The draws below stay inside these ranges and needn't reach their ends.
All inputs are finite; a program needn't handle non-finite values.
Results may differ from the reference program's by a relative error of at most 0.0064.
Values may be sent and summed in bfloat16 or wider, within the bound.
No kernel may reach another device: no remote copies, remote signals or barrier semaphores. Data moves between devices by JAX's collectives and lax.ppermute only.
A program may use at most 64 MiB of HBM per device.

```python
import math
import jax
import jax.numpy as jnp
from jax import lax

NK = 32
NORB = 512
PTS_DEV = 256
COLS_DEV = 4
NC = 32
NPTS = 2048
N_PTS = 8


def block_scale(key, extent, shards, smallest, high):
    level, own = 1.0, jax.random.fold_in(key, 6)
    for dim, shards_of in shards:
        draws = jnp.exp(jax.random.uniform(jax.random.fold_in(own, dim), (shards_of,), jnp.float32, smallest / len(shards), high / len(shards)))
        level = level * jnp.repeat(draws, extent[dim] // shards_of).reshape([-1 if axis == dim else 1 for axis in range(len(extent))])
    return level


def normal_values(own_key, dims, deviation, most, split=(), held_as=jnp.bfloat16):
    factor_of = block_scale(own_key, dims, split, -0.22, 0.18) if split else 1.0
    result = jax.random.normal(own_key, dims, jnp.float32) * deviation * factor_of
    return jnp.minimum(jnp.maximum(result, -most), most).astype(held_as)


def setup_inputs(seed: int = 0) -> dict:
    splits = jax.random.split(jax.random.key(seed), 3)
    return {
        "orbitals": normal_values(splits[0], (NK, 2, NORB, NPTS), 0.18, 1.078125, ((0, 4), (3, 8))),
        "coulomb": normal_values(splits[1], (NK, NC, NPTS), 1.0, 6.0, ((0, 4), (2, 8))),
    }


def phase_tables(left_idx, right_idx, modulus):
    product = left_idx[:, None] * right_idx[None, :] % modulus
    angles = product.astype(jnp.float32) * (2.0 * math.pi / modulus)
    return (jnp.cos(angles), jnp.sin(angles))

def reference(orbitals, coulomb):
    col_total = COLS_DEV * N_PTS
    point_total = PTS_DEV * N_PTS
    columns = orbitals.reshape(NK, 2, NORB, N_PTS, PTS_DEV)[:, :, :, :, :COLS_DEV].reshape(NK, 2, NORB, col_total)

    def density(pieces):
        column_set, orbital_set = pieces
        real_part = jnp.dot(column_set[0].T, orbital_set[0], preferred_element_type=jnp.float32) + jnp.dot(column_set[1].T, orbital_set[1], preferred_element_type=jnp.float32)
        imag_part = jnp.dot(column_set[0].T, orbital_set[1], preferred_element_type=jnp.float32) - jnp.dot(column_set[1].T, orbital_set[0], preferred_element_type=jnp.float32)
        return jnp.stack([real_part, imag_part]).astype(jnp.bfloat16)
    tile_set = lax.map(density, (columns, orbitals))
    k_index = jnp.arange(NK, dtype=jnp.int32)
    cosine, sine_table = phase_tables(k_index, k_index, NK)
    tiles_wide = tile_set.astype(jnp.float32)

    def phase_sum(weights, values):
        return jnp.einsum('q,qcm->cm', weights, values, precision=lax.Precision.HIGHEST)

    def forward(pieces):
        cos_row, sin_row, coulomb_row = pieces
        real_part = phase_sum(cos_row, tiles_wide[:, 0]) - phase_sum(sin_row, tiles_wide[:, 1])
        imag_part = phase_sum(sin_row, tiles_wide[:, 0]) + phase_sum(cos_row, tiles_wide[:, 1])
        return (jnp.stack([real_part, imag_part]) * coulomb_row.astype(jnp.float32)[None]).astype(jnp.bfloat16)
    cell_tiles = lax.map(forward, (cosine, sine_table, coulomb))
    cells_wide = cell_tiles.astype(jnp.float32)

    def backward(pieces):
        cos_row, sin_row = pieces
        real_part = phase_sum(cos_row, cells_wide[:, 0]) + phase_sum(sin_row, cells_wide[:, 1])
        imag_part = phase_sum(cos_row, cells_wide[:, 1]) - phase_sum(sin_row, cells_wide[:, 0])
        return (jnp.stack([real_part, imag_part]) / NK).astype(jnp.bfloat16)
    kernel = lax.map(backward, (cosine, sine_table))
    factor = 1.0 / math.sqrt(point_total)

    def apply_kernel(pieces):
        kernel_k, column_set, orbital_set = pieces
        w_re = jnp.dot(orbital_set[0], kernel_k[0].T, preferred_element_type=jnp.float32) + jnp.dot(orbital_set[1], kernel_k[1].T, preferred_element_type=jnp.float32)
        w_im = jnp.dot(orbital_set[0], kernel_k[1].T, preferred_element_type=jnp.float32) - jnp.dot(orbital_set[1], kernel_k[0].T, preferred_element_type=jnp.float32)
        col_re = column_set[0].astype(jnp.float32).T
        col_im = column_set[1].astype(jnp.float32).T
        hp = lax.Precision.HIGHEST
        mat_re = jnp.dot(w_re, col_re, precision=hp) - jnp.dot(w_im, col_im, precision=hp)
        mat_im = jnp.dot(w_re, col_im, precision=hp) + jnp.dot(w_im, col_re, precision=hp)
        return jnp.stack([mat_re, mat_im])
    matrices = lax.map(apply_kernel, (kernel, columns, orbitals))
    return (jnp.transpose(matrices, (2, 0, 1, 3)) * factor).astype(jnp.bfloat16)
```

```python
import functools
import math

import jax
import jax.numpy as jnp
import ml_dtypes
import numpy as np
from jax import lax
from jax.experimental import pallas as pl
from jax.experimental.pallas import tpu as pltpu
from jax.sharding import PartitionSpec as P

BF16 = jnp.bfloat16
F32 = jnp.float32
LANES = 128
ROWS = 16
MIB = 1 << 20


def split_terms(table):
    high = table.astype(ml_dtypes.bfloat16)
    low = (table - high.astype(np.float64)).astype(ml_dtypes.bfloat16)
    return np.concatenate([high, low], axis=1)


def phase_tables(total):
    index = np.arange(total)
    angles = (index[:, None] * index[None, :] % total) * (2.0 * math.pi / total)
    cosine, sine = np.cos(angles), np.sin(angles)
    forward = np.zeros((2, total, total, 2))
    forward[0, :, :, 0] = cosine
    forward[0, :, :, 1] = -sine
    forward[1, :, :, 0] = sine
    forward[1, :, :, 1] = cosine
    backward = np.zeros((total, 2, 2, total))
    backward[:, 0, 0] = cosine
    backward[:, 0, 1] = sine
    backward[:, 1, 1] = cosine
    backward[:, 1, 0] = -sine
    size = 2 * total
    return (
        split_terms(forward.reshape(size, size)),
        split_terms(backward.reshape(size, size) / total),
    )


def column_selector(group, blocks, per_block, shares):
    total = blocks * per_block
    share = total // shares
    table = np.zeros((group, 2, shares, 2, share, blocks, group, 2, per_block), np.float32)
    for k in range(group):
        for col in range(total):
            d, c = divmod(col, share)
            b, j = divmod(col, per_block)
            table[k, 0, d, 0, c, b, k, 0, j] = 1.0
            table[k, 0, d, 1, c, b, k, 1, j] = -1.0
            table[k, 1, d, 0, c, b, k, 1, j] = 1.0
            table[k, 1, d, 1, c, b, k, 0, j] = 1.0
    return table.reshape(group * 4 * total, blocks * group * 2 * per_block).astype(ml_dtypes.bfloat16)


def dot(left, right, dims=((1,), (0,))):
    return lax.dot_general(left, right, (dims, ((), ())), preferred_element_type=F32)


def spread(wide, start, stride, value):
    for t in range(wide.shape[0]):
        wide[t, pl.ds(start, value.shape[0], stride=stride), :] = value[:, t * LANES : (t + 1) * LANES]


def take(wide, start, size):
    return jnp.concatenate([wide[t, pl.ds(start, size), :] for t in range(wide.shape[0])], axis=1)


def tiled(rows, lanes):
    return pltpu.VMEM((lanes // LANES, rows, LANES), F32)


def call(kernel, out_shape, n_in, scratch=(), limit=24, flops=0, size=0):
    whole = pl.BlockSpec(memory_space=pltpu.VMEM)
    return pl.pallas_call(
        kernel,
        out_shape=out_shape,
        in_specs=[whole] * n_in,
        out_specs=jax.tree.map(lambda _: whole, out_shape),
        scratch_shapes=list(scratch),
        compiler_params=pltpu.CompilerParams(vmem_limit_bytes=limit * MIB),
        cost_estimate=pl.CostEstimate(flops=flops, bytes_accessed=size, transcendentals=0),
    )


def edge_kernel(per_block, orb_ref, out_ref):
    group = orb_ref.shape[0]
    row = lax.broadcasted_iota(jnp.int32, (2 * per_block, LANES), 0)
    lane = lax.broadcasted_iota(jnp.int32, (2 * per_block, LANES), 1)
    first = jnp.where(row < per_block, (row == lane).astype(F32), 0.0).astype(BF16)
    second = jnp.where(row >= per_block, (row - per_block == lane).astype(F32), 0.0).astype(BF16)
    rows = []
    for k in range(group):
        rows.append(
            dot(first, orb_ref[k, 0], ((1,), (1,))) + dot(second, orb_ref[k, 1], ((1,), (1,)))
        )
    out_ref[...] = jnp.concatenate(rows, axis=0).astype(BF16)


def coulomb_kernel(shares, coulomb_ref, *refs):
    outs, wide = refs[:shares], refs[shares]
    cells, columns, points = coulomb_ref.shape
    share = columns // shares
    me = lax.axis_index("ka")
    wide[...] = coulomb_ref[...].astype(F32)
    for s in range(shares):
        dest = jnp.bitwise_xor(me, s)
        start = pl.multiple_of(dest * share, share)
        for r in range(cells):
            outs[s][r] = wide[r, pl.ds(start, share), :].astype(BF16)


def tile_kernel(shares, blocks, per_block, *refs):
    edges, orb_ref, sel_ref = refs[:blocks], refs[blocks], refs[blocks + 1]
    outs = refs[blocks + 2 : blocks + 2 + shares]
    form_ref, gathered, wide = refs[blocks + 2 + shares :]
    local_k, _, norb, points = orb_ref.shape
    group = ROWS // (2 * per_block)
    total = blocks * per_block
    share = total // shares
    rows = 2 * total
    me = lax.axis_index("ka")
    block = lax.axis_index("pts")
    for s in range(blocks):
        gathered[jnp.bitwise_xor(block, s)] = edges[s][...]
    for g in range(local_k // group):
        stacked = jnp.concatenate(
            [gathered[b, g * ROWS : (g + 1) * ROWS] for b in range(blocks)], axis=0
        )
        forms = dot(sel_ref[...], stacked).astype(BF16)
        for kk in range(group):
            k = g * group + kk
            left = forms[2 * kk * rows : (2 * kk + 1) * rows]
            right = forms[(2 * kk + 1) * rows : (2 * kk + 2) * rows]
            form = jnp.concatenate([left, right], axis=1)
            form_ref[k] = form
            tile = dot(form, orb_ref[k].reshape(2 * norb, points))
            for d in range(shares):
                for part in range(2):
                    low = (2 * d + part) * share
                    start = d * share * 2 * local_k + 2 * k + part
                    spread(wide, start, 2 * local_k, tile[low : low + share])
    size = share * 2 * local_k
    for s in range(shares):
        dest = jnp.bitwise_xor(me, s)
        outs[s][...] = take(wide, pl.multiple_of(dest * size, size), size).astype(BF16)


def transform_kernel(shares, total, share, *refs):
    tiles, coulombs = refs[:shares], refs[shares : 2 * shares]
    fwd_ref, bwd_ref = refs[2 * shares : 2 * shares + 2]
    outs = refs[2 * shares + 2 : 3 * shares + 2]
    gathered, weight, wide = refs[3 * shares + 2 :]
    local_k = total // shares
    me = lax.axis_index("ka")
    for s in range(shares):
        src = jnp.bitwise_xor(me, s)
        gathered[src] = tiles[s][...].astype(gathered.dtype)
        for r in range(local_k):
            spread(weight, src * local_k + r, total, coulombs[s][r].astype(F32))
    rows = 2 * local_k
    columns = []
    for c in range(share):
        columns.append(
            jnp.concatenate([gathered[a, c * rows : (c + 1) * rows] for a in range(shares)], axis=0).astype(BF16)
        )
    values = jnp.concatenate(columns, axis=1)
    cells = dot(fwd_ref[...], jnp.concatenate([values, values], axis=0))
    scale = jnp.concatenate([take(weight, c * total, total) for c in range(share)], axis=1)
    cells = (cells * jnp.concatenate([scale, scale], axis=0)).astype(BF16)
    kernel = dot(bwd_ref[...], jnp.concatenate([cells, cells], axis=0))
    points = kernel.shape[1] // share
    for c in range(share):
        spread(wide, c, share, kernel[:, c * points : (c + 1) * points])
    size = 2 * local_k * share
    for s in range(shares):
        dest = jnp.bitwise_xor(me, s)
        outs[s][...] = take(wide, pl.multiple_of(dest * size, size), size).astype(BF16)


def weight_kernel(shares, flip, out_rows, *refs):
    pieces, orb_ref, out_ref, gathered = refs[:shares], refs[shares], refs[shares + 1], refs[shares + 2]
    local_k, _, norb, points = orb_ref.shape
    total_rows = gathered.shape[1]
    half = total_rows // local_k // 2
    me = lax.axis_index("ka")
    core = jnp.bitwise_xor(jnp.bitwise_and(lax.axis_index("pts"), 1), flip)
    for s in range(shares):
        gathered[jnp.bitwise_xor(me, s)] = pieces[s][...]
    lanes = 2 * half * shares
    group = max(1, LANES // lanes)
    chunks = norb // out_rows // 2
    for g in range(local_k // group):
        right, left = [], []
        for kk in range(group):
            k = g * group + kk
            first, second = [], []
            for a in range(shares):
                piece = gathered[a, k * 2 * half : (k + 1) * 2 * half].astype(F32)
                first.append(piece)
                second.extend([piece[half:], -piece[:half]])
            first = jnp.concatenate(first, axis=0).astype(BF16)
            second = jnp.concatenate(second, axis=0).astype(BF16)
            zero = jnp.zeros_like(first)
            parts = [zero] * (2 * group)
            parts[2 * kk], parts[2 * kk + 1] = first, second
            right.append(jnp.concatenate(parts, axis=1))
            left.append(k)
        right = jnp.concatenate(right, axis=0)
        for z in range(chunks):
            start = pl.multiple_of((2 * z + core) * out_rows, out_rows)
            rows = jnp.concatenate(
                [orb_ref[k, part, pl.ds(start, out_rows), :] for k in left for part in range(2)], axis=1
            )
            out_ref[z, :, g * group * lanes : (g + 1) * group * lanes] = dot(
                rows, right, ((1,), (1,))
            ).astype(out_ref.dtype)


def pair_kernel(chunks, keep_ref, came_ref, own_ref, *outs):
    z = lax.shift_right_logical(lax.axis_index("pts"), 1)
    for s in range(chunks):
        dest = jnp.bitwise_xor(z, s)
        value = keep_ref[dest] + came_ref[dest].astype(F32)
        if s == 0:
            own_ref[...] = value
        else:
            outs[s - 1][...] = value.astype(BF16)


def exchange_kernel(chunks, scale, *refs):
    pieces, form_ref, out_ref, wide = refs[:chunks], refs[chunks], refs[chunks + 1], refs[chunks + 2]
    local_k, lanes, twice = form_ref.shape
    norb = twice // 2
    out_rows = pieces[0].shape[0]
    total = pieces[0][...]
    for s in range(1, chunks):
        total = total + pieces[s][...].astype(F32)
    total = total * scale
    high = total.astype(BF16)
    low = (total - high.astype(F32)).astype(BF16)
    group = max(1, LANES // lanes)
    width = group * lanes
    lane = lax.broadcasted_iota(jnp.int32, (out_rows, width), 1)
    zero = jnp.zeros((out_rows, width), BF16)
    for g in range(local_k // group):
        high_g = high[:, g * width : (g + 1) * width]
        low_g = low[:, g * width : (g + 1) * width]
        left = []
        for kk in range(group):
            keep = (lane >= kk * lanes) & (lane < (kk + 1) * lanes)
            left.append(
                jnp.concatenate([jnp.where(keep, high_g, zero), jnp.where(keep, low_g, zero)], axis=1)
            )
        forms = [form_ref[g * group + kk] for kk in range(group)]
        result = dot(jnp.concatenate(left, axis=0), jnp.concatenate(forms + forms, axis=0))
        for kk in range(group):
            k = g * group + kk
            for part in range(2):
                value = result[kk * out_rows : (kk + 1) * out_rows, part * norb : (part + 1) * norb]
                spread(wide, 2 * k + part, 2 * local_k, value)
    for t in range(norb // LANES):
        value = wide[t].astype(BF16).reshape(out_rows, local_k, 2, LANES)
        out_ref[:, :, :, t * LANES : (t + 1) * LANES] = value


def swap(value, axis, mask):
    size = lax.axis_size(axis)
    return lax.ppermute(value, axis, [(i, i ^ mask) for i in range(size)])


def body(orbitals, coulomb):
    shares, blocks = lax.axis_size("ka"), lax.axis_size("pts")
    local_k, _, norb, points = orbitals.shape
    columns = coulomb.shape[1]
    per_block = columns // blocks
    share = columns // shares
    total = local_k * shares
    out_rows = norb // blocks
    chunks = blocks // 2
    group = ROWS // (2 * per_block)
    shape = jax.ShapeDtypeStruct

    edge = pl.pallas_call(
        functools.partial(edge_kernel, per_block),
        out_shape=shape((local_k * 2 * per_block, norb), BF16),
        grid=(local_k // group,),
        in_specs=[pl.BlockSpec((group, 2, norb, LANES), lambda g: (g, 0, 0, 0))],
        out_specs=pl.BlockSpec((ROWS, norb), lambda g: (g, 0)),
        cost_estimate=pl.CostEstimate(flops=0, bytes_accessed=2 * MIB, transcendentals=0),
    )(orbitals)
    edges = [edge] + [None] * (blocks - 1)
    for s in range(1, chunks):
        edges[2 * s] = swap(edge, "pts", 2 * s)
    for s in range(chunks):
        edges[2 * s + 1] = swap(edges[2 * s], "pts", 1)

    own = call(
        functools.partial(coulomb_kernel, shares),
        [shape((local_k, share, points), BF16)] * shares,
        1,
        [pltpu.VMEM((local_k, columns, points), F32)],
        size=2 * MIB,
    )(coulomb)
    coulombs = [own[0]] + [swap(own[s], "ka", s) for s in range(1, shares)]

    selector = jnp.asarray(column_selector(group, blocks, per_block, shares))
    piece = shape((share * 2 * local_k, points), BF16)
    *tiles, forms = call(
        functools.partial(tile_kernel, shares, blocks, per_block),
        [piece] * shares + [shape((local_k, 2 * columns, 2 * norb), BF16)],
        blocks + 2,
        [
            pltpu.VMEM((blocks, local_k * 2 * per_block, norb), BF16),
            tiled(columns * 2 * local_k, points),
        ],
        size=8 * MIB,
    )(*edges, orbitals, selector)
    tiles = [tiles[0]] + [swap(tiles[s], "ka", s) for s in range(1, shares)]

    forward, backward = phase_tables(total)
    kernels = call(
        functools.partial(transform_kernel, shares, total, share),
        [piece] * shares,
        2 * shares + 2,
        [
            pltpu.VMEM((shares, share * 2 * local_k, points), BF16 if local_k % 8 == 0 else F32),
            tiled(share * total, points),
            tiled(2 * total * share, points),
        ],
        size=2 * MIB,
    )(*tiles, *coulombs, jnp.asarray(forward), jnp.asarray(backward))
    kernels = [kernels[0]] + [swap(kernels[s], "ka", s) for s in range(1, shares)]

    lanes = local_k * 2 * columns
    halves = []
    for flip, kind in ((1, BF16), (0, F32)):
        halves.append(
            call(
                functools.partial(weight_kernel, shares, flip, out_rows),
                shape((chunks, out_rows, lanes), kind),
                shares + 1,
                [pltpu.VMEM((shares, share * 2 * local_k, points), BF16)],
                size=6 * MIB,
            )(*kernels, orbitals)
        )
    came = swap(halves[0], "pts", 1)
    own_sum, *sums = call(
        functools.partial(pair_kernel, chunks),
        [shape((out_rows, lanes), F32)] + [shape((out_rows, lanes), BF16)] * (chunks - 1),
        2,
        size=1 * MIB,
    )(halves[1], came)
    sums = [own_sum] + [swap(sums[s - 1], "pts", 2 * s) for s in range(1, chunks)]
    return call(
        functools.partial(exchange_kernel, chunks, 1.0 / math.sqrt(points * blocks)),
        shape((out_rows, local_k, 2, norb), BF16),
        chunks + 1,
        [tiled(out_rows * 2 * local_k, norb)],
        size=4 * MIB,
    )(*sums, forms)


def solution(mesh):
    in_specs = (P("ka", None, None, "pts"), P("ka", None, "pts"))
    out_specs = P("pts", "ka", None, None)
    return jax.shard_map(body, mesh=mesh, in_specs=in_specs, out_specs=out_specs, check_vma=False)
```

```python
import functools
import math

import jax
import jax.numpy as jnp
import ml_dtypes
import numpy as np
from jax import lax
from jax.experimental import pallas as pl
from jax.experimental.pallas import tpu as pltpu
from jax.sharding import PartitionSpec as P

BF16 = jnp.bfloat16
F32 = jnp.float32
LANES = 128
ROWS = 16
MIB = 1 << 20


def split_terms(table):
    high = table.astype(ml_dtypes.bfloat16)
    low = (table - high.astype(np.float64)).astype(ml_dtypes.bfloat16)
    return np.concatenate([high, low], axis=1)


def phase_tables(total):
    index = np.arange(total)
    angles = (index[:, None] * index[None, :] % total) * (2.0 * math.pi / total)
    cosine, sine = np.cos(angles), np.sin(angles)
    forward = np.zeros((2, total, total, 2))
    forward[0, :, :, 0] = cosine
    forward[0, :, :, 1] = -sine
    forward[1, :, :, 0] = sine
    forward[1, :, :, 1] = cosine
    backward = np.zeros((total, 2, 2, total))
    backward[:, 0, 0] = cosine
    backward[:, 0, 1] = sine
    backward[:, 1, 1] = cosine
    backward[:, 1, 0] = -sine
    size = 2 * total
    return (
        split_terms(forward.reshape(size, size)),
        split_terms(backward.reshape(size, size) / total),
    )


def column_selector(group, blocks, per_block, shares):
    total = blocks * per_block
    share = total // shares
    table = np.zeros((group, 2, shares, 2, share, blocks, group, 2, per_block), np.float32)
    for k in range(group):
        for col in range(total):
            d, c = divmod(col, share)
            b, j = divmod(col, per_block)
            table[k, 0, d, 0, c, b, k, 0, j] = 1.0
            table[k, 0, d, 1, c, b, k, 1, j] = -1.0
            table[k, 1, d, 0, c, b, k, 1, j] = 1.0
            table[k, 1, d, 1, c, b, k, 0, j] = 1.0
    return table.reshape(group * 4 * total, blocks * group * 2 * per_block).astype(ml_dtypes.bfloat16)


def dot(left, right, dims=((1,), (0,))):
    return lax.dot_general(left, right, (dims, ((), ())), preferred_element_type=F32)


def spread(wide, start, stride, value):
    for t in range(wide.shape[0]):
        wide[t, pl.ds(start, value.shape[0], stride=stride), :] = value[:, t * LANES : (t + 1) * LANES]


def take(wide, start, size):
    return jnp.concatenate([wide[t, pl.ds(start, size), :] for t in range(wide.shape[0])], axis=1)


def tiled(rows, lanes):
    return pltpu.VMEM((lanes // LANES, rows, LANES), F32)


def call(kernel, out_shape, n_in, scratch=(), limit=24, flops=0, size=0, unread=0):
    whole, anywhere = pl.BlockSpec(memory_space=pltpu.VMEM), pl.BlockSpec(memory_space=pl.ANY)
    return pl.pallas_call(
        kernel,
        out_shape=out_shape,
        in_specs=[whole] * n_in + [anywhere] * unread,
        out_specs=jax.tree.map(lambda _: whole, out_shape),
        scratch_shapes=list(scratch),
        compiler_params=pltpu.CompilerParams(vmem_limit_bytes=limit * MIB),
        cost_estimate=pl.CostEstimate(flops=flops, bytes_accessed=size, transcendentals=0),
    )


def edge_kernel(per_block, orb_hbm, edge_ref, orb_ref, sems):
    local_k = orb_hbm.shape[0]
    copies = [pltpu.make_async_copy(orb_hbm.at[k], orb_ref.at[k], sems.at[k]) for k in range(local_k)]
    for copy in copies:
        copy.start()
    row = lax.broadcasted_iota(jnp.int32, (2 * per_block, LANES), 0)
    lane = lax.broadcasted_iota(jnp.int32, (2 * per_block, LANES), 1)
    one, zero = jnp.ones(row.shape, F32), jnp.zeros(row.shape, F32)
    first = jnp.where((row < per_block) & (row == lane), one, zero).astype(BF16)
    second = jnp.where((row >= per_block) & (row == lane + per_block), one, zero).astype(BF16)
    group = ROWS // (2 * per_block)
    for g in range(local_k // group):
        rows = []
        for k in range(g * group, (g + 1) * group):
            copies[k].wait()
            rows.append(
                dot(first, orb_ref[k, 0, :, :LANES], ((1,), (1,)))
                + dot(second, orb_ref[k, 1, :, :LANES], ((1,), (1,)))
            )
        edge_ref[g * ROWS : (g + 1) * ROWS] = jnp.concatenate(rows, axis=0).astype(BF16)


def coulomb_kernel(shares, coulomb_ref, _, *refs):
    outs, wide = refs[:shares], refs[shares]
    cells, columns, points = coulomb_ref.shape
    share = columns // shares
    me = lax.axis_index("ka")
    wide[...] = coulomb_ref[...].astype(F32)
    for s in range(shares):
        dest = jnp.bitwise_xor(me, s)
        start = pl.multiple_of(dest * share, share)
        for r in range(cells):
            outs[s][r] = wide[r, pl.ds(start, share), :].astype(BF16)


def tile_kernel(shares, blocks, per_block, *refs):
    edges, orb_ref, sel_ref = refs[:blocks], refs[blocks], refs[blocks + 1]
    refs = refs[blocks + 2 + shares - 1 :]
    outs = refs[:shares]
    form_ref, gathered, wide = refs[shares:]
    local_k, _, norb, points = orb_ref.shape
    group = ROWS // (2 * per_block)
    total = blocks * per_block
    share = total // shares
    rows = 2 * total
    me = lax.axis_index("ka")
    block = lax.axis_index("pts")
    for s in range(blocks):
        gathered[jnp.bitwise_xor(block, s)] = edges[s][...]
    for g in range(local_k // group):
        stacked = jnp.concatenate(
            [gathered[b, g * ROWS : (g + 1) * ROWS] for b in range(blocks)], axis=0
        )
        forms = dot(sel_ref[...], stacked).astype(BF16)
        for kk in range(group):
            k = g * group + kk
            left = forms[2 * kk * rows : (2 * kk + 1) * rows]
            right = forms[(2 * kk + 1) * rows : (2 * kk + 2) * rows]
            form = jnp.concatenate([left, right], axis=1)
            form_ref[k] = form
            tile = dot(form, orb_ref[k].reshape(2 * norb, points))
            for d in range(shares):
                for part in range(2):
                    low = (2 * d + part) * share
                    start = d * share * 2 * local_k + 2 * k + part
                    spread(wide, start, 2 * local_k, tile[low : low + share])
    size = share * 2 * local_k
    for s in range(shares):
        dest = jnp.bitwise_xor(me, s)
        outs[s][...] = take(wide, pl.multiple_of(dest * size, size), size).astype(BF16)


def transform_kernel(shares, total, share, *refs):
    tiles, coulombs = refs[:shares], refs[shares : 2 * shares]
    fwd_ref, bwd_ref = refs[2 * shares : 2 * shares + 2]
    outs = refs[2 * shares + 2 : 3 * shares + 2]
    gathered, weight, wide = refs[3 * shares + 2 :]
    local_k = total // shares
    me = lax.axis_index("ka")
    for s in range(shares):
        src = jnp.bitwise_xor(me, s)
        gathered[src] = tiles[s][...].astype(gathered.dtype)
        for r in range(local_k):
            spread(weight, src * local_k + r, total, coulombs[s][r].astype(F32))
    rows = 2 * local_k
    columns = []
    for c in range(share):
        columns.append(
            jnp.concatenate([gathered[a, c * rows : (c + 1) * rows] for a in range(shares)], axis=0).astype(BF16)
        )
    values = jnp.concatenate(columns, axis=1)
    cells = dot(fwd_ref[...], jnp.concatenate([values, values], axis=0))
    scale = jnp.concatenate([take(weight, c * total, total) for c in range(share)], axis=1)
    cells = (cells * jnp.concatenate([scale, scale], axis=0)).astype(BF16)
    kernel = dot(bwd_ref[...], jnp.concatenate([cells, cells], axis=0))
    points = kernel.shape[1] // share
    for c in range(share):
        spread(wide, c, share, kernel[:, c * points : (c + 1) * points])
    size = 2 * local_k * share
    for s in range(shares):
        dest = jnp.bitwise_xor(me, s)
        outs[s][...] = take(wide, pl.multiple_of(dest * size, size), size).astype(BF16)


def weight_kernel(shares, flip, out_rows, *refs):
    pieces, orb_ref, out_ref, gathered = refs[:shares], refs[shares], refs[shares + 1], refs[shares + 2]
    local_k, _, norb, points = orb_ref.shape
    total_rows = gathered.shape[1]
    half = total_rows // local_k // 2
    me = lax.axis_index("ka")
    core = jnp.bitwise_xor(jnp.bitwise_and(lax.axis_index("pts"), 1), flip)
    for s in range(shares):
        gathered[jnp.bitwise_xor(me, s)] = pieces[s][...]
    lanes = 2 * half * shares
    group = max(1, LANES // lanes)
    chunks = norb // out_rows // 2
    for g in range(local_k // group):
        right, left = [], []
        for kk in range(group):
            k = g * group + kk
            first, second = [], []
            for a in range(shares):
                piece = gathered[a, k * 2 * half : (k + 1) * 2 * half].astype(F32)
                first.append(piece)
                second.extend([piece[half:], -piece[:half]])
            first = jnp.concatenate(first, axis=0).astype(BF16)
            second = jnp.concatenate(second, axis=0).astype(BF16)
            zero = jnp.zeros_like(first)
            parts = [zero] * (2 * group)
            parts[2 * kk], parts[2 * kk + 1] = first, second
            right.append(jnp.concatenate(parts, axis=1))
            left.append(k)
        right = jnp.concatenate(right, axis=0)
        for z in range(chunks):
            start = pl.multiple_of((2 * z + core) * out_rows, out_rows)
            rows = jnp.concatenate(
                [orb_ref[k, part, pl.ds(start, out_rows), :] for k in left for part in range(2)], axis=1
            )
            out_ref[z, :, g * group * lanes : (g + 1) * group * lanes] = dot(
                rows, right, ((1,), (1,))
            ).astype(out_ref.dtype)


def pair_kernel(chunks, keep_ref, came_ref, own_ref, *outs):
    z = lax.shift_right_logical(lax.axis_index("pts"), 1)
    for s in range(chunks):
        dest = jnp.bitwise_xor(z, s)
        value = keep_ref[dest] + came_ref[dest].astype(F32)
        if s == 0:
            own_ref[...] = value
        else:
            outs[s - 1][...] = value.astype(BF16)


def exchange_kernel(chunks, scale, *refs):
    pieces, form_ref, out_hbm = refs[:chunks], refs[chunks], refs[chunks + 1]
    wide, out_ref, sems = refs[chunks + 2 :]
    local_k, lanes, twice = form_ref.shape
    norb = twice // 2
    out_rows = pieces[0].shape[0]
    total = pieces[0][...]
    for s in range(1, chunks):
        total = total + pieces[s][...].astype(F32)
    total = total * scale
    high = total.astype(BF16)
    low = (total - high.astype(F32)).astype(BF16)
    group = max(1, LANES // lanes)
    width = group * lanes
    lane = lax.broadcasted_iota(jnp.int32, (out_rows, width), 1)
    zero = jnp.zeros((out_rows, width), BF16)
    for g in range(local_k // group):
        high_g = high[:, g * width : (g + 1) * width]
        low_g = low[:, g * width : (g + 1) * width]
        left = []
        for kk in range(group):
            keep = (lane >= kk * lanes) & (lane < (kk + 1) * lanes)
            left.append(
                jnp.concatenate([jnp.where(keep, high_g, zero), jnp.where(keep, low_g, zero)], axis=1)
            )
        forms = [form_ref[g * group + kk] for kk in range(group)]
        result = dot(jnp.concatenate(left, axis=0), jnp.concatenate(forms + forms, axis=0))
        for kk in range(group):
            k = g * group + kk
            for part in range(2):
                value = result[kk * out_rows : (kk + 1) * out_rows, part * norb : (part + 1) * norb]
                spread(wide, 2 * k + part, 2 * local_k, value)
    steps = sems.shape[0]
    step = out_rows // steps
    copies = []
    for i in range(steps):
        rows = pl.ds(i * step, step)
        for t in range(norb // LANES):
            value = wide[t, i * step * 2 * local_k : (i + 1) * step * 2 * local_k].astype(BF16)
            out_ref[rows, :, :, t * LANES : (t + 1) * LANES] = value.reshape(step, local_k, 2, LANES)
        copies.append(pltpu.make_async_copy(out_ref.at[rows], out_hbm.at[rows], sems.at[i]))
        copies[-1].start()
    for copy in copies:
        copy.wait()


def swap(value, axis, mask):
    size = lax.axis_size(axis)
    return lax.ppermute(value, axis, [(i, i ^ mask) for i in range(size)])


def body(orbitals, coulomb):
    shares, blocks = lax.axis_size("ka"), lax.axis_size("pts")
    local_k, _, norb, points = orbitals.shape
    columns = coulomb.shape[1]
    per_block = columns // blocks
    share = columns // shares
    total = local_k * shares
    out_rows = norb // blocks
    chunks = blocks // 2
    group = ROWS // (2 * per_block)
    shape = jax.ShapeDtypeStruct

    vmem, anywhere = pl.BlockSpec(memory_space=pltpu.VMEM), pl.BlockSpec(memory_space=pl.ANY)
    edge, orbitals = pl.pallas_call(
        functools.partial(edge_kernel, per_block),
        out_shape=[shape((local_k * 2 * per_block, norb), BF16), shape(orbitals.shape, BF16)],
        in_specs=[pl.BlockSpec(memory_space=pltpu.HBM)],
        out_specs=[vmem, vmem],
        scratch_shapes=[pltpu.SemaphoreType.DMA((local_k,))],
        compiler_params=pltpu.CompilerParams(vmem_limit_bytes=57 * MIB),
        cost_estimate=pl.CostEstimate(flops=0, bytes_accessed=8 * MIB, transcendentals=0),
    )(orbitals)
    edges = [edge] + [None] * (blocks - 1)
    for s in range(1, chunks):
        edges[2 * s] = swap(edge, "pts", 2 * s)
    for s in range(chunks):
        edges[2 * s + 1] = swap(edges[2 * s], "pts", 1)

    own = call(
        functools.partial(coulomb_kernel, shares),
        [shape((local_k, share, points), BF16)] * shares,
        1,
        [pltpu.VMEM((local_k, columns, points), F32)],
        size=2 * MIB,
        unread=1,
    )(coulomb, edges[1])
    coulombs = [own[0]] + [swap(own[s], "ka", s) for s in range(1, shares)]

    selector = jnp.asarray(column_selector(group, blocks, per_block, shares))
    piece = shape((share * 2 * local_k, points), BF16)
    *tiles, forms = call(
        functools.partial(tile_kernel, shares, blocks, per_block),
        [piece] * shares + [shape((local_k, 2 * columns, 2 * norb), BF16)],
        blocks + 2,
        [
            pltpu.VMEM((blocks, local_k * 2 * per_block, norb), BF16),
            tiled(columns * 2 * local_k, points),
        ],
        size=8 * MIB,
        unread=shares - 1,
    )(*edges, orbitals, selector, *coulombs[1:])
    tiles = [tiles[0]] + [swap(tiles[s], "ka", s) for s in range(1, shares)]

    forward, backward = phase_tables(total)
    kernels = call(
        functools.partial(transform_kernel, shares, total, share),
        [piece] * shares,
        2 * shares + 2,
        [
            pltpu.VMEM((shares, share * 2 * local_k, points), BF16 if local_k % 8 == 0 else F32),
            tiled(share * total, points),
            tiled(2 * total * share, points),
        ],
        size=2 * MIB,
    )(*tiles, *coulombs, jnp.asarray(forward), jnp.asarray(backward))
    kernels = [kernels[0]] + [swap(kernels[s], "ka", s) for s in range(1, shares)]

    lanes = local_k * 2 * columns
    halves = []
    for flip, kind in ((1, BF16), (0, F32)):
        halves.append(
            call(
                functools.partial(weight_kernel, shares, flip, out_rows),
                shape((chunks, out_rows, lanes), kind),
                shares + 1,
                [pltpu.VMEM((shares, share * 2 * local_k, points), BF16)],
                size=6 * MIB,
            )(*kernels, orbitals)
        )
    came = swap(halves[0], "pts", 1)
    own_sum, *sums = call(
        functools.partial(pair_kernel, chunks),
        [shape((out_rows, lanes), F32)] + [shape((out_rows, lanes), BF16)] * (chunks - 1),
        2,
        size=1 * MIB,
    )(halves[1], came)
    sums = [own_sum] + [swap(sums[s - 1], "pts", 2 * s) for s in range(1, chunks)]
    return pl.pallas_call(
        functools.partial(exchange_kernel, chunks, 1.0 / math.sqrt(points * blocks)),
        out_shape=shape((out_rows, local_k, 2, norb), BF16),
        in_specs=[vmem] * (chunks + 1),
        out_specs=pl.BlockSpec(memory_space=pltpu.HBM),
        scratch_shapes=[
            tiled(out_rows * 2 * local_k, norb),
            pltpu.VMEM((out_rows, local_k, 2, norb), BF16),
            pltpu.SemaphoreType.DMA((4,)),
        ],
        compiler_params=pltpu.CompilerParams(vmem_limit_bytes=24 * MIB),
        cost_estimate=pl.CostEstimate(flops=0, bytes_accessed=4 * MIB, transcendentals=0),
    )(*sums, forms)


def solution(mesh):
    in_specs = (P("ka", None, None, "pts"), P("ka", None, "pts"))
    out_specs = P("pts", "ka", None, None)
    return jax.shard_map(body, mesh=mesh, in_specs=in_specs, out_specs=out_specs, check_vma=False)
```

```python
import functools
import math

import jax
import jax.numpy as jnp
import ml_dtypes
import numpy as np
from jax import lax
from jax.experimental import pallas as pl
from jax.experimental.pallas import tpu as pltpu
from jax.sharding import PartitionSpec as P

BF16 = jnp.bfloat16
F32 = jnp.float32
LANES = 128
ROWS = 16
MIB = 1 << 20


def split_terms(table):
    high = table.astype(ml_dtypes.bfloat16)
    low = (table - high.astype(np.float64)).astype(ml_dtypes.bfloat16)
    return np.concatenate([high, low], axis=1)


def phase_tables(total):
    index = np.arange(total)
    angles = (index[:, None] * index[None, :] % total) * (2.0 * math.pi / total)
    cosine, sine = np.cos(angles), np.sin(angles)
    forward = np.zeros((2, total, total, 2))
    forward[0, :, :, 0] = cosine
    forward[0, :, :, 1] = -sine
    forward[1, :, :, 0] = sine
    forward[1, :, :, 1] = cosine
    backward = np.zeros((total, 2, 2, total))
    backward[:, 0, 0] = cosine
    backward[:, 0, 1] = sine
    backward[:, 1, 1] = cosine
    backward[:, 1, 0] = -sine
    size = 2 * total
    return (
        split_terms(forward.reshape(size, size)),
        split_terms(backward.reshape(size, size) / total),
    )


def column_selector(group, blocks, per_block, shares):
    total = blocks * per_block
    share = total // shares
    table = np.zeros((group, 2, shares, 2, share, blocks, group, 2, per_block), np.float32)
    for k in range(group):
        for col in range(total):
            d, c = divmod(col, share)
            b, j = divmod(col, per_block)
            table[k, 0, d, 0, c, b, k, 0, j] = 1.0
            table[k, 0, d, 1, c, b, k, 1, j] = -1.0
            table[k, 1, d, 0, c, b, k, 1, j] = 1.0
            table[k, 1, d, 1, c, b, k, 0, j] = 1.0
    return table.reshape(group * 4 * total, blocks * group * 2 * per_block).astype(ml_dtypes.bfloat16)


def dot(left, right, dims=((1,), (0,))):
    return lax.dot_general(left, right, (dims, ((), ())), preferred_element_type=F32)


def spread(wide, start, stride, value):
    for t in range(wide.shape[0]):
        wide[t, pl.ds(start, value.shape[0], stride=stride), :] = value[:, t * LANES : (t + 1) * LANES]


def take(wide, start, size):
    return jnp.concatenate([wide[t, pl.ds(start, size), :] for t in range(wide.shape[0])], axis=1)


def tiled(rows, lanes):
    return pltpu.VMEM((lanes // LANES, rows, LANES), F32)


def call(kernel, out_shape, n_in, scratch=(), limit=24, flops=0, size=0):
    whole = pl.BlockSpec(memory_space=pltpu.VMEM)
    return pl.pallas_call(
        kernel,
        out_shape=out_shape,
        in_specs=[whole] * n_in,
        out_specs=jax.tree.map(lambda _: whole, out_shape),
        scratch_shapes=list(scratch),
        compiler_params=pltpu.CompilerParams(vmem_limit_bytes=limit * MIB),
        cost_estimate=pl.CostEstimate(flops=flops, bytes_accessed=size, transcendentals=0),
    )


def edge_kernel(per_block, orb_ref, edge_ref):
    local_k = orb_ref.shape[0]
    row = lax.broadcasted_iota(jnp.int32, (2 * per_block, LANES), 0)
    lane = lax.broadcasted_iota(jnp.int32, (2 * per_block, LANES), 1)
    one, zero = jnp.ones(row.shape, F32), jnp.zeros(row.shape, F32)
    first = jnp.where((row < per_block) & (row == lane), one, zero).astype(BF16)
    second = jnp.where((row >= per_block) & (row == lane + per_block), one, zero).astype(BF16)
    group = ROWS // (2 * per_block)
    for g in range(local_k // group):
        rows = []
        for k in range(g * group, (g + 1) * group):
            rows.append(
                dot(first, orb_ref[k, 0, :, :LANES], ((1,), (1,)))
                + dot(second, orb_ref[k, 1, :, :LANES], ((1,), (1,)))
            )
        edge_ref[g * ROWS : (g + 1) * ROWS] = jnp.concatenate(rows, axis=0).astype(BF16)


def tile_kernel(shares, blocks, per_block, *refs):
    edges, orb_ref, sel_ref, coulomb_ref = refs[:blocks], refs[blocks], refs[blocks + 1], refs[blocks + 2]
    outs, (form_ref, gathered, wide, cells) = refs[blocks + 3 : blocks + 3 + shares], refs[blocks + 3 + shares :]
    local_k, _, norb, points = orb_ref.shape
    group = ROWS // (2 * per_block)
    total = blocks * per_block
    share = total // shares
    rows = 2 * total
    me = lax.axis_index("ka")
    block = lax.axis_index("pts")
    cells[...] = coulomb_ref[...].astype(F32)
    for s in range(blocks):
        gathered[jnp.bitwise_xor(block, s)] = edges[s][...]
    for g in range(local_k // group):
        stacked = jnp.concatenate(
            [gathered[b, g * ROWS : (g + 1) * ROWS] for b in range(blocks)], axis=0
        )
        forms = dot(sel_ref[...], stacked).astype(BF16)
        for kk in range(group):
            k = g * group + kk
            left = forms[2 * kk * rows : (2 * kk + 1) * rows]
            right = forms[(2 * kk + 1) * rows : (2 * kk + 2) * rows]
            form = jnp.concatenate([left, right], axis=1)
            form_ref[k] = form
            tile = dot(form, orb_ref[k].reshape(2 * norb, points))
            for d in range(shares):
                for part in range(2):
                    low = (2 * d + part) * share
                    start = d * share * 2 * local_k + 2 * k + part
                    spread(wide, start, 2 * local_k, tile[low : low + share])
    size = share * 2 * local_k
    for s in range(shares):
        dest = jnp.bitwise_xor(me, s)
        outs[s][:size] = take(wide, pl.multiple_of(dest * size, size), size).astype(BF16)
        start = pl.multiple_of(dest * share, share)
        pair = [cells[r, pl.ds(start, share), :] for r in range(local_k)]
        outs[s][size:] = jnp.concatenate(pair, axis=0).astype(BF16)


def transform_kernel(shares, total, share, *refs):
    tiles, (fwd_ref, bwd_ref) = refs[:shares][::-1], refs[shares : shares + 2]
    outs, (gathered, weight, wide) = refs[shares + 2 : 2 * shares + 2], refs[2 * shares + 2 :]
    local_k = total // shares
    size = 2 * local_k * share
    me = lax.axis_index("ka")
    for s in range(shares):
        src = jnp.bitwise_xor(me, s)
        gathered[src] = tiles[s][:size].astype(gathered.dtype)
        cells = tiles[s][size:].astype(F32)
        for r in range(local_k):
            spread(weight, src * local_k + r, total, cells[r * share : (r + 1) * share])
    rows = 2 * local_k
    columns = []
    for c in range(share):
        columns.append(
            jnp.concatenate([gathered[a, c * rows : (c + 1) * rows] for a in range(shares)], axis=0).astype(BF16)
        )
    values = jnp.concatenate(columns, axis=1)
    cells = dot(fwd_ref[...], jnp.concatenate([values, values], axis=0))
    scale = jnp.concatenate([take(weight, c * total, total) for c in range(share)], axis=1)
    cells = (cells * jnp.concatenate([scale, scale], axis=0)).astype(BF16)
    kernel = dot(bwd_ref[...], jnp.concatenate([cells, cells], axis=0))
    points = kernel.shape[1] // share
    for c in range(share):
        spread(wide, c, share, kernel[:, c * points : (c + 1) * points])
    for s in range(shares):
        dest = jnp.bitwise_xor(me, s)
        outs[s][...] = take(wide, pl.multiple_of(dest * size, size), size).astype(BF16)


def weight_kernel(shares, flip, out_rows, *refs):
    pieces, orb_ref, out_ref, gathered = refs[:shares][::-1], refs[shares], refs[shares + 1], refs[shares + 2]
    local_k, _, norb, points = orb_ref.shape
    total_rows = gathered.shape[1]
    half = total_rows // local_k // 2
    me = lax.axis_index("ka")
    core = jnp.bitwise_xor(jnp.bitwise_and(lax.axis_index("pts"), 1), flip)
    for s in range(shares):
        gathered[jnp.bitwise_xor(me, s)] = pieces[s][...]
    lanes = 2 * half * shares
    group = max(1, LANES // lanes)
    chunks = norb // out_rows // 2
    for g in range(local_k // group):
        right, left = [], []
        for kk in range(group):
            k = g * group + kk
            first, second = [], []
            for a in range(shares):
                piece = gathered[a, k * 2 * half : (k + 1) * 2 * half].astype(F32)
                first.append(piece)
                second.extend([piece[half:], -piece[:half]])
            first = jnp.concatenate(first, axis=0).astype(BF16)
            second = jnp.concatenate(second, axis=0).astype(BF16)
            zero = jnp.zeros_like(first)
            parts = [zero] * (2 * group)
            parts[2 * kk], parts[2 * kk + 1] = first, second
            right.append(jnp.concatenate(parts, axis=1))
            left.append(k)
        right = jnp.concatenate(right, axis=0)
        for z in range(chunks):
            start = pl.multiple_of((2 * z + core) * out_rows, out_rows)
            rows = jnp.concatenate(
                [orb_ref[k, part, pl.ds(start, out_rows), :] for k in left for part in range(2)], axis=1
            )
            out_ref[z, :, g * group * lanes : (g + 1) * group * lanes] = dot(
                rows, right, ((1,), (1,))
            ).astype(out_ref.dtype)


def pair_kernel(chunks, keep_ref, came_ref, own_ref, *outs):
    z = lax.shift_right_logical(lax.axis_index("pts"), 1)
    for s in range(chunks):
        dest = jnp.bitwise_xor(z, s)
        value = keep_ref[dest] + came_ref[dest].astype(F32)
        if s == 0:
            own_ref[...] = value
        else:
            outs[s - 1][...] = value.astype(BF16)


def exchange_kernel(chunks, scale, *refs):
    pieces, form_ref, out_ref, wide = refs[:chunks][::-1], refs[chunks], refs[chunks + 1], refs[chunks + 2]
    local_k, lanes, twice = form_ref.shape
    norb = twice // 2
    spans = norb // LANES
    out_rows = pieces[0].shape[0]
    total = pieces[0][...]
    for s in range(1, chunks):
        total = total + pieces[s][...].astype(F32)
    total = total * scale
    high = total.astype(BF16)
    low = (total - high.astype(F32)).astype(BF16)
    group = max(1, LANES // lanes)
    width = group * lanes
    lane = lax.broadcasted_iota(jnp.int32, (out_rows, width), 1)
    zero = jnp.zeros((out_rows, width), BF16)
    for g in range(local_k // group):
        high_g = high[:, g * width : (g + 1) * width]
        low_g = low[:, g * width : (g + 1) * width]
        left = []
        for kk in range(group):
            keep = (lane >= kk * lanes) & (lane < (kk + 1) * lanes)
            left.append(
                jnp.concatenate([jnp.where(keep, high_g, zero), jnp.where(keep, low_g, zero)], axis=1)
            )
        forms = [form_ref[g * group + kk] for kk in range(group)]
        result = dot(jnp.concatenate(left, axis=0), jnp.concatenate(forms + forms, axis=0))
        for kk in range(group):
            k = g * group + kk
            for part in range(2):
                for t in range(spans):
                    lane_start = part * norb + t * LANES
                    value = result[kk * out_rows : (kk + 1) * out_rows, lane_start : lane_start + LANES]
                    start = (k * spans + t) * 2 + part
                    wide[pl.ds(start, out_rows, stride=2 * spans * local_k), :] = value
    out_ref[...] = wide[...].astype(BF16)


def swap(value, axis, mask):
    size = lax.axis_size(axis)
    return lax.ppermute(value, axis, [(i, i ^ mask) for i in range(size)])


def trade(pieces, axis, step):
    return [swap(pieces[s], axis, s * step) for s in reversed(range(1, len(pieces)))] + [pieces[0]]


def body(orbitals, coulomb):
    shares, blocks = lax.axis_size("ka"), lax.axis_size("pts")
    local_k, _, norb, points = orbitals.shape
    columns = coulomb.shape[1]
    per_block = columns // blocks
    share = columns // shares
    total = local_k * shares
    out_rows = norb // blocks
    chunks = blocks // 2
    group = ROWS // (2 * per_block)
    shape = jax.ShapeDtypeStruct

    edge = call(
        functools.partial(edge_kernel, per_block),
        shape((local_k * 2 * per_block, norb), BF16),
        1,
        size=4 * MIB,
    )(orbitals)
    edges = [edge] + [None] * (blocks - 1)
    for s in range(1, chunks):
        edges[2 * s] = swap(edge, "pts", 2 * s)
    for s in range(chunks):
        edges[2 * s + 1] = swap(edges[2 * s], "pts", 1)

    selector = jnp.asarray(column_selector(group, blocks, per_block, shares))
    piece = shape((share * 2 * local_k, points), BF16)
    both = shape((share * 3 * local_k, points), BF16)
    *tiles, forms = call(
        functools.partial(tile_kernel, shares, blocks, per_block),
        [both] * shares + [shape((local_k, 2 * columns, 2 * norb), BF16)],
        blocks + 3,
        [
            pltpu.VMEM((blocks, local_k * 2 * per_block, norb), BF16),
            tiled(columns * 2 * local_k, points),
            pltpu.VMEM((local_k, columns, points), F32),
        ],
        size=8 * MIB,
    )(*edges, orbitals, selector, coulomb)
    tiles = trade(tiles, "ka", 1)

    forward, backward = phase_tables(total)
    kernels = call(
        functools.partial(transform_kernel, shares, total, share),
        [piece] * shares,
        shares + 2,
        [
            pltpu.VMEM((shares, share * 2 * local_k, points), BF16 if local_k % 8 == 0 else F32),
            tiled(share * total, points),
            tiled(2 * total * share, points),
        ],
        size=2 * MIB,
    )(*tiles, jnp.asarray(forward), jnp.asarray(backward))
    kernels = trade(kernels, "ka", 1)

    lanes = local_k * 2 * columns
    halves = []
    for flip, kind in ((1, BF16), (0, F32)):
        halves.append(
            call(
                functools.partial(weight_kernel, shares, flip, out_rows),
                shape((chunks, out_rows, lanes), kind),
                shares + 1,
                [pltpu.VMEM((shares, share * 2 * local_k, points), BF16)],
                size=6 * MIB,
            )(*kernels, orbitals)
        )
    came = swap(halves[0], "pts", 1)
    own_sum, *sums = call(
        functools.partial(pair_kernel, chunks),
        [shape((out_rows, lanes), F32)] + [shape((out_rows, lanes), BF16)] * (chunks - 1),
        2,
        size=1 * MIB,
    )(halves[1], came)
    sums = trade([own_sum, *sums], "pts", 2)
    spans = norb // LANES
    rows = out_rows * local_k * spans * 2
    result = call(
        functools.partial(exchange_kernel, chunks, 1.0 / math.sqrt(points * blocks)),
        shape((rows, LANES), BF16),
        chunks + 1,
        [pltpu.VMEM((rows, LANES), F32)],
        size=4 * MIB,
    )(*sums, forms)
    result = result.reshape(out_rows, local_k, spans, 2, LANES)
    return result.transpose(0, 1, 3, 2, 4).reshape(out_rows, local_k, 2, norb)


def solution(mesh):
    in_specs = (P("ka", None, None, "pts"), P("ka", None, "pts"))
    out_specs = P("pts", "ka", None, None)
    return jax.shard_map(body, mesh=mesh, in_specs=in_specs, out_specs=out_specs, check_vma=False)
```

```python
import functools
import math

import jax
import jax.numpy as jnp
import ml_dtypes
import numpy as np
from jax import lax
from jax.experimental import pallas as pl
from jax.experimental.pallas import tpu as pltpu
from jax.sharding import PartitionSpec as P

BF16 = jnp.bfloat16
F32 = jnp.float32
LANES = 128
ROWS = 16
MIB = 1 << 20


def split_terms(table):
    high = table.astype(ml_dtypes.bfloat16)
    low = (table - high.astype(np.float64)).astype(ml_dtypes.bfloat16)
    return np.concatenate([high, low], axis=1)


def phase_tables(total):
    index = np.arange(total)
    angles = (index[:, None] * index[None, :] % total) * (2.0 * math.pi / total)
    cosine, sine = np.cos(angles), np.sin(angles)
    forward = np.zeros((2, total, total, 2))
    forward[0, :, :, 0] = cosine
    forward[0, :, :, 1] = -sine
    forward[1, :, :, 0] = sine
    forward[1, :, :, 1] = cosine
    backward = np.zeros((total, 2, 2, total))
    backward[:, 0, 0] = cosine
    backward[:, 0, 1] = sine
    backward[:, 1, 1] = cosine
    backward[:, 1, 0] = -sine
    size = 2 * total
    return (
        split_terms(forward.reshape(size, size)),
        split_terms(backward.reshape(size, size) / total),
    )


def column_selector(group, blocks, per_block, shares):
    total = blocks * per_block
    share = total // shares
    table = np.zeros((group, 2, shares, 2, share, blocks, group, 2, per_block), np.float32)
    for k in range(group):
        for col in range(total):
            d, c = divmod(col, share)
            b, j = divmod(col, per_block)
            table[k, 0, d, 0, c, b, k, 0, j] = 1.0
            table[k, 0, d, 1, c, b, k, 1, j] = -1.0
            table[k, 1, d, 0, c, b, k, 1, j] = 1.0
            table[k, 1, d, 1, c, b, k, 0, j] = 1.0
    return table.reshape(group * 4 * total, blocks * group * 2 * per_block).astype(ml_dtypes.bfloat16)


def dot(left, right, dims=((1,), (0,))):
    return lax.dot_general(left, right, (dims, ((), ())), preferred_element_type=F32)


def spread(wide, start, stride, value):
    for t in range(wide.shape[0]):
        wide[t, pl.ds(start, value.shape[0], stride=stride), :] = value[:, t * LANES : (t + 1) * LANES]


def take(wide, start, size):
    return jnp.concatenate([wide[t, pl.ds(start, size), :] for t in range(wide.shape[0])], axis=1)


def tiled(rows, lanes):
    return pltpu.VMEM((lanes // LANES, rows, LANES), F32)


def call(kernel, out_shape, n_in, scratch=(), limit=24, flops=0, size=0, more=(), result=pltpu.VMEM):
    whole = pl.BlockSpec(memory_space=pltpu.VMEM)
    return pl.pallas_call(
        kernel,
        out_shape=out_shape,
        in_specs=[whole] * n_in + [pl.BlockSpec(memory_space=place) for place in more],
        out_specs=jax.tree.map(lambda _: pl.BlockSpec(memory_space=result), out_shape),
        scratch_shapes=list(scratch),
        compiler_params=pltpu.CompilerParams(vmem_limit_bytes=limit * MIB),
        cost_estimate=pl.CostEstimate(flops=flops, bytes_accessed=size, transcendentals=0),
    )


def edge_kernel(per_block, orb_hbm, edge_ref, orb_ref, sems):
    local_k = orb_hbm.shape[0]
    copies = [pltpu.make_async_copy(orb_hbm.at[k], orb_ref.at[k], sems.at[k]) for k in range(local_k)]
    for copy in copies:
        copy.start()
    row = lax.broadcasted_iota(jnp.int32, (2 * per_block, LANES), 0)
    lane = lax.broadcasted_iota(jnp.int32, (2 * per_block, LANES), 1)
    one, zero = jnp.ones(row.shape, F32), jnp.zeros(row.shape, F32)
    first = jnp.where((row < per_block) & (row == lane), one, zero).astype(BF16)
    second = jnp.where((row >= per_block) & (row == lane + per_block), one, zero).astype(BF16)
    group = ROWS // (2 * per_block)
    for g in range(local_k // group):
        rows = []
        for k in range(g * group, (g + 1) * group):
            copies[k].wait()
            rows.append(
                dot(first, orb_ref[k, 0, :, :LANES], ((1,), (1,)))
                + dot(second, orb_ref[k, 1, :, :LANES], ((1,), (1,)))
            )
        edge_ref[g * ROWS : (g + 1) * ROWS] = jnp.concatenate(rows, axis=0).astype(BF16)


def coulomb_kernel(shares, coulomb_ref, edge_ref, _, out_ref, own_ref, wide):
    cells, columns, points = coulomb_ref.shape
    share = columns // shares
    me = lax.axis_index("ka")
    own_ref[...] = edge_ref[...]
    wide[...] = coulomb_ref[...].astype(F32)
    for s in range(shares):
        start = pl.multiple_of(jnp.bitwise_xor(me, s) * share, share)
        pieces = [wide[r, pl.ds(start, share), :] for r in range(cells)]
        out_ref[s] = jnp.concatenate(pieces, axis=0).astype(BF16)


def tile_kernel(shares, blocks, per_block, *refs):
    edges, orb_ref, sel_ref, coulomb_ref = refs[:blocks], refs[blocks], refs[blocks + 1], refs[blocks + 2]
    outs, (form_ref, gathered, wide) = refs[blocks + 3 : blocks + 3 + shares], refs[blocks + 3 + shares :]
    local_k, _, norb, points = orb_ref.shape
    group = ROWS // (2 * per_block)
    total = blocks * per_block
    share = total // shares
    rows = 2 * total
    me = lax.axis_index("ka")
    block = lax.axis_index("pts")
    for s in range(blocks):
        gathered[jnp.bitwise_xor(block, s)] = edges[s][...]
    for g in range(local_k // group):
        stacked = jnp.concatenate(
            [gathered[b, g * ROWS : (g + 1) * ROWS] for b in range(blocks)], axis=0
        )
        forms = dot(sel_ref[...], stacked).astype(BF16)
        for kk in range(group):
            k = g * group + kk
            left = forms[2 * kk * rows : (2 * kk + 1) * rows]
            right = forms[(2 * kk + 1) * rows : (2 * kk + 2) * rows]
            form = jnp.concatenate([left, right], axis=1)
            form_ref[k] = form
            tile = dot(form, orb_ref[k].reshape(2 * norb, points))
            for d in range(shares):
                for part in range(2):
                    low = (2 * d + part) * share
                    start = d * share * 2 * local_k + 2 * k + part
                    spread(wide, start, 2 * local_k, tile[low : low + share])
    size = share * 2 * local_k
    for s in range(shares):
        dest = jnp.bitwise_xor(me, s)
        outs[s][:size] = take(wide, pl.multiple_of(dest * size, size), size).astype(BF16)
        outs[s][size:] = coulomb_ref[s]


def transform_kernel(shares, total, share, *refs):
    tiles, (fwd_ref, bwd_ref) = refs[:shares][::-1], refs[shares : shares + 2]
    outs, (gathered, weight, wide) = refs[shares + 2 : 2 * shares + 2], refs[2 * shares + 2 :]
    local_k = total // shares
    size = 2 * local_k * share
    me = lax.axis_index("ka")
    for s in range(shares):
        src = jnp.bitwise_xor(me, s)
        gathered[src] = tiles[s][:size].astype(gathered.dtype)
        cells = tiles[s][size:].astype(F32)
        for r in range(local_k):
            spread(weight, src * local_k + r, total, cells[r * share : (r + 1) * share])
    rows = 2 * local_k
    columns = []
    for c in range(share):
        columns.append(
            jnp.concatenate([gathered[a, c * rows : (c + 1) * rows] for a in range(shares)], axis=0).astype(BF16)
        )
    values = jnp.concatenate(columns, axis=1)
    cells = dot(fwd_ref[...], jnp.concatenate([values, values], axis=0))
    scale = jnp.concatenate([take(weight, c * total, total) for c in range(share)], axis=1)
    cells = (cells * jnp.concatenate([scale, scale], axis=0)).astype(BF16)
    kernel = dot(bwd_ref[...], jnp.concatenate([cells, cells], axis=0))
    points = kernel.shape[1] // share
    for c in range(share):
        spread(wide, c, share, kernel[:, c * points : (c + 1) * points])
    for s in range(shares):
        dest = jnp.bitwise_xor(me, s)
        outs[s][...] = take(wide, pl.multiple_of(dest * size, size), size).astype(BF16)


def weight_kernel(shares, flip, out_rows, *refs):
    pieces, orb_ref, out_ref, gathered = refs[:shares][::-1], refs[shares], refs[shares + 1], refs[shares + 2]
    local_k, _, norb, points = orb_ref.shape
    total_rows = gathered.shape[1]
    half = total_rows // local_k // 2
    me = lax.axis_index("ka")
    core = jnp.bitwise_xor(jnp.bitwise_and(lax.axis_index("pts"), 1), flip)
    for s in range(shares):
        gathered[jnp.bitwise_xor(me, s)] = pieces[s][...]
    lanes = 2 * half * shares
    group = max(1, LANES // lanes)
    chunks = norb // out_rows // 2
    for g in range(local_k // group):
        right, left = [], []
        for kk in range(group):
            k = g * group + kk
            first, second = [], []
            for a in range(shares):
                piece = gathered[a, k * 2 * half : (k + 1) * 2 * half].astype(F32)
                first.append(piece)
                second.extend([piece[half:], -piece[:half]])
            first = jnp.concatenate(first, axis=0).astype(BF16)
            second = jnp.concatenate(second, axis=0).astype(BF16)
            zero = jnp.zeros_like(first)
            parts = [zero] * (2 * group)
            parts[2 * kk], parts[2 * kk + 1] = first, second
            right.append(jnp.concatenate(parts, axis=1))
            left.append(k)
        right = jnp.concatenate(right, axis=0)
        for z in range(chunks):
            start = pl.multiple_of((2 * z + core) * out_rows, out_rows)
            rows = jnp.concatenate(
                [orb_ref[k, part, pl.ds(start, out_rows), :] for k in left for part in range(2)], axis=1
            )
            out_ref[z, :, g * group * lanes : (g + 1) * group * lanes] = dot(
                rows, right, ((1,), (1,))
            ).astype(out_ref.dtype)


def pair_kernel(chunks, keep_ref, came_ref, own_ref, *outs):
    z = lax.shift_right_logical(lax.axis_index("pts"), 1)
    for s in range(chunks):
        dest = jnp.bitwise_xor(z, s)
        value = keep_ref[dest] + came_ref[dest].astype(F32)
        if s == 0:
            own_ref[...] = value
        else:
            outs[s - 1][...] = value.astype(BF16)


def exchange_kernel(chunks, scale, *refs):
    pieces, form_ref, out_hbm = refs[:chunks][::-1], refs[chunks], refs[chunks + 1]
    wide, out_ref, sems = refs[chunks + 2 :]
    local_k, lanes, twice = form_ref.shape
    norb = twice // 2
    spans = norb // LANES
    out_rows = pieces[0].shape[0]
    total = pieces[0][...]
    for s in range(1, chunks):
        total = total + pieces[s][...].astype(F32)
    total = total * scale
    high = total.astype(BF16)
    low = (total - high.astype(F32)).astype(BF16)
    group = max(1, LANES // lanes)
    width = group * lanes
    lane = lax.broadcasted_iota(jnp.int32, (out_rows, width), 1)
    zero = jnp.zeros((out_rows, width), BF16)
    copies = []
    for g in range(local_k // group):
        high_g = high[:, g * width : (g + 1) * width]
        low_g = low[:, g * width : (g + 1) * width]
        left = []
        for kk in range(group):
            keep = (lane >= kk * lanes) & (lane < (kk + 1) * lanes)
            left.append(
                jnp.concatenate([jnp.where(keep, high_g, zero), jnp.where(keep, low_g, zero)], axis=1)
            )
        forms = [form_ref[g * group + kk] for kk in range(group)]
        result = dot(jnp.concatenate(left, axis=0), jnp.concatenate(forms + forms, axis=0))
        for kk in range(group):
            for part in range(2):
                for t in range(spans):
                    lane_start = part * norb + t * LANES
                    value = result[kk * out_rows : (kk + 1) * out_rows, lane_start : lane_start + LANES]
                    start = (kk * spans + t) * 2 + part
                    wide[g, pl.ds(start, out_rows, stride=2 * spans * group), :] = value
        out_ref[g] = wide[g].astype(BF16).reshape(out_ref.shape[1:])
        copies.append(pltpu.make_async_copy(out_ref.at[g], out_hbm.at[:, g], sems.at[g]))
        copies[-1].start()
    for copy in copies:
        copy.wait()


def swap(value, axis, mask):
    size = lax.axis_size(axis)
    return lax.ppermute(value, axis, [(i, i ^ mask) for i in range(size)])


def trade(pieces, axis, step):
    return [swap(pieces[s], axis, s * step) for s in reversed(range(1, len(pieces)))] + [pieces[0]]


def body(orbitals, coulomb):
    shares, blocks = lax.axis_size("ka"), lax.axis_size("pts")
    local_k, _, norb, points = orbitals.shape
    columns = coulomb.shape[1]
    per_block = columns // blocks
    share = columns // shares
    total = local_k * shares
    out_rows = norb // blocks
    chunks = blocks // 2
    group = ROWS // (2 * per_block)
    shape = jax.ShapeDtypeStruct

    edge = call(
        functools.partial(edge_kernel, per_block),
        shape((local_k * 2 * per_block, norb), BF16),
        0,
        [pltpu.VMEM(orbitals.shape, BF16), pltpu.SemaphoreType.DMA((local_k,))],
        limit=57,
        size=4 * MIB,
        more=[pltpu.HBM],
    )(orbitals)
    edges = [edge] + [None] * (blocks - 1)
    for s in range(1, chunks):
        edges[2 * s] = swap(edge, "pts", 2 * s)
    for s in range(chunks):
        edges[2 * s + 1] = swap(edges[2 * s], "pts", 1)

    coulombs, edges[0] = call(
        functools.partial(coulomb_kernel, shares),
        [shape((shares, local_k * share, points), BF16), shape(edge.shape, BF16)],
        2,
        [pltpu.VMEM(coulomb.shape, F32)],
        size=1 * MIB,
        more=[pl.ANY],
    )(coulomb, edge, edges[1])

    selector = jnp.asarray(column_selector(group, blocks, per_block, shares))
    piece = shape((share * 2 * local_k, points), BF16)
    both = shape((share * 3 * local_k, points), BF16)
    *tiles, forms = call(
        functools.partial(tile_kernel, shares, blocks, per_block),
        [both] * shares + [shape((local_k, 2 * columns, 2 * norb), BF16)],
        blocks + 3,
        [
            pltpu.VMEM((blocks, local_k * 2 * per_block, norb), BF16),
            tiled(columns * 2 * local_k, points),
        ],
        size=8 * MIB,
    )(*edges, orbitals, selector, coulombs)
    tiles = trade(tiles, "ka", 1)

    forward, backward = phase_tables(total)
    kernels = call(
        functools.partial(transform_kernel, shares, total, share),
        [piece] * shares,
        shares + 2,
        [
            pltpu.VMEM((shares, share * 2 * local_k, points), BF16 if local_k % 8 == 0 else F32),
            tiled(share * total, points),
            tiled(2 * total * share, points),
        ],
        size=2 * MIB,
    )(*tiles, jnp.asarray(forward), jnp.asarray(backward))
    kernels = trade(kernels, "ka", 1)

    lanes = local_k * 2 * columns
    halves = []
    for flip, kind in ((1, BF16), (0, F32)):
        halves.append(
            call(
                functools.partial(weight_kernel, shares, flip, out_rows),
                shape((chunks, out_rows, lanes), kind),
                shares + 1,
                [pltpu.VMEM((shares, share * 2 * local_k, points), BF16)],
                size=6 * MIB,
            )(*kernels, orbitals)
        )
    came = swap(halves[0], "pts", 1)
    own_sum, *sums = call(
        functools.partial(pair_kernel, chunks),
        [shape((out_rows, lanes), F32)] + [shape((out_rows, lanes), BF16)] * (chunks - 1),
        2,
        size=1 * MIB,
    )(halves[1], came)
    sums = trade([own_sum, *sums], "pts", 2)
    spans = norb // LANES
    pair = max(1, LANES // (2 * columns))
    rows = pair * spans * 2
    result = call(
        functools.partial(exchange_kernel, chunks, 1.0 / math.sqrt(points * blocks)),
        shape((out_rows, local_k // pair, rows, LANES), BF16),
        chunks + 1,
        [
            pltpu.VMEM((local_k // pair, out_rows * rows, LANES), F32),
            pltpu.VMEM((local_k // pair, out_rows, rows, LANES), BF16),
            pltpu.SemaphoreType.DMA((local_k // pair,)),
        ],
        size=4 * MIB,
        result=pltpu.HBM,
    )(*sums, forms)
    result = result.reshape(out_rows, local_k, spans, 2, LANES)
    return result.transpose(0, 1, 3, 2, 4).reshape(out_rows, local_k, 2, norb)


def solution(mesh):
    in_specs = (P("ka", None, None, "pts"), P("ka", None, "pts"))
    out_specs = P("pts", "ka", None, None)
    return jax.shard_map(body, mesh=mesh, in_specs=in_specs, out_specs=out_specs, check_vma=False)
```

```python
import functools
import math

import jax
import jax.numpy as jnp
import ml_dtypes
import numpy as np
from jax import lax
from jax.experimental import pallas as pl
from jax.experimental.pallas import tpu as pltpu
from jax.sharding import PartitionSpec as P

BF16 = jnp.bfloat16
F32 = jnp.float32
LANES = 128
ROWS = 16
MIB = 1 << 20


def split_terms(table):
    high = table.astype(ml_dtypes.bfloat16)
    low = (table - high.astype(np.float64)).astype(ml_dtypes.bfloat16)
    return np.concatenate([high, low], axis=1)


def phase_tables(total):
    index = np.arange(total)
    angles = (index[:, None] * index[None, :] % total) * (2.0 * math.pi / total)
    cosine, sine = np.cos(angles), np.sin(angles)
    forward = np.zeros((2, total, total, 2))
    forward[0, :, :, 0] = cosine
    forward[0, :, :, 1] = -sine
    forward[1, :, :, 0] = sine
    forward[1, :, :, 1] = cosine
    backward = np.zeros((total, 2, 2, total))
    backward[:, 0, 0] = cosine
    backward[:, 0, 1] = sine
    backward[:, 1, 1] = cosine
    backward[:, 1, 0] = -sine
    size = 2 * total
    return (
        split_terms(forward.reshape(size, size)),
        split_terms(backward.reshape(size, size) / total),
    )


def column_selector(group, blocks, per_block, shares):
    total = blocks * per_block
    share = total // shares
    table = np.zeros((group, 2, shares, 2, share, blocks, group, 2, per_block), np.float32)
    for k in range(group):
        for col in range(total):
            d, c = divmod(col, share)
            b, j = divmod(col, per_block)
            table[k, 0, d, 0, c, b, k, 0, j] = 1.0
            table[k, 0, d, 1, c, b, k, 1, j] = -1.0
            table[k, 1, d, 0, c, b, k, 1, j] = 1.0
            table[k, 1, d, 1, c, b, k, 0, j] = 1.0
    return table.reshape(group * 4 * total, blocks * group * 2 * per_block).astype(ml_dtypes.bfloat16)


def dot(left, right, dims=((1,), (0,))):
    return lax.dot_general(left, right, (dims, ((), ())), preferred_element_type=F32)


def spread(wide, start, stride, value):
    for t in range(wide.shape[0]):
        wide[t, pl.ds(start, value.shape[0], stride=stride), :] = value[:, t * LANES : (t + 1) * LANES]


def take(wide, start, size):
    return jnp.concatenate([wide[t, pl.ds(start, size), :] for t in range(wide.shape[0])], axis=1)


def tiled(rows, lanes):
    return pltpu.VMEM((lanes // LANES, rows, LANES), F32)


def call(kernel, out_shape, n_in, scratch=(), limit=24, flops=0, size=0, result=pltpu.VMEM):
    whole = pl.BlockSpec(memory_space=pltpu.VMEM)
    return pl.pallas_call(
        kernel,
        out_shape=out_shape,
        in_specs=[whole] * n_in,
        out_specs=jax.tree.map(lambda _: pl.BlockSpec(memory_space=result), out_shape),
        scratch_shapes=list(scratch),
        compiler_params=pltpu.CompilerParams(vmem_limit_bytes=limit * MIB),
        cost_estimate=pl.CostEstimate(flops=flops, bytes_accessed=size, transcendentals=0),
    )


def edge_kernel(per_block, shares, orb_ref, coulomb_ref, edge_ref, piece_ref, wide):
    local_k = orb_ref.shape[0]
    share = coulomb_ref.shape[1] // shares
    me = lax.axis_index("ka")
    row = lax.broadcasted_iota(jnp.int32, (2 * per_block, LANES), 0)
    lane = lax.broadcasted_iota(jnp.int32, (2 * per_block, LANES), 1)
    one, zero = jnp.ones(row.shape, F32), jnp.zeros(row.shape, F32)
    first = jnp.where((row < per_block) & (row == lane), one, zero).astype(BF16)
    second = jnp.where((row >= per_block) & (row == lane + per_block), one, zero).astype(BF16)
    group = ROWS // (2 * per_block)
    for g in range(local_k // group):
        rows = []
        for k in range(g * group, (g + 1) * group):
            rows.append(
                dot(first, orb_ref[k, 0, :, :LANES], ((1,), (1,)))
                + dot(second, orb_ref[k, 1, :, :LANES], ((1,), (1,)))
            )
        edge_ref[g * ROWS : (g + 1) * ROWS] = jnp.concatenate(rows, axis=0).astype(BF16)
    wide[...] = coulomb_ref[...].astype(F32)
    for s in range(shares):
        start = pl.multiple_of(jnp.bitwise_xor(me, s) * share, share)
        pieces = [wide[r, pl.ds(start, share), :] for r in range(local_k)]
        piece_ref[s] = jnp.concatenate(pieces, axis=0).astype(BF16)


def tile_kernel(shares, blocks, per_block, *refs):
    edges, orb_ref, sel_ref, coulomb_ref = refs[:blocks], refs[blocks], refs[blocks + 1], refs[blocks + 2]
    outs, (form_ref, gathered, wide) = refs[blocks + 3 : blocks + 3 + shares], refs[blocks + 3 + shares :]
    local_k, _, norb, points = orb_ref.shape
    group = ROWS // (2 * per_block)
    total = blocks * per_block
    share = total // shares
    rows = 2 * total
    me = lax.axis_index("ka")
    block = lax.axis_index("pts")
    for s in range(blocks):
        gathered[jnp.bitwise_xor(block, s)] = edges[s][...]
    for g in range(local_k // group):
        stacked = jnp.concatenate(
            [gathered[b, g * ROWS : (g + 1) * ROWS] for b in range(blocks)], axis=0
        )
        forms = dot(sel_ref[...], stacked).astype(BF16)
        for kk in range(group):
            k = g * group + kk
            left = forms[2 * kk * rows : (2 * kk + 1) * rows]
            right = forms[(2 * kk + 1) * rows : (2 * kk + 2) * rows]
            form = jnp.concatenate([left, right], axis=1)
            form_ref[k] = form
            tile = dot(form, orb_ref[k].reshape(2 * norb, points))
            for d in range(shares):
                for part in range(2):
                    low = (2 * d + part) * share
                    start = d * share * 2 * local_k + 2 * k + part
                    spread(wide, start, 2 * local_k, tile[low : low + share])
    size = share * 2 * local_k
    for s in range(shares):
        dest = jnp.bitwise_xor(me, s)
        outs[s][:size] = take(wide, pl.multiple_of(dest * size, size), size).astype(BF16)
        outs[s][size:] = coulomb_ref[s]


def transform_kernel(shares, total, share, *refs):
    tiles, (fwd_ref, bwd_ref) = refs[:shares][::-1], refs[shares : shares + 2]
    outs, (gathered, weight, wide) = refs[shares + 2 : 2 * shares + 2], refs[2 * shares + 2 :]
    local_k = total // shares
    size = 2 * local_k * share
    me = lax.axis_index("ka")
    for s in range(shares):
        src = jnp.bitwise_xor(me, s)
        gathered[src] = tiles[s][:size].astype(gathered.dtype)
        cells = tiles[s][size:].astype(F32)
        for r in range(local_k):
            spread(weight, src * local_k + r, total, cells[r * share : (r + 1) * share])
    rows = 2 * local_k
    columns = []
    for c in range(share):
        columns.append(
            jnp.concatenate([gathered[a, c * rows : (c + 1) * rows] for a in range(shares)], axis=0).astype(BF16)
        )
    values = jnp.concatenate(columns, axis=1)
    cells = dot(fwd_ref[...], jnp.concatenate([values, values], axis=0))
    scale = jnp.concatenate([take(weight, c * total, total) for c in range(share)], axis=1)
    cells = (cells * jnp.concatenate([scale, scale], axis=0)).astype(BF16)
    kernel = dot(bwd_ref[...], jnp.concatenate([cells, cells], axis=0))
    points = kernel.shape[1] // share
    for c in range(share):
        spread(wide, c, share, kernel[:, c * points : (c + 1) * points])
    for s in range(shares):
        dest = jnp.bitwise_xor(me, s)
        outs[s][...] = take(wide, pl.multiple_of(dest * size, size), size).astype(BF16)


def weight_kernel(shares, flip, out_rows, *refs):
    pieces, orb_ref, out_ref, gathered = refs[:shares][::-1], refs[shares], refs[shares + 1], refs[shares + 2]
    local_k, _, norb, points = orb_ref.shape
    total_rows = gathered.shape[1]
    half = total_rows // local_k // 2
    me = lax.axis_index("ka")
    core = jnp.bitwise_xor(jnp.bitwise_and(lax.axis_index("pts"), 1), flip)
    for s in range(shares):
        gathered[jnp.bitwise_xor(me, s)] = pieces[s][...]
    lanes = 2 * half * shares
    group = max(1, LANES // lanes)
    chunks = norb // out_rows // 2
    for g in range(local_k // group):
        right, left = [], []
        for kk in range(group):
            k = g * group + kk
            first, second = [], []
            for a in range(shares):
                piece = gathered[a, k * 2 * half : (k + 1) * 2 * half].astype(F32)
                first.append(piece)
                second.extend([piece[half:], -piece[:half]])
            first = jnp.concatenate(first, axis=0).astype(BF16)
            second = jnp.concatenate(second, axis=0).astype(BF16)
            zero = jnp.zeros_like(first)
            parts = [zero] * (2 * group)
            parts[2 * kk], parts[2 * kk + 1] = first, second
            right.append(jnp.concatenate(parts, axis=1))
            left.append(k)
        right = jnp.concatenate(right, axis=0)
        for z in range(chunks):
            start = pl.multiple_of((2 * z + core) * out_rows, out_rows)
            rows = jnp.concatenate(
                [orb_ref[k, part, pl.ds(start, out_rows), :] for k in left for part in range(2)], axis=1
            )
            out_ref[z, :, g * group * lanes : (g + 1) * group * lanes] = dot(
                rows, right, ((1,), (1,))
            ).astype(out_ref.dtype)


def pair_kernel(chunks, keep_ref, came_ref, own_ref, *outs):
    z = lax.shift_right_logical(lax.axis_index("pts"), 1)
    for s in range(chunks):
        dest = jnp.bitwise_xor(z, s)
        value = keep_ref[dest] + came_ref[dest].astype(F32)
        if s == 0:
            own_ref[...] = value
        else:
            outs[s - 1][...] = value.astype(BF16)


def exchange_kernel(chunks, scale, *refs):
    pieces, form_ref, out_hbm = refs[:chunks][::-1], refs[chunks], refs[chunks + 1]
    wide, out_ref, sems = refs[chunks + 2 :]
    local_k, lanes, twice = form_ref.shape
    norb = twice // 2
    spans = norb // LANES
    out_rows = pieces[0].shape[0]
    total = pieces[0][...]
    for s in range(1, chunks):
        total = total + pieces[s][...].astype(F32)
    total = total * scale
    high = total.astype(BF16)
    low = (total - high.astype(F32)).astype(BF16)
    group = max(1, LANES // lanes)
    width = group * lanes
    lane = lax.broadcasted_iota(jnp.int32, (out_rows, width), 1)
    zero = jnp.zeros((out_rows, width), BF16)
    copies = []
    for g in range(local_k // group):
        high_g = high[:, g * width : (g + 1) * width]
        low_g = low[:, g * width : (g + 1) * width]
        left = []
        for kk in range(group):
            keep = (lane >= kk * lanes) & (lane < (kk + 1) * lanes)
            left.append(
                jnp.concatenate([jnp.where(keep, high_g, zero), jnp.where(keep, low_g, zero)], axis=1)
            )
        forms = [form_ref[g * group + kk] for kk in range(group)]
        result = dot(jnp.concatenate(left, axis=0), jnp.concatenate(forms + forms, axis=0))
        for kk in range(group):
            for part in range(2):
                for t in range(spans):
                    lane_start = part * norb + t * LANES
                    value = result[kk * out_rows : (kk + 1) * out_rows, lane_start : lane_start + LANES]
                    start = (kk * spans + t) * 2 + part
                    wide[g, pl.ds(start, out_rows, stride=2 * spans * group), :] = value
        out_ref[g] = wide[g].astype(BF16).reshape(out_ref.shape[1:])
        copies.append(pltpu.make_async_copy(out_ref.at[g], out_hbm.at[:, g], sems.at[g]))
        copies[-1].start()
    for copy in copies:
        copy.wait()


def swap(value, axis, mask):
    size = lax.axis_size(axis)
    return lax.ppermute(value, axis, [(i, i ^ mask) for i in range(size)])


def trade(pieces, axis, step):
    return [swap(pieces[s], axis, s * step) for s in reversed(range(1, len(pieces)))] + [pieces[0]]


def body(orbitals, coulomb):
    shares, blocks = lax.axis_size("ka"), lax.axis_size("pts")
    local_k, _, norb, points = orbitals.shape
    columns = coulomb.shape[1]
    per_block = columns // blocks
    share = columns // shares
    total = local_k * shares
    out_rows = norb // blocks
    chunks = blocks // 2
    group = ROWS // (2 * per_block)
    shape = jax.ShapeDtypeStruct

    edge, coulombs = call(
        functools.partial(edge_kernel, per_block, shares),
        [
            shape((local_k * 2 * per_block, norb), BF16),
            shape((shares, local_k * share, points), BF16),
        ],
        2,
        [pltpu.VMEM(coulomb.shape, F32)],
        size=4 * MIB,
    )(orbitals, coulomb)
    edges = [edge] + [None] * (blocks - 1)
    for s in range(1, chunks):
        edges[2 * s] = swap(edge, "pts", 2 * s)
    for s in range(chunks):
        edges[2 * s + 1] = swap(edges[2 * s], "pts", 1)

    selector = jnp.asarray(column_selector(group, blocks, per_block, shares))
    piece = shape((share * 2 * local_k, points), BF16)
    both = shape((share * 3 * local_k, points), BF16)
    *tiles, forms = call(
        functools.partial(tile_kernel, shares, blocks, per_block),
        [both] * shares + [shape((local_k, 2 * columns, 2 * norb), BF16)],
        blocks + 3,
        [
            pltpu.VMEM((blocks, local_k * 2 * per_block, norb), BF16),
            tiled(columns * 2 * local_k, points),
        ],
        size=8 * MIB,
    )(*edges, orbitals, selector, coulombs)
    tiles = trade(tiles, "ka", 1)

    forward, backward = phase_tables(total)
    kernels = call(
        functools.partial(transform_kernel, shares, total, share),
        [piece] * shares,
        shares + 2,
        [
            pltpu.VMEM((shares, share * 2 * local_k, points), BF16 if local_k % 8 == 0 else F32),
            tiled(share * total, points),
            tiled(2 * total * share, points),
        ],
        size=2 * MIB,
    )(*tiles, jnp.asarray(forward), jnp.asarray(backward))
    kernels = trade(kernels, "ka", 1)

    lanes = local_k * 2 * columns
    halves = []
    for flip, kind in ((1, BF16), (0, F32)):
        halves.append(
            call(
                functools.partial(weight_kernel, shares, flip, out_rows),
                shape((chunks, out_rows, lanes), kind),
                shares + 1,
                [pltpu.VMEM((shares, share * 2 * local_k, points), BF16)],
                size=6 * MIB,
            )(*kernels, orbitals)
        )
    came = swap(halves[0], "pts", 1)
    own_sum, *sums = call(
        functools.partial(pair_kernel, chunks),
        [shape((out_rows, lanes), F32)] + [shape((out_rows, lanes), BF16)] * (chunks - 1),
        2,
        size=1 * MIB,
    )(halves[1], came)
    sums = trade([own_sum, *sums], "pts", 2)
    spans = norb // LANES
    pair = max(1, LANES // (2 * columns))
    rows = pair * spans * 2
    result = call(
        functools.partial(exchange_kernel, chunks, 1.0 / math.sqrt(points * blocks)),
        shape((out_rows, local_k // pair, rows, LANES), BF16),
        chunks + 1,
        [
            pltpu.VMEM((local_k // pair, out_rows * rows, LANES), F32),
            pltpu.VMEM((local_k // pair, out_rows, rows, LANES), BF16),
            pltpu.SemaphoreType.DMA((local_k // pair,)),
        ],
        size=4 * MIB,
        result=pltpu.HBM,
    )(*sums, forms)
    result = result.reshape(out_rows, local_k, spans, 2, LANES)
    return result.transpose(0, 1, 3, 2, 4).reshape(out_rows, local_k, 2, norb)


def solution(mesh):
    in_specs = (P("ka", None, None, "pts"), P("ka", None, "pts"))
    out_specs = P("pts", "ka", None, None)
    return jax.shard_map(body, mesh=mesh, in_specs=in_specs, out_specs=out_specs, check_vma=False)
```

```python
import functools
import math

import jax
import jax.numpy as jnp
import ml_dtypes
import numpy as np
from jax import lax
from jax.experimental import pallas as pl
from jax.experimental.pallas import tpu as pltpu
from jax.sharding import PartitionSpec as P

BF16 = jnp.bfloat16
F32 = jnp.float32
LANES = 128
ROWS = 16
MIB = 1 << 20


def split_terms(table):
    high = table.astype(ml_dtypes.bfloat16)
    low = (table - high.astype(np.float64)).astype(ml_dtypes.bfloat16)
    return np.concatenate([high, low], axis=1)


def phase_tables(total):
    index = np.arange(total)
    angles = (index[:, None] * index[None, :] % total) * (2.0 * math.pi / total)
    cosine, sine = np.cos(angles), np.sin(angles)
    forward = np.zeros((2, total, total, 2))
    forward[0, :, :, 0] = cosine
    forward[0, :, :, 1] = -sine
    forward[1, :, :, 0] = sine
    forward[1, :, :, 1] = cosine
    backward = np.zeros((total, 2, 2, total))
    backward[:, 0, 0] = cosine
    backward[:, 0, 1] = sine
    backward[:, 1, 1] = cosine
    backward[:, 1, 0] = -sine
    size = 2 * total
    return (
        split_terms(forward.reshape(size, size)),
        split_terms(backward.reshape(size, size) / total),
    )


def column_selector(group, blocks, per_block, shares):
    total = blocks * per_block
    share = total // shares
    table = np.zeros((group, 2, shares, 2, share, blocks, group, 2, per_block), np.float32)
    for k in range(group):
        for col in range(total):
            d, c = divmod(col, share)
            b, j = divmod(col, per_block)
            table[k, 0, d, 0, c, b, k, 0, j] = 1.0
            table[k, 0, d, 1, c, b, k, 1, j] = -1.0
            table[k, 1, d, 0, c, b, k, 1, j] = 1.0
            table[k, 1, d, 1, c, b, k, 0, j] = 1.0
    return table.reshape(group * 4 * total, blocks * group * 2 * per_block).astype(ml_dtypes.bfloat16)


def dot(left, right, dims=((1,), (0,))):
    return lax.dot_general(left, right, (dims, ((), ())), preferred_element_type=F32)


def spread(wide, start, stride, value):
    for t in range(wide.shape[0]):
        wide[t, pl.ds(start, value.shape[0], stride=stride), :] = value[:, t * LANES : (t + 1) * LANES]


def take(wide, start, size):
    return jnp.concatenate([wide[t, pl.ds(start, size), :] for t in range(wide.shape[0])], axis=1)


def tiled(rows, lanes):
    return pltpu.VMEM((lanes // LANES, rows, LANES), F32)


def call(kernel, out_shape, n_in, scratch=(), limit=24, flops=0, size=0, unread=0, result=pltpu.VMEM):
    whole = pl.BlockSpec(memory_space=pltpu.VMEM)
    return pl.pallas_call(
        kernel,
        out_shape=out_shape,
        in_specs=[whole] * n_in + [pl.BlockSpec(memory_space=pl.ANY)] * unread,
        out_specs=jax.tree.map(lambda _: pl.BlockSpec(memory_space=result), out_shape),
        scratch_shapes=list(scratch),
        compiler_params=pltpu.CompilerParams(vmem_limit_bytes=limit * MIB),
        cost_estimate=pl.CostEstimate(flops=flops, bytes_accessed=size, transcendentals=0),
    )


def edge_kernel(per_block, orb_ref, edge_ref):
    local_k = orb_ref.shape[0]
    row = lax.broadcasted_iota(jnp.int32, (2 * per_block, LANES), 0)
    lane = lax.broadcasted_iota(jnp.int32, (2 * per_block, LANES), 1)
    one, zero = jnp.ones(row.shape, F32), jnp.zeros(row.shape, F32)
    first = jnp.where((row < per_block) & (row == lane), one, zero).astype(BF16)
    second = jnp.where((row >= per_block) & (row == lane + per_block), one, zero).astype(BF16)
    group = ROWS // (2 * per_block)
    for g in range(local_k // group):
        rows = []
        for k in range(g * group, (g + 1) * group):
            rows.append(
                dot(first, orb_ref[k, 0, :, :LANES], ((1,), (1,)))
                + dot(second, orb_ref[k, 1, :, :LANES], ((1,), (1,)))
            )
        edge_ref[g * ROWS : (g + 1) * ROWS] = jnp.concatenate(rows, axis=0).astype(BF16)


def coulomb_kernel(shares, coulomb_ref, _, *refs):
    outs, wide = refs[:shares], refs[shares]
    cells, columns, points = coulomb_ref.shape
    share = columns // shares
    me = lax.axis_index("ka")
    wide[...] = coulomb_ref[...].astype(F32)
    for s in range(shares):
        start = pl.multiple_of(jnp.bitwise_xor(me, s) * share, share)
        pieces = [wide[r, pl.ds(start, share), :] for r in range(cells)]
        outs[s][...] = jnp.concatenate(pieces, axis=0).astype(BF16)


def cell_kernel(shares, total, *refs):
    pieces, edge_ref, weight, pass_ref = refs[:shares][::-1], refs[shares], refs[shares + 1], refs[shares + 2]
    local_k = total // shares
    share = pieces[0].shape[0] // local_k
    me = lax.axis_index("ka")
    pass_ref[...] = edge_ref[...]
    for s in range(shares):
        src = jnp.bitwise_xor(me, s)
        cells = pieces[s][...].astype(F32)
        for r in range(local_k):
            spread(weight, src * local_k + r, total, cells[r * share : (r + 1) * share])


def tile_kernel(shares, blocks, per_block, *refs):
    edges, orb_ref, sel_ref = refs[:blocks], refs[blocks], refs[blocks + 1]
    outs, (form_ref, gathered, wide) = refs[blocks + 2 : blocks + 2 + shares], refs[blocks + 2 + shares :]
    local_k, _, norb, points = orb_ref.shape
    group = ROWS // (2 * per_block)
    total = blocks * per_block
    share = total // shares
    rows = 2 * total
    me = lax.axis_index("ka")
    block = lax.axis_index("pts")
    for s in range(blocks):
        gathered[jnp.bitwise_xor(block, s)] = edges[s][...]
    for g in range(local_k // group):
        stacked = jnp.concatenate(
            [gathered[b, g * ROWS : (g + 1) * ROWS] for b in range(blocks)], axis=0
        )
        forms = dot(sel_ref[...], stacked).astype(BF16)
        for kk in range(group):
            k = g * group + kk
            left = forms[2 * kk * rows : (2 * kk + 1) * rows]
            right = forms[(2 * kk + 1) * rows : (2 * kk + 2) * rows]
            form = jnp.concatenate([left, right], axis=1)
            form_ref[k] = form
            tile = dot(form, orb_ref[k].reshape(2 * norb, points))
            for d in range(shares):
                for part in range(2):
                    low = (2 * d + part) * share
                    start = d * share * 2 * local_k + 2 * k + part
                    spread(wide, start, 2 * local_k, tile[low : low + share])
    size = share * 2 * local_k
    for s in range(shares):
        dest = jnp.bitwise_xor(me, s)
        outs[s][...] = take(wide, pl.multiple_of(dest * size, size), size).astype(BF16)


def transform_kernel(shares, total, share, *refs):
    tiles, (fwd_ref, bwd_ref, weight) = refs[:shares][::-1], refs[shares : shares + 3]
    outs, (gathered, wide) = refs[shares + 3 : 2 * shares + 3], refs[2 * shares + 3 :]
    local_k = total // shares
    size = 2 * local_k * share
    me = lax.axis_index("ka")
    for s in range(shares):
        src = jnp.bitwise_xor(me, s)
        gathered[src] = tiles[s][...].astype(gathered.dtype)
    rows = 2 * local_k
    columns = []
    for c in range(share):
        columns.append(
            jnp.concatenate([gathered[a, c * rows : (c + 1) * rows] for a in range(shares)], axis=0).astype(BF16)
        )
    values = jnp.concatenate(columns, axis=1)
    cells = dot(fwd_ref[...], jnp.concatenate([values, values], axis=0))
    scale = jnp.concatenate([take(weight, c * total, total) for c in range(share)], axis=1)
    cells = (cells * jnp.concatenate([scale, scale], axis=0)).astype(BF16)
    kernel = dot(bwd_ref[...], jnp.concatenate([cells, cells], axis=0))
    points = kernel.shape[1] // share
    for c in range(share):
        spread(wide, c, share, kernel[:, c * points : (c + 1) * points])
    for s in range(shares):
        dest = jnp.bitwise_xor(me, s)
        outs[s][...] = take(wide, pl.multiple_of(dest * size, size), size).astype(BF16)


def weight_kernel(shares, flip, out_rows, *refs):
    pieces, orb_ref, out_ref, gathered = refs[:shares][::-1], refs[shares], refs[shares + 1], refs[shares + 2]
    local_k, _, norb, points = orb_ref.shape
    total_rows = gathered.shape[1]
    half = total_rows // local_k // 2
    me = lax.axis_index("ka")
    core = jnp.bitwise_xor(jnp.bitwise_and(lax.axis_index("pts"), 1), flip)
    for s in range(shares):
        gathered[jnp.bitwise_xor(me, s)] = pieces[s][...]
    lanes = 2 * half * shares
    group = max(1, LANES // lanes)
    chunks = norb // out_rows // 2
    for g in range(local_k // group):
        right, left = [], []
        for kk in range(group):
            k = g * group + kk
            first, second = [], []
            for a in range(shares):
                piece = gathered[a, k * 2 * half : (k + 1) * 2 * half].astype(F32)
                first.append(piece)
                second.extend([piece[half:], -piece[:half]])
            first = jnp.concatenate(first, axis=0).astype(BF16)
            second = jnp.concatenate(second, axis=0).astype(BF16)
            zero = jnp.zeros_like(first)
            parts = [zero] * (2 * group)
            parts[2 * kk], parts[2 * kk + 1] = first, second
            right.append(jnp.concatenate(parts, axis=1))
            left.append(k)
        right = jnp.concatenate(right, axis=0)
        for z in range(chunks):
            start = pl.multiple_of((2 * z + core) * out_rows, out_rows)
            rows = jnp.concatenate(
                [orb_ref[k, part, pl.ds(start, out_rows), :] for k in left for part in range(2)], axis=1
            )
            out_ref[z, :, g * group * lanes : (g + 1) * group * lanes] = dot(
                rows, right, ((1,), (1,))
            ).astype(out_ref.dtype)


def pair_kernel(chunks, keep_ref, came_ref, own_ref, *outs):
    z = lax.shift_right_logical(lax.axis_index("pts"), 1)
    for s in range(chunks):
        dest = jnp.bitwise_xor(z, s)
        value = keep_ref[dest] + came_ref[dest].astype(F32)
        if s == 0:
            own_ref[...] = value
        else:
            outs[s - 1][...] = value.astype(BF16)


def exchange_kernel(chunks, scale, *refs):
    pieces, form_ref, out_hbm = refs[:chunks][::-1], refs[chunks], refs[chunks + 1]
    wide, out_ref, sems = refs[chunks + 2 :]
    local_k, lanes, twice = form_ref.shape
    norb = twice // 2
    spans = norb // LANES
    out_rows = pieces[0].shape[0]
    total = pieces[0][...]
    for s in range(1, chunks):
        total = total + pieces[s][...].astype(F32)
    total = total * scale
    high = total.astype(BF16)
    low = (total - high.astype(F32)).astype(BF16)
    group = max(1, LANES // lanes)
    width = group * lanes
    lane = lax.broadcasted_iota(jnp.int32, (out_rows, width), 1)
    zero = jnp.zeros((out_rows, width), BF16)
    copies = []
    for g in range(local_k // group):
        high_g = high[:, g * width : (g + 1) * width]
        low_g = low[:, g * width : (g + 1) * width]
        left = []
        for kk in range(group):
            keep = (lane >= kk * lanes) & (lane < (kk + 1) * lanes)
            left.append(
                jnp.concatenate([jnp.where(keep, high_g, zero), jnp.where(keep, low_g, zero)], axis=1)
            )
        forms = [form_ref[g * group + kk] for kk in range(group)]
        result = dot(jnp.concatenate(left, axis=0), jnp.concatenate(forms + forms, axis=0))
        for kk in range(group):
            for part in range(2):
                for t in range(spans):
                    lane_start = part * norb + t * LANES
                    value = result[kk * out_rows : (kk + 1) * out_rows, lane_start : lane_start + LANES]
                    start = (kk * spans + t) * 2 + part
                    wide[g, pl.ds(start, out_rows, stride=2 * spans * group), :] = value
        out_ref[g] = wide[g].astype(BF16).reshape(out_ref.shape[1:])
        copies.append(pltpu.make_async_copy(out_ref.at[g], out_hbm.at[:, g], sems.at[g]))
        copies[-1].start()
    for copy in copies:
        copy.wait()


def swap(value, axis, mask):
    size = lax.axis_size(axis)
    return lax.ppermute(value, axis, [(i, i ^ mask) for i in range(size)])


def trade(pieces, axis, step):
    return [swap(pieces[s], axis, s * step) for s in reversed(range(1, len(pieces)))] + [pieces[0]]


def body(orbitals, coulomb):
    shares, blocks = lax.axis_size("ka"), lax.axis_size("pts")
    local_k, _, norb, points = orbitals.shape
    columns = coulomb.shape[1]
    per_block = columns // blocks
    share = columns // shares
    total = local_k * shares
    out_rows = norb // blocks
    chunks = blocks // 2
    group = ROWS // (2 * per_block)
    shape = jax.ShapeDtypeStruct

    edge = call(
        functools.partial(edge_kernel, per_block),
        shape((local_k * 2 * per_block, norb), BF16),
        1,
        size=4 * MIB,
    )(orbitals)
    edges = [edge] + [None] * (blocks - 1)
    for s in range(1, chunks):
        edges[2 * s] = swap(edge, "pts", 2 * s)
    edges[1] = swap(edge, "pts", 1)

    cells = call(
        functools.partial(coulomb_kernel, shares),
        [shape((local_k * share, points), BF16)] * shares,
        1,
        [pltpu.VMEM(coulomb.shape, F32)],
        size=1 * MIB,
        unread=1,
    )(coulomb, edges[1])
    last = chunks // 2
    weight, passed = call(
        functools.partial(cell_kernel, shares, total),
        [shape((points // LANES, share * total, LANES), F32), shape(edge.shape, BF16)],
        shares + 1,
        size=1 * MIB,
    )(*trade(cells, "ka", 1), edges[2 * last])
    for s in range(1, chunks):
        edges[2 * s + 1] = swap(passed if s == last else edges[2 * s], "pts", 1)

    selector = jnp.asarray(column_selector(group, blocks, per_block, shares))
    piece = shape((share * 2 * local_k, points), BF16)
    *tiles, forms = call(
        functools.partial(tile_kernel, shares, blocks, per_block),
        [piece] * shares + [shape((local_k, 2 * columns, 2 * norb), BF16)],
        blocks + 2,
        [
            pltpu.VMEM((blocks, local_k * 2 * per_block, norb), BF16),
            tiled(columns * 2 * local_k, points),
        ],
        size=8 * MIB,
    )(*edges, orbitals, selector)
    tiles = trade(tiles, "ka", 1)

    forward, backward = phase_tables(total)
    kernels = call(
        functools.partial(transform_kernel, shares, total, share),
        [piece] * shares,
        shares + 3,
        [
            pltpu.VMEM((shares, share * 2 * local_k, points), BF16 if local_k % 8 == 0 else F32),
            tiled(2 * total * share, points),
        ],
        size=2 * MIB,
    )(*tiles, jnp.asarray(forward), jnp.asarray(backward), weight)
    kernels = trade(kernels, "ka", 1)

    lanes = local_k * 2 * columns
    halves = []
    for flip, kind in ((1, BF16), (0, F32)):
        halves.append(
            call(
                functools.partial(weight_kernel, shares, flip, out_rows),
                shape((chunks, out_rows, lanes), kind),
                shares + 1,
                [pltpu.VMEM((shares, share * 2 * local_k, points), BF16)],
                size=6 * MIB,
            )(*kernels, orbitals)
        )
    came = swap(halves[0], "pts", 1)
    own_sum, *sums = call(
        functools.partial(pair_kernel, chunks),
        [shape((out_rows, lanes), F32)] + [shape((out_rows, lanes), BF16)] * (chunks - 1),
        2,
        size=1 * MIB,
    )(halves[1], came)
    sums = trade([own_sum, *sums], "pts", 2)
    spans = norb // LANES
    pair = max(1, LANES // (2 * columns))
    rows = pair * spans * 2
    result = call(
        functools.partial(exchange_kernel, chunks, 1.0 / math.sqrt(points * blocks)),
        shape((out_rows, local_k // pair, rows, LANES), BF16),
        chunks + 1,
        [
            pltpu.VMEM((local_k // pair, out_rows * rows, LANES), F32),
            pltpu.VMEM((local_k // pair, out_rows, rows, LANES), BF16),
            pltpu.SemaphoreType.DMA((local_k // pair,)),
        ],
        size=4 * MIB,
        result=pltpu.HBM,
    )(*sums, forms)
    result = result.reshape(out_rows, local_k, spans, 2, LANES)
    return result.transpose(0, 1, 3, 2, 4).reshape(out_rows, local_k, 2, norb)


def solution(mesh):
    in_specs = (P("ka", None, None, "pts"), P("ka", None, "pts"))
    out_specs = P("pts", "ka", None, None)
    return jax.shard_map(body, mesh=mesh, in_specs=in_specs, out_specs=out_specs, check_vma=False)
```

```python
import functools
import math

import jax
import jax.numpy as jnp
import ml_dtypes
import numpy as np
from jax import lax
from jax.experimental import pallas as pl
from jax.experimental.pallas import tpu as pltpu
from jax.sharding import PartitionSpec as P

BF16 = jnp.bfloat16
F32 = jnp.float32
LANES = 128
ROWS = 16
MIB = 1 << 20


def split_terms(table):
    high = table.astype(ml_dtypes.bfloat16)
    low = (table - high.astype(np.float64)).astype(ml_dtypes.bfloat16)
    return np.concatenate([high, low], axis=1)


def phase_tables(total):
    index = np.arange(total)
    angles = (index[:, None] * index[None, :] % total) * (2.0 * math.pi / total)
    cosine, sine = np.cos(angles), np.sin(angles)
    forward = np.zeros((2, total, total, 2))
    forward[0, :, :, 0] = cosine
    forward[0, :, :, 1] = -sine
    forward[1, :, :, 0] = sine
    forward[1, :, :, 1] = cosine
    backward = np.zeros((total, 2, 2, total))
    backward[:, 0, 0] = cosine
    backward[:, 0, 1] = sine
    backward[:, 1, 1] = cosine
    backward[:, 1, 0] = -sine
    size = 2 * total
    return (
        split_terms(forward.reshape(size, size)),
        split_terms(backward.reshape(size, size) / total),
    )


def column_selector(group, blocks, per_block, shares):
    total = blocks * per_block
    share = total // shares
    table = np.zeros((group, 2, shares, 2, share, blocks, group, 2, per_block), np.float32)
    for k in range(group):
        for col in range(total):
            d, c = divmod(col, share)
            b, j = divmod(col, per_block)
            table[k, 0, d, 0, c, b, k, 0, j] = 1.0
            table[k, 0, d, 1, c, b, k, 1, j] = -1.0
            table[k, 1, d, 0, c, b, k, 1, j] = 1.0
            table[k, 1, d, 1, c, b, k, 0, j] = 1.0
    return table.reshape(group * 4 * total, blocks * group * 2 * per_block).astype(ml_dtypes.bfloat16)


def dot(left, right, dims=((1,), (0,))):
    return lax.dot_general(left, right, (dims, ((), ())), preferred_element_type=F32)


def spread(wide, start, stride, value):
    for t in range(wide.shape[0]):
        wide[t, pl.ds(start, value.shape[0], stride=stride), :] = value[:, t * LANES : (t + 1) * LANES]


def take(wide, start, size):
    return jnp.concatenate([wide[t, pl.ds(start, size), :] for t in range(wide.shape[0])], axis=1)


def tiled(rows, lanes):
    return pltpu.VMEM((lanes // LANES, rows, LANES), F32)


def call(kernel, out_shape, n_in, scratch=(), limit=24, flops=0, size=0, unread=0, result=pltpu.VMEM):
    whole = pl.BlockSpec(memory_space=pltpu.VMEM)
    return pl.pallas_call(
        kernel,
        out_shape=out_shape,
        in_specs=[whole] * n_in + [pl.BlockSpec(memory_space=pl.ANY)] * unread,
        out_specs=jax.tree.map(lambda _: pl.BlockSpec(memory_space=result), out_shape),
        scratch_shapes=list(scratch),
        compiler_params=pltpu.CompilerParams(vmem_limit_bytes=limit * MIB),
        cost_estimate=pl.CostEstimate(flops=flops, bytes_accessed=size, transcendentals=0),
    )


def edge_kernel(per_block, orb_ref, edge_ref):
    local_k = orb_ref.shape[0]
    row = lax.broadcasted_iota(jnp.int32, (2 * per_block, LANES), 0)
    lane = lax.broadcasted_iota(jnp.int32, (2 * per_block, LANES), 1)
    one, zero = jnp.ones(row.shape, F32), jnp.zeros(row.shape, F32)
    first = jnp.where((row < per_block) & (row == lane), one, zero).astype(BF16)
    second = jnp.where((row >= per_block) & (row == lane + per_block), one, zero).astype(BF16)
    group = ROWS // (2 * per_block)
    for g in range(local_k // group):
        rows = []
        for k in range(g * group, (g + 1) * group):
            rows.append(
                dot(first, orb_ref[k, 0, :, :LANES], ((1,), (1,)))
                + dot(second, orb_ref[k, 1, :, :LANES], ((1,), (1,)))
            )
        edge_ref[g * ROWS : (g + 1) * ROWS] = jnp.concatenate(rows, axis=0).astype(BF16)


def orders(shares):
    return [[a ^ j for j in reversed(range(shares)) if a ^ j] for a in range(shares)]


def pick(table, index):
    value = jnp.int32(table[0])
    for i in range(1, len(table)):
        value = jnp.where(index == i, jnp.int32(table[i]), value)
    return value


def steps_for(j, shares):
    order = orders(shares)
    return sorted({order[a].index(a ^ j) for a in range(shares) if a ^ j})


def plane_of(shares):
    return lax.div(lax.axis_index("pts"), lax.axis_size("pts") // shares)


def tile_kernel(j, shares, per_share, per_block, *refs):
    steps = steps_for(j, shares)
    n = per_share * (1 + len(steps))
    blocks, (orb_ref, sel_ref, coulomb_ref) = refs[:n], refs[n : n + 3]
    out_ref, form_ref, gathered, wide, cells = refs[-5:]
    local_k, _, norb, points = orb_ref.shape
    group = ROWS // (2 * per_block)
    share = per_share * per_block
    me, block = lax.axis_index("ka"), lax.axis_index("pts")
    offset = jnp.bitwise_xor(me, j)
    order = orders(shares)
    for i, t in enumerate([None] + steps):
        here = 0 if t is None else pick([order[a][t] for a in range(shares)], me)

        @pl.when(offset == here)
        def _(i=i):
            for e in range(per_share):
                place = jnp.bitwise_xor(jnp.bitwise_and(block, per_share - 1), e)
                gathered[place] = blocks[i * per_share + e][...]

    for g in range(local_k // group):
        stacked = jnp.concatenate(
            [gathered[b, g * ROWS : (g + 1) * ROWS] for b in range(per_share)], axis=0
        )
        forms = dot(sel_ref[...], stacked).astype(BF16)
        rows = 2 * share
        for kk in range(group):
            k = g * group + kk
            left = forms[2 * kk * rows : (2 * kk + 1) * rows]
            right = forms[(2 * kk + 1) * rows : (2 * kk + 2) * rows]
            form = jnp.concatenate([left, right], axis=1)
            form_ref[k] = form
            tile = dot(form, orb_ref[k].reshape(2 * norb, points))
            for part in range(2):
                spread(wide, 2 * k + part, 2 * local_k, tile[part * share : (part + 1) * share])
    size = share * 2 * local_k
    out_ref[:size] = take(wide, 0, size).astype(BF16)
    start = pl.multiple_of(jnp.bitwise_xor(offset, plane_of(shares)) * share, share)
    cells[...] = coulomb_ref[...].astype(F32)
    pieces = [cells[r, pl.ds(start, share), :] for r in range(local_k)]
    out_ref[size:] = jnp.concatenate(pieces, axis=0).astype(BF16)


def transform_kernel(shares, total, share, *refs):
    tiles, (fwd_ref, bwd_ref) = refs[:shares][::-1], refs[shares : shares + 2]
    outs, (gathered, weight, wide) = refs[shares + 2 : 2 * shares + 2], refs[2 * shares + 2 :]
    local_k = total // shares
    size = 2 * local_k * share
    me = lax.axis_index("ka")
    for s in range(shares):
        src = jnp.bitwise_xor(me, s)
        gathered[src] = tiles[s][:size].astype(gathered.dtype)
        cells = tiles[s][size:].astype(F32)
        for r in range(local_k):
            spread(weight, src * local_k + r, total, cells[r * share : (r + 1) * share])
    rows = 2 * local_k
    columns = []
    for c in range(share):
        columns.append(
            jnp.concatenate([gathered[a, c * rows : (c + 1) * rows] for a in range(shares)], axis=0).astype(BF16)
        )
    values = jnp.concatenate(columns, axis=1)
    cells = dot(fwd_ref[...], jnp.concatenate([values, values], axis=0))
    scale = jnp.concatenate([take(weight, c * total, total) for c in range(share)], axis=1)
    cells = (cells * jnp.concatenate([scale, scale], axis=0)).astype(BF16)
    kernel = dot(bwd_ref[...], jnp.concatenate([cells, cells], axis=0))
    points = kernel.shape[1] // share
    for c in range(share):
        spread(wide, c, share, kernel[:, c * points : (c + 1) * points])
    for s in range(shares):
        dest = jnp.bitwise_xor(me, s)
        outs[s][...] = take(wide, pl.multiple_of(dest * size, size), size).astype(BF16)


def weight_kernel(shares, flip, out_rows, *refs):
    pieces, orb_ref, out_ref, gathered = refs[:shares][::-1], refs[shares], refs[shares + 1], refs[shares + 2]
    local_k, _, norb, points = orb_ref.shape
    total_rows = gathered.shape[1]
    half = total_rows // local_k // 2
    me = lax.axis_index("ka")
    core = jnp.bitwise_xor(jnp.bitwise_and(lax.axis_index("pts"), 1), flip)
    plane = plane_of(shares)
    for s in range(shares):
        gathered[jnp.bitwise_xor(jnp.bitwise_xor(me, s), plane)] = pieces[s][...]
    lanes = 2 * half * shares
    group = max(1, LANES // lanes)
    chunks = norb // out_rows // 2
    for g in range(local_k // group):
        right, left = [], []
        for kk in range(group):
            k = g * group + kk
            first, second = [], []
            for a in range(shares):
                piece = gathered[a, k * 2 * half : (k + 1) * 2 * half].astype(F32)
                first.append(piece)
                second.extend([piece[half:], -piece[:half]])
            first = jnp.concatenate(first, axis=0).astype(BF16)
            second = jnp.concatenate(second, axis=0).astype(BF16)
            zero = jnp.zeros_like(first)
            parts = [zero] * (2 * group)
            parts[2 * kk], parts[2 * kk + 1] = first, second
            right.append(jnp.concatenate(parts, axis=1))
            left.append(k)
        right = jnp.concatenate(right, axis=0)
        for z in range(chunks):
            start = pl.multiple_of((2 * z + core) * out_rows, out_rows)
            rows = jnp.concatenate(
                [orb_ref[k, part, pl.ds(start, out_rows), :] for k in left for part in range(2)], axis=1
            )
            out_ref[z, :, g * group * lanes : (g + 1) * group * lanes] = dot(
                rows, right, ((1,), (1,))
            ).astype(out_ref.dtype)


def pair_kernel(chunks, keep_ref, came_ref, own_ref, *outs):
    z = lax.shift_right_logical(lax.axis_index("pts"), 1)
    for s in range(chunks):
        dest = jnp.bitwise_xor(z, s)
        value = keep_ref[dest] + came_ref[dest].astype(F32)
        if s == 0:
            own_ref[...] = value
        else:
            outs[s - 1][...] = value.astype(BF16)


def exchange_kernel(chunks, shares, scale, *refs):
    pieces, form_refs, out_hbm = refs[:chunks][::-1], refs[chunks : chunks + shares], refs[chunks + shares]
    wide, out_ref, form_ref, sems = refs[chunks + shares + 1 :]
    owner = jnp.bitwise_xor(lax.axis_index("ka"), plane_of(shares))
    for j in range(shares):
        form_ref[jnp.bitwise_xor(owner, j)] = form_refs[j][...]
    _, local_k, part_lanes, twice = form_ref.shape
    lanes = shares * part_lanes
    norb = twice // 2
    spans = norb // LANES
    out_rows = pieces[0].shape[0]
    total = pieces[0][...]
    for s in range(1, chunks):
        total = total + pieces[s][...].astype(F32)
    total = total * scale
    high = total.astype(BF16)
    low = (total - high.astype(F32)).astype(BF16)
    group = max(1, LANES // lanes)
    width = group * lanes
    lane = lax.broadcasted_iota(jnp.int32, (out_rows, width), 1)
    zero = jnp.zeros((out_rows, width), BF16)
    copies = []
    for g in range(local_k // group):
        high_g = high[:, g * width : (g + 1) * width]
        low_g = low[:, g * width : (g + 1) * width]
        left = []
        for kk in range(group):
            keep = (lane >= kk * lanes) & (lane < (kk + 1) * lanes)
            left.append(
                jnp.concatenate([jnp.where(keep, high_g, zero), jnp.where(keep, low_g, zero)], axis=1)
            )
        forms = [form_ref[d, g * group + kk] for kk in range(group) for d in range(shares)]
        result = dot(jnp.concatenate(left, axis=0), jnp.concatenate(forms + forms, axis=0))
        for kk in range(group):
            for part in range(2):
                for t in range(spans):
                    lane_start = part * norb + t * LANES
                    value = result[kk * out_rows : (kk + 1) * out_rows, lane_start : lane_start + LANES]
                    start = (kk * spans + t) * 2 + part
                    wide[g, pl.ds(start, out_rows, stride=2 * spans * group), :] = value
        out_ref[g] = wide[g].astype(BF16).reshape(out_ref.shape[1:])
        copies.append(pltpu.make_async_copy(out_ref.at[g], out_hbm.at[:, g], sems.at[g]))
        copies[-1].start()
    for copy in copies:
        copy.wait()


def swap(value, axis, mask):
    size = lax.axis_size(axis)
    return lax.ppermute(value, axis, [(i, i ^ mask) for i in range(size)])


def trade(pieces, axis, step):
    return [swap(pieces[s], axis, s * step) for s in reversed(range(1, len(pieces)))] + [pieces[0]]


def body(orbitals, coulomb):
    shares, blocks = lax.axis_size("ka"), lax.axis_size("pts")
    local_k, _, norb, points = orbitals.shape
    columns = coulomb.shape[1]
    per_block = columns // blocks
    share = columns // shares
    total = local_k * shares
    out_rows = norb // blocks
    chunks = blocks // 2
    group = ROWS // (2 * per_block)
    shape = jax.ShapeDtypeStruct

    edge = call(
        functools.partial(edge_kernel, per_block),
        shape((local_k * 2 * per_block, norb), BF16),
        1,
        size=4 * MIB,
    )(orbitals)
    per_share = blocks // shares
    order = orders(shares)
    partner = swap(edge, "pts", 1)
    near = [edge, partner] + [swap(edge, "pts", 2 * e + c) for e in range(1, per_share // 2) for c in range(2)]
    came = []
    for t in range(shares - 1):
        step = []
        for e in range(per_share // 2):
            pairs = [
                (a * blocks + i, a * blocks + (i ^ (order[a][t] * per_share + 2 * e)))
                for a in range(shares)
                for i in range(blocks)
            ]
            block = lax.ppermute(edge, ("ka", "pts"), pairs)
            step += [block, swap(block, "pts", 1)]
        came.append(step)

    selector = jnp.asarray(column_selector(group, per_share, per_block, 1))
    piece = shape((share * 2 * local_k, points), BF16)
    both = shape((share * 3 * local_k, points), BF16)
    tiles, forms, before = [None] * shares, [None] * shares, []
    for j in reversed(range(shares)):
        taken = [block for t in steps_for(j, shares) for block in came[t]]
        tiles[j], forms[j] = call(
            functools.partial(tile_kernel, j, shares, per_share, per_block),
            [both, shape((local_k, 2 * share, 2 * norb), BF16)],
            len(near) + len(taken) + 3,
            [
                pltpu.VMEM((per_share, local_k * 2 * per_block, norb), BF16),
                tiled(share * 2 * local_k, points),
                pltpu.VMEM(coulomb.shape, F32),
            ],
            size=6 * MIB,
            unread=len(before),
        )(*near, *taken, orbitals, selector, coulomb, *before)
        before = [forms[j]]
    tiles = trade(tiles, "ka", 1)

    forward, backward = phase_tables(total)
    kernels = call(
        functools.partial(transform_kernel, shares, total, share),
        [piece] * shares,
        shares + 2,
        [
            pltpu.VMEM((shares, share * 2 * local_k, points), BF16 if local_k % 8 == 0 else F32),
            tiled(share * total, points),
            tiled(2 * total * share, points),
        ],
        size=2 * MIB,
    )(*tiles, jnp.asarray(forward), jnp.asarray(backward))
    kernels = trade(kernels, "ka", 1)

    lanes = local_k * 2 * columns
    halves = []
    for flip, kind in ((1, BF16), (0, F32)):
        halves.append(
            call(
                functools.partial(weight_kernel, shares, flip, out_rows),
                shape((chunks, out_rows, lanes), kind),
                shares + 1,
                [pltpu.VMEM((shares, share * 2 * local_k, points), BF16)],
                size=6 * MIB,
            )(*kernels, orbitals)
        )
    came = swap(halves[0], "pts", 1)
    own_sum, *sums = call(
        functools.partial(pair_kernel, chunks),
        [shape((out_rows, lanes), F32)] + [shape((out_rows, lanes), BF16)] * (chunks - 1),
        2,
        size=1 * MIB,
    )(halves[1], came)
    sums = trade([own_sum, *sums], "pts", 2)
    spans = norb // LANES
    pair = max(1, LANES // (2 * columns))
    rows = pair * spans * 2
    result = call(
        functools.partial(exchange_kernel, chunks, shares, 1.0 / math.sqrt(points * blocks)),
        shape((out_rows, local_k // pair, rows, LANES), BF16),
        chunks + shares,
        [
            pltpu.VMEM((local_k // pair, out_rows * rows, LANES), F32),
            pltpu.VMEM((local_k // pair, out_rows, rows, LANES), BF16),
            pltpu.VMEM((shares, local_k, 2 * share, 2 * norb), BF16),
            pltpu.SemaphoreType.DMA((local_k // pair,)),
        ],
        size=4 * MIB,
        result=pltpu.HBM,
    )(*sums, *forms)
    result = result.reshape(out_rows, local_k, spans, 2, LANES)
    return result.transpose(0, 1, 3, 2, 4).reshape(out_rows, local_k, 2, norb)


def solution(mesh):
    in_specs = (P("ka", None, None, "pts"), P("ka", None, "pts"))
    out_specs = P("pts", "ka", None, None)
    return jax.shard_map(body, mesh=mesh, in_specs=in_specs, out_specs=out_specs, check_vma=False)
```

```python
import functools
import math

import jax
import jax.numpy as jnp
import ml_dtypes
import numpy as np
from jax import lax
from jax.experimental import pallas as pl
from jax.experimental.pallas import tpu as pltpu
from jax.sharding import PartitionSpec as P

BF16 = jnp.bfloat16
F32 = jnp.float32
LANES = 128
ROWS = 16
MIB = 1 << 20


def split_terms(table):
    high = table.astype(ml_dtypes.bfloat16)
    low = (table - high.astype(np.float64)).astype(ml_dtypes.bfloat16)
    return np.concatenate([high, low], axis=1)


def phase_tables(total):
    index = np.arange(total)
    angles = (index[:, None] * index[None, :] % total) * (2.0 * math.pi / total)
    cosine, sine = np.cos(angles), np.sin(angles)
    forward = np.zeros((2, total, total, 2))
    forward[0, :, :, 0] = cosine
    forward[0, :, :, 1] = -sine
    forward[1, :, :, 0] = sine
    forward[1, :, :, 1] = cosine
    backward = np.zeros((total, 2, 2, total))
    backward[:, 0, 0] = cosine
    backward[:, 0, 1] = sine
    backward[:, 1, 1] = cosine
    backward[:, 1, 0] = -sine
    size = 2 * total
    return (
        split_terms(forward.reshape(size, size)),
        split_terms(backward.reshape(size, size) / total),
    )


def column_selector(group, blocks, per_block, shares):
    total = blocks * per_block
    share = total // shares
    table = np.zeros((group, 2, shares, 2, share, blocks, group, 2, per_block), np.float32)
    for k in range(group):
        for col in range(total):
            d, c = divmod(col, share)
            b, j = divmod(col, per_block)
            table[k, 0, d, 0, c, b, k, 0, j] = 1.0
            table[k, 0, d, 1, c, b, k, 1, j] = -1.0
            table[k, 1, d, 0, c, b, k, 1, j] = 1.0
            table[k, 1, d, 1, c, b, k, 0, j] = 1.0
    return table.reshape(group * 4 * total, blocks * group * 2 * per_block).astype(ml_dtypes.bfloat16)


def dot(left, right, dims=((1,), (0,))):
    return lax.dot_general(left, right, (dims, ((), ())), preferred_element_type=F32)


def spread(wide, start, stride, value):
    for t in range(wide.shape[0]):
        wide[t, pl.ds(start, value.shape[0], stride=stride), :] = value[:, t * LANES : (t + 1) * LANES]


def take(wide, start, size):
    return jnp.concatenate([wide[t, pl.ds(start, size), :] for t in range(wide.shape[0])], axis=1)


def tiled(rows, lanes):
    return pltpu.VMEM((lanes // LANES, rows, LANES), F32)


def call(kernel, out_shape, n_in, scratch=(), limit=24, flops=0, size=0, unread=0, result=pltpu.VMEM):
    whole = pl.BlockSpec(memory_space=pltpu.VMEM)
    return pl.pallas_call(
        kernel,
        out_shape=out_shape,
        in_specs=[whole] * n_in + [pl.BlockSpec(memory_space=pl.ANY)] * unread,
        out_specs=jax.tree.map(lambda _: pl.BlockSpec(memory_space=result), out_shape),
        scratch_shapes=list(scratch),
        compiler_params=pltpu.CompilerParams(vmem_limit_bytes=limit * MIB),
        cost_estimate=pl.CostEstimate(flops=flops, bytes_accessed=size, transcendentals=0),
    )


def edge_kernel(per_block, orb_ref, edge_ref):
    local_k = orb_ref.shape[0]
    row = lax.broadcasted_iota(jnp.int32, (2 * per_block, LANES), 0)
    lane = lax.broadcasted_iota(jnp.int32, (2 * per_block, LANES), 1)
    one, zero = jnp.ones(row.shape, F32), jnp.zeros(row.shape, F32)
    first = jnp.where((row < per_block) & (row == lane), one, zero).astype(BF16)
    second = jnp.where((row >= per_block) & (row == lane + per_block), one, zero).astype(BF16)
    group = ROWS // (2 * per_block)
    for g in range(local_k // group):
        rows = []
        for k in range(g * group, (g + 1) * group):
            rows.append(
                dot(first, orb_ref[k, 0, :, :LANES], ((1,), (1,)))
                + dot(second, orb_ref[k, 1, :, :LANES], ((1,), (1,)))
            )
        edge_ref[g * ROWS : (g + 1) * ROWS] = jnp.concatenate(rows, axis=0).astype(BF16)


def orders(shares):
    return [[a ^ j for j in reversed(range(shares)) if a ^ j] for a in range(shares)]


def pick(table, index):
    value = jnp.int32(table[0])
    for i in range(1, len(table)):
        value = jnp.where(index == i, jnp.int32(table[i]), value)
    return value


def steps_for(j, shares):
    order = orders(shares)
    return sorted({order[a].index(a ^ j) for a in range(shares) if a ^ j})


def pieces_of(shares):
    half = shares // 2
    return [list(reversed(range(half, shares))), list(reversed(range(half)))]


def plane_of(shares):
    return lax.div(lax.axis_index("pts"), lax.axis_size("pts") // shares)


def tile_kernel(targets, shares, per_share, per_block, *refs):
    steps = sorted({t for j in targets for t in steps_for(j, shares)})
    n, many = per_share * (1 + len(steps)), len(targets)
    blocks, (orb_ref, sel_ref, coulomb_ref) = refs[:n], refs[n : n + 3]
    *refs, gathered, wide, cells = refs[-2 * many - 3 :]
    outs, form_refs = refs[:many], refs[many:]
    local_k, _, norb, points = orb_ref.shape
    group = ROWS // (2 * per_block)
    share = per_share * per_block
    rows = 2 * share
    me, block = lax.axis_index("ka"), lax.axis_index("pts")
    order = orders(shares)
    for i, t in enumerate([None] + steps):
        here = 0 if t is None else pick([order[a][t] for a in range(shares)], me)
        for slot, j in enumerate(targets):

            @pl.when(jnp.bitwise_xor(me, j) == here)
            def _(i=i, slot=slot):
                for e in range(per_share):
                    place = jnp.bitwise_xor(jnp.bitwise_and(block, per_share - 1), e)
                    gathered[slot, place] = blocks[i * per_share + e][...]

    for g in range(local_k // group):
        forms = []
        for slot in range(many):
            stacked = jnp.concatenate(
                [gathered[slot, b, g * ROWS : (g + 1) * ROWS] for b in range(per_share)], axis=0
            )
            forms.append(dot(sel_ref[...], stacked).astype(BF16))
        for kk in range(group):
            k = g * group + kk
            left = [form[2 * kk * rows : (2 * kk + 1) * rows] for form in forms]
            right = [form[(2 * kk + 1) * rows : (2 * kk + 2) * rows] for form in forms]
            form = jnp.concatenate(
                [jnp.concatenate(left, axis=0), jnp.concatenate(right, axis=0)], axis=1
            )
            tile = dot(form, orb_ref[k].reshape(2 * norb, points))
            for slot in range(many):
                form_refs[slot][k] = form[slot * rows : (slot + 1) * rows]
                for part in range(2):
                    low = slot * rows + part * share
                    start = slot * share * 2 * local_k + 2 * k + part
                    spread(wide, start, 2 * local_k, tile[low : low + share])
    size = share * 2 * local_k
    cells[...] = coulomb_ref[...].astype(F32)
    for slot, j in enumerate(targets):
        outs[slot][:size] = take(wide, slot * size, size).astype(BF16)
        owned = jnp.bitwise_xor(jnp.bitwise_xor(me, j), plane_of(shares))
        start = pl.multiple_of(owned * share, share)
        pieces = [cells[r, pl.ds(start, share), :] for r in range(local_k)]
        outs[slot][size:] = jnp.concatenate(pieces, axis=0).astype(BF16)


def transform_kernel(shares, total, share, *refs):
    tiles, (fwd_ref, bwd_ref) = refs[:shares][::-1], refs[shares : shares + 2]
    outs, (gathered, weight, wide) = refs[shares + 2 : 2 * shares + 2], refs[2 * shares + 2 :]
    local_k = total // shares
    size = 2 * local_k * share
    me = lax.axis_index("ka")
    for s in range(shares):
        src = jnp.bitwise_xor(me, s)
        gathered[src] = tiles[s][:size].astype(gathered.dtype)
        cells = tiles[s][size:].astype(F32)
        for r in range(local_k):
            spread(weight, src * local_k + r, total, cells[r * share : (r + 1) * share])
    rows = 2 * local_k
    columns = []
    for c in range(share):
        columns.append(
            jnp.concatenate([gathered[a, c * rows : (c + 1) * rows] for a in range(shares)], axis=0).astype(BF16)
        )
    values = jnp.concatenate(columns, axis=1)
    cells = dot(fwd_ref[...], jnp.concatenate([values, values], axis=0))
    scale = jnp.concatenate([take(weight, c * total, total) for c in range(share)], axis=1)
    cells = (cells * jnp.concatenate([scale, scale], axis=0)).astype(BF16)
    kernel = dot(bwd_ref[...], jnp.concatenate([cells, cells], axis=0))
    points = kernel.shape[1] // share
    for c in range(share):
        spread(wide, c, share, kernel[:, c * points : (c + 1) * points])
    for s in range(shares):
        dest = jnp.bitwise_xor(me, s)
        outs[s][...] = take(wide, pl.multiple_of(dest * size, size), size).astype(BF16)


def weight_kernel(shares, flip, out_rows, *refs):
    pieces, orb_ref, out_ref, gathered = refs[:shares][::-1], refs[shares], refs[shares + 1], refs[shares + 2]
    local_k, _, norb, points = orb_ref.shape
    total_rows = gathered.shape[1]
    half = total_rows // local_k // 2
    me = lax.axis_index("ka")
    core = jnp.bitwise_xor(jnp.bitwise_and(lax.axis_index("pts"), 1), flip)
    plane = plane_of(shares)
    for s in range(shares):
        gathered[jnp.bitwise_xor(jnp.bitwise_xor(me, s), plane)] = pieces[s][...]
    lanes = 2 * half * shares
    group = max(1, LANES // lanes)
    chunks = norb // out_rows // 2
    for g in range(local_k // group):
        right, left = [], []
        for kk in range(group):
            k = g * group + kk
            first, second = [], []
            for a in range(shares):
                piece = gathered[a, k * 2 * half : (k + 1) * 2 * half].astype(F32)
                first.append(piece)
                second.extend([piece[half:], -piece[:half]])
            first = jnp.concatenate(first, axis=0).astype(BF16)
            second = jnp.concatenate(second, axis=0).astype(BF16)
            zero = jnp.zeros_like(first)
            parts = [zero] * (2 * group)
            parts[2 * kk], parts[2 * kk + 1] = first, second
            right.append(jnp.concatenate(parts, axis=1))
            left.append(k)
        right = jnp.concatenate(right, axis=0)
        for z in range(chunks):
            start = pl.multiple_of((2 * z + core) * out_rows, out_rows)
            rows = jnp.concatenate(
                [orb_ref[k, part, pl.ds(start, out_rows), :] for k in left for part in range(2)], axis=1
            )
            out_ref[z, :, g * group * lanes : (g + 1) * group * lanes] = dot(
                rows, right, ((1,), (1,))
            ).astype(out_ref.dtype)


def pair_kernel(chunks, keep_ref, came_ref, own_ref, *outs):
    z = lax.shift_right_logical(lax.axis_index("pts"), 1)
    for s in range(chunks):
        dest = jnp.bitwise_xor(z, s)
        value = keep_ref[dest] + came_ref[dest].astype(F32)
        if s == 0:
            own_ref[...] = value
        else:
            outs[s - 1][...] = value.astype(BF16)


def exchange_kernel(chunks, shares, scale, *refs):
    pieces, form_refs, out_hbm = refs[:chunks][::-1], refs[chunks : chunks + shares], refs[chunks + shares]
    wide, out_ref, form_ref, sems = refs[chunks + shares + 1 :]
    owner = jnp.bitwise_xor(lax.axis_index("ka"), plane_of(shares))
    for j in range(shares):
        form_ref[jnp.bitwise_xor(owner, j)] = form_refs[j][...]
    _, local_k, part_lanes, twice = form_ref.shape
    lanes = shares * part_lanes
    norb = twice // 2
    spans = norb // LANES
    out_rows = pieces[0].shape[0]
    total = pieces[0][...]
    for s in range(1, chunks):
        total = total + pieces[s][...].astype(F32)
    total = total * scale
    high = total.astype(BF16)
    low = (total - high.astype(F32)).astype(BF16)
    group = max(1, LANES // lanes)
    width = group * lanes
    lane = lax.broadcasted_iota(jnp.int32, (out_rows, width), 1)
    zero = jnp.zeros((out_rows, width), BF16)
    copies = []
    for g in range(local_k // group):
        high_g = high[:, g * width : (g + 1) * width]
        low_g = low[:, g * width : (g + 1) * width]
        left = []
        for kk in range(group):
            keep = (lane >= kk * lanes) & (lane < (kk + 1) * lanes)
            left.append(
                jnp.concatenate([jnp.where(keep, high_g, zero), jnp.where(keep, low_g, zero)], axis=1)
            )
        forms = [form_ref[d, g * group + kk] for kk in range(group) for d in range(shares)]
        result = dot(jnp.concatenate(left, axis=0), jnp.concatenate(forms + forms, axis=0))
        for kk in range(group):
            for part in range(2):
                for t in range(spans):
                    lane_start = part * norb + t * LANES
                    value = result[kk * out_rows : (kk + 1) * out_rows, lane_start : lane_start + LANES]
                    start = (kk * spans + t) * 2 + part
                    wide[g, pl.ds(start, out_rows, stride=2 * spans * group), :] = value
        out_ref[g] = wide[g].astype(BF16).reshape(out_ref.shape[1:])
        copies.append(pltpu.make_async_copy(out_ref.at[g], out_hbm.at[:, g], sems.at[g]))
        copies[-1].start()
    for copy in copies:
        copy.wait()


def swap(value, axis, mask):
    size = lax.axis_size(axis)
    return lax.ppermute(value, axis, [(i, i ^ mask) for i in range(size)])


def trade(pieces, axis, step):
    return [swap(pieces[s], axis, s * step) for s in reversed(range(1, len(pieces)))] + [pieces[0]]


def body(orbitals, coulomb):
    shares, blocks = lax.axis_size("ka"), lax.axis_size("pts")
    local_k, _, norb, points = orbitals.shape
    columns = coulomb.shape[1]
    per_block = columns // blocks
    share = columns // shares
    total = local_k * shares
    out_rows = norb // blocks
    chunks = blocks // 2
    group = ROWS // (2 * per_block)
    shape = jax.ShapeDtypeStruct

    edge = call(
        functools.partial(edge_kernel, per_block),
        shape((local_k * 2 * per_block, norb), BF16),
        1,
        size=4 * MIB,
    )(orbitals)
    per_share = blocks // shares
    order = orders(shares)
    partner = swap(edge, "pts", 1)
    near = [edge, partner] + [swap(edge, "pts", 2 * e + c) for e in range(1, per_share // 2) for c in range(2)]
    came = []
    for t in range(shares - 1):
        step = []
        for e in range(per_share // 2):
            pairs = [
                (a * blocks + i, a * blocks + (i ^ (order[a][t] * per_share + 2 * e)))
                for a in range(shares)
                for i in range(blocks)
            ]
            block = lax.ppermute(edge, ("ka", "pts"), pairs)
            step += [block, swap(block, "pts", 1)]
        came.append(step)

    selector = jnp.asarray(column_selector(group, per_share, per_block, 1))
    piece = shape((share * 2 * local_k, points), BF16)
    both = shape((share * 3 * local_k, points), BF16)
    tiles, forms, before = [None] * shares, [None] * shares, []
    for targets in pieces_of(shares):
        many = len(targets)
        steps = sorted({t for j in targets for t in steps_for(j, shares)})
        taken = [block for t in steps for block in came[t]]
        result = call(
            functools.partial(tile_kernel, targets, shares, per_share, per_block),
            [both] * many + [shape((local_k, 2 * share, 2 * norb), BF16)] * many,
            len(near) + len(taken) + 3,
            [
                pltpu.VMEM((many, per_share, local_k * 2 * per_block, norb), BF16),
                tiled(many * share * 2 * local_k, points),
                pltpu.VMEM(coulomb.shape, F32),
            ],
            size=6 * MIB,
            unread=len(before),
        )(*near, *taken, orbitals, selector, coulomb, *before)
        for slot, j in enumerate(targets):
            tiles[j], forms[j] = result[slot], result[many + slot]
        before = [forms[targets[0]]]
    tiles = trade(tiles, "ka", 1)

    forward, backward = phase_tables(total)
    kernels = call(
        functools.partial(transform_kernel, shares, total, share),
        [piece] * shares,
        shares + 2,
        [
            pltpu.VMEM((shares, share * 2 * local_k, points), BF16 if local_k % 8 == 0 else F32),
            tiled(share * total, points),
            tiled(2 * total * share, points),
        ],
        size=2 * MIB,
    )(*tiles, jnp.asarray(forward), jnp.asarray(backward))
    kernels = trade(kernels, "ka", 1)

    lanes = local_k * 2 * columns
    halves = []
    for flip, kind in ((1, BF16), (0, F32)):
        halves.append(
            call(
                functools.partial(weight_kernel, shares, flip, out_rows),
                shape((chunks, out_rows, lanes), kind),
                shares + 1,
                [pltpu.VMEM((shares, share * 2 * local_k, points), BF16)],
                size=6 * MIB,
            )(*kernels, orbitals)
        )
    came = swap(halves[0], "pts", 1)
    own_sum, *sums = call(
        functools.partial(pair_kernel, chunks),
        [shape((out_rows, lanes), F32)] + [shape((out_rows, lanes), BF16)] * (chunks - 1),
        2,
        size=1 * MIB,
    )(halves[1], came)
    sums = trade([own_sum, *sums], "pts", 2)
    spans = norb // LANES
    pair = max(1, LANES // (2 * columns))
    rows = pair * spans * 2
    result = call(
        functools.partial(exchange_kernel, chunks, shares, 1.0 / math.sqrt(points * blocks)),
        shape((out_rows, local_k // pair, rows, LANES), BF16),
        chunks + shares,
        [
            pltpu.VMEM((local_k // pair, out_rows * rows, LANES), F32),
            pltpu.VMEM((local_k // pair, out_rows, rows, LANES), BF16),
            pltpu.VMEM((shares, local_k, 2 * share, 2 * norb), BF16),
            pltpu.SemaphoreType.DMA((local_k // pair,)),
        ],
        size=4 * MIB,
        result=pltpu.HBM,
    )(*sums, *forms)
    result = result.reshape(out_rows, local_k, spans, 2, LANES)
    return result.transpose(0, 1, 3, 2, 4).reshape(out_rows, local_k, 2, norb)


def solution(mesh):
    in_specs = (P("ka", None, None, "pts"), P("ka", None, "pts"))
    out_specs = P("pts", "ka", None, None)
    return jax.shard_map(body, mesh=mesh, in_specs=in_specs, out_specs=out_specs, check_vma=False)
```

```python
import functools
import math

import jax
import jax.numpy as jnp
import ml_dtypes
import numpy as np
from jax import lax
from jax.experimental import pallas as pl
from jax.experimental.pallas import tpu as pltpu
from jax.sharding import PartitionSpec as P

BF16 = jnp.bfloat16
F32 = jnp.float32
LANES = 128
ROWS = 16
MIB = 1 << 20


def split_terms(table):
    high = table.astype(ml_dtypes.bfloat16)
    low = (table - high.astype(np.float64)).astype(ml_dtypes.bfloat16)
    return np.concatenate([high, low], axis=1)


def phase_tables(total):
    index = np.arange(total)
    angles = (index[:, None] * index[None, :] % total) * (2.0 * math.pi / total)
    cosine, sine = np.cos(angles), np.sin(angles)
    forward = np.zeros((2, total, total, 2))
    forward[0, :, :, 0] = cosine
    forward[0, :, :, 1] = -sine
    forward[1, :, :, 0] = sine
    forward[1, :, :, 1] = cosine
    backward = np.zeros((total, 2, 2, total))
    backward[:, 0, 0] = cosine
    backward[:, 0, 1] = sine
    backward[:, 1, 1] = cosine
    backward[:, 1, 0] = -sine
    size = 2 * total
    return (
        split_terms(forward.reshape(size, size)),
        split_terms(backward.reshape(size, size) / total),
    )


def column_selector(group, blocks, per_block, shares):
    total = blocks * per_block
    share = total // shares
    table = np.zeros((group, 2, shares, 2, share, blocks, group, 2, per_block), np.float32)
    for k in range(group):
        for col in range(total):
            d, c = divmod(col, share)
            b, j = divmod(col, per_block)
            table[k, 0, d, 0, c, b, k, 0, j] = 1.0
            table[k, 0, d, 1, c, b, k, 1, j] = -1.0
            table[k, 1, d, 0, c, b, k, 1, j] = 1.0
            table[k, 1, d, 1, c, b, k, 0, j] = 1.0
    return table.reshape(group * 4 * total, blocks * group * 2 * per_block).astype(ml_dtypes.bfloat16)


def dot(left, right, dims=((1,), (0,))):
    return lax.dot_general(left, right, (dims, ((), ())), preferred_element_type=F32)


def spread(wide, start, stride, value):
    for t in range(wide.shape[0]):
        wide[t, pl.ds(start, value.shape[0], stride=stride), :] = value[:, t * LANES : (t + 1) * LANES]


def take(wide, start, size):
    return jnp.concatenate([wide[t, pl.ds(start, size), :] for t in range(wide.shape[0])], axis=1)


def tiled(rows, lanes):
    return pltpu.VMEM((lanes // LANES, rows, LANES), F32)


def call(kernel, out_shape, n_in, scratch=(), limit=24, flops=0, size=0, unread=0, result=pltpu.VMEM):
    whole = pl.BlockSpec(memory_space=pltpu.VMEM)
    return pl.pallas_call(
        kernel,
        out_shape=out_shape,
        in_specs=[whole] * n_in + [pl.BlockSpec(memory_space=pl.ANY)] * unread,
        out_specs=jax.tree.map(lambda _: pl.BlockSpec(memory_space=result), out_shape),
        scratch_shapes=list(scratch),
        compiler_params=pltpu.CompilerParams(vmem_limit_bytes=limit * MIB),
        cost_estimate=pl.CostEstimate(flops=flops, bytes_accessed=size, transcendentals=0),
    )


def edge_kernel(per_block, orb_hbm, edge_ref, orb_ref, sems):
    local_k = orb_hbm.shape[0]
    copies = [pltpu.make_async_copy(orb_hbm.at[k], orb_ref.at[k], sems.at[k]) for k in range(local_k)]
    for copy in copies:
        copy.start()
    row = lax.broadcasted_iota(jnp.int32, (2 * per_block, LANES), 0)
    lane = lax.broadcasted_iota(jnp.int32, (2 * per_block, LANES), 1)
    one, zero = jnp.ones(row.shape, F32), jnp.zeros(row.shape, F32)
    first = jnp.where((row < per_block) & (row == lane), one, zero).astype(BF16)
    second = jnp.where((row >= per_block) & (row == lane + per_block), one, zero).astype(BF16)
    group = ROWS // (2 * per_block)
    for g in range(local_k // group):
        rows = []
        for k in range(g * group, (g + 1) * group):
            copies[k].wait()
            rows.append(
                dot(first, orb_ref[k, 0, :, :LANES], ((1,), (1,)))
                + dot(second, orb_ref[k, 1, :, :LANES], ((1,), (1,)))
            )
        edge_ref[g * ROWS : (g + 1) * ROWS] = jnp.concatenate(rows, axis=0).astype(BF16)


def orders(shares):
    return [[a ^ j for j in reversed(range(shares)) if a ^ j] for a in range(shares)]


def pick(table, index):
    value = jnp.int32(table[0])
    for i in range(1, len(table)):
        value = jnp.where(index == i, jnp.int32(table[i]), value)
    return value


def steps_for(j, shares):
    order = orders(shares)
    return sorted({order[a].index(a ^ j) for a in range(shares) if a ^ j})


def pieces_of(shares):
    half = shares // 2
    return [list(reversed(range(half, shares))), list(reversed(range(half)))]


def plane_of(shares):
    return lax.div(lax.axis_index("pts"), lax.axis_size("pts") // shares)


def tile_kernel(targets, shares, per_share, per_block, *refs):
    steps = sorted({t for j in targets for t in steps_for(j, shares)})
    n, many = per_share * (1 + len(steps)), len(targets)
    blocks, (orb_ref, sel_ref, coulomb_ref) = refs[:n], refs[n : n + 3]
    *refs, gathered, wide, cells = refs[-2 * many - 3 :]
    outs, form_refs = refs[:many], refs[many:]
    local_k, _, norb, points = orb_ref.shape
    group = ROWS // (2 * per_block)
    share = per_share * per_block
    rows = 2 * share
    me, block = lax.axis_index("ka"), lax.axis_index("pts")
    order = orders(shares)
    for i, t in enumerate([None] + steps):
        here = 0 if t is None else pick([order[a][t] for a in range(shares)], me)
        for slot, j in enumerate(targets):

            @pl.when(jnp.bitwise_xor(me, j) == here)
            def _(i=i, slot=slot):
                for e in range(per_share):
                    place = jnp.bitwise_xor(jnp.bitwise_and(block, per_share - 1), e)
                    gathered[slot, place] = blocks[i * per_share + e][...]

    for g in range(local_k // group):
        forms = []
        for slot in range(many):
            stacked = jnp.concatenate(
                [gathered[slot, b, g * ROWS : (g + 1) * ROWS] for b in range(per_share)], axis=0
            )
            forms.append(dot(sel_ref[...], stacked).astype(BF16))
        for kk in range(group):
            k = g * group + kk
            left = [form[2 * kk * rows : (2 * kk + 1) * rows] for form in forms]
            right = [form[(2 * kk + 1) * rows : (2 * kk + 2) * rows] for form in forms]
            form = jnp.concatenate(
                [jnp.concatenate(left, axis=0), jnp.concatenate(right, axis=0)], axis=1
            )
            tile = dot(form, orb_ref[k].reshape(2 * norb, points))
            for slot in range(many):
                form_refs[slot][k] = form[slot * rows : (slot + 1) * rows]
                for part in range(2):
                    low = slot * rows + part * share
                    start = slot * share * 2 * local_k + 2 * k + part
                    spread(wide, start, 2 * local_k, tile[low : low + share])
    size = share * 2 * local_k
    cells[...] = coulomb_ref[...].astype(F32)
    for slot, j in enumerate(targets):
        outs[slot][:size] = take(wide, slot * size, size).astype(BF16)
        owned = jnp.bitwise_xor(jnp.bitwise_xor(me, j), plane_of(shares))
        start = pl.multiple_of(owned * share, share)
        pieces = [cells[r, pl.ds(start, share), :] for r in range(local_k)]
        outs[slot][size:] = jnp.concatenate(pieces, axis=0).astype(BF16)


def transform_kernel(shares, total, share, *refs):
    tiles, (fwd_ref, bwd_ref) = refs[:shares][::-1], refs[shares : shares + 2]
    outs, (gathered, weight, wide) = refs[shares + 2 : 2 * shares + 2], refs[2 * shares + 2 :]
    local_k = total // shares
    size = 2 * local_k * share
    me = lax.axis_index("ka")
    for s in range(shares):
        src = jnp.bitwise_xor(me, s)
        gathered[src] = tiles[s][:size].astype(gathered.dtype)
        cells = tiles[s][size:].astype(F32)
        for r in range(local_k):
            spread(weight, src * local_k + r, total, cells[r * share : (r + 1) * share])
    rows = 2 * local_k
    columns = []
    for c in range(share):
        columns.append(
            jnp.concatenate([gathered[a, c * rows : (c + 1) * rows] for a in range(shares)], axis=0).astype(BF16)
        )
    values = jnp.concatenate(columns, axis=1)
    cells = dot(fwd_ref[...], jnp.concatenate([values, values], axis=0))
    scale = jnp.concatenate([take(weight, c * total, total) for c in range(share)], axis=1)
    cells = (cells * jnp.concatenate([scale, scale], axis=0)).astype(BF16)
    kernel = dot(bwd_ref[...], jnp.concatenate([cells, cells], axis=0))
    points = kernel.shape[1] // share
    for c in range(share):
        spread(wide, c, share, kernel[:, c * points : (c + 1) * points])
    for s in range(shares):
        dest = jnp.bitwise_xor(me, s)
        outs[s][...] = take(wide, pl.multiple_of(dest * size, size), size).astype(BF16)


def weight_kernel(shares, flip, out_rows, *refs):
    pieces, orb_ref, out_ref, gathered = refs[:shares][::-1], refs[shares], refs[shares + 1], refs[shares + 2]
    local_k, _, norb, points = orb_ref.shape
    total_rows = gathered.shape[1]
    half = total_rows // local_k // 2
    me = lax.axis_index("ka")
    core = jnp.bitwise_xor(jnp.bitwise_and(lax.axis_index("pts"), 1), flip)
    plane = plane_of(shares)
    for s in range(shares):
        gathered[jnp.bitwise_xor(jnp.bitwise_xor(me, s), plane)] = pieces[s][...]
    lanes = 2 * half * shares
    group = max(1, LANES // lanes)
    chunks = norb // out_rows // 2
    for g in range(local_k // group):
        right, left = [], []
        for kk in range(group):
            k = g * group + kk
            first, second = [], []
            for a in range(shares):
                piece = gathered[a, k * 2 * half : (k + 1) * 2 * half].astype(F32)
                first.append(piece)
                second.extend([piece[half:], -piece[:half]])
            first = jnp.concatenate(first, axis=0).astype(BF16)
            second = jnp.concatenate(second, axis=0).astype(BF16)
            zero = jnp.zeros_like(first)
            parts = [zero] * (2 * group)
            parts[2 * kk], parts[2 * kk + 1] = first, second
            right.append(jnp.concatenate(parts, axis=1))
            left.append(k)
        right = jnp.concatenate(right, axis=0)
        for z in range(chunks):
            start = pl.multiple_of((2 * z + core) * out_rows, out_rows)
            rows = jnp.concatenate(
                [orb_ref[k, part, pl.ds(start, out_rows), :] for k in left for part in range(2)], axis=1
            )
            out_ref[z, :, g * group * lanes : (g + 1) * group * lanes] = dot(
                rows, right, ((1,), (1,))
            ).astype(out_ref.dtype)


def pair_kernel(chunks, keep_ref, came_ref, own_ref, *outs):
    z = lax.shift_right_logical(lax.axis_index("pts"), 1)
    for s in range(chunks):
        dest = jnp.bitwise_xor(z, s)
        value = keep_ref[dest] + came_ref[dest].astype(F32)
        if s == 0:
            own_ref[...] = value
        else:
            outs[s - 1][...] = value.astype(BF16)


def exchange_kernel(chunks, shares, scale, *refs):
    pieces, form_refs, out_hbm = refs[:chunks][::-1], refs[chunks : chunks + shares], refs[chunks + shares]
    wide, out_ref, form_ref, sems = refs[chunks + shares + 1 :]
    owner = jnp.bitwise_xor(lax.axis_index("ka"), plane_of(shares))
    for j in range(shares):
        form_ref[jnp.bitwise_xor(owner, j)] = form_refs[j][...]
    _, local_k, part_lanes, twice = form_ref.shape
    lanes = shares * part_lanes
    norb = twice // 2
    spans = norb // LANES
    out_rows = pieces[0].shape[0]
    total = pieces[0][...]
    for s in range(1, chunks):
        total = total + pieces[s][...].astype(F32)
    total = total * scale
    high = total.astype(BF16)
    low = (total - high.astype(F32)).astype(BF16)
    group = max(1, LANES // lanes)
    width = group * lanes
    lane = lax.broadcasted_iota(jnp.int32, (out_rows, width), 1)
    zero = jnp.zeros((out_rows, width), BF16)
    copies = []
    for g in range(local_k // group):
        high_g = high[:, g * width : (g + 1) * width]
        low_g = low[:, g * width : (g + 1) * width]
        left = []
        for kk in range(group):
            keep = (lane >= kk * lanes) & (lane < (kk + 1) * lanes)
            left.append(
                jnp.concatenate([jnp.where(keep, high_g, zero), jnp.where(keep, low_g, zero)], axis=1)
            )
        forms = [form_ref[d, g * group + kk] for kk in range(group) for d in range(shares)]
        result = dot(jnp.concatenate(left, axis=0), jnp.concatenate(forms + forms, axis=0))
        for kk in range(group):
            for part in range(2):
                for t in range(spans):
                    lane_start = part * norb + t * LANES
                    value = result[kk * out_rows : (kk + 1) * out_rows, lane_start : lane_start + LANES]
                    start = (kk * spans + t) * 2 + part
                    wide[g, pl.ds(start, out_rows, stride=2 * spans * group), :] = value
        out_ref[g] = wide[g].astype(BF16).reshape(out_ref.shape[1:])
        copies.append(pltpu.make_async_copy(out_ref.at[g], out_hbm.at[:, g], sems.at[g]))
        copies[-1].start()
    for copy in copies:
        copy.wait()


def swap(value, axis, mask):
    size = lax.axis_size(axis)
    return lax.ppermute(value, axis, [(i, i ^ mask) for i in range(size)])


def trade(pieces, axis, step):
    return [swap(pieces[s], axis, s * step) for s in reversed(range(1, len(pieces)))] + [pieces[0]]


def body(orbitals, coulomb):
    shares, blocks = lax.axis_size("ka"), lax.axis_size("pts")
    local_k, _, norb, points = orbitals.shape
    columns = coulomb.shape[1]
    per_block = columns // blocks
    share = columns // shares
    total = local_k * shares
    out_rows = norb // blocks
    chunks = blocks // 2
    group = ROWS // (2 * per_block)
    shape = jax.ShapeDtypeStruct

    edge, orbitals = call(
        functools.partial(edge_kernel, per_block),
        [shape((local_k * 2 * per_block, norb), BF16), shape(orbitals.shape, BF16)],
        0,
        [pltpu.SemaphoreType.DMA((local_k,))],
        limit=47,
        size=8 * MIB,
        unread=1,
    )(orbitals)
    per_share = blocks // shares
    order = orders(shares)
    partner = swap(edge, "pts", 1)
    near = [edge, partner] + [swap(edge, "pts", 2 * e + c) for e in range(1, per_share // 2) for c in range(2)]
    came = []
    for t in range(shares - 1):
        step = []
        for e in range(per_share // 2):
            pairs = [
                (a * blocks + i, a * blocks + (i ^ (order[a][t] * per_share + 2 * e)))
                for a in range(shares)
                for i in range(blocks)
            ]
            block = lax.ppermute(edge, ("ka", "pts"), pairs)
            step += [block, swap(block, "pts", 1)]
        came.append(step)

    selector = jnp.asarray(column_selector(group, per_share, per_block, 1))
    piece = shape((share * 2 * local_k, points), BF16)
    both = shape((share * 3 * local_k, points), BF16)
    tiles, forms, before = [None] * shares, [None] * shares, []
    for targets in pieces_of(shares):
        many = len(targets)
        steps = sorted({t for j in targets for t in steps_for(j, shares)})
        taken = [block for t in steps for block in came[t]]
        result = call(
            functools.partial(tile_kernel, targets, shares, per_share, per_block),
            [both] * many + [shape((local_k, 2 * share, 2 * norb), BF16)] * many,
            len(near) + len(taken) + 3,
            [
                pltpu.VMEM((many, per_share, local_k * 2 * per_block, norb), BF16),
                tiled(many * share * 2 * local_k, points),
                pltpu.VMEM(coulomb.shape, F32),
            ],
            size=6 * MIB,
            unread=len(before),
        )(*near, *taken, orbitals, selector, coulomb, *before)
        for slot, j in enumerate(targets):
            tiles[j], forms[j] = result[slot], result[many + slot]
        before = [forms[targets[0]]]
    tiles = trade(tiles, "ka", 1)

    forward, backward = phase_tables(total)
    kernels = call(
        functools.partial(transform_kernel, shares, total, share),
        [piece] * shares,
        shares + 2,
        [
            pltpu.VMEM((shares, share * 2 * local_k, points), BF16 if local_k % 8 == 0 else F32),
            tiled(share * total, points),
            tiled(2 * total * share, points),
        ],
        size=2 * MIB,
    )(*tiles, jnp.asarray(forward), jnp.asarray(backward))
    kernels = trade(kernels, "ka", 1)

    lanes = local_k * 2 * columns
    halves = []
    for flip, kind in ((1, BF16), (0, F32)):
        halves.append(
            call(
                functools.partial(weight_kernel, shares, flip, out_rows),
                shape((chunks, out_rows, lanes), kind),
                shares + 1,
                [pltpu.VMEM((shares, share * 2 * local_k, points), BF16)],
                size=6 * MIB,
            )(*kernels, orbitals)
        )
    came = swap(halves[0], "pts", 1)
    own_sum, *sums = call(
        functools.partial(pair_kernel, chunks),
        [shape((out_rows, lanes), F32)] + [shape((out_rows, lanes), BF16)] * (chunks - 1),
        2,
        size=1 * MIB,
    )(halves[1], came)
    sums = trade([own_sum, *sums], "pts", 2)
    spans = norb // LANES
    pair = max(1, LANES // (2 * columns))
    rows = pair * spans * 2
    result = call(
        functools.partial(exchange_kernel, chunks, shares, 1.0 / math.sqrt(points * blocks)),
        shape((out_rows, local_k // pair, rows, LANES), BF16),
        chunks + shares,
        [
            pltpu.VMEM((local_k // pair, out_rows * rows, LANES), F32),
            pltpu.VMEM((local_k // pair, out_rows, rows, LANES), BF16),
            pltpu.VMEM((shares, local_k, 2 * share, 2 * norb), BF16),
            pltpu.SemaphoreType.DMA((local_k // pair,)),
        ],
        size=4 * MIB,
        result=pltpu.HBM,
    )(*sums, *forms)
    result = result.reshape(out_rows, local_k, spans, 2, LANES)
    return result.transpose(0, 1, 3, 2, 4).reshape(out_rows, local_k, 2, norb)


def solution(mesh):
    in_specs = (P("ka", None, None, "pts"), P("ka", None, "pts"))
    out_specs = P("pts", "ka", None, None)
    return jax.shard_map(body, mesh=mesh, in_specs=in_specs, out_specs=out_specs, check_vma=False)
```

```python
import functools
import math

import jax
import jax.numpy as jnp
import ml_dtypes
import numpy as np
from jax import lax
from jax.experimental import pallas as pl
from jax.experimental.pallas import tpu as pltpu
from jax.sharding import PartitionSpec as P

BF16 = jnp.bfloat16
F32 = jnp.float32
LANES = 128
ROWS = 16
MIB = 1 << 20


def split_terms(table):
    high = table.astype(ml_dtypes.bfloat16)
    low = (table - high.astype(np.float64)).astype(ml_dtypes.bfloat16)
    return np.concatenate([high, low], axis=1)


def phase_tables(total):
    index = np.arange(total)
    angles = (index[:, None] * index[None, :] % total) * (2.0 * math.pi / total)
    cosine, sine = np.cos(angles), np.sin(angles)
    forward = np.zeros((2, total, total, 2))
    forward[0, :, :, 0] = cosine
    forward[0, :, :, 1] = -sine
    forward[1, :, :, 0] = sine
    forward[1, :, :, 1] = cosine
    backward = np.zeros((total, 2, 2, total))
    backward[:, 0, 0] = cosine
    backward[:, 0, 1] = sine
    backward[:, 1, 1] = cosine
    backward[:, 1, 0] = -sine
    size = 2 * total
    return (
        split_terms(forward.reshape(size, size)),
        split_terms(backward.reshape(size, size) / total),
    )


def column_selector(group, blocks, per_block, shares):
    total = blocks * per_block
    share = total // shares
    table = np.zeros((group, 2, shares, 2, share, blocks, group, 2, per_block), np.float32)
    for k in range(group):
        for col in range(total):
            d, c = divmod(col, share)
            b, j = divmod(col, per_block)
            table[k, 0, d, 0, c, b, k, 0, j] = 1.0
            table[k, 0, d, 1, c, b, k, 1, j] = -1.0
            table[k, 1, d, 0, c, b, k, 1, j] = 1.0
            table[k, 1, d, 1, c, b, k, 0, j] = 1.0
    return table.reshape(group * 4 * total, blocks * group * 2 * per_block).astype(ml_dtypes.bfloat16)


def dot(left, right, dims=((1,), (0,))):
    return lax.dot_general(left, right, (dims, ((), ())), preferred_element_type=F32)


def spread(wide, start, stride, value):
    for t in range(wide.shape[0]):
        wide[t, pl.ds(start, value.shape[0], stride=stride), :] = value[:, t * LANES : (t + 1) * LANES]


def take(wide, start, size):
    return jnp.concatenate([wide[t, pl.ds(start, size), :] for t in range(wide.shape[0])], axis=1)


def tiled(rows, lanes):
    return pltpu.VMEM((lanes // LANES, rows, LANES), F32)


def call(kernel, out_shape, n_in, scratch=(), limit=24, flops=0, size=0, unread=0, result=pltpu.VMEM):
    whole = pl.BlockSpec(memory_space=pltpu.VMEM)
    return pl.pallas_call(
        kernel,
        out_shape=out_shape,
        in_specs=[whole] * n_in + [pl.BlockSpec(memory_space=pl.ANY)] * unread,
        out_specs=jax.tree.map(lambda _: pl.BlockSpec(memory_space=result), out_shape),
        scratch_shapes=list(scratch),
        compiler_params=pltpu.CompilerParams(vmem_limit_bytes=limit * MIB),
        cost_estimate=pl.CostEstimate(flops=flops, bytes_accessed=size, transcendentals=0),
    )


def edge_kernel(per_block, orb_hbm, edge_ref, orb_ref, sems):
    local_k = orb_hbm.shape[0]
    copies = [pltpu.make_async_copy(orb_hbm.at[k], orb_ref.at[k], sems.at[k]) for k in range(local_k)]
    for copy in copies:
        copy.start()
    row = lax.broadcasted_iota(jnp.int32, (2 * per_block, LANES), 0)
    lane = lax.broadcasted_iota(jnp.int32, (2 * per_block, LANES), 1)
    one, zero = jnp.ones(row.shape, F32), jnp.zeros(row.shape, F32)
    first = jnp.where((row < per_block) & (row == lane), one, zero).astype(BF16)
    second = jnp.where((row >= per_block) & (row == lane + per_block), one, zero).astype(BF16)
    group = ROWS // (2 * per_block)
    for g in range(local_k // group):
        rows = []
        for k in range(g * group, (g + 1) * group):
            copies[k].wait()
            rows.append(
                dot(first, orb_ref[k, 0, :, :LANES], ((1,), (1,)))
                + dot(second, orb_ref[k, 1, :, :LANES], ((1,), (1,)))
            )
        edge_ref[g * ROWS : (g + 1) * ROWS] = jnp.concatenate(rows, axis=0).astype(BF16)


def orders(shares):
    return [list(reversed(range(1, shares)))] * shares


def pick(table, index):
    value = jnp.int32(table[0])
    for i in range(1, len(table)):
        value = jnp.where(index == i, jnp.int32(table[i]), value)
    return value


def steps_for(j, shares):
    order = orders(shares)
    return sorted({order[a].index(a ^ j) for a in range(shares) if a ^ j})


def pieces_of(shares):
    return [list(reversed(range(shares)))]


def plane_of(shares):
    return lax.div(lax.axis_index("pts"), lax.axis_size("pts") // shares)


def tile_kernel(targets, shares, per_share, per_block, *refs):
    steps = sorted({t for j in targets for t in steps_for(j, shares)})
    n, many = per_share * (1 + len(steps)), len(targets)
    blocks, (orb_ref, sel_ref, coulomb_ref) = refs[:n], refs[n : n + 3]
    *refs, gathered, wide, cells = refs[-2 * many - 3 :]
    outs, form_refs = refs[:many], refs[many:]
    local_k, _, norb, points = orb_ref.shape
    group = ROWS // (2 * per_block)
    share = per_share * per_block
    rows = 2 * share
    me, block = lax.axis_index("ka"), lax.axis_index("pts")
    order = orders(shares)
    for i, t in enumerate([None] + steps):
        here = 0 if t is None else pick([order[a][t] for a in range(shares)], me)
        for slot, j in enumerate(targets):

            @pl.when(jnp.bitwise_xor(me, j) == here)
            def _(i=i, slot=slot):
                for e in range(per_share):
                    place = jnp.bitwise_xor(jnp.bitwise_and(block, per_share - 1), e)
                    gathered[slot, place] = blocks[i * per_share + e][...]

    for g in range(local_k // group):
        forms = []
        for slot in range(many):
            stacked = jnp.concatenate(
                [gathered[slot, b, g * ROWS : (g + 1) * ROWS] for b in range(per_share)], axis=0
            )
            forms.append(dot(sel_ref[...], stacked).astype(BF16))
        for kk in range(group):
            k = g * group + kk
            left = [form[2 * kk * rows : (2 * kk + 1) * rows] for form in forms]
            right = [form[(2 * kk + 1) * rows : (2 * kk + 2) * rows] for form in forms]
            form = jnp.concatenate(
                [jnp.concatenate(left, axis=0), jnp.concatenate(right, axis=0)], axis=1
            )
            tile = dot(form, orb_ref[k].reshape(2 * norb, points))
            for slot in range(many):
                form_refs[slot][k] = form[slot * rows : (slot + 1) * rows]
                for part in range(2):
                    low = slot * rows + part * share
                    start = slot * share * 2 * local_k + 2 * k + part
                    spread(wide, start, 2 * local_k, tile[low : low + share])
    size = share * 2 * local_k
    cells[...] = coulomb_ref[...].astype(F32)
    for slot, j in enumerate(targets):
        outs[slot][:size] = take(wide, slot * size, size).astype(BF16)
        owned = jnp.bitwise_xor(jnp.bitwise_xor(me, j), plane_of(shares))
        start = pl.multiple_of(owned * share, share)
        pieces = [cells[r, pl.ds(start, share), :] for r in range(local_k)]
        outs[slot][size:] = jnp.concatenate(pieces, axis=0).astype(BF16)


def transform_kernel(shares, total, share, *refs):
    tiles, (fwd_ref, bwd_ref) = refs[:shares][::-1], refs[shares : shares + 2]
    outs, (gathered, weight, wide) = refs[shares + 2 : 2 * shares + 2], refs[2 * shares + 2 :]
    local_k = total // shares
    size = 2 * local_k * share
    me = lax.axis_index("ka")
    for s in range(shares):
        src = jnp.bitwise_xor(me, s)
        gathered[src] = tiles[s][:size].astype(gathered.dtype)
        cells = tiles[s][size:].astype(F32)
        for r in range(local_k):
            spread(weight, src * local_k + r, total, cells[r * share : (r + 1) * share])
    rows = 2 * local_k
    columns = []
    for c in range(share):
        columns.append(
            jnp.concatenate([gathered[a, c * rows : (c + 1) * rows] for a in range(shares)], axis=0).astype(BF16)
        )
    values = jnp.concatenate(columns, axis=1)
    cells = dot(fwd_ref[...], jnp.concatenate([values, values], axis=0))
    scale = jnp.concatenate([take(weight, c * total, total) for c in range(share)], axis=1)
    cells = (cells * jnp.concatenate([scale, scale], axis=0)).astype(BF16)
    kernel = dot(bwd_ref[...], jnp.concatenate([cells, cells], axis=0))
    points = kernel.shape[1] // share
    for c in range(share):
        spread(wide, c, share, kernel[:, c * points : (c + 1) * points])
    for s in range(shares):
        dest = jnp.bitwise_xor(me, s)
        outs[s][...] = take(wide, pl.multiple_of(dest * size, size), size).astype(BF16)


def weight_kernel(shares, flip, out_rows, *refs):
    pieces, orb_ref, out_ref, gathered = refs[:shares][::-1], refs[shares], refs[shares + 1], refs[shares + 2]
    local_k, _, norb, points = orb_ref.shape
    total_rows = gathered.shape[1]
    half = total_rows // local_k // 2
    me = lax.axis_index("ka")
    core = jnp.bitwise_xor(jnp.bitwise_and(lax.axis_index("pts"), 1), flip)
    plane = plane_of(shares)
    for s in range(shares):
        gathered[jnp.bitwise_xor(jnp.bitwise_xor(me, s), plane)] = pieces[s][...]
    lanes = 2 * half * shares
    group = max(1, LANES // lanes)
    chunks = norb // out_rows // 2
    for g in range(local_k // group):
        right, left = [], []
        for kk in range(group):
            k = g * group + kk
            first, second = [], []
            for a in range(shares):
                piece = gathered[a, k * 2 * half : (k + 1) * 2 * half].astype(F32)
                first.append(piece)
                second.extend([piece[half:], -piece[:half]])
            first = jnp.concatenate(first, axis=0).astype(BF16)
            second = jnp.concatenate(second, axis=0).astype(BF16)
            zero = jnp.zeros_like(first)
            parts = [zero] * (2 * group)
            parts[2 * kk], parts[2 * kk + 1] = first, second
            right.append(jnp.concatenate(parts, axis=1))
            left.append(k)
        right = jnp.concatenate(right, axis=0)
        for z in range(chunks):
            start = pl.multiple_of((2 * z + core) * out_rows, out_rows)
            rows = jnp.concatenate(
                [orb_ref[k, part, pl.ds(start, out_rows), :] for k in left for part in range(2)], axis=1
            )
            out_ref[z, :, g * group * lanes : (g + 1) * group * lanes] = dot(
                rows, right, ((1,), (1,))
            ).astype(out_ref.dtype)


def pair_kernel(chunks, keep_ref, came_ref, own_ref, *outs):
    z = lax.shift_right_logical(lax.axis_index("pts"), 1)
    for s in range(chunks):
        dest = jnp.bitwise_xor(z, s)
        value = keep_ref[dest] + came_ref[dest].astype(F32)
        if s == 0:
            own_ref[...] = value
        else:
            outs[s - 1][...] = value.astype(BF16)


def exchange_kernel(chunks, shares, scale, *refs):
    pieces, form_refs, out_hbm = refs[:chunks][::-1], refs[chunks : chunks + shares], refs[chunks + shares]
    wide, out_ref, form_ref, sems = refs[chunks + shares + 1 :]
    owner = jnp.bitwise_xor(lax.axis_index("ka"), plane_of(shares))
    for j in range(shares):
        form_ref[jnp.bitwise_xor(owner, j)] = form_refs[j][...]
    _, local_k, part_lanes, twice = form_ref.shape
    lanes = shares * part_lanes
    norb = twice // 2
    spans = norb // LANES
    out_rows = pieces[0].shape[0]
    total = pieces[0][...]
    for s in range(1, chunks):
        total = total + pieces[s][...].astype(F32)
    total = total * scale
    high = total.astype(BF16)
    low = (total - high.astype(F32)).astype(BF16)
    group = max(1, LANES // lanes)
    width = group * lanes
    lane = lax.broadcasted_iota(jnp.int32, (out_rows, width), 1)
    zero = jnp.zeros((out_rows, width), BF16)
    copies = []
    for g in range(local_k // group):
        high_g = high[:, g * width : (g + 1) * width]
        low_g = low[:, g * width : (g + 1) * width]
        left = []
        for kk in range(group):
            keep = (lane >= kk * lanes) & (lane < (kk + 1) * lanes)
            left.append(
                jnp.concatenate([jnp.where(keep, high_g, zero), jnp.where(keep, low_g, zero)], axis=1)
            )
        forms = [form_ref[d, g * group + kk] for kk in range(group) for d in range(shares)]
        result = dot(jnp.concatenate(left, axis=0), jnp.concatenate(forms + forms, axis=0))
        for kk in range(group):
            for part in range(2):
                for t in range(spans):
                    lane_start = part * norb + t * LANES
                    value = result[kk * out_rows : (kk + 1) * out_rows, lane_start : lane_start + LANES]
                    start = (kk * spans + t) * 2 + part
                    wide[g, pl.ds(start, out_rows, stride=2 * spans * group), :] = value
        out_ref[g] = wide[g].astype(BF16).reshape(out_ref.shape[1:])
        copies.append(pltpu.make_async_copy(out_ref.at[g], out_hbm.at[:, g], sems.at[g]))
        copies[-1].start()
    for copy in copies:
        copy.wait()


def swap(value, axis, mask):
    size = lax.axis_size(axis)
    return lax.ppermute(value, axis, [(i, i ^ mask) for i in range(size)])


def trade(pieces, axis, step):
    return [swap(pieces[s], axis, s * step) for s in reversed(range(1, len(pieces)))] + [pieces[0]]


def body(orbitals, coulomb):
    shares, blocks = lax.axis_size("ka"), lax.axis_size("pts")
    local_k, _, norb, points = orbitals.shape
    columns = coulomb.shape[1]
    per_block = columns // blocks
    share = columns // shares
    total = local_k * shares
    out_rows = norb // blocks
    chunks = blocks // 2
    group = ROWS // (2 * per_block)
    shape = jax.ShapeDtypeStruct

    edge, orbitals = call(
        functools.partial(edge_kernel, per_block),
        [shape((local_k * 2 * per_block, norb), BF16), shape(orbitals.shape, BF16)],
        0,
        [pltpu.SemaphoreType.DMA((local_k,))],
        limit=47,
        size=8 * MIB,
        unread=1,
    )(orbitals)
    per_share = blocks // shares
    order = orders(shares)
    partner = swap(edge, "pts", 1)
    near = [edge, partner] + [swap(edge, "pts", 2 * e + c) for e in range(1, per_share // 2) for c in range(2)]
    came = []
    for t in range(shares - 1):
        step = []
        for e in range(per_share // 2):
            pairs = [
                (a * blocks + i, a * blocks + (i ^ (order[a][t] * per_share + 2 * e)))
                for a in range(shares)
                for i in range(blocks)
            ]
            block = lax.ppermute(edge, ("ka", "pts"), pairs)
            step += [block, swap(block, "pts", 1)]
        came.append(step)

    selector = jnp.asarray(column_selector(group, per_share, per_block, 1))
    piece = shape((share * 2 * local_k, points), BF16)
    both = shape((share * 3 * local_k, points), BF16)
    tiles, forms, before = [None] * shares, [None] * shares, []
    for targets in pieces_of(shares):
        many = len(targets)
        steps = sorted({t for j in targets for t in steps_for(j, shares)})
        taken = [block for t in steps for block in came[t]]
        result = call(
            functools.partial(tile_kernel, targets, shares, per_share, per_block),
            [both] * many + [shape((local_k, 2 * share, 2 * norb), BF16)] * many,
            len(near) + len(taken) + 3,
            [
                pltpu.VMEM((many, per_share, local_k * 2 * per_block, norb), BF16),
                tiled(many * share * 2 * local_k, points),
                pltpu.VMEM(coulomb.shape, F32),
            ],
            size=6 * MIB,
            unread=len(before),
        )(*near, *taken, orbitals, selector, coulomb, *before)
        for slot, j in enumerate(targets):
            tiles[j], forms[j] = result[slot], result[many + slot]
        before = [forms[targets[0]]]
    tiles = trade(tiles, "ka", 1)

    forward, backward = phase_tables(total)
    kernels = call(
        functools.partial(transform_kernel, shares, total, share),
        [piece] * shares,
        shares + 2,
        [
            pltpu.VMEM((shares, share * 2 * local_k, points), BF16 if local_k % 8 == 0 else F32),
            tiled(share * total, points),
            tiled(2 * total * share, points),
        ],
        size=2 * MIB,
    )(*tiles, jnp.asarray(forward), jnp.asarray(backward))
    kernels = trade(kernels, "ka", 1)

    lanes = local_k * 2 * columns
    halves = []
    for flip, kind in ((1, BF16), (0, F32)):
        halves.append(
            call(
                functools.partial(weight_kernel, shares, flip, out_rows),
                shape((chunks, out_rows, lanes), kind),
                shares + 1,
                [pltpu.VMEM((shares, share * 2 * local_k, points), BF16)],
                size=6 * MIB,
            )(*kernels, orbitals)
        )
    came = swap(halves[0], "pts", 1)
    own_sum, *sums = call(
        functools.partial(pair_kernel, chunks),
        [shape((out_rows, lanes), F32)] + [shape((out_rows, lanes), BF16)] * (chunks - 1),
        2,
        size=1 * MIB,
    )(halves[1], came)
    sums = trade([own_sum, *sums], "pts", 2)
    spans = norb // LANES
    pair = max(1, LANES // (2 * columns))
    rows = pair * spans * 2
    result = call(
        functools.partial(exchange_kernel, chunks, shares, 1.0 / math.sqrt(points * blocks)),
        shape((out_rows, local_k // pair, rows, LANES), BF16),
        chunks + shares,
        [
            pltpu.VMEM((local_k // pair, out_rows * rows, LANES), F32),
            pltpu.VMEM((local_k // pair, out_rows, rows, LANES), BF16),
            pltpu.VMEM((shares, local_k, 2 * share, 2 * norb), BF16),
            pltpu.SemaphoreType.DMA((local_k // pair,)),
        ],
        size=4 * MIB,
        result=pltpu.HBM,
    )(*sums, *forms)
    result = result.reshape(out_rows, local_k, spans, 2, LANES)
    return result.transpose(0, 1, 3, 2, 4).reshape(out_rows, local_k, 2, norb)


def solution(mesh):
    in_specs = (P("ka", None, None, "pts"), P("ka", None, "pts"))
    out_specs = P("pts", "ka", None, None)
    return jax.shard_map(body, mesh=mesh, in_specs=in_specs, out_specs=out_specs, check_vma=False)
```

```python
import functools
import math

import jax
import jax.numpy as jnp
import ml_dtypes
import numpy as np
from jax import lax
from jax.experimental import pallas as pl
from jax.experimental.pallas import tpu as pltpu
from jax.sharding import PartitionSpec as P

BF16 = jnp.bfloat16
F32 = jnp.float32
LANES = 128
ROWS = 16
MIB = 1 << 20


def split_terms(table):
    high = table.astype(ml_dtypes.bfloat16)
    low = (table - high.astype(np.float64)).astype(ml_dtypes.bfloat16)
    return np.concatenate([high, low], axis=1)


def phase_tables(total):
    index = np.arange(total)
    angles = (index[:, None] * index[None, :] % total) * (2.0 * math.pi / total)
    cosine, sine = np.cos(angles), np.sin(angles)
    forward = np.zeros((2, total, total, 2))
    forward[0, :, :, 0] = cosine
    forward[0, :, :, 1] = -sine
    forward[1, :, :, 0] = sine
    forward[1, :, :, 1] = cosine
    backward = np.zeros((total, 2, 2, total))
    backward[:, 0, 0] = cosine
    backward[:, 0, 1] = sine
    backward[:, 1, 1] = cosine
    backward[:, 1, 0] = -sine
    size = 2 * total
    return (
        split_terms(forward.reshape(size, size)),
        split_terms(backward.reshape(size, size) / total),
    )


def column_selector(group, blocks, per_block, shares):
    total = blocks * per_block
    share = total // shares
    table = np.zeros((group, 2, shares, 2, share, blocks, group, 2, per_block), np.float32)
    for k in range(group):
        for col in range(total):
            d, c = divmod(col, share)
            b, j = divmod(col, per_block)
            table[k, 0, d, 0, c, b, k, 0, j] = 1.0
            table[k, 0, d, 1, c, b, k, 1, j] = -1.0
            table[k, 1, d, 0, c, b, k, 1, j] = 1.0
            table[k, 1, d, 1, c, b, k, 0, j] = 1.0
    return table.reshape(group * 4 * total, blocks * group * 2 * per_block).astype(ml_dtypes.bfloat16)


def dot(left, right, dims=((1,), (0,))):
    return lax.dot_general(left, right, (dims, ((), ())), preferred_element_type=F32)


def spread(wide, start, stride, value):
    for t in range(wide.shape[0]):
        wide[t, pl.ds(start, value.shape[0], stride=stride), :] = value[:, t * LANES : (t + 1) * LANES]


def take(wide, start, size):
    return jnp.concatenate([wide[t, pl.ds(start, size), :] for t in range(wide.shape[0])], axis=1)


def tiled(rows, lanes):
    return pltpu.VMEM((lanes // LANES, rows, LANES), F32)


def call(kernel, out_shape, n_in, scratch=(), limit=24, flops=0, size=0, unread=0, result=pltpu.VMEM):
    whole = pl.BlockSpec(memory_space=pltpu.VMEM)
    return pl.pallas_call(
        kernel,
        out_shape=out_shape,
        in_specs=[whole] * n_in + [pl.BlockSpec(memory_space=pl.ANY)] * unread,
        out_specs=jax.tree.map(lambda _: pl.BlockSpec(memory_space=result), out_shape),
        scratch_shapes=list(scratch),
        compiler_params=pltpu.CompilerParams(vmem_limit_bytes=limit * MIB),
        cost_estimate=pl.CostEstimate(flops=flops, bytes_accessed=size, transcendentals=0),
    )


def edge_kernel(per_block, orb_hbm, edge_ref, orb_ref, sems):
    local_k = orb_hbm.shape[0]
    copies = [pltpu.make_async_copy(orb_hbm.at[k], orb_ref.at[k], sems.at[k]) for k in range(local_k)]
    for copy in copies:
        copy.start()
    row = lax.broadcasted_iota(jnp.int32, (2 * per_block, LANES), 0)
    lane = lax.broadcasted_iota(jnp.int32, (2 * per_block, LANES), 1)
    one, zero = jnp.ones(row.shape, F32), jnp.zeros(row.shape, F32)
    first = jnp.where((row < per_block) & (row == lane), one, zero).astype(BF16)
    second = jnp.where((row >= per_block) & (row == lane + per_block), one, zero).astype(BF16)
    group = ROWS // (2 * per_block)
    for g in range(local_k // group):
        rows = []
        for k in range(g * group, (g + 1) * group):
            copies[k].wait()
            rows.append(
                dot(first, orb_ref[k, 0, :, :LANES], ((1,), (1,)))
                + dot(second, orb_ref[k, 1, :, :LANES], ((1,), (1,)))
            )
        edge_ref[g * ROWS : (g + 1) * ROWS] = jnp.concatenate(rows, axis=0).astype(BF16)


def orders(shares):
    return [list(range(1, shares))] * shares


def pick(table, index):
    value = jnp.int32(table[0])
    for i in range(1, len(table)):
        value = jnp.where(index == i, jnp.int32(table[i]), value)
    return value


def steps_for(j, shares):
    order = orders(shares)
    return sorted({order[a].index(a ^ j) for a in range(shares) if a ^ j})


def pieces_of(shares):
    return [list(reversed(range(shares)))]


def plane_of(shares):
    return lax.div(lax.axis_index("pts"), lax.axis_size("pts") // shares)


def tile_kernel(targets, shares, per_share, per_block, *refs):
    steps = sorted({t for j in targets for t in steps_for(j, shares)})
    n, many = per_share * (1 + len(steps)), len(targets)
    blocks, (orb_ref, sel_ref, coulomb_ref) = refs[:n], refs[n : n + 3]
    *refs, gathered, wide, cells = refs[-2 * many - 3 :]
    outs, form_refs = refs[:many], refs[many:]
    local_k, _, norb, points = orb_ref.shape
    group = ROWS // (2 * per_block)
    share = per_share * per_block
    rows = 2 * share
    me, block = lax.axis_index("ka"), lax.axis_index("pts")
    order = orders(shares)
    for i, t in enumerate([None] + steps):
        here = 0 if t is None else pick([order[a][t] for a in range(shares)], me)
        for slot, j in enumerate(targets):

            @pl.when(jnp.bitwise_xor(me, j) == here)
            def _(i=i, slot=slot):
                for e in range(per_share):
                    place = jnp.bitwise_xor(jnp.bitwise_and(block, per_share - 1), e)
                    gathered[slot, place] = blocks[i * per_share + e][...]

    for g in range(local_k // group):
        forms = []
        for slot in range(many):
            stacked = jnp.concatenate(
                [gathered[slot, b, g * ROWS : (g + 1) * ROWS] for b in range(per_share)], axis=0
            )
            forms.append(dot(sel_ref[...], stacked).astype(BF16))
        for kk in range(group):
            k = g * group + kk
            left = [form[2 * kk * rows : (2 * kk + 1) * rows] for form in forms]
            right = [form[(2 * kk + 1) * rows : (2 * kk + 2) * rows] for form in forms]
            form = jnp.concatenate(
                [jnp.concatenate(left, axis=0), jnp.concatenate(right, axis=0)], axis=1
            )
            tile = dot(form, orb_ref[k].reshape(2 * norb, points))
            for slot in range(many):
                form_refs[slot][k] = form[slot * rows : (slot + 1) * rows]
                for part in range(2):
                    low = slot * rows + part * share
                    start = slot * share * 2 * local_k + 2 * k + part
                    spread(wide, start, 2 * local_k, tile[low : low + share])
    size = share * 2 * local_k
    cells[...] = coulomb_ref[...].astype(F32)
    for slot, j in enumerate(targets):
        outs[slot][:size] = take(wide, slot * size, size).astype(BF16)
        owned = jnp.bitwise_xor(jnp.bitwise_xor(me, j), plane_of(shares))
        start = pl.multiple_of(owned * share, share)
        pieces = [cells[r, pl.ds(start, share), :] for r in range(local_k)]
        outs[slot][size:] = jnp.concatenate(pieces, axis=0).astype(BF16)


def transform_kernel(shares, total, share, *refs):
    tiles, (fwd_ref, bwd_ref) = refs[:shares][::-1], refs[shares : shares + 2]
    outs, (gathered, weight, wide) = refs[shares + 2 : 2 * shares + 2], refs[2 * shares + 2 :]
    local_k = total // shares
    size = 2 * local_k * share
    me = lax.axis_index("ka")
    for s in range(shares):
        src = jnp.bitwise_xor(me, s)
        gathered[src] = tiles[s][:size].astype(gathered.dtype)
        cells = tiles[s][size:].astype(F32)
        for r in range(local_k):
            spread(weight, src * local_k + r, total, cells[r * share : (r + 1) * share])
    rows = 2 * local_k
    columns = []
    for c in range(share):
        columns.append(
            jnp.concatenate([gathered[a, c * rows : (c + 1) * rows] for a in range(shares)], axis=0).astype(BF16)
        )
    values = jnp.concatenate(columns, axis=1)
    cells = dot(fwd_ref[...], jnp.concatenate([values, values], axis=0))
    scale = jnp.concatenate([take(weight, c * total, total) for c in range(share)], axis=1)
    cells = (cells * jnp.concatenate([scale, scale], axis=0)).astype(BF16)
    kernel = dot(bwd_ref[...], jnp.concatenate([cells, cells], axis=0))
    points = kernel.shape[1] // share
    for c in range(share):
        spread(wide, c, share, kernel[:, c * points : (c + 1) * points])
    for s in range(shares):
        dest = jnp.bitwise_xor(me, s)
        outs[s][...] = take(wide, pl.multiple_of(dest * size, size), size).astype(BF16)


def weight_kernel(shares, flip, out_rows, *refs):
    pieces, orb_ref, out_ref, gathered = refs[:shares][::-1], refs[shares], refs[shares + 1], refs[shares + 2]
    local_k, _, norb, points = orb_ref.shape
    total_rows = gathered.shape[1]
    half = total_rows // local_k // 2
    me = lax.axis_index("ka")
    core = jnp.bitwise_xor(jnp.bitwise_and(lax.axis_index("pts"), 1), flip)
    plane = plane_of(shares)
    for s in range(shares):
        gathered[jnp.bitwise_xor(jnp.bitwise_xor(me, s), plane)] = pieces[s][...]
    lanes = 2 * half * shares
    group = max(1, LANES // lanes)
    chunks = norb // out_rows // 2
    for g in range(local_k // group):
        right, left = [], []
        for kk in range(group):
            k = g * group + kk
            first, second = [], []
            for a in range(shares):
                piece = gathered[a, k * 2 * half : (k + 1) * 2 * half].astype(F32)
                first.append(piece)
                second.extend([piece[half:], -piece[:half]])
            first = jnp.concatenate(first, axis=0).astype(BF16)
            second = jnp.concatenate(second, axis=0).astype(BF16)
            zero = jnp.zeros_like(first)
            parts = [zero] * (2 * group)
            parts[2 * kk], parts[2 * kk + 1] = first, second
            right.append(jnp.concatenate(parts, axis=1))
            left.append(k)
        right = jnp.concatenate(right, axis=0)
        for z in range(chunks):
            start = pl.multiple_of((2 * z + core) * out_rows, out_rows)
            rows = jnp.concatenate(
                [orb_ref[k, part, pl.ds(start, out_rows), :] for k in left for part in range(2)], axis=1
            )
            out_ref[z, :, g * group * lanes : (g + 1) * group * lanes] = dot(
                rows, right, ((1,), (1,))
            ).astype(out_ref.dtype)


def pair_kernel(chunks, keep_ref, came_ref, own_ref, *outs):
    z = lax.shift_right_logical(lax.axis_index("pts"), 1)
    for s in range(chunks):
        dest = jnp.bitwise_xor(z, s)
        value = keep_ref[dest] + came_ref[dest].astype(F32)
        if s == 0:
            own_ref[...] = value
        else:
            outs[s - 1][...] = value.astype(BF16)


def exchange_kernel(chunks, shares, scale, *refs):
    pieces, form_refs, out_hbm = refs[:chunks][::-1], refs[chunks : chunks + shares], refs[chunks + shares]
    wide, out_ref, form_ref, sems = refs[chunks + shares + 1 :]
    owner = jnp.bitwise_xor(lax.axis_index("ka"), plane_of(shares))
    for j in range(shares):
        form_ref[jnp.bitwise_xor(owner, j)] = form_refs[j][...]
    _, local_k, part_lanes, twice = form_ref.shape
    lanes = shares * part_lanes
    norb = twice // 2
    spans = norb // LANES
    out_rows = pieces[0].shape[0]
    total = pieces[0][...]
    for s in range(1, chunks):
        total = total + pieces[s][...].astype(F32)
    total = total * scale
    high = total.astype(BF16)
    low = (total - high.astype(F32)).astype(BF16)
    group = max(1, LANES // lanes)
    width = group * lanes
    lane = lax.broadcasted_iota(jnp.int32, (out_rows, width), 1)
    zero = jnp.zeros((out_rows, width), BF16)
    copies = []
    for g in range(local_k // group):
        high_g = high[:, g * width : (g + 1) * width]
        low_g = low[:, g * width : (g + 1) * width]
        left = []
        for kk in range(group):
            keep = (lane >= kk * lanes) & (lane < (kk + 1) * lanes)
            left.append(
                jnp.concatenate([jnp.where(keep, high_g, zero), jnp.where(keep, low_g, zero)], axis=1)
            )
        forms = [form_ref[d, g * group + kk] for kk in range(group) for d in range(shares)]
        result = dot(jnp.concatenate(left, axis=0), jnp.concatenate(forms + forms, axis=0))
        for kk in range(group):
            for part in range(2):
                for t in range(spans):
                    lane_start = part * norb + t * LANES
                    value = result[kk * out_rows : (kk + 1) * out_rows, lane_start : lane_start + LANES]
                    start = (kk * spans + t) * 2 + part
                    wide[g, pl.ds(start, out_rows, stride=2 * spans * group), :] = value
        out_ref[g] = wide[g].astype(BF16).reshape(out_ref.shape[1:])
        copies.append(pltpu.make_async_copy(out_ref.at[g], out_hbm.at[:, g], sems.at[g]))
        copies[-1].start()
    for copy in copies:
        copy.wait()


def swap(value, axis, mask):
    size = lax.axis_size(axis)
    return lax.ppermute(value, axis, [(i, i ^ mask) for i in range(size)])


def trade(pieces, axis, step):
    return [swap(pieces[s], axis, s * step) for s in reversed(range(1, len(pieces)))] + [pieces[0]]


def body(orbitals, coulomb):
    shares, blocks = lax.axis_size("ka"), lax.axis_size("pts")
    local_k, _, norb, points = orbitals.shape
    columns = coulomb.shape[1]
    per_block = columns // blocks
    share = columns // shares
    total = local_k * shares
    out_rows = norb // blocks
    chunks = blocks // 2
    group = ROWS // (2 * per_block)
    shape = jax.ShapeDtypeStruct

    edge, orbitals = call(
        functools.partial(edge_kernel, per_block),
        [shape((local_k * 2 * per_block, norb), BF16), shape(orbitals.shape, BF16)],
        0,
        [pltpu.SemaphoreType.DMA((local_k,))],
        limit=47,
        size=8 * MIB,
        unread=1,
    )(orbitals)
    per_share = blocks // shares
    order = orders(shares)
    partner = swap(edge, "pts", 1)
    near = [edge, partner] + [swap(edge, "pts", 2 * e + c) for e in range(1, per_share // 2) for c in range(2)]
    came = []
    for t in range(shares - 1):
        step = []
        for e in range(per_share // 2):
            pairs = [
                (a * blocks + i, a * blocks + (i ^ (order[a][t] * per_share + 2 * e)))
                for a in range(shares)
                for i in range(blocks)
            ]
            block = lax.ppermute(edge, ("ka", "pts"), pairs)
            step += [block, swap(block, "pts", 1)]
        came.append(step)

    selector = jnp.asarray(column_selector(group, per_share, per_block, 1))
    piece = shape((share * 2 * local_k, points), BF16)
    both = shape((share * 3 * local_k, points), BF16)
    tiles, forms, before = [None] * shares, [None] * shares, []
    for targets in pieces_of(shares):
        many = len(targets)
        steps = sorted({t for j in targets for t in steps_for(j, shares)})
        taken = [block for t in steps for block in came[t]]
        result = call(
            functools.partial(tile_kernel, targets, shares, per_share, per_block),
            [both] * many + [shape((local_k, 2 * share, 2 * norb), BF16)] * many,
            len(near) + len(taken) + 3,
            [
                pltpu.VMEM((many, per_share, local_k * 2 * per_block, norb), BF16),
                tiled(many * share * 2 * local_k, points),
                pltpu.VMEM(coulomb.shape, F32),
            ],
            size=6 * MIB,
            unread=len(before),
        )(*near, *taken, orbitals, selector, coulomb, *before)
        for slot, j in enumerate(targets):
            tiles[j], forms[j] = result[slot], result[many + slot]
        before = [forms[targets[0]]]
    tiles = trade(tiles, "ka", 1)

    forward, backward = phase_tables(total)
    kernels = call(
        functools.partial(transform_kernel, shares, total, share),
        [piece] * shares,
        shares + 2,
        [
            pltpu.VMEM((shares, share * 2 * local_k, points), BF16 if local_k % 8 == 0 else F32),
            tiled(share * total, points),
            tiled(2 * total * share, points),
        ],
        size=2 * MIB,
    )(*tiles, jnp.asarray(forward), jnp.asarray(backward))
    kernels = trade(kernels, "ka", 1)

    lanes = local_k * 2 * columns
    halves = []
    for flip, kind in ((1, BF16), (0, F32)):
        halves.append(
            call(
                functools.partial(weight_kernel, shares, flip, out_rows),
                shape((chunks, out_rows, lanes), kind),
                shares + 1,
                [pltpu.VMEM((shares, share * 2 * local_k, points), BF16)],
                size=6 * MIB,
            )(*kernels, orbitals)
        )
    came = swap(halves[0], "pts", 1)
    own_sum, *sums = call(
        functools.partial(pair_kernel, chunks),
        [shape((out_rows, lanes), F32)] + [shape((out_rows, lanes), BF16)] * (chunks - 1),
        2,
        size=1 * MIB,
    )(halves[1], came)
    sums = trade([own_sum, *sums], "pts", 2)
    spans = norb // LANES
    pair = max(1, LANES // (2 * columns))
    rows = pair * spans * 2
    result = call(
        functools.partial(exchange_kernel, chunks, shares, 1.0 / math.sqrt(points * blocks)),
        shape((out_rows, local_k // pair, rows, LANES), BF16),
        chunks + shares,
        [
            pltpu.VMEM((local_k // pair, out_rows * rows, LANES), F32),
            pltpu.VMEM((local_k // pair, out_rows, rows, LANES), BF16),
            pltpu.VMEM((shares, local_k, 2 * share, 2 * norb), BF16),
            pltpu.SemaphoreType.DMA((local_k // pair,)),
        ],
        size=4 * MIB,
        result=pltpu.HBM,
    )(*sums, *forms)
    result = result.reshape(out_rows, local_k, spans, 2, LANES)
    return result.transpose(0, 1, 3, 2, 4).reshape(out_rows, local_k, 2, norb)


def solution(mesh):
    in_specs = (P("ka", None, None, "pts"), P("ka", None, "pts"))
    out_specs = P("pts", "ka", None, None)
    return jax.shard_map(body, mesh=mesh, in_specs=in_specs, out_specs=out_specs, check_vma=False)
```

```python
import functools
import math

import jax
import jax.numpy as jnp
import ml_dtypes
import numpy as np
from jax import lax
from jax.experimental import pallas as pl
from jax.experimental.pallas import tpu as pltpu
from jax.sharding import PartitionSpec as P

BF16 = jnp.bfloat16
F32 = jnp.float32
LANES = 128
ROWS = 16
MIB = 1 << 20


def split_terms(table):
    high = table.astype(ml_dtypes.bfloat16)
    low = (table - high.astype(np.float64)).astype(ml_dtypes.bfloat16)
    return np.concatenate([high, low], axis=1)


def phase_tables(total):
    index = np.arange(total)
    angles = (index[:, None] * index[None, :] % total) * (2.0 * math.pi / total)
    cosine, sine = np.cos(angles), np.sin(angles)
    forward = np.zeros((2, total, total, 2))
    forward[0, :, :, 0] = cosine
    forward[0, :, :, 1] = -sine
    forward[1, :, :, 0] = sine
    forward[1, :, :, 1] = cosine
    backward = np.zeros((total, 2, 2, total))
    backward[:, 0, 0] = cosine
    backward[:, 0, 1] = sine
    backward[:, 1, 1] = cosine
    backward[:, 1, 0] = -sine
    size = 2 * total
    return (
        split_terms(forward.reshape(size, size)),
        split_terms(backward.reshape(size, size) / total),
    )


def column_selector(group, blocks, per_block, shares):
    total = blocks * per_block
    share = total // shares
    table = np.zeros((group, 2, shares, 2, share, blocks, group, 2, per_block), np.float32)
    for k in range(group):
        for col in range(total):
            d, c = divmod(col, share)
            b, j = divmod(col, per_block)
            table[k, 0, d, 0, c, b, k, 0, j] = 1.0
            table[k, 0, d, 1, c, b, k, 1, j] = -1.0
            table[k, 1, d, 0, c, b, k, 1, j] = 1.0
            table[k, 1, d, 1, c, b, k, 0, j] = 1.0
    return table.reshape(group * 4 * total, blocks * group * 2 * per_block).astype(ml_dtypes.bfloat16)


def dot(left, right, dims=((1,), (0,))):
    return lax.dot_general(left, right, (dims, ((), ())), preferred_element_type=F32)


def spread(wide, start, stride, value):
    for t in range(wide.shape[0]):
        wide[t, pl.ds(start, value.shape[0], stride=stride), :] = value[:, t * LANES : (t + 1) * LANES]


def take(wide, start, size):
    return jnp.concatenate([wide[t, pl.ds(start, size), :] for t in range(wide.shape[0])], axis=1)


def tiled(rows, lanes):
    return pltpu.VMEM((lanes // LANES, rows, LANES), F32)


def call(kernel, out_shape, n_in, scratch=(), limit=24, flops=0, size=0, unread=0, result=pltpu.VMEM):
    whole = pl.BlockSpec(memory_space=pltpu.VMEM)
    return pl.pallas_call(
        kernel,
        out_shape=out_shape,
        in_specs=[whole] * n_in + [pl.BlockSpec(memory_space=pl.ANY)] * unread,
        out_specs=jax.tree.map(lambda _: pl.BlockSpec(memory_space=result), out_shape),
        scratch_shapes=list(scratch),
        compiler_params=pltpu.CompilerParams(vmem_limit_bytes=limit * MIB),
        cost_estimate=pl.CostEstimate(flops=flops, bytes_accessed=size, transcendentals=0),
    )


def load_copies(orb_hbm, orb_ref, sems, start):
    lanes = pl.ds(start, orb_ref.shape[3])
    copies = [
        pltpu.make_async_copy(orb_hbm.at[k, :, :, lanes], orb_ref.at[k], sems.at[k])
        for k in range(orb_ref.shape[0])
    ]
    for copy in copies:
        copy.start()
    return copies


def rest_kernel(orb_hbm, edge_hbm, pass_ref, orb_ref, sems, pass_sem):
    copies = load_copies(orb_hbm, orb_ref, sems, LANES)
    copies.append(pltpu.make_async_copy(edge_hbm, pass_ref, pass_sem))
    copies[-1].start()
    for copy in copies:
        copy.wait()


def edge_kernel(per_block, orb_hbm, edge_ref, orb_ref, sems):
    local_k = orb_hbm.shape[0]
    copies = load_copies(orb_hbm, orb_ref, sems, 0)
    row = lax.broadcasted_iota(jnp.int32, (2 * per_block, LANES), 0)
    lane = lax.broadcasted_iota(jnp.int32, (2 * per_block, LANES), 1)
    one, zero = jnp.ones(row.shape, F32), jnp.zeros(row.shape, F32)
    first = jnp.where((row < per_block) & (row == lane), one, zero).astype(BF16)
    second = jnp.where((row >= per_block) & (row == lane + per_block), one, zero).astype(BF16)
    group = ROWS // (2 * per_block)
    for g in range(local_k // group):
        rows = []
        for k in range(g * group, (g + 1) * group):
            copies[k].wait()
            rows.append(
                dot(first, orb_ref[k, 0], ((1,), (1,)))
                + dot(second, orb_ref[k, 1], ((1,), (1,)))
            )
        edge_ref[g * ROWS : (g + 1) * ROWS] = jnp.concatenate(rows, axis=0).astype(BF16)


def orders(shares):
    return [list(range(1, shares))] * shares


def pick(table, index):
    value = jnp.int32(table[0])
    for i in range(1, len(table)):
        value = jnp.where(index == i, jnp.int32(table[i]), value)
    return value


def steps_for(j, shares):
    order = orders(shares)
    return sorted({order[a].index(a ^ j) for a in range(shares) if a ^ j})


def pieces_of(shares):
    return [list(reversed(range(shares)))]


def plane_of(shares):
    return lax.div(lax.axis_index("pts"), lax.axis_size("pts") // shares)


def tile_kernel(targets, shares, per_share, per_block, *refs):
    steps = sorted({t for j in targets for t in steps_for(j, shares)})
    n, many = per_share * (1 + len(steps)), len(targets)
    blocks, (orb_ref, rest_ref, sel_ref, coulomb_ref) = refs[:n], refs[n : n + 4]
    *refs, gathered, wide, cells = refs[-2 * many - 3 :]
    outs, form_refs = refs[:many], refs[many:]
    local_k, _, norb, _ = orb_ref.shape
    group = ROWS // (2 * per_block)
    share = per_share * per_block
    rows = 2 * share
    me, block = lax.axis_index("ka"), lax.axis_index("pts")
    order = orders(shares)
    for i, t in enumerate([None] + steps):
        here = 0 if t is None else pick([order[a][t] for a in range(shares)], me)
        for slot, j in enumerate(targets):

            @pl.when(jnp.bitwise_xor(me, j) == here)
            def _(i=i, slot=slot):
                for e in range(per_share):
                    place = jnp.bitwise_xor(jnp.bitwise_and(block, per_share - 1), e)
                    gathered[slot, place] = blocks[i * per_share + e][...]

    for g in range(local_k // group):
        forms = []
        for slot in range(many):
            stacked = jnp.concatenate(
                [gathered[slot, b, g * ROWS : (g + 1) * ROWS] for b in range(per_share)], axis=0
            )
            forms.append(dot(sel_ref[...], stacked).astype(BF16))
        for kk in range(group):
            k = g * group + kk
            left = [form[2 * kk * rows : (2 * kk + 1) * rows] for form in forms]
            right = [form[(2 * kk + 1) * rows : (2 * kk + 2) * rows] for form in forms]
            form = jnp.concatenate(
                [jnp.concatenate(left, axis=0), jnp.concatenate(right, axis=0)], axis=1
            )
            halves = [ref[k].reshape(2 * norb, ref.shape[3]) for ref in (orb_ref, rest_ref)]
            tile = dot(form, jnp.concatenate(halves, axis=1))
            for slot in range(many):
                form_refs[slot][k] = form[slot * rows : (slot + 1) * rows]
                for part in range(2):
                    low = slot * rows + part * share
                    start = slot * share * 2 * local_k + 2 * k + part
                    spread(wide, start, 2 * local_k, tile[low : low + share])
    size = share * 2 * local_k
    cells[...] = coulomb_ref[...].astype(F32)
    for slot, j in enumerate(targets):
        outs[slot][:size] = take(wide, slot * size, size).astype(BF16)
        owned = jnp.bitwise_xor(jnp.bitwise_xor(me, j), plane_of(shares))
        start = pl.multiple_of(owned * share, share)
        pieces = [cells[r, pl.ds(start, share), :] for r in range(local_k)]
        outs[slot][size:] = jnp.concatenate(pieces, axis=0).astype(BF16)


def transform_kernel(shares, total, share, *refs):
    tiles, (fwd_ref, bwd_ref) = refs[:shares][::-1], refs[shares : shares + 2]
    outs, (gathered, weight, wide) = refs[shares + 2 : 2 * shares + 2], refs[2 * shares + 2 :]
    local_k = total // shares
    size = 2 * local_k * share
    me = lax.axis_index("ka")
    for s in range(shares):
        src = jnp.bitwise_xor(me, s)
        gathered[src] = tiles[s][:size].astype(gathered.dtype)
        cells = tiles[s][size:].astype(F32)
        for r in range(local_k):
            spread(weight, src * local_k + r, total, cells[r * share : (r + 1) * share])
    rows = 2 * local_k
    columns = []
    for c in range(share):
        columns.append(
            jnp.concatenate([gathered[a, c * rows : (c + 1) * rows] for a in range(shares)], axis=0).astype(BF16)
        )
    values = jnp.concatenate(columns, axis=1)
    cells = dot(fwd_ref[...], jnp.concatenate([values, values], axis=0))
    scale = jnp.concatenate([take(weight, c * total, total) for c in range(share)], axis=1)
    cells = (cells * jnp.concatenate([scale, scale], axis=0)).astype(BF16)
    kernel = dot(bwd_ref[...], jnp.concatenate([cells, cells], axis=0))
    points = kernel.shape[1] // share
    for c in range(share):
        spread(wide, c, share, kernel[:, c * points : (c + 1) * points])
    for s in range(shares):
        dest = jnp.bitwise_xor(me, s)
        outs[s][...] = take(wide, pl.multiple_of(dest * size, size), size).astype(BF16)


def weight_kernel(shares, flip, out_rows, *refs):
    pieces, (orb_ref, rest_ref, out_ref, gathered) = refs[:shares][::-1], refs[shares:]
    local_k, _, norb, _ = orb_ref.shape
    total_rows = gathered.shape[1]
    half = total_rows // local_k // 2
    me = lax.axis_index("ka")
    core = jnp.bitwise_xor(jnp.bitwise_and(lax.axis_index("pts"), 1), flip)
    plane = plane_of(shares)
    for s in range(shares):
        gathered[jnp.bitwise_xor(jnp.bitwise_xor(me, s), plane)] = pieces[s][...]
    lanes = 2 * half * shares
    group = max(1, LANES // lanes)
    chunks = norb // out_rows // 2
    for g in range(local_k // group):
        right, left = [], []
        for kk in range(group):
            k = g * group + kk
            first, second = [], []
            for a in range(shares):
                piece = gathered[a, k * 2 * half : (k + 1) * 2 * half].astype(F32)
                first.append(piece)
                second.extend([piece[half:], -piece[:half]])
            first = jnp.concatenate(first, axis=0).astype(BF16)
            second = jnp.concatenate(second, axis=0).astype(BF16)
            zero = jnp.zeros_like(first)
            parts = [zero] * (2 * group)
            parts[2 * kk], parts[2 * kk + 1] = first, second
            right.append(jnp.concatenate(parts, axis=1))
            left.append(k)
        right = jnp.concatenate(right, axis=0)
        for z in range(chunks):
            start = pl.multiple_of((2 * z + core) * out_rows, out_rows)
            rows = jnp.concatenate(
                [
                    ref[k, part, pl.ds(start, out_rows), :]
                    for k in left
                    for part in range(2)
                    for ref in (orb_ref, rest_ref)
                ],
                axis=1,
            )
            out_ref[z, :, g * group * lanes : (g + 1) * group * lanes] = dot(
                rows, right, ((1,), (1,))
            ).astype(out_ref.dtype)


def pair_kernel(chunks, keep_ref, came_ref, own_ref, *outs):
    z = lax.shift_right_logical(lax.axis_index("pts"), 1)
    for s in range(chunks):
        dest = jnp.bitwise_xor(z, s)
        value = keep_ref[dest] + came_ref[dest].astype(F32)
        if s == 0:
            own_ref[...] = value
        else:
            outs[s - 1][...] = value.astype(BF16)


def exchange_kernel(chunks, shares, scale, *refs):
    pieces, form_refs, out_hbm = refs[:chunks][::-1], refs[chunks : chunks + shares], refs[chunks + shares]
    wide, out_ref, form_ref, sems = refs[chunks + shares + 1 :]
    owner = jnp.bitwise_xor(lax.axis_index("ka"), plane_of(shares))
    for j in range(shares):
        form_ref[jnp.bitwise_xor(owner, j)] = form_refs[j][...]
    _, local_k, part_lanes, twice = form_ref.shape
    lanes = shares * part_lanes
    norb = twice // 2
    spans = norb // LANES
    out_rows = pieces[0].shape[0]
    total = pieces[0][...]
    for s in range(1, chunks):
        total = total + pieces[s][...].astype(F32)
    total = total * scale
    high = total.astype(BF16)
    low = (total - high.astype(F32)).astype(BF16)
    group = max(1, LANES // lanes)
    width = group * lanes
    lane = lax.broadcasted_iota(jnp.int32, (out_rows, width), 1)
    zero = jnp.zeros((out_rows, width), BF16)
    copies = []
    for g in range(local_k // group):
        high_g = high[:, g * width : (g + 1) * width]
        low_g = low[:, g * width : (g + 1) * width]
        left = []
        for kk in range(group):
            keep = (lane >= kk * lanes) & (lane < (kk + 1) * lanes)
            left.append(
                jnp.concatenate([jnp.where(keep, high_g, zero), jnp.where(keep, low_g, zero)], axis=1)
            )
        forms = [form_ref[d, g * group + kk] for kk in range(group) for d in range(shares)]
        result = dot(jnp.concatenate(left, axis=0), jnp.concatenate(forms + forms, axis=0))
        for kk in range(group):
            for part in range(2):
                for t in range(spans):
                    lane_start = part * norb + t * LANES
                    value = result[kk * out_rows : (kk + 1) * out_rows, lane_start : lane_start + LANES]
                    start = (kk * spans + t) * 2 + part
                    wide[g, pl.ds(start, out_rows, stride=2 * spans * group), :] = value
        out_ref[g] = wide[g].astype(BF16).reshape(out_ref.shape[1:])
        copies.append(pltpu.make_async_copy(out_ref.at[g], out_hbm.at[:, g], sems.at[g]))
        copies[-1].start()
    for copy in copies:
        copy.wait()


def swap(value, axis, mask):
    size = lax.axis_size(axis)
    return lax.ppermute(value, axis, [(i, i ^ mask) for i in range(size)])


def trade(pieces, axis, step):
    return [swap(pieces[s], axis, s * step) for s in reversed(range(1, len(pieces)))] + [pieces[0]]


def body(orbitals, coulomb):
    shares, blocks = lax.axis_size("ka"), lax.axis_size("pts")
    local_k, _, norb, points = orbitals.shape
    columns = coulomb.shape[1]
    per_block = columns // blocks
    share = columns // shares
    total = local_k * shares
    out_rows = norb // blocks
    chunks = blocks // 2
    group = ROWS // (2 * per_block)
    shape = jax.ShapeDtypeStruct

    edge, first = call(
        functools.partial(edge_kernel, per_block),
        [
            shape((local_k * 2 * per_block, norb), BF16),
            shape((local_k, 2, norb, LANES), BF16),
        ],
        0,
        [pltpu.SemaphoreType.DMA((local_k,))],
        limit=50,
        size=4 * MIB,
        unread=1,
    )(orbitals)
    passed_edge, rest = call(
        rest_kernel,
        [shape(edge.shape, BF16), shape((local_k, 2, norb, points - LANES), BF16)],
        0,
        [pltpu.SemaphoreType.DMA((local_k,)), pltpu.SemaphoreType.DMA],
        limit=49,
        size=4 * MIB,
        unread=2,
    )(orbitals, edge)
    per_share = blocks // shares
    order = orders(shares)
    partner = swap(passed_edge, "pts", 1)
    near = [edge, partner] + [swap(edge, "pts", 2 * e + c) for e in range(1, per_share // 2) for c in range(2)]
    came = []
    for t in range(shares - 1):
        step = []
        for e in range(per_share // 2):
            pairs = [
                (a * blocks + i, a * blocks + (i ^ (order[a][t] * per_share + 2 * e)))
                for a in range(shares)
                for i in range(blocks)
            ]
            block = lax.ppermute(edge, ("ka", "pts"), pairs)
            step += [block, swap(block, "pts", 1)]
        came.append(step)

    selector = jnp.asarray(column_selector(group, per_share, per_block, 1))
    piece = shape((share * 2 * local_k, points), BF16)
    both = shape((share * 3 * local_k, points), BF16)
    tiles, forms, before = [None] * shares, [None] * shares, []
    for targets in pieces_of(shares):
        many = len(targets)
        steps = sorted({t for j in targets for t in steps_for(j, shares)})
        taken = [block for t in steps for block in came[t]]
        result = call(
            functools.partial(tile_kernel, targets, shares, per_share, per_block),
            [both] * many + [shape((local_k, 2 * share, 2 * norb), BF16)] * many,
            len(near) + len(taken) + 4,
            [
                pltpu.VMEM((many, per_share, local_k * 2 * per_block, norb), BF16),
                tiled(many * share * 2 * local_k, points),
                pltpu.VMEM(coulomb.shape, F32),
            ],
            size=6 * MIB,
            unread=len(before),
        )(*near, *taken, first, rest, selector, coulomb, *before)
        for slot, j in enumerate(targets):
            tiles[j], forms[j] = result[slot], result[many + slot]
        before = [forms[targets[0]]]
    tiles = trade(tiles, "ka", 1)

    forward, backward = phase_tables(total)
    kernels = call(
        functools.partial(transform_kernel, shares, total, share),
        [piece] * shares,
        shares + 2,
        [
            pltpu.VMEM((shares, share * 2 * local_k, points), BF16 if local_k % 8 == 0 else F32),
            tiled(share * total, points),
            tiled(2 * total * share, points),
        ],
        size=2 * MIB,
    )(*tiles, jnp.asarray(forward), jnp.asarray(backward))
    kernels = trade(kernels, "ka", 1)

    lanes = local_k * 2 * columns
    halves = []
    for flip, kind in ((1, BF16), (0, F32)):
        halves.append(
            call(
                functools.partial(weight_kernel, shares, flip, out_rows),
                shape((chunks, out_rows, lanes), kind),
                shares + 2,
                [pltpu.VMEM((shares, share * 2 * local_k, points), BF16)],
                size=6 * MIB,
            )(*kernels, first, rest)
        )
    came = swap(halves[0], "pts", 1)
    own_sum, *sums = call(
        functools.partial(pair_kernel, chunks),
        [shape((out_rows, lanes), F32)] + [shape((out_rows, lanes), BF16)] * (chunks - 1),
        2,
        size=1 * MIB,
    )(halves[1], came)
    sums = trade([own_sum, *sums], "pts", 2)
    spans = norb // LANES
    pair = max(1, LANES // (2 * columns))
    rows = pair * spans * 2
    result = call(
        functools.partial(exchange_kernel, chunks, shares, 1.0 / math.sqrt(points * blocks)),
        shape((out_rows, local_k // pair, rows, LANES), BF16),
        chunks + shares,
        [
            pltpu.VMEM((local_k // pair, out_rows * rows, LANES), F32),
            pltpu.VMEM((local_k // pair, out_rows, rows, LANES), BF16),
            pltpu.VMEM((shares, local_k, 2 * share, 2 * norb), BF16),
            pltpu.SemaphoreType.DMA((local_k // pair,)),
        ],
        size=4 * MIB,
        result=pltpu.HBM,
    )(*sums, *forms)
    result = result.reshape(out_rows, local_k, spans, 2, LANES)
    return result.transpose(0, 1, 3, 2, 4).reshape(out_rows, local_k, 2, norb)


def solution(mesh):
    in_specs = (P("ka", None, None, "pts"), P("ka", None, "pts"))
    out_specs = P("pts", "ka", None, None)
    return jax.shard_map(body, mesh=mesh, in_specs=in_specs, out_specs=out_specs, check_vma=False)
```

```python
import functools
import math

import jax
import jax.numpy as jnp
import ml_dtypes
import numpy as np
from jax import lax
from jax.experimental import pallas as pl
from jax.experimental.pallas import tpu as pltpu
from jax.sharding import PartitionSpec as P

BF16 = jnp.bfloat16
F32 = jnp.float32
LANES = 128
ROWS = 16
MIB = 1 << 20


def split_terms(table):
    high = table.astype(ml_dtypes.bfloat16)
    low = (table - high.astype(np.float64)).astype(ml_dtypes.bfloat16)
    return np.concatenate([high, low], axis=1)


def phase_tables(total):
    index = np.arange(total)
    angles = (index[:, None] * index[None, :] % total) * (2.0 * math.pi / total)
    cosine, sine = np.cos(angles), np.sin(angles)
    forward = np.zeros((2, total, total, 2))
    forward[0, :, :, 0] = cosine
    forward[0, :, :, 1] = -sine
    forward[1, :, :, 0] = sine
    forward[1, :, :, 1] = cosine
    backward = np.zeros((total, 2, 2, total))
    backward[:, 0, 0] = cosine
    backward[:, 0, 1] = sine
    backward[:, 1, 1] = cosine
    backward[:, 1, 0] = -sine
    size = 2 * total
    return (
        split_terms(forward.reshape(size, size)),
        split_terms(backward.reshape(size, size) / total),
    )


def column_selector(group, blocks, per_block, shares):
    total = blocks * per_block
    share = total // shares
    table = np.zeros((group, 2, shares, 2, share, blocks, group, 2, per_block), np.float32)
    for k in range(group):
        for col in range(total):
            d, c = divmod(col, share)
            b, j = divmod(col, per_block)
            table[k, 0, d, 0, c, b, k, 0, j] = 1.0
            table[k, 0, d, 1, c, b, k, 1, j] = -1.0
            table[k, 1, d, 0, c, b, k, 1, j] = 1.0
            table[k, 1, d, 1, c, b, k, 0, j] = 1.0
    return table.reshape(group * 4 * total, blocks * group * 2 * per_block).astype(ml_dtypes.bfloat16)


def dot(left, right, dims=((1,), (0,))):
    return lax.dot_general(left, right, (dims, ((), ())), preferred_element_type=F32)


def spread(wide, start, stride, value):
    for t in range(wide.shape[0]):
        wide[t, pl.ds(start, value.shape[0], stride=stride), :] = value[:, t * LANES : (t + 1) * LANES]


def take(wide, start, size):
    return jnp.concatenate([wide[t, pl.ds(start, size), :] for t in range(wide.shape[0])], axis=1)


def tiled(rows, lanes):
    return pltpu.VMEM((lanes // LANES, rows, LANES), F32)


def call(kernel, out_shape, n_in, scratch=(), limit=24, flops=0, size=0, unread=0, result=pltpu.VMEM):
    whole = pl.BlockSpec(memory_space=pltpu.VMEM)
    return pl.pallas_call(
        kernel,
        out_shape=out_shape,
        in_specs=[whole] * n_in + [pl.BlockSpec(memory_space=pl.ANY)] * unread,
        out_specs=jax.tree.map(lambda _: pl.BlockSpec(memory_space=result), out_shape),
        scratch_shapes=list(scratch),
        compiler_params=pltpu.CompilerParams(vmem_limit_bytes=limit * MIB),
        cost_estimate=pl.CostEstimate(flops=flops, bytes_accessed=size, transcendentals=0),
    )


def edge_kernel(per_block, orb_hbm, edge_ref, orb_ref, sems):
    local_k = orb_hbm.shape[0]
    copies = [pltpu.make_async_copy(orb_hbm.at[k], orb_ref.at[k], sems.at[k]) for k in range(local_k)]
    for copy in copies:
        copy.start()
    row = lax.broadcasted_iota(jnp.int32, (2 * per_block, LANES), 0)
    lane = lax.broadcasted_iota(jnp.int32, (2 * per_block, LANES), 1)
    one, zero = jnp.ones(row.shape, F32), jnp.zeros(row.shape, F32)
    first = jnp.where((row < per_block) & (row == lane), one, zero).astype(BF16)
    second = jnp.where((row >= per_block) & (row == lane + per_block), one, zero).astype(BF16)
    group = ROWS // (2 * per_block)
    for g in range(local_k // group):
        rows = []
        for k in range(g * group, (g + 1) * group):
            copies[k].wait()
            rows.append(
                dot(first, orb_ref[k, 0, :, :LANES], ((1,), (1,)))
                + dot(second, orb_ref[k, 1, :, :LANES], ((1,), (1,)))
            )
        edge_ref[g * ROWS : (g + 1) * ROWS] = jnp.concatenate(rows, axis=0).astype(BF16)


def orders(shares):
    return [list(range(1, shares))] * shares


def pick(table, index):
    value = jnp.int32(table[0])
    for i in range(1, len(table)):
        value = jnp.where(index == i, jnp.int32(table[i]), value)
    return value


def steps_for(j, shares):
    order = orders(shares)
    return sorted({order[a].index(a ^ j) for a in range(shares) if a ^ j})


def pieces_of(shares):
    return [list(reversed(range(shares)))]


def crossed(s):
    return (s & ~3) | ((s & 1) << 1) | ((s >> 1) & 1)


def turn(s):
    return jnp.where(jnp.bitwise_and(lax.axis_index("pts"), 1) == 0, jnp.int32(s), jnp.int32(crossed(s)))


def plane_of(shares):
    return lax.div(lax.axis_index("pts"), lax.axis_size("pts") // shares)


def tile_kernel(targets, shares, per_share, per_block, *refs):
    steps = sorted({t for j in targets for t in steps_for(j, shares)})
    n, many = per_share * (1 + len(steps)), len(targets)
    blocks, (orb_ref, sel_ref, coulomb_ref) = refs[:n], refs[n : n + 3]
    *refs, gathered, wide, cells = refs[-2 * many - 3 :]
    outs, form_refs = refs[:many], refs[many:]
    local_k, _, norb, points = orb_ref.shape
    group = ROWS // (2 * per_block)
    share = per_share * per_block
    rows = 2 * share
    me, block = lax.axis_index("ka"), lax.axis_index("pts")
    order = orders(shares)
    for i, t in enumerate([None] + steps):
        here = 0 if t is None else pick([order[a][t] for a in range(shares)], me)
        for slot, j in enumerate(targets):

            @pl.when(jnp.bitwise_xor(me, turn(j)) == here)
            def _(i=i, slot=slot):
                for e in range(per_share):
                    place = jnp.bitwise_xor(jnp.bitwise_and(block, per_share - 1), e)
                    gathered[slot, place] = blocks[i * per_share + e][...]

    for g in range(local_k // group):
        forms = []
        for slot in range(many):
            stacked = jnp.concatenate(
                [gathered[slot, b, g * ROWS : (g + 1) * ROWS] for b in range(per_share)], axis=0
            )
            forms.append(dot(sel_ref[...], stacked).astype(BF16))
        for kk in range(group):
            k = g * group + kk
            left = [form[2 * kk * rows : (2 * kk + 1) * rows] for form in forms]
            right = [form[(2 * kk + 1) * rows : (2 * kk + 2) * rows] for form in forms]
            form = jnp.concatenate(
                [jnp.concatenate(left, axis=0), jnp.concatenate(right, axis=0)], axis=1
            )
            tile = dot(form, orb_ref[k].reshape(2 * norb, points))
            for slot in range(many):
                form_refs[slot][k] = form[slot * rows : (slot + 1) * rows]
                for part in range(2):
                    low = slot * rows + part * share
                    start = slot * share * 2 * local_k + 2 * k + part
                    spread(wide, start, 2 * local_k, tile[low : low + share])
    size = share * 2 * local_k
    cells[...] = coulomb_ref[...].astype(F32)
    for slot, j in enumerate(targets):
        outs[slot][:size] = take(wide, slot * size, size).astype(BF16)
        owned = jnp.bitwise_xor(jnp.bitwise_xor(me, turn(j)), plane_of(shares))
        start = pl.multiple_of(owned * share, share)
        pieces = [cells[r, pl.ds(start, share), :] for r in range(local_k)]
        outs[slot][size:] = jnp.concatenate(pieces, axis=0).astype(BF16)


def transform_kernel(shares, total, share, *refs):
    tiles, (fwd_ref, bwd_ref) = refs[:shares][::-1], refs[shares : shares + 2]
    outs, (gathered, weight, wide) = refs[shares + 2 : 2 * shares + 2], refs[2 * shares + 2 :]
    local_k = total // shares
    size = 2 * local_k * share
    me = lax.axis_index("ka")
    for s in range(shares):
        src = jnp.bitwise_xor(me, turn(s))
        gathered[src] = tiles[s][:size].astype(gathered.dtype)
        cells = tiles[s][size:].astype(F32)
        for r in range(local_k):
            spread(weight, src * local_k + r, total, cells[r * share : (r + 1) * share])
    rows = 2 * local_k
    columns = []
    for c in range(share):
        columns.append(
            jnp.concatenate([gathered[a, c * rows : (c + 1) * rows] for a in range(shares)], axis=0).astype(BF16)
        )
    values = jnp.concatenate(columns, axis=1)
    cells = dot(fwd_ref[...], jnp.concatenate([values, values], axis=0))
    scale = jnp.concatenate([take(weight, c * total, total) for c in range(share)], axis=1)
    cells = (cells * jnp.concatenate([scale, scale], axis=0)).astype(BF16)
    kernel = dot(bwd_ref[...], jnp.concatenate([cells, cells], axis=0))
    points = kernel.shape[1] // share
    for c in range(share):
        spread(wide, c, share, kernel[:, c * points : (c + 1) * points])
    for s in range(shares):
        dest = jnp.bitwise_xor(me, turn(s))
        outs[s][...] = take(wide, pl.multiple_of(dest * size, size), size).astype(BF16)


def weight_kernel(shares, flip, out_rows, *refs):
    pieces, orb_ref, out_ref, gathered = refs[:shares][::-1], refs[shares], refs[shares + 1], refs[shares + 2]
    local_k, _, norb, points = orb_ref.shape
    total_rows = gathered.shape[1]
    half = total_rows // local_k // 2
    me = lax.axis_index("ka")
    core = jnp.bitwise_xor(jnp.bitwise_and(lax.axis_index("pts"), 1), flip)
    plane = plane_of(shares)
    for s in range(shares):
        gathered[jnp.bitwise_xor(jnp.bitwise_xor(me, turn(s)), plane)] = pieces[s][...]
    lanes = 2 * half * shares
    group = max(1, LANES // lanes)
    chunks = norb // out_rows // 2
    for g in range(local_k // group):
        right, left = [], []
        for kk in range(group):
            k = g * group + kk
            first, second = [], []
            for a in range(shares):
                piece = gathered[a, k * 2 * half : (k + 1) * 2 * half].astype(F32)
                first.append(piece)
                second.extend([piece[half:], -piece[:half]])
            first = jnp.concatenate(first, axis=0).astype(BF16)
            second = jnp.concatenate(second, axis=0).astype(BF16)
            zero = jnp.zeros_like(first)
            parts = [zero] * (2 * group)
            parts[2 * kk], parts[2 * kk + 1] = first, second
            right.append(jnp.concatenate(parts, axis=1))
            left.append(k)
        right = jnp.concatenate(right, axis=0)
        for z in range(chunks):
            start = pl.multiple_of((2 * z + core) * out_rows, out_rows)
            rows = jnp.concatenate(
                [orb_ref[k, part, pl.ds(start, out_rows), :] for k in left for part in range(2)], axis=1
            )
            out_ref[z, :, g * group * lanes : (g + 1) * group * lanes] = dot(
                rows, right, ((1,), (1,))
            ).astype(out_ref.dtype)


def pair_kernel(chunks, keep_ref, came_ref, own_ref, *outs):
    z = lax.shift_right_logical(lax.axis_index("pts"), 1)
    for s in range(chunks):
        dest = jnp.bitwise_xor(z, s)
        value = keep_ref[dest] + came_ref[dest].astype(F32)
        if s == 0:
            own_ref[...] = value
        else:
            outs[s - 1][...] = value.astype(BF16)


def exchange_kernel(chunks, shares, scale, *refs):
    pieces, form_refs, out_hbm = refs[:chunks][::-1], refs[chunks : chunks + shares], refs[chunks + shares]
    wide, out_ref, form_ref, sems = refs[chunks + shares + 1 :]
    owner = jnp.bitwise_xor(lax.axis_index("ka"), plane_of(shares))
    for j in range(shares):
        form_ref[jnp.bitwise_xor(owner, turn(j))] = form_refs[j][...]
    _, local_k, part_lanes, twice = form_ref.shape
    lanes = shares * part_lanes
    norb = twice // 2
    spans = norb // LANES
    out_rows = pieces[0].shape[0]
    total = pieces[0][...]
    for s in range(1, chunks):
        total = total + pieces[s][...].astype(F32)
    total = total * scale
    high = total.astype(BF16)
    low = (total - high.astype(F32)).astype(BF16)
    group = max(1, LANES // lanes)
    width = group * lanes
    lane = lax.broadcasted_iota(jnp.int32, (out_rows, width), 1)
    zero = jnp.zeros((out_rows, width), BF16)
    copies = []
    for g in range(local_k // group):
        high_g = high[:, g * width : (g + 1) * width]
        low_g = low[:, g * width : (g + 1) * width]
        left = []
        for kk in range(group):
            keep = (lane >= kk * lanes) & (lane < (kk + 1) * lanes)
            left.append(
                jnp.concatenate([jnp.where(keep, high_g, zero), jnp.where(keep, low_g, zero)], axis=1)
            )
        forms = [form_ref[d, g * group + kk] for kk in range(group) for d in range(shares)]
        result = dot(jnp.concatenate(left, axis=0), jnp.concatenate(forms + forms, axis=0))
        for kk in range(group):
            for part in range(2):
                for t in range(spans):
                    lane_start = part * norb + t * LANES
                    value = result[kk * out_rows : (kk + 1) * out_rows, lane_start : lane_start + LANES]
                    start = (kk * spans + t) * 2 + part
                    wide[g, pl.ds(start, out_rows, stride=2 * spans * group), :] = value
        out_ref[g] = wide[g].astype(BF16).reshape(out_ref.shape[1:])
        copies.append(pltpu.make_async_copy(out_ref.at[g], out_hbm.at[:, g], sems.at[g]))
        copies[-1].start()
    for copy in copies:
        copy.wait()


def swap(value, axis, mask):
    size = lax.axis_size(axis)
    return lax.ppermute(value, axis, [(i, i ^ mask) for i in range(size)])


def trade(pieces):
    shares, blocks = lax.axis_size("ka"), lax.axis_size("pts")
    came = []
    for s in reversed(range(1, shares)):
        pairs = [
            (a * blocks + i, (a ^ (crossed(s) if i & 1 else s)) * blocks + i)
            for a in range(shares)
            for i in range(blocks)
        ]
        came.append(lax.ppermute(pieces[s], ("ka", "pts"), pairs))
    return came + [pieces[0]]


def trade_sums(pieces):
    return [swap(pieces[s], "pts", 2 * s) for s in reversed(range(1, len(pieces)))] + [pieces[0]]


def body(orbitals, coulomb):
    shares, blocks = lax.axis_size("ka"), lax.axis_size("pts")
    local_k, _, norb, points = orbitals.shape
    columns = coulomb.shape[1]
    per_block = columns // blocks
    share = columns // shares
    total = local_k * shares
    out_rows = norb // blocks
    chunks = blocks // 2
    group = ROWS // (2 * per_block)
    shape = jax.ShapeDtypeStruct

    edge, orbitals = call(
        functools.partial(edge_kernel, per_block),
        [shape((local_k * 2 * per_block, norb), BF16), shape(orbitals.shape, BF16)],
        0,
        [pltpu.SemaphoreType.DMA((local_k,))],
        limit=47,
        size=8 * MIB,
        unread=1,
    )(orbitals)
    per_share = blocks // shares
    order = orders(shares)
    partner = swap(edge, "pts", 1)
    near = [edge, partner] + [swap(edge, "pts", 2 * e + c) for e in range(1, per_share // 2) for c in range(2)]
    came = []
    for t in range(shares - 1):
        step = []
        for e in range(per_share // 2):
            pairs = [
                (a * blocks + i, a * blocks + (i ^ (order[a][t] * per_share + 2 * e)))
                for a in range(shares)
                for i in range(blocks)
            ]
            block = lax.ppermute(edge, ("ka", "pts"), pairs)
            step += [block, swap(block, "pts", 1)]
        came.append(step)

    selector = jnp.asarray(column_selector(group, per_share, per_block, 1))
    piece = shape((share * 2 * local_k, points), BF16)
    both = shape((share * 3 * local_k, points), BF16)
    tiles, forms, before = [None] * shares, [None] * shares, []
    for targets in pieces_of(shares):
        many = len(targets)
        steps = sorted({t for j in targets for t in steps_for(j, shares)})
        taken = [block for t in steps for block in came[t]]
        result = call(
            functools.partial(tile_kernel, targets, shares, per_share, per_block),
            [both] * many + [shape((local_k, 2 * share, 2 * norb), BF16)] * many,
            len(near) + len(taken) + 3,
            [
                pltpu.VMEM((many, per_share, local_k * 2 * per_block, norb), BF16),
                tiled(many * share * 2 * local_k, points),
                pltpu.VMEM(coulomb.shape, F32),
            ],
            size=6 * MIB,
            unread=len(before),
        )(*near, *taken, orbitals, selector, coulomb, *before)
        for slot, j in enumerate(targets):
            tiles[j], forms[j] = result[slot], result[many + slot]
        before = [forms[targets[0]]]
    tiles = trade(tiles)

    forward, backward = phase_tables(total)
    kernels = call(
        functools.partial(transform_kernel, shares, total, share),
        [piece] * shares,
        shares + 2,
        [
            pltpu.VMEM((shares, share * 2 * local_k, points), BF16 if local_k % 8 == 0 else F32),
            tiled(share * total, points),
            tiled(2 * total * share, points),
        ],
        size=2 * MIB,
    )(*tiles, jnp.asarray(forward), jnp.asarray(backward))
    kernels = trade(kernels)

    lanes = local_k * 2 * columns
    halves = []
    for flip, kind in ((1, BF16), (0, F32)):
        halves.append(
            call(
                functools.partial(weight_kernel, shares, flip, out_rows),
                shape((chunks, out_rows, lanes), kind),
                shares + 1,
                [pltpu.VMEM((shares, share * 2 * local_k, points), BF16)],
                size=6 * MIB,
            )(*kernels, orbitals)
        )
    came = swap(halves[0], "pts", 1)
    own_sum, *sums = call(
        functools.partial(pair_kernel, chunks),
        [shape((out_rows, lanes), F32)] + [shape((out_rows, lanes), BF16)] * (chunks - 1),
        2,
        size=1 * MIB,
    )(halves[1], came)
    sums = trade_sums([own_sum, *sums])
    spans = norb // LANES
    pair = max(1, LANES // (2 * columns))
    rows = pair * spans * 2
    result = call(
        functools.partial(exchange_kernel, chunks, shares, 1.0 / math.sqrt(points * blocks)),
        shape((out_rows, local_k // pair, rows, LANES), BF16),
        chunks + shares,
        [
            pltpu.VMEM((local_k // pair, out_rows * rows, LANES), F32),
            pltpu.VMEM((local_k // pair, out_rows, rows, LANES), BF16),
            pltpu.VMEM((shares, local_k, 2 * share, 2 * norb), BF16),
            pltpu.SemaphoreType.DMA((local_k // pair,)),
        ],
        size=4 * MIB,
        result=pltpu.HBM,
    )(*sums, *forms)
    result = result.reshape(out_rows, local_k, spans, 2, LANES)
    return result.transpose(0, 1, 3, 2, 4).reshape(out_rows, local_k, 2, norb)


def solution(mesh):
    in_specs = (P("ka", None, None, "pts"), P("ka", None, "pts"))
    out_specs = P("pts", "ka", None, None)
    return jax.shard_map(body, mesh=mesh, in_specs=in_specs, out_specs=out_specs, check_vma=False)
```

```python
import functools
import math

import jax
import jax.numpy as jnp
import ml_dtypes
import numpy as np
from jax import lax
from jax.experimental import pallas as pl
from jax.experimental.pallas import tpu as pltpu
from jax.sharding import PartitionSpec as P

BF16 = jnp.bfloat16
F32 = jnp.float32
LANES = 128
ROWS = 16
MIB = 1 << 20


def split_terms(table):
    high = table.astype(ml_dtypes.bfloat16)
    low = (table - high.astype(np.float64)).astype(ml_dtypes.bfloat16)
    return np.concatenate([high, low], axis=1)


def phase_tables(total):
    index = np.arange(total)
    angles = (index[:, None] * index[None, :] % total) * (2.0 * math.pi / total)
    cosine, sine = np.cos(angles), np.sin(angles)
    forward = np.zeros((2, total, total, 2))
    forward[0, :, :, 0] = cosine
    forward[0, :, :, 1] = -sine
    forward[1, :, :, 0] = sine
    forward[1, :, :, 1] = cosine
    backward = np.zeros((total, 2, 2, total))
    backward[:, 0, 0] = cosine
    backward[:, 0, 1] = sine
    backward[:, 1, 1] = cosine
    backward[:, 1, 0] = -sine
    size = 2 * total
    return (
        split_terms(forward.reshape(size, size)),
        split_terms(backward.reshape(size, size) / total),
    )


def column_selector(group, blocks, per_block, shares):
    total = blocks * per_block
    share = total // shares
    table = np.zeros((group, 2, shares, 2, share, blocks, group, 2, per_block), np.float32)
    for k in range(group):
        for col in range(total):
            d, c = divmod(col, share)
            b, j = divmod(col, per_block)
            table[k, 0, d, 0, c, b, k, 0, j] = 1.0
            table[k, 0, d, 1, c, b, k, 1, j] = -1.0
            table[k, 1, d, 0, c, b, k, 1, j] = 1.0
            table[k, 1, d, 1, c, b, k, 0, j] = 1.0
    return table.reshape(group * 4 * total, blocks * group * 2 * per_block).astype(ml_dtypes.bfloat16)


def dot(left, right, dims=((1,), (0,))):
    return lax.dot_general(left, right, (dims, ((), ())), preferred_element_type=F32)


def spread(wide, start, stride, value):
    for t in range(wide.shape[0]):
        wide[t, pl.ds(start, value.shape[0], stride=stride), :] = value[:, t * LANES : (t + 1) * LANES]


def take(wide, start, size):
    return jnp.concatenate([wide[t, pl.ds(start, size), :] for t in range(wide.shape[0])], axis=1)


def tiled(rows, lanes):
    return pltpu.VMEM((lanes // LANES, rows, LANES), F32)


def call(kernel, out_shape, n_in, scratch=(), limit=24, flops=0, size=0, unread=0, result=pltpu.VMEM):
    whole = pl.BlockSpec(memory_space=pltpu.VMEM)
    return pl.pallas_call(
        kernel,
        out_shape=out_shape,
        in_specs=[whole] * n_in + [pl.BlockSpec(memory_space=pl.ANY)] * unread,
        out_specs=jax.tree.map(lambda _: pl.BlockSpec(memory_space=result), out_shape),
        scratch_shapes=list(scratch),
        compiler_params=pltpu.CompilerParams(vmem_limit_bytes=limit * MIB),
        cost_estimate=pl.CostEstimate(flops=flops, bytes_accessed=size, transcendentals=0),
    )


def edge_kernel(per_block, orb_hbm, edge_ref, orb_ref, sems):
    local_k = orb_hbm.shape[0]
    copies = [pltpu.make_async_copy(orb_hbm.at[k], orb_ref.at[k], sems.at[k]) for k in range(local_k)]
    for copy in copies:
        copy.start()
    row = lax.broadcasted_iota(jnp.int32, (2 * per_block, LANES), 0)
    lane = lax.broadcasted_iota(jnp.int32, (2 * per_block, LANES), 1)
    one, zero = jnp.ones(row.shape, F32), jnp.zeros(row.shape, F32)
    first = jnp.where((row < per_block) & (row == lane), one, zero).astype(BF16)
    second = jnp.where((row >= per_block) & (row == lane + per_block), one, zero).astype(BF16)
    group = ROWS // (2 * per_block)
    for g in range(local_k // group):
        rows = []
        for k in range(g * group, (g + 1) * group):
            copies[k].wait()
            rows.append(
                dot(first, orb_ref[k, 0, :, :LANES], ((1,), (1,)))
                + dot(second, orb_ref[k, 1, :, :LANES], ((1,), (1,)))
            )
        edge_ref[g * ROWS : (g + 1) * ROWS] = jnp.concatenate(rows, axis=0).astype(BF16)


def asked(shares):
    return [2, 1, *range(3, shares)]


def plane_of(shares):
    return lax.div(lax.axis_index("pts"), lax.axis_size("pts") // shares)


def tile_kernel(shares, per_share, per_block, *refs):
    blocks, (orb_ref, sel_ref, coulomb_ref) = refs[: shares * per_share], refs[shares * per_share :][:3]
    *outs, form_ref, wide, cells = refs[shares * per_share + 3 :]
    local_k, _, norb, points = orb_ref.shape
    group = ROWS // (2 * per_block)
    share = per_share * per_block
    rows = 2 * share
    me, block = lax.axis_index("ka"), lax.axis_index("pts")
    plane = plane_of(shares)
    selector = sel_ref[jnp.bitwise_and(block, per_share - 1)]
    order = [0, *asked(shares)]
    for g in range(local_k // group):
        forms = []
        for offset in range(shares):
            stacked = jnp.concatenate(
                [
                    blocks[order.index(offset) * per_share + e][g * ROWS : (g + 1) * ROWS]
                    for e in range(per_share)
                ],
                axis=0,
            )
            forms.append(dot(selector, stacked).astype(BF16))
        for kk in range(group):
            k = g * group + kk
            left = [form[2 * kk * rows : (2 * kk + 1) * rows] for form in forms]
            right = [form[(2 * kk + 1) * rows : (2 * kk + 2) * rows] for form in forms]
            form = jnp.concatenate(
                [jnp.concatenate(left, axis=0), jnp.concatenate(right, axis=0)], axis=1
            )
            tile = dot(form, orb_ref[k].reshape(2 * norb, points))
            for offset in range(shares):
                form_ref[jnp.bitwise_xor(plane, offset), k] = form[offset * rows : (offset + 1) * rows]
                for part in range(2):
                    low = offset * rows + part * share
                    start = offset * share * 2 * local_k + 2 * k + part
                    spread(wide, start, 2 * local_k, tile[low : low + share])
    size = share * 2 * local_k
    cells[...] = coulomb_ref[...].astype(F32)
    for s in range(shares):
        offset = jnp.bitwise_xor(me, s)
        outs[s][:size] = take(wide, pl.multiple_of(offset * size, size), size).astype(BF16)
        start = pl.multiple_of(jnp.bitwise_xor(offset, plane) * share, share)
        pieces = [cells[r, pl.ds(start, share), :] for r in range(local_k)]
        outs[s][size:] = jnp.concatenate(pieces, axis=0).astype(BF16)


def transform_kernel(shares, total, share, *refs):
    tiles, (fwd_ref, bwd_ref) = refs[:shares][::-1], refs[shares : shares + 2]
    outs, (gathered, weight, wide) = refs[shares + 2 : 2 * shares + 2], refs[2 * shares + 2 :]
    local_k = total // shares
    size = 2 * local_k * share
    me = lax.axis_index("ka")
    for s in range(shares):
        src = jnp.bitwise_xor(me, s)
        gathered[src] = tiles[s][:size].astype(gathered.dtype)
        cells = tiles[s][size:].astype(F32)
        for r in range(local_k):
            spread(weight, src * local_k + r, total, cells[r * share : (r + 1) * share])
    rows = 2 * local_k
    columns = []
    for c in range(share):
        columns.append(
            jnp.concatenate([gathered[a, c * rows : (c + 1) * rows] for a in range(shares)], axis=0).astype(BF16)
        )
    values = jnp.concatenate(columns, axis=1)
    cells = dot(fwd_ref[...], jnp.concatenate([values, values], axis=0))
    scale = jnp.concatenate([take(weight, c * total, total) for c in range(share)], axis=1)
    cells = (cells * jnp.concatenate([scale, scale], axis=0)).astype(BF16)
    kernel = dot(bwd_ref[...], jnp.concatenate([cells, cells], axis=0))
    points = kernel.shape[1] // share
    for c in range(share):
        spread(wide, c, share, kernel[:, c * points : (c + 1) * points])
    for s in range(shares):
        dest = jnp.bitwise_xor(me, s)
        outs[s][...] = take(wide, pl.multiple_of(dest * size, size), size).astype(BF16)


def weight_kernel(shares, flip, out_rows, *refs):
    pieces, orb_ref, out_ref, gathered = refs[:shares][::-1], refs[shares], refs[shares + 1], refs[shares + 2]
    local_k, _, norb, points = orb_ref.shape
    total_rows = gathered.shape[1]
    half = total_rows // local_k // 2
    me = lax.axis_index("ka")
    core = jnp.bitwise_xor(jnp.bitwise_and(lax.axis_index("pts"), 1), flip)
    plane = plane_of(shares)
    for s in range(shares):
        gathered[jnp.bitwise_xor(jnp.bitwise_xor(me, s), plane)] = pieces[s][...]
    lanes = 2 * half * shares
    group = max(1, LANES // lanes)
    chunks = norb // out_rows // 2
    for g in range(local_k // group):
        right, left = [], []
        for kk in range(group):
            k = g * group + kk
            first, second = [], []
            for a in range(shares):
                piece = gathered[a, k * 2 * half : (k + 1) * 2 * half].astype(F32)
                first.append(piece)
                second.extend([piece[half:], -piece[:half]])
            first = jnp.concatenate(first, axis=0).astype(BF16)
            second = jnp.concatenate(second, axis=0).astype(BF16)
            zero = jnp.zeros_like(first)
            parts = [zero] * (2 * group)
            parts[2 * kk], parts[2 * kk + 1] = first, second
            right.append(jnp.concatenate(parts, axis=1))
            left.append(k)
        right = jnp.concatenate(right, axis=0)
        for z in range(chunks):
            start = pl.multiple_of((2 * z + core) * out_rows, out_rows)
            rows = jnp.concatenate(
                [orb_ref[k, part, pl.ds(start, out_rows), :] for k in left for part in range(2)], axis=1
            )
            out_ref[z, :, g * group * lanes : (g + 1) * group * lanes] = dot(
                rows, right, ((1,), (1,))
            ).astype(out_ref.dtype)


def pair_kernel(chunks, keep_ref, came_ref, own_ref, *outs):
    z = lax.shift_right_logical(lax.axis_index("pts"), 1)
    for s in range(chunks):
        dest = jnp.bitwise_xor(z, s)
        value = keep_ref[dest] + came_ref[dest].astype(F32)
        if s == 0:
            own_ref[...] = value
        else:
            outs[s - 1][...] = value.astype(BF16)


def exchange_kernel(chunks, scale, *refs):
    pieces, (form_ref, out_hbm, wide, out_ref, sems) = refs[:chunks][::-1], refs[chunks:]
    shares, local_k, part_lanes, twice = form_ref.shape
    lanes = shares * part_lanes
    norb = twice // 2
    spans = norb // LANES
    out_rows = pieces[0].shape[0]
    total = pieces[0][...]
    for s in range(1, chunks):
        total = total + pieces[s][...].astype(F32)
    total = total * scale
    high = total.astype(BF16)
    low = (total - high.astype(F32)).astype(BF16)
    group = max(1, LANES // lanes)
    width = group * lanes
    lane = lax.broadcasted_iota(jnp.int32, (out_rows, width), 1)
    zero = jnp.zeros((out_rows, width), BF16)
    copies = []
    for g in range(local_k // group):
        high_g = high[:, g * width : (g + 1) * width]
        low_g = low[:, g * width : (g + 1) * width]
        left = []
        for kk in range(group):
            keep = (lane >= kk * lanes) & (lane < (kk + 1) * lanes)
            left.append(
                jnp.concatenate([jnp.where(keep, high_g, zero), jnp.where(keep, low_g, zero)], axis=1)
            )
        forms = [form_ref[d, g * group + kk] for kk in range(group) for d in range(shares)]
        result = dot(jnp.concatenate(left, axis=0), jnp.concatenate(forms + forms, axis=0))
        for kk in range(group):
            for part in range(2):
                for t in range(spans):
                    lane_start = part * norb + t * LANES
                    value = result[kk * out_rows : (kk + 1) * out_rows, lane_start : lane_start + LANES]
                    start = (kk * spans + t) * 2 + part
                    wide[g, pl.ds(start, out_rows, stride=2 * spans * group), :] = value
        out_ref[g] = wide[g].astype(BF16).reshape(out_ref.shape[1:])
        copies.append(pltpu.make_async_copy(out_ref.at[g], out_hbm.at[:, g], sems.at[g]))
        copies[-1].start()
    for copy in copies:
        copy.wait()


def swap(value, axis, mask):
    size = lax.axis_size(axis)
    return lax.ppermute(value, axis, [(i, i ^ mask) for i in range(size)])


def trade(pieces, axis, step):
    return [swap(pieces[s], axis, s * step) for s in reversed(range(1, len(pieces)))] + [pieces[0]]


def body(orbitals, coulomb):
    shares, blocks = lax.axis_size("ka"), lax.axis_size("pts")
    local_k, _, norb, points = orbitals.shape
    columns = coulomb.shape[1]
    per_block = columns // blocks
    share = columns // shares
    total = local_k * shares
    out_rows = norb // blocks
    chunks = blocks // 2
    group = ROWS // (2 * per_block)
    shape = jax.ShapeDtypeStruct

    edge, orbitals = call(
        functools.partial(edge_kernel, per_block),
        [shape((local_k * 2 * per_block, norb), BF16), shape(orbitals.shape, BF16)],
        0,
        [pltpu.SemaphoreType.DMA((local_k,))],
        limit=47,
        size=8 * MIB,
        unread=1,
    )(orbitals)
    per_share = blocks // shares
    partner = swap(edge, "pts", 1)
    came = [edge, partner] + [swap(edge, "pts", 2 * e + c) for e in range(1, per_share // 2) for c in range(2)]
    came = {0: came}
    for offset in asked(shares):
        came[offset] = []
        for e in range(per_share // 2):
            block = swap(edge, "pts", offset * per_share + 2 * e)
            came[offset] += [block, swap(block, "pts", 1)]
    table = column_selector(group, per_share, per_block, 1).reshape(-1, per_share, ROWS)
    places = [[place ^ e for e in range(per_share)] for place in range(per_share)]
    selector = jnp.asarray(np.stack([table[:, place].reshape(table.shape[0], -1) for place in places]))
    piece = shape((share * 2 * local_k, points), BF16)
    both = shape((share * 3 * local_k, points), BF16)
    *tiles, forms = call(
        functools.partial(tile_kernel, shares, per_share, per_block),
        [both] * shares + [shape((shares, local_k, 2 * share, 2 * norb), BF16)],
        blocks + 3,
        [
            tiled(shares * share * 2 * local_k, points),
            pltpu.VMEM(coulomb.shape, F32),
        ],
        size=6 * MIB,
    )(*[block for offset in [0, *asked(shares)] for block in came[offset]], orbitals, selector, coulomb)
    tiles = trade(tiles, "ka", 1)

    forward, backward = phase_tables(total)
    kernels = call(
        functools.partial(transform_kernel, shares, total, share),
        [piece] * shares,
        shares + 2,
        [
            pltpu.VMEM((shares, share * 2 * local_k, points), BF16 if local_k % 8 == 0 else F32),
            tiled(share * total, points),
            tiled(2 * total * share, points),
        ],
        size=2 * MIB,
    )(*tiles, jnp.asarray(forward), jnp.asarray(backward))
    kernels = trade(kernels, "ka", 1)

    lanes = local_k * 2 * columns
    halves = []
    for flip, kind in ((1, BF16), (0, F32)):
        halves.append(
            call(
                functools.partial(weight_kernel, shares, flip, out_rows),
                shape((chunks, out_rows, lanes), kind),
                shares + 1,
                [pltpu.VMEM((shares, share * 2 * local_k, points), BF16)],
                size=6 * MIB,
            )(*kernels, orbitals)
        )
    came = swap(halves[0], "pts", 1)
    own_sum, *sums = call(
        functools.partial(pair_kernel, chunks),
        [shape((out_rows, lanes), F32)] + [shape((out_rows, lanes), BF16)] * (chunks - 1),
        2,
        size=1 * MIB,
    )(halves[1], came)
    sums = trade([own_sum, *sums], "pts", 2)
    spans = norb // LANES
    pair = max(1, LANES // (2 * columns))
    rows = pair * spans * 2
    result = call(
        functools.partial(exchange_kernel, chunks, 1.0 / math.sqrt(points * blocks)),
        shape((out_rows, local_k // pair, rows, LANES), BF16),
        chunks + 1,
        [
            pltpu.VMEM((local_k // pair, out_rows * rows, LANES), F32),
            pltpu.VMEM((local_k // pair, out_rows, rows, LANES), BF16),
            pltpu.SemaphoreType.DMA((local_k // pair,)),
        ],
        size=4 * MIB,
        result=pltpu.HBM,
    )(*sums, forms)
    result = result.reshape(out_rows, local_k, spans, 2, LANES)
    return result.transpose(0, 1, 3, 2, 4).reshape(out_rows, local_k, 2, norb)


def solution(mesh):
    in_specs = (P("ka", None, None, "pts"), P("ka", None, "pts"))
    out_specs = P("pts", "ka", None, None)
    return jax.shard_map(body, mesh=mesh, in_specs=in_specs, out_specs=out_specs, check_vma=False)
```

```python
import functools
import math

import jax
import jax.numpy as jnp
import ml_dtypes
import numpy as np
from jax import lax
from jax.experimental import pallas as pl
from jax.experimental.pallas import tpu as pltpu
from jax.sharding import PartitionSpec as P

BF16 = jnp.bfloat16
F32 = jnp.float32
LANES = 128
ROWS = 16
MIB = 1 << 20


def split_terms(table):
    high = table.astype(ml_dtypes.bfloat16)
    low = (table - high.astype(np.float64)).astype(ml_dtypes.bfloat16)
    return np.concatenate([high, low], axis=1)


def phase_tables(total):
    index = np.arange(total)
    angles = (index[:, None] * index[None, :] % total) * (2.0 * math.pi / total)
    cosine, sine = np.cos(angles), np.sin(angles)
    forward = np.zeros((2, total, total, 2))
    forward[0, :, :, 0] = cosine
    forward[0, :, :, 1] = -sine
    forward[1, :, :, 0] = sine
    forward[1, :, :, 1] = cosine
    backward = np.zeros((total, 2, 2, total))
    backward[:, 0, 0] = cosine
    backward[:, 0, 1] = sine
    backward[:, 1, 1] = cosine
    backward[:, 1, 0] = -sine
    size = 2 * total
    return (
        split_terms(forward.reshape(size, size)),
        split_terms(backward.reshape(size, size) / total),
    )


def column_selector(group, blocks, per_block, shares):
    total = blocks * per_block
    share = total // shares
    table = np.zeros((group, 2, shares, 2, share, blocks, group, 2, per_block), np.float32)
    for k in range(group):
        for col in range(total):
            d, c = divmod(col, share)
            b, j = divmod(col, per_block)
            table[k, 0, d, 0, c, b, k, 0, j] = 1.0
            table[k, 0, d, 1, c, b, k, 1, j] = -1.0
            table[k, 1, d, 0, c, b, k, 1, j] = 1.0
            table[k, 1, d, 1, c, b, k, 0, j] = 1.0
    return table.reshape(group * 4 * total, blocks * group * 2 * per_block).astype(ml_dtypes.bfloat16)


def dot(left, right, dims=((1,), (0,))):
    return lax.dot_general(left, right, (dims, ((), ())), preferred_element_type=F32)


def spread(wide, start, stride, value):
    for t in range(wide.shape[0]):
        wide[t, pl.ds(start, value.shape[0], stride=stride), :] = value[:, t * LANES : (t + 1) * LANES]


def take(wide, start, size):
    return jnp.concatenate([wide[t, pl.ds(start, size), :] for t in range(wide.shape[0])], axis=1)


def tiled(rows, lanes):
    return pltpu.VMEM((lanes // LANES, rows, LANES), F32)


def call(kernel, out_shape, n_in, scratch=(), limit=24, flops=0, size=0, unread=0, result=pltpu.VMEM):
    whole = pl.BlockSpec(memory_space=pltpu.VMEM)
    return pl.pallas_call(
        kernel,
        out_shape=out_shape,
        in_specs=[whole] * n_in + [pl.BlockSpec(memory_space=pl.ANY)] * unread,
        out_specs=jax.tree.map(lambda _: pl.BlockSpec(memory_space=result), out_shape),
        scratch_shapes=list(scratch),
        compiler_params=pltpu.CompilerParams(vmem_limit_bytes=limit * MIB),
        cost_estimate=pl.CostEstimate(flops=flops, bytes_accessed=size, transcendentals=0),
    )


def edge_kernel(per_block, orb_hbm, edge_ref, orb_ref, sems):
    local_k = orb_hbm.shape[0]
    copies = [pltpu.make_async_copy(orb_hbm.at[k], orb_ref.at[k], sems.at[k]) for k in range(local_k)]
    for copy in copies:
        copy.start()
    row = lax.broadcasted_iota(jnp.int32, (2 * per_block, LANES), 0)
    lane = lax.broadcasted_iota(jnp.int32, (2 * per_block, LANES), 1)
    one, zero = jnp.ones(row.shape, F32), jnp.zeros(row.shape, F32)
    first = jnp.where((row < per_block) & (row == lane), one, zero).astype(BF16)
    second = jnp.where((row >= per_block) & (row == lane + per_block), one, zero).astype(BF16)
    group = ROWS // (2 * per_block)
    for g in range(local_k // group):
        rows = []
        for k in range(g * group, (g + 1) * group):
            copies[k].wait()
            rows.append(
                dot(first, orb_ref[k, 0, :, :LANES], ((1,), (1,)))
                + dot(second, orb_ref[k, 1, :, :LANES], ((1,), (1,)))
            )
        edge_ref[g * ROWS : (g + 1) * ROWS] = jnp.concatenate(rows, axis=0).astype(BF16)


def asked(shares):
    return [2, 1, *range(3, shares)]


def plane_of(shares):
    return lax.div(lax.axis_index("pts"), lax.axis_size("pts") // shares)


def tile_kernel(shares, per_share, per_block, *refs):
    blocks, (orb_ref, sel_ref, coulomb_ref) = refs[: shares * per_share], refs[shares * per_share :][:3]
    *outs, form_ref, wide, cells = refs[shares * per_share + 3 :]
    local_k, _, norb, points = orb_ref.shape
    group = ROWS // (2 * per_block)
    share = per_share * per_block
    rows = 2 * share
    me, block = lax.axis_index("ka"), lax.axis_index("pts")
    plane = plane_of(shares)
    selector = sel_ref[jnp.bitwise_and(block, per_share - 1)]
    order = [0, *asked(shares)]
    for g in range(local_k // group):
        forms = []
        for offset in range(shares):
            stacked = jnp.concatenate(
                [
                    blocks[order.index(offset) * per_share + e][g * ROWS : (g + 1) * ROWS]
                    for e in range(per_share)
                ],
                axis=0,
            )
            forms.append(dot(selector, stacked).astype(BF16))
        for kk in range(group):
            k = g * group + kk
            left = [form[2 * kk * rows : (2 * kk + 1) * rows] for form in forms]
            right = [form[(2 * kk + 1) * rows : (2 * kk + 2) * rows] for form in forms]
            form = jnp.concatenate(
                [jnp.concatenate(left, axis=0), jnp.concatenate(right, axis=0)], axis=1
            )
            tile = dot(form, orb_ref[k].reshape(2 * norb, points))
            for offset in range(shares):
                form_ref[jnp.bitwise_xor(plane, offset), k] = form[offset * rows : (offset + 1) * rows]
                for part in range(2):
                    low = offset * rows + part * share
                    start = offset * share * 2 * local_k + 2 * k + part
                    spread(wide, start, 2 * local_k, tile[low : low + share])
    size = share * 2 * local_k
    cells[...] = coulomb_ref[...].astype(F32)
    for s in range(shares):
        offset = jnp.bitwise_xor(me, s)
        outs[s][:size] = take(wide, pl.multiple_of(offset * size, size), size).astype(BF16)
        start = pl.multiple_of(jnp.bitwise_xor(offset, plane) * share, share)
        pieces = [cells[r, pl.ds(start, share), :] for r in range(local_k)]
        outs[s][size:] = jnp.concatenate(pieces, axis=0).astype(BF16)


def transform_kernel(shares, total, share, *refs):
    tiles, (fwd_ref, bwd_ref) = refs[:shares][::-1], refs[shares : shares + 2]
    outs, (gathered, weight, wide) = refs[shares + 2 : 2 * shares + 2], refs[2 * shares + 2 :]
    local_k = total // shares
    size = 2 * local_k * share
    me = lax.axis_index("ka")
    for s in range(shares):
        src = jnp.bitwise_xor(me, s)
        gathered[src] = tiles[s][:size].astype(gathered.dtype)
        cells = tiles[s][size:].astype(F32)
        for r in range(local_k):
            spread(weight, src * local_k + r, total, cells[r * share : (r + 1) * share])
    rows = 2 * local_k
    columns = []
    for c in range(share):
        columns.append(
            jnp.concatenate([gathered[a, c * rows : (c + 1) * rows] for a in range(shares)], axis=0).astype(BF16)
        )
    values = jnp.concatenate(columns, axis=1)
    cells = dot(fwd_ref[...], jnp.concatenate([values, values], axis=0))
    scale = jnp.concatenate([take(weight, c * total, total) for c in range(share)], axis=1)
    cells = (cells * jnp.concatenate([scale, scale], axis=0)).astype(BF16)
    kernel = dot(bwd_ref[...], jnp.concatenate([cells, cells], axis=0))
    points = kernel.shape[1] // share
    for c in range(share):
        spread(wide, c, share, kernel[:, c * points : (c + 1) * points])
    for s in range(shares):
        dest = jnp.bitwise_xor(me, s)
        outs[s][...] = take(wide, pl.multiple_of(dest * size, size), size).astype(BF16)


def weight_kernel(shares, flip, out_rows, *refs):
    pieces, orb_ref, out_ref, gathered = refs[:shares][::-1], refs[shares], refs[shares + 1], refs[shares + 2]
    local_k, _, norb, points = orb_ref.shape
    total_rows = gathered.shape[1]
    half = total_rows // local_k // 2
    me = lax.axis_index("ka")
    core = jnp.bitwise_xor(jnp.bitwise_and(lax.axis_index("pts"), 1), flip)
    plane = plane_of(shares)
    for s in range(shares):
        gathered[jnp.bitwise_xor(jnp.bitwise_xor(me, s), plane)] = pieces[s][...]
    lanes = 2 * half * shares
    group = max(1, LANES // lanes)
    chunks = norb // out_rows // 2
    for g in range(local_k // group):
        right, left = [], []
        for kk in range(group):
            k = g * group + kk
            first, second = [], []
            for a in range(shares):
                piece = gathered[a, k * 2 * half : (k + 1) * 2 * half].astype(F32)
                first.append(piece)
                second.extend([piece[half:], -piece[:half]])
            first = jnp.concatenate(first, axis=0).astype(BF16)
            second = jnp.concatenate(second, axis=0).astype(BF16)
            zero = jnp.zeros_like(first)
            parts = [zero] * (2 * group)
            parts[2 * kk], parts[2 * kk + 1] = first, second
            right.append(jnp.concatenate(parts, axis=1))
            left.append(k)
        right = jnp.concatenate(right, axis=0)
        for z in range(chunks):
            start = pl.multiple_of((2 * z + core) * out_rows, out_rows)
            rows = jnp.concatenate(
                [orb_ref[k, part, pl.ds(start, out_rows), :] for k in left for part in range(2)], axis=1
            )
            out_ref[z, :, g * group * lanes : (g + 1) * group * lanes] = dot(
                rows, right, ((1,), (1,))
            ).astype(out_ref.dtype)


def pair_kernel(chunks, keep_ref, came_ref, own_ref, *outs):
    z = lax.shift_right_logical(lax.axis_index("pts"), 1)
    for s in range(chunks):
        dest = lax.rem(z + s, chunks)
        value = keep_ref[dest] + came_ref[dest].astype(F32)
        if s == 0:
            own_ref[...] = value
        else:
            outs[s - 1][...] = value.astype(BF16)


def exchange_kernel(chunks, scale, *refs):
    pieces, (form_ref, out_hbm, wide, out_ref, sems) = refs[:chunks][::-1], refs[chunks:]
    shares, local_k, part_lanes, twice = form_ref.shape
    lanes = shares * part_lanes
    norb = twice // 2
    spans = norb // LANES
    out_rows = pieces[0].shape[0]
    total = pieces[0][...]
    for s in range(1, chunks):
        total = total + pieces[s][...].astype(F32)
    total = total * scale
    high = total.astype(BF16)
    low = (total - high.astype(F32)).astype(BF16)
    group = max(1, LANES // lanes)
    width = group * lanes
    lane = lax.broadcasted_iota(jnp.int32, (out_rows, width), 1)
    zero = jnp.zeros((out_rows, width), BF16)
    copies = []
    for g in range(local_k // group):
        high_g = high[:, g * width : (g + 1) * width]
        low_g = low[:, g * width : (g + 1) * width]
        left = []
        for kk in range(group):
            keep = (lane >= kk * lanes) & (lane < (kk + 1) * lanes)
            left.append(
                jnp.concatenate([jnp.where(keep, high_g, zero), jnp.where(keep, low_g, zero)], axis=1)
            )
        forms = [form_ref[d, g * group + kk] for kk in range(group) for d in range(shares)]
        result = dot(jnp.concatenate(left, axis=0), jnp.concatenate(forms + forms, axis=0))
        for kk in range(group):
            for part in range(2):
                for t in range(spans):
                    lane_start = part * norb + t * LANES
                    value = result[kk * out_rows : (kk + 1) * out_rows, lane_start : lane_start + LANES]
                    start = (kk * spans + t) * 2 + part
                    wide[g, pl.ds(start, out_rows, stride=2 * spans * group), :] = value
        out_ref[g] = wide[g].astype(BF16).reshape(out_ref.shape[1:])
        copies.append(pltpu.make_async_copy(out_ref.at[g], out_hbm.at[:, g], sems.at[g]))
        copies[-1].start()
    for copy in copies:
        copy.wait()


def swap(value, axis, mask):
    size = lax.axis_size(axis)
    return lax.ppermute(value, axis, [(i, i ^ mask) for i in range(size)])


def trade(pieces, axis, step):
    return [swap(pieces[s], axis, s * step) for s in reversed(range(1, len(pieces)))] + [pieces[0]]


def shift_along(pieces):
    chunks = len(pieces)
    came = []
    for s in range(1, chunks):
        pairs = [(2 * z + core, 2 * ((z + s) % chunks) + core) for z in range(chunks) for core in range(2)]
        came.append(lax.ppermute(pieces[s], "pts", pairs))
    return came + [pieces[0]]


def body(orbitals, coulomb):
    shares, blocks = lax.axis_size("ka"), lax.axis_size("pts")
    local_k, _, norb, points = orbitals.shape
    columns = coulomb.shape[1]
    per_block = columns // blocks
    share = columns // shares
    total = local_k * shares
    out_rows = norb // blocks
    chunks = blocks // 2
    group = ROWS // (2 * per_block)
    shape = jax.ShapeDtypeStruct

    edge, orbitals = call(
        functools.partial(edge_kernel, per_block),
        [shape((local_k * 2 * per_block, norb), BF16), shape(orbitals.shape, BF16)],
        0,
        [pltpu.SemaphoreType.DMA((local_k,))],
        limit=47,
        size=8 * MIB,
        unread=1,
    )(orbitals)
    per_share = blocks // shares
    partner = swap(edge, "pts", 1)
    came = [edge, partner] + [swap(edge, "pts", 2 * e + c) for e in range(1, per_share // 2) for c in range(2)]
    came = {0: came}
    for offset in asked(shares):
        came[offset] = []
        for e in range(per_share // 2):
            block = swap(edge, "pts", offset * per_share + 2 * e)
            came[offset] += [block, swap(block, "pts", 1)]
    table = column_selector(group, per_share, per_block, 1).reshape(-1, per_share, ROWS)
    places = [[place ^ e for e in range(per_share)] for place in range(per_share)]
    selector = jnp.asarray(np.stack([table[:, place].reshape(table.shape[0], -1) for place in places]))
    piece = shape((share * 2 * local_k, points), BF16)
    both = shape((share * 3 * local_k, points), BF16)
    *tiles, forms = call(
        functools.partial(tile_kernel, shares, per_share, per_block),
        [both] * shares + [shape((shares, local_k, 2 * share, 2 * norb), BF16)],
        blocks + 3,
        [
            tiled(shares * share * 2 * local_k, points),
            pltpu.VMEM(coulomb.shape, F32),
        ],
        size=6 * MIB,
    )(*[block for offset in [0, *asked(shares)] for block in came[offset]], orbitals, selector, coulomb)
    tiles = trade(tiles, "ka", 1)

    forward, backward = phase_tables(total)
    kernels = call(
        functools.partial(transform_kernel, shares, total, share),
        [piece] * shares,
        shares + 2,
        [
            pltpu.VMEM((shares, share * 2 * local_k, points), BF16 if local_k % 8 == 0 else F32),
            tiled(share * total, points),
            tiled(2 * total * share, points),
        ],
        size=2 * MIB,
    )(*tiles, jnp.asarray(forward), jnp.asarray(backward))
    kernels = trade(kernels, "ka", 1)

    lanes = local_k * 2 * columns
    halves = []
    for flip, kind in ((1, BF16), (0, F32)):
        halves.append(
            call(
                functools.partial(weight_kernel, shares, flip, out_rows),
                shape((chunks, out_rows, lanes), kind),
                shares + 1,
                [pltpu.VMEM((shares, share * 2 * local_k, points), BF16)],
                size=6 * MIB,
            )(*kernels, orbitals)
        )
    came = swap(halves[0], "pts", 1)
    own_sum, *sums = call(
        functools.partial(pair_kernel, chunks),
        [shape((out_rows, lanes), F32)] + [shape((out_rows, lanes), BF16)] * (chunks - 1),
        2,
        size=1 * MIB,
    )(halves[1], came)
    sums = shift_along([own_sum, *sums])
    spans = norb // LANES
    pair = max(1, LANES // (2 * columns))
    rows = pair * spans * 2
    result = call(
        functools.partial(exchange_kernel, chunks, 1.0 / math.sqrt(points * blocks)),
        shape((out_rows, local_k // pair, rows, LANES), BF16),
        chunks + 1,
        [
            pltpu.VMEM((local_k // pair, out_rows * rows, LANES), F32),
            pltpu.VMEM((local_k // pair, out_rows, rows, LANES), BF16),
            pltpu.SemaphoreType.DMA((local_k // pair,)),
        ],
        size=4 * MIB,
        result=pltpu.HBM,
    )(*sums, forms)
    result = result.reshape(out_rows, local_k, spans, 2, LANES)
    return result.transpose(0, 1, 3, 2, 4).reshape(out_rows, local_k, 2, norb)


def solution(mesh):
    in_specs = (P("ka", None, None, "pts"), P("ka", None, "pts"))
    out_specs = P("pts", "ka", None, None)
    return jax.shard_map(body, mesh=mesh, in_specs=in_specs, out_specs=out_specs, check_vma=False)
```

```python
import functools
import math

import jax
import jax.numpy as jnp
import ml_dtypes
import numpy as np
from jax import lax
from jax.experimental import pallas as pl
from jax.experimental.pallas import tpu as pltpu
from jax.sharding import PartitionSpec as P

BF16 = jnp.bfloat16
F32 = jnp.float32
LANES = 128
ROWS = 16
MIB = 1 << 20


def split_terms(table):
    high = table.astype(ml_dtypes.bfloat16)
    low = (table - high.astype(np.float64)).astype(ml_dtypes.bfloat16)
    return np.concatenate([high, low], axis=1)


def phase_tables(total):
    index = np.arange(total)
    angles = (index[:, None] * index[None, :] % total) * (2.0 * math.pi / total)
    cosine, sine = np.cos(angles), np.sin(angles)
    forward = np.zeros((2, total, total, 2))
    forward[0, :, :, 0] = cosine
    forward[0, :, :, 1] = -sine
    forward[1, :, :, 0] = sine
    forward[1, :, :, 1] = cosine
    backward = np.zeros((total, 2, 2, total))
    backward[:, 0, 0] = cosine
    backward[:, 0, 1] = sine
    backward[:, 1, 1] = cosine
    backward[:, 1, 0] = -sine
    size = 2 * total
    return (
        split_terms(forward.reshape(size, size)),
        split_terms(backward.reshape(size, size) / total),
    )


def column_selector(group, blocks, per_block, shares):
    total = blocks * per_block
    share = total // shares
    table = np.zeros((group, 2, shares, 2, share, blocks, group, 2, per_block), np.float32)
    for k in range(group):
        for col in range(total):
            d, c = divmod(col, share)
            b, j = divmod(col, per_block)
            table[k, 0, d, 0, c, b, k, 0, j] = 1.0
            table[k, 0, d, 1, c, b, k, 1, j] = -1.0
            table[k, 1, d, 0, c, b, k, 1, j] = 1.0
            table[k, 1, d, 1, c, b, k, 0, j] = 1.0
    return table.reshape(group * 4 * total, blocks * group * 2 * per_block).astype(ml_dtypes.bfloat16)


def dot(left, right, dims=((1,), (0,))):
    return lax.dot_general(left, right, (dims, ((), ())), preferred_element_type=F32)


def spread(wide, start, stride, value):
    for t in range(wide.shape[0]):
        wide[t, pl.ds(start, value.shape[0], stride=stride), :] = value[:, t * LANES : (t + 1) * LANES]


def take(wide, start, size):
    return jnp.concatenate([wide[t, pl.ds(start, size), :] for t in range(wide.shape[0])], axis=1)


def tiled(rows, lanes):
    return pltpu.VMEM((lanes // LANES, rows, LANES), F32)


def call(kernel, out_shape, n_in, scratch=(), limit=24, flops=0, size=0, unread=0, result=pltpu.VMEM):
    whole = pl.BlockSpec(memory_space=pltpu.VMEM)
    return pl.pallas_call(
        kernel,
        out_shape=out_shape,
        in_specs=[whole] * n_in + [pl.BlockSpec(memory_space=pl.ANY)] * unread,
        out_specs=jax.tree.map(lambda _: pl.BlockSpec(memory_space=result), out_shape),
        scratch_shapes=list(scratch),
        compiler_params=pltpu.CompilerParams(vmem_limit_bytes=limit * MIB),
        cost_estimate=pl.CostEstimate(flops=flops, bytes_accessed=size, transcendentals=0),
    )


def load_copies(orb_hbm, orb_ref, sems, start):
    lanes = pl.ds(start, orb_ref.shape[3])
    copies = [
        pltpu.make_async_copy(orb_hbm.at[k, :, :, lanes], orb_ref.at[k], sems.at[k])
        for k in range(orb_ref.shape[0])
    ]
    for copy in copies:
        copy.start()
    return copies


def rest_kernel(orb_hbm, edge_hbm, pass_ref, orb_ref, sems, pass_sem):
    copies = load_copies(orb_hbm, orb_ref, sems, LANES)
    copies.append(pltpu.make_async_copy(edge_hbm, pass_ref, pass_sem))
    copies[-1].start()
    for copy in copies:
        copy.wait()


def edge_kernel(per_block, orb_hbm, edge_ref, orb_ref, sems):
    local_k = orb_hbm.shape[0]
    copies = load_copies(orb_hbm, orb_ref, sems, 0)
    row = lax.broadcasted_iota(jnp.int32, (2 * per_block, 2 * LANES), 0)
    lane = lax.broadcasted_iota(jnp.int32, (2 * per_block, 2 * LANES), 1)
    column = jnp.where(row < per_block, row, row - per_block + LANES)
    chosen = jnp.where(lane == column, jnp.ones(row.shape, F32), jnp.zeros(row.shape, F32)).astype(BF16)
    group = ROWS // (2 * per_block)
    for g in range(local_k // group):
        rows = []
        for k in range(g * group, (g + 1) * group):
            copies[k].wait()
            both = jnp.concatenate([orb_ref[k, 0], orb_ref[k, 1]], axis=1)
            rows.append(dot(chosen, both, ((1,), (1,))))
        edge_ref[g * ROWS : (g + 1) * ROWS] = jnp.concatenate(rows, axis=0).astype(BF16)


def asked(shares):
    return [2, 1, *range(3, shares)]


def plane_of(shares):
    return lax.div(lax.axis_index("pts"), lax.axis_size("pts") // shares)


def tile_kernel(shares, per_share, per_block, *refs):
    blocks, (orb_ref, rest_ref, sel_ref, coulomb_ref) = refs[: shares * per_share], refs[shares * per_share :][:4]
    *outs, form_ref, wide, cells = refs[shares * per_share + 4 :]
    local_k, _, norb, _ = orb_ref.shape
    group = ROWS // (2 * per_block)
    share = per_share * per_block
    rows = 2 * share
    me, block = lax.axis_index("ka"), lax.axis_index("pts")
    plane = plane_of(shares)
    selector = sel_ref[jnp.bitwise_and(block, per_share - 1)]
    order = [0, *asked(shares)]
    for g in range(local_k // group):
        forms = []
        for offset in range(shares):
            stacked = jnp.concatenate(
                [
                    blocks[order.index(offset) * per_share + e][g * ROWS : (g + 1) * ROWS]
                    for e in range(per_share)
                ],
                axis=0,
            )
            forms.append(dot(selector, stacked).astype(BF16))
        for kk in range(group):
            k = g * group + kk
            left = [form[2 * kk * rows : (2 * kk + 1) * rows] for form in forms]
            right = [form[(2 * kk + 1) * rows : (2 * kk + 2) * rows] for form in forms]
            form = jnp.concatenate(
                [jnp.concatenate(left, axis=0), jnp.concatenate(right, axis=0)], axis=1
            )
            halves = [ref[k].reshape(2 * norb, ref.shape[3]) for ref in (orb_ref, rest_ref)]
            tile = dot(form, jnp.concatenate(halves, axis=1))
            for offset in range(shares):
                form_ref[jnp.bitwise_xor(plane, offset), k] = form[offset * rows : (offset + 1) * rows]
                for part in range(2):
                    low = offset * rows + part * share
                    start = offset * share * 2 * local_k + 2 * k + part
                    spread(wide, start, 2 * local_k, tile[low : low + share])
    size = share * 2 * local_k
    cells[...] = coulomb_ref[...].astype(F32)
    for s in range(shares):
        offset = jnp.bitwise_xor(me, s)
        outs[s][:size] = take(wide, pl.multiple_of(offset * size, size), size).astype(BF16)
        start = pl.multiple_of(jnp.bitwise_xor(offset, plane) * share, share)
        pieces = [cells[r, pl.ds(start, share), :] for r in range(local_k)]
        outs[s][size:] = jnp.concatenate(pieces, axis=0).astype(BF16)


def transform_kernel(shares, total, share, *refs):
    tiles, (fwd_ref, bwd_ref) = refs[:shares][::-1], refs[shares : shares + 2]
    outs, (gathered, weight, wide) = refs[shares + 2 : 2 * shares + 2], refs[2 * shares + 2 :]
    local_k = total // shares
    size = 2 * local_k * share
    me = lax.axis_index("ka")
    for s in range(shares):
        src = jnp.bitwise_xor(me, s)
        gathered[src] = tiles[s][:size].astype(gathered.dtype)
        cells = tiles[s][size:].astype(F32)
        for r in range(local_k):
            spread(weight, src * local_k + r, total, cells[r * share : (r + 1) * share])
    rows = 2 * local_k
    columns = []
    for c in range(share):
        columns.append(
            jnp.concatenate([gathered[a, c * rows : (c + 1) * rows] for a in range(shares)], axis=0).astype(BF16)
        )
    values = jnp.concatenate(columns, axis=1)
    cells = dot(fwd_ref[...], jnp.concatenate([values, values], axis=0))
    scale = jnp.concatenate([take(weight, c * total, total) for c in range(share)], axis=1)
    cells = (cells * jnp.concatenate([scale, scale], axis=0)).astype(BF16)
    kernel = dot(bwd_ref[...], jnp.concatenate([cells, cells], axis=0))
    points = kernel.shape[1] // share
    for c in range(share):
        spread(wide, c, share, kernel[:, c * points : (c + 1) * points])
    for s in range(shares):
        dest = jnp.bitwise_xor(me, s)
        outs[s][...] = take(wide, pl.multiple_of(dest * size, size), size).astype(BF16)


def weight_kernel(shares, flip, out_rows, *refs):
    pieces, (orb_ref, rest_ref, out_ref, gathered) = refs[:shares][::-1], refs[shares:]
    local_k, _, norb, _ = orb_ref.shape
    total_rows = gathered.shape[1]
    half = total_rows // local_k // 2
    me = lax.axis_index("ka")
    core = jnp.bitwise_xor(jnp.bitwise_and(lax.axis_index("pts"), 1), flip)
    plane = plane_of(shares)
    for s in range(shares):
        gathered[jnp.bitwise_xor(jnp.bitwise_xor(me, s), plane)] = pieces[s][...]
    lanes = 2 * half * shares
    group = max(1, LANES // lanes)
    chunks = norb // out_rows // 2
    for g in range(local_k // group):
        right, left = [], []
        for kk in range(group):
            k = g * group + kk
            first, second = [], []
            for a in range(shares):
                piece = gathered[a, k * 2 * half : (k + 1) * 2 * half].astype(F32)
                first.append(piece)
                second.extend([piece[half:], -piece[:half]])
            first = jnp.concatenate(first, axis=0).astype(BF16)
            second = jnp.concatenate(second, axis=0).astype(BF16)
            zero = jnp.zeros_like(first)
            parts = [zero] * (2 * group)
            parts[2 * kk], parts[2 * kk + 1] = first, second
            right.append(jnp.concatenate(parts, axis=1))
            left.append(k)
        right = jnp.concatenate(right, axis=0)
        for z in range(chunks):
            start = pl.multiple_of((2 * z + core) * out_rows, out_rows)
            rows = jnp.concatenate(
                [
                    ref[k, part, pl.ds(start, out_rows), :]
                    for k in left
                    for part in range(2)
                    for ref in (orb_ref, rest_ref)
                ],
                axis=1,
            )
            out_ref[z, :, g * group * lanes : (g + 1) * group * lanes] = dot(
                rows, right, ((1,), (1,))
            ).astype(out_ref.dtype)


def pair_kernel(chunks, keep_ref, came_ref, own_ref, *outs):
    z = lax.shift_right_logical(lax.axis_index("pts"), 1)
    for s in range(chunks):
        dest = lax.rem(z + s, chunks)
        value = keep_ref[dest] + came_ref[dest].astype(F32)
        if s == 0:
            own_ref[...] = value
        else:
            outs[s - 1][...] = value.astype(BF16)


def exchange_kernel(chunks, scale, *refs):
    pieces, (form_ref, out_hbm, wide, out_ref, sems) = refs[:chunks][::-1], refs[chunks:]
    shares, local_k, part_lanes, twice = form_ref.shape
    lanes = shares * part_lanes
    norb = twice // 2
    spans = norb // LANES
    out_rows = pieces[0].shape[0]
    total = pieces[0][...]
    for s in range(1, chunks):
        total = total + pieces[s][...].astype(F32)
    total = total * scale
    high = total.astype(BF16)
    low = (total - high.astype(F32)).astype(BF16)
    group = max(1, LANES // lanes)
    width = group * lanes
    lane = lax.broadcasted_iota(jnp.int32, (out_rows, width), 1)
    zero = jnp.zeros((out_rows, width), BF16)
    copies = []
    for g in range(local_k // group):
        high_g = high[:, g * width : (g + 1) * width]
        low_g = low[:, g * width : (g + 1) * width]
        left = []
        for kk in range(group):
            keep = (lane >= kk * lanes) & (lane < (kk + 1) * lanes)
            left.append(
                jnp.concatenate([jnp.where(keep, high_g, zero), jnp.where(keep, low_g, zero)], axis=1)
            )
        forms = [form_ref[d, g * group + kk] for kk in range(group) for d in range(shares)]
        result = dot(jnp.concatenate(left, axis=0), jnp.concatenate(forms + forms, axis=0))
        for kk in range(group):
            for part in range(2):
                for t in range(spans):
                    lane_start = part * norb + t * LANES
                    value = result[kk * out_rows : (kk + 1) * out_rows, lane_start : lane_start + LANES]
                    start = (kk * spans + t) * 2 + part
                    wide[g, pl.ds(start, out_rows, stride=2 * spans * group), :] = value
        out_ref[g] = wide[g].astype(BF16).reshape(out_ref.shape[1:])
        copies.append(pltpu.make_async_copy(out_ref.at[g], out_hbm.at[:, g], sems.at[g]))
        copies[-1].start()
    for copy in copies:
        copy.wait()


def swap(value, axis, mask):
    size = lax.axis_size(axis)
    return lax.ppermute(value, axis, [(i, i ^ mask) for i in range(size)])


def trade(pieces, axis, step):
    return [swap(pieces[s], axis, s * step) for s in reversed(range(1, len(pieces)))] + [pieces[0]]


def shift_along(pieces):
    chunks = len(pieces)
    came = []
    for s in range(1, chunks):
        pairs = [(2 * z + core, 2 * ((z + s) % chunks) + core) for z in range(chunks) for core in range(2)]
        came.append(lax.ppermute(pieces[s], "pts", pairs))
    return came + [pieces[0]]


def body(orbitals, coulomb):
    shares, blocks = lax.axis_size("ka"), lax.axis_size("pts")
    local_k, _, norb, points = orbitals.shape
    columns = coulomb.shape[1]
    per_block = columns // blocks
    share = columns // shares
    total = local_k * shares
    out_rows = norb // blocks
    chunks = blocks // 2
    group = ROWS // (2 * per_block)
    shape = jax.ShapeDtypeStruct

    edge, first = call(
        functools.partial(edge_kernel, per_block),
        [
            shape((local_k * 2 * per_block, norb), BF16),
            shape((local_k, 2, norb, LANES), BF16),
        ],
        0,
        [pltpu.SemaphoreType.DMA((local_k,))],
        limit=50,
        size=4 * MIB,
        unread=1,
    )(orbitals)
    passed_edge, rest = call(
        rest_kernel,
        [shape(edge.shape, BF16), shape((local_k, 2, norb, points - LANES), BF16)],
        0,
        [pltpu.SemaphoreType.DMA((local_k,)), pltpu.SemaphoreType.DMA],
        limit=49,
        size=4 * MIB,
        unread=2,
    )(orbitals, edge)
    per_share = blocks // shares
    partner = swap(passed_edge, "pts", 1)
    came = [edge, partner] + [swap(edge, "pts", 2 * e + c) for e in range(1, per_share // 2) for c in range(2)]
    came = {0: came}
    for offset in asked(shares):
        came[offset] = []
        for e in range(per_share // 2):
            block = swap(edge, "pts", offset * per_share + 2 * e)
            came[offset] += [block, swap(block, "pts", 1)]
    table = column_selector(group, per_share, per_block, 1).reshape(-1, per_share, ROWS)
    places = [[place ^ e for e in range(per_share)] for place in range(per_share)]
    selector = jnp.asarray(np.stack([table[:, place].reshape(table.shape[0], -1) for place in places]))
    piece = shape((share * 2 * local_k, points), BF16)
    both = shape((share * 3 * local_k, points), BF16)
    *tiles, forms = call(
        functools.partial(tile_kernel, shares, per_share, per_block),
        [both] * shares + [shape((shares, local_k, 2 * share, 2 * norb), BF16)],
        blocks + 4,
        [
            tiled(shares * share * 2 * local_k, points),
            pltpu.VMEM(coulomb.shape, F32),
        ],
        size=6 * MIB,
    )(*[block for offset in [0, *asked(shares)] for block in came[offset]], first, rest, selector, coulomb)
    tiles = trade(tiles, "ka", 1)

    forward, backward = phase_tables(total)
    kernels = call(
        functools.partial(transform_kernel, shares, total, share),
        [piece] * shares,
        shares + 2,
        [
            pltpu.VMEM((shares, share * 2 * local_k, points), BF16 if local_k % 8 == 0 else F32),
            tiled(share * total, points),
            tiled(2 * total * share, points),
        ],
        size=2 * MIB,
    )(*tiles, jnp.asarray(forward), jnp.asarray(backward))
    kernels = trade(kernels, "ka", 1)

    lanes = local_k * 2 * columns
    halves = []
    for flip, kind in ((1, BF16), (0, F32)):
        halves.append(
            call(
                functools.partial(weight_kernel, shares, flip, out_rows),
                shape((chunks, out_rows, lanes), kind),
                shares + 2,
                [pltpu.VMEM((shares, share * 2 * local_k, points), BF16)],
                size=6 * MIB,
            )(*kernels, first, rest)
        )
    came = swap(halves[0], "pts", 1)
    own_sum, *sums = call(
        functools.partial(pair_kernel, chunks),
        [shape((out_rows, lanes), F32)] + [shape((out_rows, lanes), BF16)] * (chunks - 1),
        2,
        size=1 * MIB,
    )(halves[1], came)
    sums = shift_along([own_sum, *sums])
    spans = norb // LANES
    pair = max(1, LANES // (2 * columns))
    rows = pair * spans * 2
    result = call(
        functools.partial(exchange_kernel, chunks, 1.0 / math.sqrt(points * blocks)),
        shape((out_rows, local_k // pair, rows, LANES), BF16),
        chunks + 1,
        [
            pltpu.VMEM((local_k // pair, out_rows * rows, LANES), F32),
            pltpu.VMEM((local_k // pair, out_rows, rows, LANES), BF16),
            pltpu.SemaphoreType.DMA((local_k // pair,)),
        ],
        size=4 * MIB,
        result=pltpu.HBM,
    )(*sums, forms)
    result = result.reshape(out_rows, local_k, spans, 2, LANES)
    return result.transpose(0, 1, 3, 2, 4).reshape(out_rows, local_k, 2, norb)


def solution(mesh):
    in_specs = (P("ka", None, None, "pts"), P("ka", None, "pts"))
    out_specs = P("pts", "ka", None, None)
    return jax.shard_map(body, mesh=mesh, in_specs=in_specs, out_specs=out_specs, check_vma=False)
```

```python
import functools
import math

import jax
import jax.numpy as jnp
import ml_dtypes
import numpy as np
from jax import lax
from jax.experimental import pallas as pl
from jax.experimental.pallas import tpu as pltpu
from jax.sharding import PartitionSpec as P

BF16 = jnp.bfloat16
F32 = jnp.float32
LANES = 128
ROWS = 16
MIB = 1 << 20


def split_terms(table):
    high = table.astype(ml_dtypes.bfloat16)
    low = (table - high.astype(np.float64)).astype(ml_dtypes.bfloat16)
    return np.concatenate([high, low], axis=1)


def phase_tables(total):
    index = np.arange(total)
    angles = (index[:, None] * index[None, :] % total) * (2.0 * math.pi / total)
    cosine, sine = np.cos(angles), np.sin(angles)
    forward = np.zeros((2, total, total, 2))
    forward[0, :, :, 0] = cosine
    forward[0, :, :, 1] = -sine
    forward[1, :, :, 0] = sine
    forward[1, :, :, 1] = cosine
    backward = np.zeros((total, 2, 2, total))
    backward[:, 0, 0] = cosine
    backward[:, 0, 1] = sine
    backward[:, 1, 1] = cosine
    backward[:, 1, 0] = -sine
    size = 2 * total
    return (
        split_terms(forward.reshape(size, size)),
        split_terms(backward.reshape(size, size) / total),
    )


def column_selector(group, blocks, per_block, shares):
    total = blocks * per_block
    share = total // shares
    table = np.zeros((group, 2, shares, 2, share, blocks, group, 2, per_block), np.float32)
    for k in range(group):
        for col in range(total):
            d, c = divmod(col, share)
            b, j = divmod(col, per_block)
            table[k, 0, d, 0, c, b, k, 0, j] = 1.0
            table[k, 0, d, 1, c, b, k, 1, j] = -1.0
            table[k, 1, d, 0, c, b, k, 1, j] = 1.0
            table[k, 1, d, 1, c, b, k, 0, j] = 1.0
    return table.reshape(group * 4 * total, blocks * group * 2 * per_block).astype(ml_dtypes.bfloat16)


def dot(left, right, dims=((1,), (0,))):
    return lax.dot_general(left, right, (dims, ((), ())), preferred_element_type=F32)


def spread(wide, start, stride, value):
    for t in range(wide.shape[0]):
        wide[t, pl.ds(start, value.shape[0], stride=stride), :] = value[:, t * LANES : (t + 1) * LANES]


def take(wide, start, size):
    return jnp.concatenate([wide[t, pl.ds(start, size), :] for t in range(wide.shape[0])], axis=1)


def tiled(rows, lanes):
    return pltpu.VMEM((lanes // LANES, rows, LANES), F32)


def call(kernel, out_shape, n_in, scratch=(), limit=24, flops=0, size=0, unread=0, result=pltpu.VMEM):
    whole = pl.BlockSpec(memory_space=pltpu.VMEM)
    return pl.pallas_call(
        kernel,
        out_shape=out_shape,
        in_specs=[whole] * n_in + [pl.BlockSpec(memory_space=pl.ANY)] * unread,
        out_specs=jax.tree.map(lambda _: pl.BlockSpec(memory_space=result), out_shape),
        scratch_shapes=list(scratch),
        compiler_params=pltpu.CompilerParams(vmem_limit_bytes=limit * MIB),
        cost_estimate=pl.CostEstimate(flops=flops, bytes_accessed=size, transcendentals=0),
    )


def load_copies(orb_hbm, orb_ref, sems, start):
    lanes = pl.ds(start, orb_ref.shape[3])
    copies = [
        pltpu.make_async_copy(orb_hbm.at[k, :, :, lanes], orb_ref.at[k], sems.at[k])
        for k in range(orb_ref.shape[0])
    ]
    for copy in copies:
        copy.start()
    return copies


def rest_kernel(orb_hbm, edge_hbm, pass_ref, orb_ref, sems, pass_sem):
    copies = load_copies(orb_hbm, orb_ref, sems, LANES)
    copies.append(pltpu.make_async_copy(edge_hbm, pass_ref, pass_sem))
    copies[-1].start()
    for copy in copies:
        copy.wait()


def edge_kernel(per_block, orb_hbm, edge_ref, orb_ref, sems):
    local_k = orb_hbm.shape[0]
    copies = load_copies(orb_hbm, orb_ref, sems, 0)
    row = lax.broadcasted_iota(jnp.int32, (2 * per_block, 2 * LANES), 0)
    lane = lax.broadcasted_iota(jnp.int32, (2 * per_block, 2 * LANES), 1)
    column = jnp.where(row < per_block, row, row - per_block + LANES)
    chosen = jnp.where(lane == column, jnp.ones(row.shape, F32), jnp.zeros(row.shape, F32)).astype(BF16)
    group = ROWS // (2 * per_block)
    for g in range(local_k // group):
        rows = []
        for k in range(g * group, (g + 1) * group):
            copies[k].wait()
            both = jnp.concatenate([orb_ref[k, 0], orb_ref[k, 1]], axis=1)
            rows.append(dot(chosen, both, ((1,), (1,))))
        edge_ref[g * ROWS : (g + 1) * ROWS] = jnp.concatenate(rows, axis=0).astype(BF16)


def asked(shares):
    return [2, 1, *range(3, shares)]


def plane_of(shares):
    return lax.div(lax.axis_index("pts"), lax.axis_size("pts") // shares)


def tile_kernel(shares, per_share, per_block, *refs):
    blocks, (orb_ref, rest_ref, sel_ref, coulomb_ref) = refs[: shares * per_share], refs[shares * per_share :][:4]
    *outs, form_ref, wide, cells = refs[shares * per_share + 4 :]
    local_k, _, norb, _ = orb_ref.shape
    group = ROWS // (2 * per_block)
    share = per_share * per_block
    rows = 2 * share
    me, block = lax.axis_index("ka"), lax.axis_index("pts")
    plane = plane_of(shares)
    selector = sel_ref[jnp.bitwise_and(block, per_share - 1)]
    order = [0, *asked(shares)]
    for g in range(local_k // group):
        forms = []
        for offset in range(shares):
            stacked = jnp.concatenate(
                [
                    blocks[order.index(offset) * per_share + e][g * ROWS : (g + 1) * ROWS]
                    for e in range(per_share)
                ],
                axis=0,
            )
            forms.append(dot(selector, stacked).astype(BF16))
        for kk in range(group):
            k = g * group + kk
            left = [form[2 * kk * rows : (2 * kk + 1) * rows] for form in forms]
            right = [form[(2 * kk + 1) * rows : (2 * kk + 2) * rows] for form in forms]
            form = jnp.concatenate(
                [jnp.concatenate(left, axis=0), jnp.concatenate(right, axis=0)], axis=1
            )
            halves = [ref[k].reshape(2 * norb, ref.shape[3]) for ref in (orb_ref, rest_ref)]
            tile = dot(form, jnp.concatenate(halves, axis=1))
            for offset in range(shares):
                form_ref[jnp.bitwise_xor(plane, offset), k] = form[offset * rows : (offset + 1) * rows]
                for part in range(2):
                    low = offset * rows + part * share
                    start = offset * share * 2 * local_k + 2 * k + part
                    spread(wide, start, 2 * local_k, tile[low : low + share])
    size = share * 2 * local_k
    cells[...] = coulomb_ref[...].astype(F32)
    for s in range(shares):
        offset = jnp.bitwise_xor(me, s)
        outs[s][:size] = take(wide, pl.multiple_of(offset * size, size), size).astype(BF16)
        start = pl.multiple_of(jnp.bitwise_xor(offset, plane) * share, share)
        pieces = [cells[r, pl.ds(start, share), :] for r in range(local_k)]
        outs[s][size:] = jnp.concatenate(pieces, axis=0).astype(BF16)


def transform_kernel(shares, total, share, *refs):
    tiles, (fwd_ref, bwd_ref) = refs[:shares][::-1], refs[shares : shares + 2]
    outs, (gathered, weight, wide) = refs[shares + 2 : 2 * shares + 2], refs[2 * shares + 2 :]
    local_k = total // shares
    size = 2 * local_k * share
    me = lax.axis_index("ka")
    for s in range(shares):
        src = jnp.bitwise_xor(me, s)
        gathered[src] = tiles[s][:size].astype(gathered.dtype)
        cells = tiles[s][size:].astype(F32)
        for r in range(local_k):
            spread(weight, src * local_k + r, total, cells[r * share : (r + 1) * share])
    rows = 2 * local_k
    columns = []
    for c in range(share):
        columns.append(
            jnp.concatenate([gathered[a, c * rows : (c + 1) * rows] for a in range(shares)], axis=0).astype(BF16)
        )
    values = jnp.concatenate(columns, axis=1)
    cells = dot(fwd_ref[...], jnp.concatenate([values, values], axis=0))
    scale = jnp.concatenate([take(weight, c * total, total) for c in range(share)], axis=1)
    cells = (cells * jnp.concatenate([scale, scale], axis=0)).astype(BF16)
    kernel = dot(bwd_ref[...], jnp.concatenate([cells, cells], axis=0))
    points = kernel.shape[1] // share
    for c in range(share):
        spread(wide, c, share, kernel[:, c * points : (c + 1) * points])
    for s in range(shares):
        dest = jnp.bitwise_xor(me, s)
        outs[s][...] = take(wide, pl.multiple_of(dest * size, size), size).astype(BF16)


def weight_operands(pieces, right_ref, gathered):
    shares = len(pieces)
    groups, lanes, depth = right_ref.shape
    me, plane = lax.axis_index("ka"), plane_of(shares)
    for s in range(shares):
        gathered[jnp.bitwise_xor(jnp.bitwise_xor(me, s), plane)] = pieces[s][...]
    group = depth // (2 * gathered.shape[2])
    half = gathered.shape[1] // (groups * group) // 2
    for g in range(groups):
        right = []
        for kk in range(group):
            k = g * group + kk
            first, second = [], []
            for a in range(shares):
                piece = gathered[a, k * 2 * half : (k + 1) * 2 * half].astype(F32)
                first.append(piece)
                second.extend([piece[half:], -piece[:half]])
            first = jnp.concatenate(first, axis=0).astype(BF16)
            second = jnp.concatenate(second, axis=0).astype(BF16)
            parts = [jnp.zeros_like(first)] * (2 * group)
            parts[2 * kk], parts[2 * kk + 1] = first, second
            right.append(jnp.concatenate(parts, axis=1))
        right_ref[g] = jnp.concatenate(right, axis=0)


def weight_rows(offsets, flip, out_rows, right_ref, orb_ref, rest_ref, out_ref):
    groups, lanes, _ = right_ref.shape
    local_k, _, norb, _ = orb_ref.shape
    group = local_k // groups
    block = lax.axis_index("pts")
    core = jnp.bitwise_xor(jnp.bitwise_and(block, 1), flip)
    z = lax.shift_right_logical(block, 1)
    chunks = norb // out_rows // 2
    for g in range(groups):
        for i, offset in enumerate(offsets):
            start = pl.multiple_of((2 * lax.rem(z + offset, chunks) + core) * out_rows, out_rows)
            rows = jnp.concatenate(
                [
                    ref[k, part, pl.ds(start, out_rows), :]
                    for k in range(g * group, (g + 1) * group)
                    for part in range(2)
                    for ref in (orb_ref, rest_ref)
                ],
                axis=1,
            )
            out_ref[i, :, g * lanes : (g + 1) * lanes] = dot(rows, right_ref[g], ((1,), (1,))).astype(
                out_ref.dtype
            )


def first_weight_kernel(shares, offsets, out_rows, *refs):
    pieces, (orb_ref, rest_ref, out_ref, right_ref, gathered) = refs[:shares][::-1], refs[shares:]
    weight_operands(pieces, right_ref, gathered)
    weight_rows(offsets, 1, out_rows, right_ref, orb_ref, rest_ref, out_ref)


def next_weight_kernel(offsets, flip, out_rows, right_ref, orb_ref, rest_ref, *refs):
    weight_rows(offsets, flip, out_rows, right_ref, orb_ref, rest_ref, refs[-1])


def pair_kernel(keep_ref, came_ref, *outs):
    for i, out_ref in enumerate(outs):
        out_ref[...] = (keep_ref[i] + came_ref[i].astype(F32)).astype(out_ref.dtype)


def exchange_kernel(chunks, scale, *refs):
    pieces, (form_ref, out_hbm, wide, out_ref, sems) = refs[:chunks][::-1], refs[chunks:]
    shares, local_k, part_lanes, twice = form_ref.shape
    lanes = shares * part_lanes
    norb = twice // 2
    spans = norb // LANES
    out_rows = pieces[0].shape[0]
    total = pieces[0][...]
    for s in range(1, chunks):
        total = total + pieces[s][...].astype(F32)
    total = total * scale
    high = total.astype(BF16)
    low = (total - high.astype(F32)).astype(BF16)
    group = max(1, LANES // lanes)
    width = group * lanes
    lane = lax.broadcasted_iota(jnp.int32, (out_rows, width), 1)
    zero = jnp.zeros((out_rows, width), BF16)
    copies = []
    for g in range(local_k // group):
        high_g = high[:, g * width : (g + 1) * width]
        low_g = low[:, g * width : (g + 1) * width]
        left = []
        for kk in range(group):
            keep = (lane >= kk * lanes) & (lane < (kk + 1) * lanes)
            left.append(
                jnp.concatenate([jnp.where(keep, high_g, zero), jnp.where(keep, low_g, zero)], axis=1)
            )
        forms = [form_ref[d, g * group + kk] for kk in range(group) for d in range(shares)]
        result = dot(jnp.concatenate(left, axis=0), jnp.concatenate(forms + forms, axis=0))
        for kk in range(group):
            for part in range(2):
                for t in range(spans):
                    lane_start = part * norb + t * LANES
                    value = result[kk * out_rows : (kk + 1) * out_rows, lane_start : lane_start + LANES]
                    start = (kk * spans + t) * 2 + part
                    wide[g, pl.ds(start, out_rows, stride=2 * spans * group), :] = value
        out_ref[g] = wide[g].astype(BF16).reshape(out_ref.shape[1:])
        copies.append(pltpu.make_async_copy(out_ref.at[g], out_hbm.at[:, g], sems.at[g]))
        copies[-1].start()
    for copy in copies:
        copy.wait()


def swap(value, axis, mask):
    size = lax.axis_size(axis)
    return lax.ppermute(value, axis, [(i, i ^ mask) for i in range(size)])


def trade(pieces, axis, step):
    return [swap(pieces[s], axis, s * step) for s in reversed(range(1, len(pieces)))] + [pieces[0]]


def shift_along(pieces):
    chunks = len(pieces)
    came = []
    for s in range(1, chunks):
        pairs = [(2 * z + core, 2 * ((z - s) % chunks) + core) for z in range(chunks) for core in range(2)]
        came.append(lax.ppermute(pieces[s], "pts", pairs))
    return came[::-1] + [pieces[0]]


def body(orbitals, coulomb):
    shares, blocks = lax.axis_size("ka"), lax.axis_size("pts")
    local_k, _, norb, points = orbitals.shape
    columns = coulomb.shape[1]
    per_block = columns // blocks
    share = columns // shares
    total = local_k * shares
    out_rows = norb // blocks
    chunks = blocks // 2
    group = ROWS // (2 * per_block)
    shape = jax.ShapeDtypeStruct

    edge, first = call(
        functools.partial(edge_kernel, per_block),
        [
            shape((local_k * 2 * per_block, norb), BF16),
            shape((local_k, 2, norb, LANES), BF16),
        ],
        0,
        [pltpu.SemaphoreType.DMA((local_k,))],
        limit=50,
        size=4 * MIB,
        unread=1,
    )(orbitals)
    passed_edge, rest = call(
        rest_kernel,
        [shape(edge.shape, BF16), shape((local_k, 2, norb, points - LANES), BF16)],
        0,
        [pltpu.SemaphoreType.DMA((local_k,)), pltpu.SemaphoreType.DMA],
        limit=49,
        size=4 * MIB,
        unread=2,
    )(orbitals, edge)
    per_share = blocks // shares
    partner = swap(passed_edge, "pts", 1)
    came = [edge, partner] + [swap(edge, "pts", 2 * e + c) for e in range(1, per_share // 2) for c in range(2)]
    came = {0: came}
    for offset in asked(shares):
        came[offset] = []
        for e in range(per_share // 2):
            block = swap(edge, "pts", offset * per_share + 2 * e)
            came[offset] += [block, swap(block, "pts", 1)]
    table = column_selector(group, per_share, per_block, 1).reshape(-1, per_share, ROWS)
    places = [[place ^ e for e in range(per_share)] for place in range(per_share)]
    selector = jnp.asarray(np.stack([table[:, place].reshape(table.shape[0], -1) for place in places]))
    piece = shape((share * 2 * local_k, points), BF16)
    both = shape((share * 3 * local_k, points), BF16)
    *tiles, forms = call(
        functools.partial(tile_kernel, shares, per_share, per_block),
        [both] * shares + [shape((shares, local_k, 2 * share, 2 * norb), BF16)],
        blocks + 4,
        [
            tiled(shares * share * 2 * local_k, points),
            pltpu.VMEM(coulomb.shape, F32),
        ],
        size=6 * MIB,
    )(*[block for offset in [0, *asked(shares)] for block in came[offset]], first, rest, selector, coulomb)
    tiles = trade(tiles, "ka", 1)

    forward, backward = phase_tables(total)
    kernels = call(
        functools.partial(transform_kernel, shares, total, share),
        [piece] * shares,
        shares + 2,
        [
            pltpu.VMEM((shares, share * 2 * local_k, points), BF16 if local_k % 8 == 0 else F32),
            tiled(share * total, points),
            tiled(2 * total * share, points),
        ],
        size=2 * MIB,
    )(*tiles, jnp.asarray(forward), jnp.asarray(backward))
    kernels = trade(kernels, "ka", 1)

    lanes = local_k * 2 * columns
    pair = max(1, LANES // (2 * columns))
    early, late = list(reversed(range(1, chunks))), [0]
    sent, right = call(
        functools.partial(first_weight_kernel, shares, early, out_rows),
        [
            shape((len(early), out_rows, lanes), BF16),
            shape((local_k // pair, pair * 2 * columns, pair * 2 * points), BF16),
        ],
        shares + 2,
        [pltpu.VMEM((shares, share * 2 * local_k, points), BF16)],
    )(*kernels, first, rest)

    def rows_of(offsets, flip, kind, before):
        return call(
            functools.partial(next_weight_kernel, offsets, flip, out_rows),
            shape((len(offsets), out_rows, lanes), kind),
            3,
            unread=1,
        )(right, first, rest, before)

    def summed(offsets, keep, came):
        kinds = [shape((out_rows, lanes), BF16 if offset else F32) for offset in offsets]
        return call(pair_kernel, kinds, 2)(keep, came)

    sent_late = rows_of(late, 1, BF16, sent)
    early_sums = summed(early, rows_of(early, 0, F32, sent_late), swap(sent, "pts", 1))
    late_sums = summed(late, rows_of(late, 0, F32, early_sums[0]), swap(sent_late, "pts", 1))
    sums = [*late_sums, *early_sums]
    sums = shift_along(sums)
    spans = norb // LANES
    rows = pair * spans * 2
    result = call(
        functools.partial(exchange_kernel, chunks, 1.0 / math.sqrt(points * blocks)),
        shape((out_rows, local_k // pair, rows, LANES), BF16),
        chunks + 1,
        [
            pltpu.VMEM((local_k // pair, out_rows * rows, LANES), F32),
            pltpu.VMEM((local_k // pair, out_rows, rows, LANES), BF16),
            pltpu.SemaphoreType.DMA((local_k // pair,)),
        ],
        size=4 * MIB,
        result=pltpu.HBM,
    )(*sums, forms)
    result = result.reshape(out_rows, local_k, spans, 2, LANES)
    return result.transpose(0, 1, 3, 2, 4).reshape(out_rows, local_k, 2, norb)


def solution(mesh):
    in_specs = (P("ka", None, None, "pts"), P("ka", None, "pts"))
    out_specs = P("pts", "ka", None, None)
    return jax.shard_map(body, mesh=mesh, in_specs=in_specs, out_specs=out_specs, check_vma=False)
```

```python
import functools
import math

import jax
import jax.numpy as jnp
import ml_dtypes
import numpy as np
from jax import lax
from jax.experimental import pallas as pl
from jax.experimental.pallas import tpu as pltpu
from jax.sharding import PartitionSpec as P

BF16 = jnp.bfloat16
F32 = jnp.float32
LANES = 128
ROWS = 16
MIB = 1 << 20


def split_terms(table):
    high = table.astype(ml_dtypes.bfloat16)
    low = (table - high.astype(np.float64)).astype(ml_dtypes.bfloat16)
    return np.concatenate([high, low], axis=1)


def phase_tables(total):
    index = np.arange(total)
    angles = (index[:, None] * index[None, :] % total) * (2.0 * math.pi / total)
    cosine, sine = np.cos(angles), np.sin(angles)
    forward = np.zeros((2, total, total, 2))
    forward[0, :, :, 0] = cosine
    forward[0, :, :, 1] = -sine
    forward[1, :, :, 0] = sine
    forward[1, :, :, 1] = cosine
    backward = np.zeros((total, 2, 2, total))
    backward[:, 0, 0] = cosine
    backward[:, 0, 1] = sine
    backward[:, 1, 1] = cosine
    backward[:, 1, 0] = -sine
    size = 2 * total
    return (
        split_terms(forward.reshape(size, size)),
        split_terms(backward.reshape(size, size) / total),
    )


def column_selector(group, blocks, per_block, shares):
    total = blocks * per_block
    share = total // shares
    table = np.zeros((group, 2, shares, 2, share, blocks, group, 2, per_block), np.float32)
    for k in range(group):
        for col in range(total):
            d, c = divmod(col, share)
            b, j = divmod(col, per_block)
            table[k, 0, d, 0, c, b, k, 0, j] = 1.0
            table[k, 0, d, 1, c, b, k, 1, j] = -1.0
            table[k, 1, d, 0, c, b, k, 1, j] = 1.0
            table[k, 1, d, 1, c, b, k, 0, j] = 1.0
    return table.reshape(group * 4 * total, blocks * group * 2 * per_block).astype(ml_dtypes.bfloat16)


def dot(left, right, dims=((1,), (0,))):
    return lax.dot_general(left, right, (dims, ((), ())), preferred_element_type=F32)


def spread(wide, start, stride, value):
    for t in range(wide.shape[0]):
        wide[t, pl.ds(start, value.shape[0], stride=stride), :] = value[:, t * LANES : (t + 1) * LANES]


def take(wide, start, size):
    return jnp.concatenate([wide[t, pl.ds(start, size), :] for t in range(wide.shape[0])], axis=1)


def tiled(rows, lanes):
    return pltpu.VMEM((lanes // LANES, rows, LANES), F32)


def call(kernel, out_shape, n_in, scratch=(), limit=24, flops=0, size=0, unread=0, result=pltpu.VMEM):
    whole = pl.BlockSpec(memory_space=pltpu.VMEM)
    return pl.pallas_call(
        kernel,
        out_shape=out_shape,
        in_specs=[whole] * n_in + [pl.BlockSpec(memory_space=pl.ANY)] * unread,
        out_specs=jax.tree.map(lambda _: pl.BlockSpec(memory_space=result), out_shape),
        scratch_shapes=list(scratch),
        compiler_params=pltpu.CompilerParams(vmem_limit_bytes=limit * MIB),
        cost_estimate=pl.CostEstimate(flops=flops, bytes_accessed=size, transcendentals=0),
    )


def load_copies(orb_hbm, orb_ref, sems, start):
    lanes = pl.ds(start, orb_ref.shape[3])
    copies = [
        pltpu.make_async_copy(orb_hbm.at[k, :, :, lanes], orb_ref.at[k], sems.at[k])
        for k in range(orb_ref.shape[0])
    ]
    for copy in copies:
        copy.start()
    return copies


def rest_kernel(orb_hbm, edge_hbm, pass_ref, orb_ref, sems, pass_sem):
    copies = load_copies(orb_hbm, orb_ref, sems, LANES)
    copies.append(pltpu.make_async_copy(edge_hbm, pass_ref, pass_sem))
    copies[-1].start()
    for copy in copies:
        copy.wait()


def edge_kernel(per_block, orb_hbm, edge_ref, orb_ref, sems):
    local_k = orb_hbm.shape[0]
    copies = load_copies(orb_hbm, orb_ref, sems, 0)
    row = lax.broadcasted_iota(jnp.int32, (2 * per_block, 2 * LANES), 0)
    lane = lax.broadcasted_iota(jnp.int32, (2 * per_block, 2 * LANES), 1)
    column = jnp.where(row < per_block, row, row - per_block + LANES)
    chosen = jnp.where(lane == column, jnp.ones(row.shape, F32), jnp.zeros(row.shape, F32)).astype(BF16)
    group = ROWS // (2 * per_block)
    for g in range(local_k // group):
        rows = []
        for k in range(g * group, (g + 1) * group):
            copies[k].wait()
            both = jnp.concatenate([orb_ref[k, 0], orb_ref[k, 1]], axis=1)
            rows.append(dot(chosen, both, ((1,), (1,))))
        edge_ref[g * ROWS : (g + 1) * ROWS] = jnp.concatenate(rows, axis=0).astype(BF16)


def asked(shares):
    return [2, 1, *range(3, shares)]


def plane_of(shares):
    return lax.div(lax.axis_index("pts"), lax.axis_size("pts") // shares)


def tile_kernel(shares, per_share, per_block, *refs):
    blocks, (orb_ref, rest_ref, sel_ref, coulomb_ref) = refs[: shares * per_share], refs[shares * per_share :][:4]
    *outs, form_ref, wide, cells = refs[shares * per_share + 4 :]
    local_k, _, norb, _ = orb_ref.shape
    group = ROWS // (2 * per_block)
    share = per_share * per_block
    rows = 2 * share
    me, block = lax.axis_index("ka"), lax.axis_index("pts")
    plane = plane_of(shares)
    selector = sel_ref[jnp.bitwise_and(block, per_share - 1)]
    order = [0, *asked(shares)]
    for g in range(local_k // group):
        stacked = jnp.concatenate(
            [
                blocks[order.index(offset) * per_share + e][g * ROWS : (g + 1) * ROWS]
                for offset in range(shares)
                for e in range(per_share)
            ],
            axis=0,
        )
        chosen = dot(selector, stacked).astype(BF16)
        size = 2 * group * rows
        forms = [chosen[offset * size : (offset + 1) * size] for offset in range(shares)]
        for kk in range(group):
            k = g * group + kk
            left = [form[2 * kk * rows : (2 * kk + 1) * rows] for form in forms]
            right = [form[(2 * kk + 1) * rows : (2 * kk + 2) * rows] for form in forms]
            form = jnp.concatenate(
                [jnp.concatenate(left, axis=0), jnp.concatenate(right, axis=0)], axis=1
            )
            halves = [ref[k].reshape(2 * norb, ref.shape[3]) for ref in (orb_ref, rest_ref)]
            tile = dot(form, jnp.concatenate(halves, axis=1))
            for offset in range(shares):
                form_ref[jnp.bitwise_xor(plane, offset), k] = form[offset * rows : (offset + 1) * rows]
                for part in range(2):
                    low = offset * rows + part * share
                    start = offset * share * 2 * local_k + 2 * k + part
                    spread(wide, start, 2 * local_k, tile[low : low + share])
    size = share * 2 * local_k
    cells[...] = coulomb_ref[...].astype(F32)
    for s in range(shares):
        offset = jnp.bitwise_xor(me, s)
        outs[s][:size] = take(wide, pl.multiple_of(offset * size, size), size).astype(BF16)
        start = pl.multiple_of(jnp.bitwise_xor(offset, plane) * share, share)
        pieces = [cells[r, pl.ds(start, share), :] for r in range(local_k)]
        outs[s][size:] = jnp.concatenate(pieces, axis=0).astype(BF16)


def transform_kernel(shares, total, share, *refs):
    tiles, (fwd_ref, bwd_ref) = refs[:shares][::-1], refs[shares : shares + 2]
    outs, (gathered, weight, wide) = refs[shares + 2 : 2 * shares + 2], refs[2 * shares + 2 :]
    local_k = total // shares
    size = 2 * local_k * share
    me = lax.axis_index("ka")
    for s in range(shares):
        src = jnp.bitwise_xor(me, s)
        gathered[src] = tiles[s][:size].astype(gathered.dtype)
        cells = tiles[s][size:].astype(F32)
        for r in range(local_k):
            spread(weight, src * local_k + r, total, cells[r * share : (r + 1) * share])
    rows = 2 * local_k
    columns = []
    for c in range(share):
        columns.append(
            jnp.concatenate([gathered[a, c * rows : (c + 1) * rows] for a in range(shares)], axis=0).astype(BF16)
        )
    values = jnp.concatenate(columns, axis=1)
    cells = dot(fwd_ref[...], jnp.concatenate([values, values], axis=0))
    scale = jnp.concatenate([take(weight, c * total, total) for c in range(share)], axis=1)
    cells = (cells * jnp.concatenate([scale, scale], axis=0)).astype(BF16)
    kernel = dot(bwd_ref[...], jnp.concatenate([cells, cells], axis=0))
    points = kernel.shape[1] // share
    for c in range(share):
        spread(wide, c, share, kernel[:, c * points : (c + 1) * points])
    for s in range(shares):
        dest = jnp.bitwise_xor(me, s)
        outs[s][...] = take(wide, pl.multiple_of(dest * size, size), size).astype(BF16)


def weight_operands(pieces, right_ref, gathered):
    shares = len(pieces)
    groups, lanes, depth = right_ref.shape
    me, plane = lax.axis_index("ka"), plane_of(shares)
    for s in range(shares):
        gathered[jnp.bitwise_xor(jnp.bitwise_xor(me, s), plane)] = pieces[s][...]
    group = depth // (2 * gathered.shape[2])
    half = gathered.shape[1] // (groups * group) // 2
    for g in range(groups):
        right = []
        for kk in range(group):
            k = g * group + kk
            first, second = [], []
            for a in range(shares):
                piece = gathered[a, k * 2 * half : (k + 1) * 2 * half].astype(F32)
                first.append(piece)
                second.extend([piece[half:], -piece[:half]])
            first = jnp.concatenate(first, axis=0).astype(BF16)
            second = jnp.concatenate(second, axis=0).astype(BF16)
            parts = [jnp.zeros_like(first)] * (2 * group)
            parts[2 * kk], parts[2 * kk + 1] = first, second
            right.append(jnp.concatenate(parts, axis=1))
        right_ref[g] = jnp.concatenate(right, axis=0)


def weight_rows(offsets, flip, out_rows, right_ref, orb_ref, rest_ref, out_ref):
    groups, lanes, _ = right_ref.shape
    local_k, _, norb, _ = orb_ref.shape
    group = local_k // groups
    block = lax.axis_index("pts")
    core = jnp.bitwise_xor(jnp.bitwise_and(block, 1), flip)
    z = lax.shift_right_logical(block, 1)
    chunks = norb // out_rows // 2
    for g in range(groups):
        rows = []
        for offset in offsets:
            start = pl.multiple_of((2 * lax.rem(z + offset, chunks) + core) * out_rows, out_rows)
            parts = [
                ref[k, part, pl.ds(start, out_rows), :]
                for k in range(g * group, (g + 1) * group)
                for part in range(2)
                for ref in (orb_ref, rest_ref)
            ]
            rows.append(jnp.concatenate(parts, axis=1))
        result = dot(jnp.concatenate(rows, axis=0), right_ref[g], ((1,), (1,))).astype(out_ref.dtype)
        for i in range(len(offsets)):
            out_ref[i, :, g * lanes : (g + 1) * lanes] = result[i * out_rows : (i + 1) * out_rows]


def first_weight_kernel(shares, offsets, out_rows, *refs):
    pieces, (orb_ref, rest_ref, out_ref, right_ref, gathered) = refs[:shares][::-1], refs[shares:]
    weight_operands(pieces, right_ref, gathered)
    weight_rows(offsets, 1, out_rows, right_ref, orb_ref, rest_ref, out_ref)


def next_weight_kernel(offsets, flip, out_rows, right_ref, orb_ref, rest_ref, *refs):
    weight_rows(offsets, flip, out_rows, right_ref, orb_ref, rest_ref, refs[-1])


def pair_kernel(keep_ref, came_ref, *outs):
    for i, out_ref in enumerate(outs):
        out_ref[...] = (keep_ref[i] + came_ref[i].astype(F32)).astype(out_ref.dtype)


def exchange_kernel(chunks, scale, *refs):
    pieces, (form_ref, out_hbm, wide, out_ref, sems) = refs[:chunks][::-1], refs[chunks:]
    shares, local_k, part_lanes, twice = form_ref.shape
    lanes = shares * part_lanes
    norb = twice // 2
    spans = norb // LANES
    out_rows = pieces[0].shape[0]
    total = pieces[0][...]
    for s in range(1, chunks):
        total = total + pieces[s][...].astype(F32)
    total = total * scale
    high = total.astype(BF16)
    low = (total - high.astype(F32)).astype(BF16)
    group = max(1, LANES // lanes)
    width = group * lanes
    lane = lax.broadcasted_iota(jnp.int32, (out_rows, width), 1)
    zero = jnp.zeros((out_rows, width), BF16)
    copies = []
    for g in range(local_k // group):
        high_g = high[:, g * width : (g + 1) * width]
        low_g = low[:, g * width : (g + 1) * width]
        left = []
        for kk in range(group):
            keep = (lane >= kk * lanes) & (lane < (kk + 1) * lanes)
            left.append(
                jnp.concatenate([jnp.where(keep, high_g, zero), jnp.where(keep, low_g, zero)], axis=1)
            )
        forms = [form_ref[d, g * group + kk] for kk in range(group) for d in range(shares)]
        result = dot(jnp.concatenate(left, axis=0), jnp.concatenate(forms + forms, axis=0))
        for kk in range(group):
            for part in range(2):
                for t in range(spans):
                    lane_start = part * norb + t * LANES
                    value = result[kk * out_rows : (kk + 1) * out_rows, lane_start : lane_start + LANES]
                    start = (kk * spans + t) * 2 + part
                    wide[g, pl.ds(start, out_rows, stride=2 * spans * group), :] = value
        out_ref[g] = wide[g].astype(BF16).reshape(out_ref.shape[1:])
        copies.append(pltpu.make_async_copy(out_ref.at[g], out_hbm.at[:, g], sems.at[g]))
        copies[-1].start()
    for copy in copies:
        copy.wait()


def swap(value, axis, mask):
    size = lax.axis_size(axis)
    return lax.ppermute(value, axis, [(i, i ^ mask) for i in range(size)])


def trade(pieces, axis, step):
    return [swap(pieces[s], axis, s * step) for s in reversed(range(1, len(pieces)))] + [pieces[0]]


def shift_along(pieces):
    chunks = len(pieces)
    came = []
    for s in range(1, chunks):
        pairs = [(2 * z + core, 2 * ((z - s) % chunks) + core) for z in range(chunks) for core in range(2)]
        came.append(lax.ppermute(pieces[s], "pts", pairs))
    return came[::-1] + [pieces[0]]


def body(orbitals, coulomb):
    shares, blocks = lax.axis_size("ka"), lax.axis_size("pts")
    local_k, _, norb, points = orbitals.shape
    columns = coulomb.shape[1]
    per_block = columns // blocks
    share = columns // shares
    total = local_k * shares
    out_rows = norb // blocks
    chunks = blocks // 2
    group = ROWS // (2 * per_block)
    shape = jax.ShapeDtypeStruct

    edge, first = call(
        functools.partial(edge_kernel, per_block),
        [
            shape((local_k * 2 * per_block, norb), BF16),
            shape((local_k, 2, norb, LANES), BF16),
        ],
        0,
        [pltpu.SemaphoreType.DMA((local_k,))],
        limit=50,
        size=4 * MIB,
        unread=1,
    )(orbitals)
    passed_edge, rest = call(
        rest_kernel,
        [shape(edge.shape, BF16), shape((local_k, 2, norb, points - LANES), BF16)],
        0,
        [pltpu.SemaphoreType.DMA((local_k,)), pltpu.SemaphoreType.DMA],
        limit=49,
        size=4 * MIB,
        unread=2,
    )(orbitals, edge)
    per_share = blocks // shares
    partner = swap(passed_edge, "pts", 1)
    came = [edge, partner] + [swap(edge, "pts", 2 * e + c) for e in range(1, per_share // 2) for c in range(2)]
    came = {0: came}
    for offset in asked(shares):
        came[offset] = []
        for e in range(per_share // 2):
            block = swap(edge, "pts", offset * per_share + 2 * e)
            came[offset] += [block, swap(block, "pts", 1)]
    table = column_selector(group, per_share, per_block, 1).reshape(-1, per_share, ROWS)
    places = [[place ^ e for e in range(per_share)] for place in range(per_share)]
    tables = [table[:, place].reshape(table.shape[0], -1).astype(np.float32) for place in places]
    selector = jnp.asarray(np.stack([np.kron(np.eye(shares, dtype=np.float32), t) for t in tables]), BF16)
    piece = shape((share * 2 * local_k, points), BF16)
    both = shape((share * 3 * local_k, points), BF16)
    *tiles, forms = call(
        functools.partial(tile_kernel, shares, per_share, per_block),
        [both] * shares + [shape((shares, local_k, 2 * share, 2 * norb), BF16)],
        blocks + 4,
        [
            tiled(shares * share * 2 * local_k, points),
            pltpu.VMEM(coulomb.shape, F32),
        ],
        size=6 * MIB,
    )(*[block for offset in [0, *asked(shares)] for block in came[offset]], first, rest, selector, coulomb)
    tiles = trade(tiles, "ka", 1)

    forward, backward = phase_tables(total)
    kernels = call(
        functools.partial(transform_kernel, shares, total, share),
        [piece] * shares,
        shares + 2,
        [
            pltpu.VMEM((shares, share * 2 * local_k, points), BF16 if local_k % 8 == 0 else F32),
            tiled(share * total, points),
            tiled(2 * total * share, points),
        ],
        size=2 * MIB,
    )(*tiles, jnp.asarray(forward), jnp.asarray(backward))
    kernels = trade(kernels, "ka", 1)

    lanes = local_k * 2 * columns
    pair = max(1, LANES // (2 * columns))
    early, late = list(reversed(range(1, chunks))), [0]
    sent, right = call(
        functools.partial(first_weight_kernel, shares, early, out_rows),
        [
            shape((len(early), out_rows, lanes), BF16),
            shape((local_k // pair, pair * 2 * columns, pair * 2 * points), BF16),
        ],
        shares + 2,
        [pltpu.VMEM((shares, share * 2 * local_k, points), BF16)],
    )(*kernels, first, rest)

    def rows_of(offsets, flip, kind, before):
        return call(
            functools.partial(next_weight_kernel, offsets, flip, out_rows),
            shape((len(offsets), out_rows, lanes), kind),
            3,
            unread=1,
        )(right, first, rest, before)

    def summed(offsets, keep, came):
        kinds = [shape((out_rows, lanes), BF16 if offset else F32) for offset in offsets]
        return call(pair_kernel, kinds, 2)(keep, came)

    sent_late = rows_of(late, 1, BF16, sent)
    early_sums = summed(early, rows_of(early, 0, F32, sent_late), swap(sent, "pts", 1))
    late_sums = summed(late, rows_of(late, 0, F32, early_sums[0]), swap(sent_late, "pts", 1))
    sums = [*late_sums, *early_sums]
    sums = shift_along(sums)
    spans = norb // LANES
    rows = pair * spans * 2
    result = call(
        functools.partial(exchange_kernel, chunks, 1.0 / math.sqrt(points * blocks)),
        shape((out_rows, local_k // pair, rows, LANES), BF16),
        chunks + 1,
        [
            pltpu.VMEM((local_k // pair, out_rows * rows, LANES), F32),
            pltpu.VMEM((local_k // pair, out_rows, rows, LANES), BF16),
            pltpu.SemaphoreType.DMA((local_k // pair,)),
        ],
        size=4 * MIB,
        result=pltpu.HBM,
    )(*sums, forms)
    result = result.reshape(out_rows, local_k, spans, 2, LANES)
    return result.transpose(0, 1, 3, 2, 4).reshape(out_rows, local_k, 2, norb)


def solution(mesh):
    in_specs = (P("ka", None, None, "pts"), P("ka", None, "pts"))
    out_specs = P("pts", "ka", None, None)
    return jax.shard_map(body, mesh=mesh, in_specs=in_specs, out_specs=out_specs, check_vma=False)
```

```python
import functools
import math

import jax
import jax.numpy as jnp
import ml_dtypes
import numpy as np
from jax import lax
from jax.experimental import pallas as pl
from jax.experimental.pallas import tpu as pltpu
from jax.sharding import PartitionSpec as P

BF16 = jnp.bfloat16
F32 = jnp.float32
LANES = 128
ROWS = 16
MIB = 1 << 20


def split_terms(table):
    high = table.astype(ml_dtypes.bfloat16)
    low = (table - high.astype(np.float64)).astype(ml_dtypes.bfloat16)
    return np.concatenate([high, low], axis=1)


def phase_tables(total):
    index = np.arange(total)
    angles = (index[:, None] * index[None, :] % total) * (2.0 * math.pi / total)
    cosine, sine = np.cos(angles), np.sin(angles)
    forward = np.zeros((2, total, total, 2))
    forward[0, :, :, 0] = cosine
    forward[0, :, :, 1] = -sine
    forward[1, :, :, 0] = sine
    forward[1, :, :, 1] = cosine
    backward = np.zeros((total, 2, 2, total))
    backward[:, 0, 0] = cosine
    backward[:, 0, 1] = sine
    backward[:, 1, 1] = cosine
    backward[:, 1, 0] = -sine
    size = 2 * total
    return (
        split_terms(forward.reshape(size, size)),
        split_terms(backward.reshape(size, size) / total),
    )


def column_selector(group, blocks, per_block, shares):
    total = blocks * per_block
    share = total // shares
    table = np.zeros((group, 2, shares, 2, share, blocks, group, 2, per_block), np.float32)
    for k in range(group):
        for col in range(total):
            d, c = divmod(col, share)
            b, j = divmod(col, per_block)
            table[k, 0, d, 0, c, b, k, 0, j] = 1.0
            table[k, 0, d, 1, c, b, k, 1, j] = -1.0
            table[k, 1, d, 0, c, b, k, 1, j] = 1.0
            table[k, 1, d, 1, c, b, k, 0, j] = 1.0
    return table.reshape(group * 4 * total, blocks * group * 2 * per_block).astype(ml_dtypes.bfloat16)


def dot(left, right, dims=((1,), (0,))):
    return lax.dot_general(left, right, (dims, ((), ())), preferred_element_type=F32)


def spread(wide, start, stride, value):
    for t in range(wide.shape[0]):
        wide[t, pl.ds(start, value.shape[0], stride=stride), :] = value[:, t * LANES : (t + 1) * LANES]


def take(wide, start, size):
    return jnp.concatenate([wide[t, pl.ds(start, size), :] for t in range(wide.shape[0])], axis=1)


def tiled(rows, lanes):
    return pltpu.VMEM((lanes // LANES, rows, LANES), F32)


def call(kernel, out_shape, n_in, scratch=(), limit=24, flops=0, size=0, unread=0, result=pltpu.VMEM):
    whole = pl.BlockSpec(memory_space=pltpu.VMEM)
    return pl.pallas_call(
        kernel,
        out_shape=out_shape,
        in_specs=[whole] * n_in + [pl.BlockSpec(memory_space=pl.ANY)] * unread,
        out_specs=jax.tree.map(lambda _: pl.BlockSpec(memory_space=result), out_shape),
        scratch_shapes=list(scratch),
        compiler_params=pltpu.CompilerParams(vmem_limit_bytes=limit * MIB),
        cost_estimate=pl.CostEstimate(flops=flops, bytes_accessed=size, transcendentals=0),
    )


def load_copies(orb_hbm, orb_ref, sems, start):
    lanes = pl.ds(start, orb_ref.shape[3])
    copies = [
        pltpu.make_async_copy(orb_hbm.at[k, :, :, lanes], orb_ref.at[k], sems.at[k])
        for k in range(orb_ref.shape[0])
    ]
    for copy in copies:
        copy.start()
    return copies


def rest_kernel(orb_hbm, edge_hbm, pass_ref, orb_ref, sems, pass_sem):
    copies = load_copies(orb_hbm, orb_ref, sems, LANES)
    copies.append(pltpu.make_async_copy(edge_hbm, pass_ref, pass_sem))
    copies[-1].start()
    for copy in copies:
        copy.wait()


def edge_kernel(per_block, orb_hbm, edge_ref, orb_ref, sems):
    local_k = orb_hbm.shape[0]
    copies = load_copies(orb_hbm, orb_ref, sems, 0)
    row = lax.broadcasted_iota(jnp.int32, (2 * per_block, 2 * LANES), 0)
    lane = lax.broadcasted_iota(jnp.int32, (2 * per_block, 2 * LANES), 1)
    column = jnp.where(row < per_block, row, row - per_block + LANES)
    chosen = jnp.where(lane == column, jnp.ones(row.shape, F32), jnp.zeros(row.shape, F32)).astype(BF16)
    group = ROWS // (2 * per_block)
    for g in range(local_k // group):
        rows = []
        for k in range(g * group, (g + 1) * group):
            copies[k].wait()
            both = jnp.concatenate([orb_ref[k, 0], orb_ref[k, 1]], axis=1)
            rows.append(dot(chosen, both, ((1,), (1,))))
        edge_ref[g * ROWS : (g + 1) * ROWS] = jnp.concatenate(rows, axis=0).astype(BF16)


def asked(shares):
    return [2, 1, *range(3, shares)]


def plane_of(shares):
    return lax.div(lax.axis_index("pts"), lax.axis_size("pts") // shares)


def tile_kernel(shares, per_share, per_block, *refs):
    blocks, (orb_ref, rest_ref, sel_ref, coulomb_ref) = refs[: shares * per_share], refs[shares * per_share :][:4]
    *outs, form_ref, wide, cells = refs[shares * per_share + 4 :]
    local_k, _, norb, _ = orb_ref.shape
    group = ROWS // (2 * per_block)
    share = per_share * per_block
    rows = 2 * share
    me, block = lax.axis_index("ka"), lax.axis_index("pts")
    plane = plane_of(shares)
    selector = sel_ref[jnp.bitwise_and(block, per_share - 1)]
    order = [0, *asked(shares)]
    for g in range(local_k // group):
        stacked = jnp.concatenate(
            [
                blocks[order.index(offset) * per_share + e][g * ROWS : (g + 1) * ROWS]
                for offset in range(shares)
                for e in range(per_share)
            ],
            axis=0,
        )
        chosen = dot(selector, stacked).astype(BF16)
        size = 2 * group * rows
        forms = [chosen[offset * size : (offset + 1) * size] for offset in range(shares)]
        for kk in range(group):
            k = g * group + kk
            left = [form[2 * kk * rows : (2 * kk + 1) * rows] for form in forms]
            right = [form[(2 * kk + 1) * rows : (2 * kk + 2) * rows] for form in forms]
            form = jnp.concatenate(
                [jnp.concatenate(left, axis=0), jnp.concatenate(right, axis=0)], axis=1
            )
            halves = [ref[k].reshape(2 * norb, ref.shape[3]) for ref in (orb_ref, rest_ref)]
            tile = dot(form, jnp.concatenate(halves, axis=1))
            for offset in range(shares):
                form_ref[jnp.bitwise_xor(plane, offset), k] = form[offset * rows : (offset + 1) * rows]
                for part in range(2):
                    low = offset * rows + part * share
                    start = offset * share * 2 * local_k + 2 * k + part
                    spread(wide, start, 2 * local_k, tile[low : low + share])
    size = share * 2 * local_k
    cells[...] = coulomb_ref[...].astype(F32)
    for s in range(shares):
        offset = jnp.bitwise_xor(me, s)
        outs[s][:size] = take(wide, pl.multiple_of(offset * size, size), size).astype(BF16)
        start = pl.multiple_of(jnp.bitwise_xor(offset, plane) * share, share)
        pieces = [cells[r, pl.ds(start, share), :] for r in range(local_k)]
        outs[s][size:] = jnp.concatenate(pieces, axis=0).astype(BF16)


def transform_kernel(shares, total, share, *refs):
    tiles, (fwd_ref, bwd_ref) = refs[:shares][::-1], refs[shares : shares + 2]
    outs, (gathered, weight, wide) = refs[shares + 2 : 2 * shares + 2], refs[2 * shares + 2 :]
    local_k = total // shares
    size = 2 * local_k * share
    me = lax.axis_index("ka")
    for s in range(shares):
        src = jnp.bitwise_xor(me, s)
        gathered[src] = tiles[s][:size].astype(gathered.dtype)
        cells = tiles[s][size:].astype(F32)
        for r in range(local_k):
            spread(weight, src * local_k + r, total, cells[r * share : (r + 1) * share])
    rows = 2 * local_k
    columns = []
    for c in range(share):
        columns.append(
            jnp.concatenate([gathered[a, c * rows : (c + 1) * rows] for a in range(shares)], axis=0).astype(BF16)
        )
    values = jnp.concatenate(columns, axis=1)
    cells = dot(fwd_ref[...], jnp.concatenate([values, values], axis=0))
    scale = jnp.concatenate([take(weight, c * total, total) for c in range(share)], axis=1)
    cells = (cells * jnp.concatenate([scale, scale], axis=0)).astype(BF16)
    kernel = dot(bwd_ref[...], jnp.concatenate([cells, cells], axis=0))
    points = kernel.shape[1] // share
    for c in range(share):
        spread(wide, c, share, kernel[:, c * points : (c + 1) * points])
    for s in range(shares):
        dest = jnp.bitwise_xor(me, s)
        outs[s][...] = take(wide, pl.multiple_of(dest * size, size), size).astype(BF16)


def weight_operands(pieces, right_ref, gathered):
    shares = len(pieces)
    groups, lanes, depth = right_ref.shape
    me, plane = lax.axis_index("ka"), plane_of(shares)
    for s in range(shares):
        gathered[jnp.bitwise_xor(jnp.bitwise_xor(me, s), plane)] = pieces[s][...]
    group = depth // (2 * gathered.shape[2])
    half = gathered.shape[1] // (groups * group) // 2
    for g in range(groups):
        right = []
        for kk in range(group):
            k = g * group + kk
            first, second = [], []
            for a in range(shares):
                piece = gathered[a, k * 2 * half : (k + 1) * 2 * half].astype(F32)
                first.append(piece)
                second.extend([piece[half:], -piece[:half]])
            first = jnp.concatenate(first, axis=0).astype(BF16)
            second = jnp.concatenate(second, axis=0).astype(BF16)
            parts = [jnp.zeros_like(first)] * (2 * group)
            parts[2 * kk], parts[2 * kk + 1] = first, second
            right.append(jnp.concatenate(parts, axis=1))
        right_ref[g] = jnp.concatenate(right, axis=0)


def weight_rows(offsets, flip, out_rows, right_ref, orb_ref, rest_ref, out_ref):
    groups, lanes, _ = right_ref.shape
    local_k, _, norb, _ = orb_ref.shape
    group = local_k // groups
    block = lax.axis_index("pts")
    core = jnp.bitwise_xor(jnp.bitwise_and(block, 1), flip)
    z = lax.shift_right_logical(block, 1)
    chunks = norb // out_rows // 2
    for g in range(groups):
        rows = []
        for offset in offsets:
            start = pl.multiple_of((2 * lax.rem(z + offset, chunks) + core) * out_rows, out_rows)
            parts = [
                ref[k, part, pl.ds(start, out_rows), :]
                for k in range(g * group, (g + 1) * group)
                for part in range(2)
                for ref in (orb_ref, rest_ref)
            ]
            rows.append(jnp.concatenate(parts, axis=1))
        result = dot(jnp.concatenate(rows, axis=0), right_ref[g], ((1,), (1,))).astype(out_ref.dtype)
        for i in range(len(offsets)):
            out_ref[i, :, g * lanes : (g + 1) * lanes] = result[i * out_rows : (i + 1) * out_rows]


def first_weight_kernel(shares, offsets, out_rows, *refs):
    pieces, (orb_ref, rest_ref, out_ref, right_ref, gathered) = refs[:shares][::-1], refs[shares:]
    weight_operands(pieces, right_ref, gathered)
    weight_rows(offsets, 1, out_rows, right_ref, orb_ref, rest_ref, out_ref)


def next_weight_kernel(offsets, flip, out_rows, right_ref, orb_ref, rest_ref, *refs):
    weight_rows(offsets, flip, out_rows, right_ref, orb_ref, rest_ref, refs[-1])


def pair_kernel(keep_ref, came_ref, *outs):
    for i, out_ref in enumerate(outs):
        out_ref[...] = (keep_ref[i] + came_ref[i].astype(F32)).astype(out_ref.dtype)


def exchange_kernel(chunks, scale, *refs):
    pieces, (form_ref, out_hbm, wide, out_ref, sems) = refs[:chunks][::-1], refs[chunks:]
    shares, local_k, part_lanes, twice = form_ref.shape
    lanes = shares * part_lanes
    norb = twice // 2
    spans = norb // LANES
    out_rows = pieces[0].shape[0]
    total = pieces[0][...]
    for s in range(1, chunks):
        total = total + pieces[s][...].astype(F32)
    total = (total * scale).astype(BF16)
    pair = max(1, LANES // lanes)
    group = min(local_k, max(1, 2 * LANES // lanes))
    width = group * lanes
    lane = lax.broadcasted_iota(jnp.int32, (out_rows, width), 1)
    zero = jnp.zeros((out_rows, width), BF16)
    copies = []
    for g in range(local_k // group):
        part_g = total[:, g * width : (g + 1) * width]
        left = [
            jnp.where((lane >= kk * lanes) & (lane < (kk + 1) * lanes), part_g, zero) for kk in range(group)
        ]
        forms = [form_ref[d, g * group + kk] for kk in range(group) for d in range(shares)]
        result = dot(jnp.concatenate(left, axis=0), jnp.concatenate(forms, axis=0))
        for kk in range(group):
            place, slot = divmod(g * group + kk, pair)
            for part in range(2):
                for t in range(spans):
                    lane_start = part * norb + t * LANES
                    value = result[kk * out_rows : (kk + 1) * out_rows, lane_start : lane_start + LANES]
                    start = (slot * spans + t) * 2 + part
                    wide[place, pl.ds(start, out_rows, stride=2 * spans * pair), :] = value
            if slot == pair - 1:
                out_ref[place] = wide[place].astype(BF16).reshape(out_ref.shape[1:])
                copies.append(pltpu.make_async_copy(out_ref.at[place], out_hbm.at[:, place], sems.at[place]))
                copies[-1].start()
    for copy in copies:
        copy.wait()


def swap(value, axis, mask):
    size = lax.axis_size(axis)
    return lax.ppermute(value, axis, [(i, i ^ mask) for i in range(size)])


def trade(pieces, axis, step):
    return [swap(pieces[s], axis, s * step) for s in reversed(range(1, len(pieces)))] + [pieces[0]]


def shift_along(pieces):
    chunks = len(pieces)
    came = []
    for s in range(1, chunks):
        pairs = [(2 * z + core, 2 * ((z - s) % chunks) + core) for z in range(chunks) for core in range(2)]
        came.append(lax.ppermute(pieces[s], "pts", pairs))
    return came[::-1] + [pieces[0]]


def body(orbitals, coulomb):
    shares, blocks = lax.axis_size("ka"), lax.axis_size("pts")
    local_k, _, norb, points = orbitals.shape
    columns = coulomb.shape[1]
    per_block = columns // blocks
    share = columns // shares
    total = local_k * shares
    out_rows = norb // blocks
    chunks = blocks // 2
    group = ROWS // (2 * per_block)
    shape = jax.ShapeDtypeStruct

    edge, first = call(
        functools.partial(edge_kernel, per_block),
        [
            shape((local_k * 2 * per_block, norb), BF16),
            shape((local_k, 2, norb, LANES), BF16),
        ],
        0,
        [pltpu.SemaphoreType.DMA((local_k,))],
        limit=50,
        size=4 * MIB,
        unread=1,
    )(orbitals)
    passed_edge, rest = call(
        rest_kernel,
        [shape(edge.shape, BF16), shape((local_k, 2, norb, points - LANES), BF16)],
        0,
        [pltpu.SemaphoreType.DMA((local_k,)), pltpu.SemaphoreType.DMA],
        limit=49,
        size=4 * MIB,
        unread=2,
    )(orbitals, edge)
    per_share = blocks // shares
    partner = swap(passed_edge, "pts", 1)
    came = [edge, partner] + [swap(edge, "pts", 2 * e + c) for e in range(1, per_share // 2) for c in range(2)]
    came = {0: came}
    for offset in asked(shares):
        came[offset] = []
        for e in range(per_share // 2):
            block = swap(edge, "pts", offset * per_share + 2 * e)
            came[offset] += [block, swap(block, "pts", 1)]
    table = column_selector(group, per_share, per_block, 1).reshape(-1, per_share, ROWS)
    places = [[place ^ e for e in range(per_share)] for place in range(per_share)]
    tables = [table[:, place].reshape(table.shape[0], -1).astype(np.float32) for place in places]
    selector = jnp.asarray(np.stack([np.kron(np.eye(shares, dtype=np.float32), t) for t in tables]), BF16)
    piece = shape((share * 2 * local_k, points), BF16)
    both = shape((share * 3 * local_k, points), BF16)
    *tiles, forms = call(
        functools.partial(tile_kernel, shares, per_share, per_block),
        [both] * shares + [shape((shares, local_k, 2 * share, 2 * norb), BF16)],
        blocks + 4,
        [
            tiled(shares * share * 2 * local_k, points),
            pltpu.VMEM(coulomb.shape, F32),
        ],
        size=6 * MIB,
    )(*[block for offset in [0, *asked(shares)] for block in came[offset]], first, rest, selector, coulomb)
    tiles = trade(tiles, "ka", 1)

    forward, backward = phase_tables(total)
    kernels = call(
        functools.partial(transform_kernel, shares, total, share),
        [piece] * shares,
        shares + 2,
        [
            pltpu.VMEM((shares, share * 2 * local_k, points), BF16 if local_k % 8 == 0 else F32),
            tiled(share * total, points),
            tiled(2 * total * share, points),
        ],
        size=2 * MIB,
    )(*tiles, jnp.asarray(forward), jnp.asarray(backward))
    kernels = trade(kernels, "ka", 1)

    lanes = local_k * 2 * columns
    pair = max(1, LANES // (2 * columns))
    early, late = list(reversed(range(1, chunks))), [0]
    sent, right = call(
        functools.partial(first_weight_kernel, shares, early, out_rows),
        [
            shape((len(early), out_rows, lanes), BF16),
            shape((local_k // pair, pair * 2 * columns, pair * 2 * points), BF16),
        ],
        shares + 2,
        [pltpu.VMEM((shares, share * 2 * local_k, points), BF16)],
    )(*kernels, first, rest)

    def rows_of(offsets, flip, kind, before):
        return call(
            functools.partial(next_weight_kernel, offsets, flip, out_rows),
            shape((len(offsets), out_rows, lanes), kind),
            3,
            unread=1,
        )(right, first, rest, before)

    def summed(offsets, keep, came):
        kinds = [shape((out_rows, lanes), BF16 if offset else F32) for offset in offsets]
        return call(pair_kernel, kinds, 2)(keep, came)

    early_sums = summed(early, rows_of(early, 0, F32, sent), swap(sent, "pts", 1))
    sent_late = rows_of(late, 1, BF16, early_sums[0])
    late_sums = summed(late, rows_of(late, 0, F32, sent_late), swap(sent_late, "pts", 1))
    sums = [*late_sums, *early_sums]
    sums = shift_along(sums)
    spans = norb // LANES
    rows = pair * spans * 2
    result = call(
        functools.partial(exchange_kernel, chunks, 1.0 / math.sqrt(points * blocks)),
        shape((out_rows, local_k // pair, rows, LANES), BF16),
        chunks + 1,
        [
            pltpu.VMEM((local_k // pair, out_rows * rows, LANES), F32),
            pltpu.VMEM((local_k // pair, out_rows, rows, LANES), BF16),
            pltpu.SemaphoreType.DMA((local_k // pair,)),
        ],
        size=4 * MIB,
        result=pltpu.HBM,
    )(*sums, forms)
    result = result.reshape(out_rows, local_k, spans, 2, LANES)
    return result.transpose(0, 1, 3, 2, 4).reshape(out_rows, local_k, 2, norb)


def solution(mesh):
    in_specs = (P("ka", None, None, "pts"), P("ka", None, "pts"))
    out_specs = P("pts", "ka", None, None)
    return jax.shard_map(body, mesh=mesh, in_specs=in_specs, out_specs=out_specs, check_vma=False)
```

```python
import functools
import math

import jax
import jax.numpy as jnp
import ml_dtypes
import numpy as np
from jax import lax
from jax.experimental import pallas as pl
from jax.experimental.pallas import tpu as pltpu
from jax.sharding import PartitionSpec as P

BF16 = jnp.bfloat16
F32 = jnp.float32
LANES = 128
ROWS = 16
MIB = 1 << 20


def split_terms(table):
    high = table.astype(ml_dtypes.bfloat16)
    low = (table - high.astype(np.float64)).astype(ml_dtypes.bfloat16)
    return np.concatenate([high, low], axis=1)


def phase_tables(total):
    index = np.arange(total)
    angles = (index[:, None] * index[None, :] % total) * (2.0 * math.pi / total)
    cosine, sine = np.cos(angles), np.sin(angles)
    forward = np.zeros((2, total, total, 2))
    forward[0, :, :, 0] = cosine
    forward[0, :, :, 1] = -sine
    forward[1, :, :, 0] = sine
    forward[1, :, :, 1] = cosine
    backward = np.zeros((total, 2, 2, total))
    backward[:, 0, 0] = cosine
    backward[:, 0, 1] = sine
    backward[:, 1, 1] = cosine
    backward[:, 1, 0] = -sine
    size = 2 * total
    return (
        split_terms(forward.reshape(size, size)),
        split_terms(backward.reshape(size, size) / total),
    )


def column_selector(group, blocks, per_block, shares):
    total = blocks * per_block
    share = total // shares
    table = np.zeros((group, 2, shares, 2, share, blocks, group, 2, per_block), np.float32)
    for k in range(group):
        for col in range(total):
            d, c = divmod(col, share)
            b, j = divmod(col, per_block)
            table[k, 0, d, 0, c, b, k, 0, j] = 1.0
            table[k, 0, d, 1, c, b, k, 1, j] = -1.0
            table[k, 1, d, 0, c, b, k, 1, j] = 1.0
            table[k, 1, d, 1, c, b, k, 0, j] = 1.0
    return table.reshape(group * 4 * total, blocks * group * 2 * per_block).astype(ml_dtypes.bfloat16)


def dot(left, right, dims=((1,), (0,))):
    return lax.dot_general(left, right, (dims, ((), ())), preferred_element_type=F32)


def spread(wide, start, stride, value):
    for t in range(wide.shape[0]):
        wide[t, pl.ds(start, value.shape[0], stride=stride), :] = value[:, t * LANES : (t + 1) * LANES]


def take(wide, start, size):
    return jnp.concatenate([wide[t, pl.ds(start, size), :] for t in range(wide.shape[0])], axis=1)


def tiled(rows, lanes):
    return pltpu.VMEM((lanes // LANES, rows, LANES), F32)


def call(kernel, out_shape, n_in, scratch=(), limit=24, flops=0, size=0, unread=0, result=pltpu.VMEM):
    whole = pl.BlockSpec(memory_space=pltpu.VMEM)
    return pl.pallas_call(
        kernel,
        out_shape=out_shape,
        in_specs=[whole] * n_in + [pl.BlockSpec(memory_space=pl.ANY)] * unread,
        out_specs=jax.tree.map(lambda _: pl.BlockSpec(memory_space=result), out_shape),
        scratch_shapes=list(scratch),
        compiler_params=pltpu.CompilerParams(vmem_limit_bytes=limit * MIB),
        cost_estimate=pl.CostEstimate(flops=flops, bytes_accessed=size, transcendentals=0),
    )


def coulomb_kernel(shares, coulomb_ref, out_ref, wide):
    cells, columns, points = coulomb_ref.shape
    share = columns // shares
    plane = plane_of(shares)
    wide[...] = coulomb_ref[...].astype(F32)
    for owner in range(shares):
        start = pl.multiple_of(jnp.bitwise_xor(owner, plane) * share, share)
        pieces = [wide[r, pl.ds(start, share), :] for r in range(cells)]
        out_ref[owner] = jnp.concatenate(pieces, axis=0).astype(BF16)


def edge_kernel(per_block, orb_ref, edge_ref):
    local_k = orb_ref.shape[0]
    row = lax.broadcasted_iota(jnp.int32, (2 * per_block, 2 * LANES), 0)
    lane = lax.broadcasted_iota(jnp.int32, (2 * per_block, 2 * LANES), 1)
    column = jnp.where(row < per_block, row, row - per_block + LANES)
    chosen = jnp.where(lane == column, jnp.ones(row.shape, F32), jnp.zeros(row.shape, F32)).astype(BF16)
    group = ROWS // (2 * per_block)
    for g in range(local_k // group):
        rows = []
        for k in range(g * group, (g + 1) * group):
            both = jnp.concatenate([orb_ref[k, 0, :, :LANES], orb_ref[k, 1, :, :LANES]], axis=1)
            rows.append(dot(chosen, both, ((1,), (1,))))
        edge_ref[g * ROWS : (g + 1) * ROWS] = jnp.concatenate(rows, axis=0).astype(BF16)


def asked(shares):
    return [2, 1, *range(3, shares)]


def plane_of(shares):
    return lax.div(lax.axis_index("pts"), lax.axis_size("pts") // shares)


def tile_kernel(shares, per_share, per_block, *refs):
    blocks, (orb_ref, sel_ref) = refs[: shares * per_share], refs[shares * per_share :][:2]
    *outs, form_ref, wide = refs[shares * per_share + 2 :]
    local_k, _, norb, points = orb_ref.shape
    group = ROWS // (2 * per_block)
    share = per_share * per_block
    rows = 2 * share
    me, block = lax.axis_index("ka"), lax.axis_index("pts")
    plane = plane_of(shares)
    selector = sel_ref[jnp.bitwise_and(block, per_share - 1)]
    order = [0, *asked(shares)]
    for g in range(local_k // group):
        stacked = jnp.concatenate(
            [
                blocks[order.index(offset) * per_share + e][g * ROWS : (g + 1) * ROWS]
                for offset in range(shares)
                for e in range(per_share)
            ],
            axis=0,
        )
        chosen = dot(selector, stacked).astype(BF16)
        size = 2 * group * rows
        forms = [chosen[offset * size : (offset + 1) * size] for offset in range(shares)]
        for kk in range(group):
            k = g * group + kk
            left = [form[2 * kk * rows : (2 * kk + 1) * rows] for form in forms]
            right = [form[(2 * kk + 1) * rows : (2 * kk + 2) * rows] for form in forms]
            form = jnp.concatenate(
                [jnp.concatenate(left, axis=0), jnp.concatenate(right, axis=0)], axis=1
            )
            tile = dot(form, orb_ref[k].reshape(2 * norb, points))
            for offset in range(shares):
                form_ref[jnp.bitwise_xor(plane, offset), k] = form[offset * rows : (offset + 1) * rows]
                for part in range(2):
                    low = offset * rows + part * share
                    start = offset * share * 2 * local_k + 2 * k + part
                    spread(wide, start, 2 * local_k, tile[low : low + share])
    size = share * 2 * local_k
    for s in range(shares):
        offset = jnp.bitwise_xor(me, s)
        outs[s][...] = take(wide, pl.multiple_of(offset * size, size), size).astype(BF16)


def transform_kernel(shares, total, share, *refs):
    tiles, (fwd_ref, bwd_ref, cell_ref) = refs[:shares][::-1], refs[shares : shares + 3]
    outs, (gathered, weight, wide) = refs[shares + 3 : 2 * shares + 3], refs[2 * shares + 3 :]
    local_k = total // shares
    size = 2 * local_k * share
    me = lax.axis_index("ka")
    for s in range(shares):
        src = jnp.bitwise_xor(me, s)
        gathered[src] = tiles[s][...].astype(gathered.dtype)
        cells = cell_ref[s].astype(F32)
        for r in range(local_k):
            spread(weight, s * local_k + r, total, cells[r * share : (r + 1) * share])
    rows = 2 * local_k
    columns = []
    for c in range(share):
        columns.append(
            jnp.concatenate([gathered[a, c * rows : (c + 1) * rows] for a in range(shares)], axis=0).astype(BF16)
        )
    values = jnp.concatenate(columns, axis=1)
    cells = dot(fwd_ref[...], jnp.concatenate([values, values], axis=0))
    scale = jnp.concatenate([take(weight, c * total, total) for c in range(share)], axis=1)
    cells = (cells * jnp.concatenate([scale, scale], axis=0)).astype(BF16)
    kernel = dot(bwd_ref[...], jnp.concatenate([cells, cells], axis=0))
    points = kernel.shape[1] // share
    for c in range(share):
        spread(wide, c, share, kernel[:, c * points : (c + 1) * points])
    for s in range(shares):
        dest = jnp.bitwise_xor(me, s)
        outs[s][...] = take(wide, pl.multiple_of(dest * size, size), size).astype(BF16)


def weight_operands(pieces, right_ref, gathered):
    shares = len(pieces)
    groups, lanes, depth = right_ref.shape
    me, plane = lax.axis_index("ka"), plane_of(shares)
    for s in range(shares):
        gathered[jnp.bitwise_xor(jnp.bitwise_xor(me, s), plane)] = pieces[s][...]
    group = depth // (2 * gathered.shape[2])
    half = gathered.shape[1] // (groups * group) // 2
    for g in range(groups):
        right = []
        for kk in range(group):
            k = g * group + kk
            first, second = [], []
            for a in range(shares):
                piece = gathered[a, k * 2 * half : (k + 1) * 2 * half].astype(F32)
                first.append(piece)
                second.extend([piece[half:], -piece[:half]])
            first = jnp.concatenate(first, axis=0).astype(BF16)
            second = jnp.concatenate(second, axis=0).astype(BF16)
            parts = [jnp.zeros_like(first)] * (2 * group)
            parts[2 * kk], parts[2 * kk + 1] = first, second
            right.append(jnp.concatenate(parts, axis=1))
        right_ref[g] = jnp.concatenate(right, axis=0)


def weight_rows(offsets, flip, out_rows, right_ref, orb_ref, out_ref):
    groups, lanes, _ = right_ref.shape
    local_k, _, norb, _ = orb_ref.shape
    group = local_k // groups
    block = lax.axis_index("pts")
    core = jnp.bitwise_xor(jnp.bitwise_and(block, 1), flip)
    z = lax.shift_right_logical(block, 1)
    chunks = norb // out_rows // 2
    for g in range(groups):
        rows = []
        for offset in offsets:
            start = pl.multiple_of((2 * lax.rem(z + offset, chunks) + core) * out_rows, out_rows)
            parts = [
                orb_ref[k, part, pl.ds(start, out_rows), :]
                for k in range(g * group, (g + 1) * group)
                for part in range(2)
            ]
            rows.append(jnp.concatenate(parts, axis=1))
        result = dot(jnp.concatenate(rows, axis=0), right_ref[g], ((1,), (1,))).astype(out_ref.dtype)
        for i in range(len(offsets)):
            out_ref[i, :, g * lanes : (g + 1) * lanes] = result[i * out_rows : (i + 1) * out_rows]


def first_weight_kernel(shares, offsets, out_rows, *refs):
    pieces, (orb_ref, out_ref, right_ref, gathered) = refs[:shares][::-1], refs[shares:]
    weight_operands(pieces, right_ref, gathered)
    weight_rows(offsets, 1, out_rows, right_ref, orb_ref, out_ref)


def next_weight_kernel(offsets, flip, out_rows, right_ref, orb_ref, *refs):
    weight_rows(offsets, flip, out_rows, right_ref, orb_ref, refs[-1])


def pair_kernel(keep_ref, came_ref, *outs):
    for i, out_ref in enumerate(outs):
        out_ref[...] = (keep_ref[i] + came_ref[i].astype(F32)).astype(out_ref.dtype)


def exchange_kernel(chunks, scale, *refs):
    pieces, (form_ref, out_hbm, wide, out_ref, sems) = refs[:chunks][::-1], refs[chunks:]
    shares, local_k, part_lanes, twice = form_ref.shape
    lanes = shares * part_lanes
    norb = twice // 2
    spans = norb // LANES
    out_rows = pieces[0].shape[0]
    total = pieces[0][...]
    for s in range(1, chunks):
        total = total + pieces[s][...].astype(F32)
    total = total * scale
    high = total.astype(BF16)
    low = (total - high.astype(F32)).astype(BF16)
    group = max(1, LANES // lanes)
    width = group * lanes
    lane = lax.broadcasted_iota(jnp.int32, (out_rows, width), 1)
    zero = jnp.zeros((out_rows, width), BF16)
    copies = []
    for g in range(local_k // group):
        high_g = high[:, g * width : (g + 1) * width]
        low_g = low[:, g * width : (g + 1) * width]
        left = []
        for kk in range(group):
            keep = (lane >= kk * lanes) & (lane < (kk + 1) * lanes)
            left.append(
                jnp.concatenate([jnp.where(keep, high_g, zero), jnp.where(keep, low_g, zero)], axis=1)
            )
        forms = [form_ref[d, g * group + kk] for kk in range(group) for d in range(shares)]
        result = dot(jnp.concatenate(left, axis=0), jnp.concatenate(forms + forms, axis=0))
        for kk in range(group):
            for part in range(2):
                for t in range(spans):
                    lane_start = part * norb + t * LANES
                    value = result[kk * out_rows : (kk + 1) * out_rows, lane_start : lane_start + LANES]
                    start = (kk * spans + t) * 2 + part
                    wide[g, pl.ds(start, out_rows, stride=2 * spans * group), :] = value
        out_ref[g] = wide[g].astype(BF16).reshape(out_ref.shape[1:])
        copies.append(pltpu.make_async_copy(out_ref.at[g], out_hbm.at[:, g], sems.at[g]))
        copies[-1].start()
    for copy in copies:
        copy.wait()


def swap(value, axis, mask):
    size = lax.axis_size(axis)
    return lax.ppermute(value, axis, [(i, i ^ mask) for i in range(size)])


def trade(pieces, axis, step):
    return [swap(pieces[s], axis, s * step) for s in reversed(range(1, len(pieces)))] + [pieces[0]]


def shift_along(pieces):
    chunks = len(pieces)
    came = []
    for s in range(1, chunks):
        pairs = [(2 * z + core, 2 * ((z - s) % chunks) + core) for z in range(chunks) for core in range(2)]
        came.append(lax.ppermute(pieces[s], "pts", pairs))
    return came[::-1] + [pieces[0]]


def body(orbitals, coulomb):
    shares, blocks = lax.axis_size("ka"), lax.axis_size("pts")
    local_k, _, norb, points = orbitals.shape
    columns = coulomb.shape[1]
    per_block = columns // blocks
    share = columns // shares
    total = local_k * shares
    out_rows = norb // blocks
    chunks = blocks // 2
    group = ROWS // (2 * per_block)
    shape = jax.ShapeDtypeStruct

    cells = call(
        functools.partial(coulomb_kernel, shares),
        shape((shares, local_k * share, points), BF16),
        1,
        [pltpu.VMEM(coulomb.shape, F32)],
    )(coulomb)
    cells = lax.all_to_all(cells, "ka", split_axis=0, concat_axis=0, tiled=True)
    edge = call(
        functools.partial(edge_kernel, per_block),
        shape((local_k * 2 * per_block, norb), BF16),
        1,
    )(orbitals)
    per_share = blocks // shares
    partner = swap(edge, "pts", 1)
    came = [edge, partner] + [swap(edge, "pts", 2 * e + c) for e in range(1, per_share // 2) for c in range(2)]
    came = {0: came}
    for offset in asked(shares):
        came[offset] = []
        for e in range(per_share // 2):
            block = swap(edge, "pts", offset * per_share + 2 * e)
            came[offset] += [block, swap(block, "pts", 1)]
    table = column_selector(group, per_share, per_block, 1).reshape(-1, per_share, ROWS)
    places = [[place ^ e for e in range(per_share)] for place in range(per_share)]
    tables = [table[:, place].reshape(table.shape[0], -1).astype(np.float32) for place in places]
    selector = jnp.asarray(np.stack([np.kron(np.eye(shares, dtype=np.float32), t) for t in tables]), BF16)
    piece = shape((share * 2 * local_k, points), BF16)
    *tiles, forms = call(
        functools.partial(tile_kernel, shares, per_share, per_block),
        [piece] * shares + [shape((shares, local_k, 2 * share, 2 * norb), BF16)],
        blocks + 2,
        [
            tiled(shares * share * 2 * local_k, points),
        ],
        size=6 * MIB,
    )(*[block for offset in [0, *asked(shares)] for block in came[offset]], orbitals, selector)
    tiles = trade(tiles, "ka", 1)

    forward, backward = phase_tables(total)
    kernels = call(
        functools.partial(transform_kernel, shares, total, share),
        [piece] * shares,
        shares + 3,
        [
            pltpu.VMEM((shares, share * 2 * local_k, points), BF16 if local_k % 8 == 0 else F32),
            tiled(share * total, points),
            tiled(2 * total * share, points),
        ],
        size=2 * MIB,
    )(*tiles, jnp.asarray(forward), jnp.asarray(backward), cells)
    kernels = trade(kernels, "ka", 1)

    lanes = local_k * 2 * columns
    pair = max(1, LANES // (2 * columns))
    early, late = list(reversed(range(1, chunks))), [0]
    sent, right = call(
        functools.partial(first_weight_kernel, shares, early, out_rows),
        [
            shape((len(early), out_rows, lanes), BF16),
            shape((local_k // pair, pair * 2 * columns, pair * 2 * points), BF16),
        ],
        shares + 1,
        [pltpu.VMEM((shares, share * 2 * local_k, points), BF16)],
    )(*kernels, orbitals)

    def rows_of(offsets, flip, kind, before):
        return call(
            functools.partial(next_weight_kernel, offsets, flip, out_rows),
            shape((len(offsets), out_rows, lanes), kind),
            2,
            unread=1,
        )(right, orbitals, before)

    def summed(offsets, keep, came):
        kinds = [shape((out_rows, lanes), BF16 if offset else F32) for offset in offsets]
        return call(pair_kernel, kinds, 2)(keep, came)

    sent_late = rows_of(late, 1, BF16, sent)
    early_sums = summed(early, rows_of(early, 0, F32, sent_late), swap(sent, "pts", 1))
    late_sums = summed(late, rows_of(late, 0, F32, early_sums[0]), swap(sent_late, "pts", 1))
    sums = [*late_sums, *early_sums]
    sums = shift_along(sums)
    spans = norb // LANES
    rows = pair * spans * 2
    result = call(
        functools.partial(exchange_kernel, chunks, 1.0 / math.sqrt(points * blocks)),
        shape((out_rows, local_k // pair, rows, LANES), BF16),
        chunks + 1,
        [
            pltpu.VMEM((local_k // pair, out_rows * rows, LANES), F32),
            pltpu.VMEM((local_k // pair, out_rows, rows, LANES), BF16),
            pltpu.SemaphoreType.DMA((local_k // pair,)),
        ],
        size=4 * MIB,
        result=pltpu.HBM,
    )(*sums, forms)
    result = result.reshape(out_rows, local_k, spans, 2, LANES)
    return result.transpose(0, 1, 3, 2, 4).reshape(out_rows, local_k, 2, norb)


def solution(mesh):
    in_specs = (P("ka", None, None, "pts"), P("ka", None, "pts"))
    out_specs = P("pts", "ka", None, None)
    return jax.shard_map(body, mesh=mesh, in_specs=in_specs, out_specs=out_specs, check_vma=False)
```

```python
import functools
import math

import jax
import jax.numpy as jnp
import ml_dtypes
import numpy as np
from jax import lax
from jax.experimental import pallas as pl
from jax.experimental.pallas import tpu as pltpu
from jax.sharding import PartitionSpec as P

BF16 = jnp.bfloat16
F32 = jnp.float32
LANES = 128
ROWS = 16
MIB = 1 << 20


def split_terms(table):
    high = table.astype(ml_dtypes.bfloat16)
    low = (table - high.astype(np.float64)).astype(ml_dtypes.bfloat16)
    return np.concatenate([high, low], axis=1)


def phase_tables(total):
    index = np.arange(total)
    angles = (index[:, None] * index[None, :] % total) * (2.0 * math.pi / total)
    cosine, sine = np.cos(angles), np.sin(angles)
    forward = np.zeros((2, total, total, 2))
    forward[0, :, :, 0] = cosine
    forward[0, :, :, 1] = -sine
    forward[1, :, :, 0] = sine
    forward[1, :, :, 1] = cosine
    backward = np.zeros((total, 2, 2, total))
    backward[:, 0, 0] = cosine
    backward[:, 0, 1] = sine
    backward[:, 1, 1] = cosine
    backward[:, 1, 0] = -sine
    size = 2 * total
    return (
        split_terms(forward.reshape(size, size)),
        split_terms(backward.reshape(size, size) / total),
    )


def column_selector(group, blocks, per_block, shares):
    total = blocks * per_block
    share = total // shares
    table = np.zeros((group, 2, shares, 2, share, blocks, group, 2, per_block), np.float32)
    for k in range(group):
        for col in range(total):
            d, c = divmod(col, share)
            b, j = divmod(col, per_block)
            table[k, 0, d, 0, c, b, k, 0, j] = 1.0
            table[k, 0, d, 1, c, b, k, 1, j] = -1.0
            table[k, 1, d, 0, c, b, k, 1, j] = 1.0
            table[k, 1, d, 1, c, b, k, 0, j] = 1.0
    return table.reshape(group * 4 * total, blocks * group * 2 * per_block).astype(ml_dtypes.bfloat16)


def dot(left, right, dims=((1,), (0,))):
    return lax.dot_general(left, right, (dims, ((), ())), preferred_element_type=F32)


def spread(wide, start, stride, value):
    for t in range(wide.shape[0]):
        wide[t, pl.ds(start, value.shape[0], stride=stride), :] = value[:, t * LANES : (t + 1) * LANES]


def take(wide, start, size):
    return jnp.concatenate([wide[t, pl.ds(start, size), :] for t in range(wide.shape[0])], axis=1)


def tiled(rows, lanes):
    return pltpu.VMEM((lanes // LANES, rows, LANES), F32)


def call(kernel, out_shape, n_in, scratch=(), limit=24, flops=0, size=0, unread=0, result=pltpu.VMEM):
    whole = pl.BlockSpec(memory_space=pltpu.VMEM)
    return pl.pallas_call(
        kernel,
        out_shape=out_shape,
        in_specs=[whole] * n_in + [pl.BlockSpec(memory_space=pl.ANY)] * unread,
        out_specs=jax.tree.map(lambda _: pl.BlockSpec(memory_space=result), out_shape),
        scratch_shapes=list(scratch),
        compiler_params=pltpu.CompilerParams(vmem_limit_bytes=limit * MIB),
        cost_estimate=pl.CostEstimate(flops=flops, bytes_accessed=size, transcendentals=0),
    )


def load_copies(orb_hbm, orb_ref, sems, start):
    lanes = pl.ds(start, orb_ref.shape[3])
    copies = [
        pltpu.make_async_copy(orb_hbm.at[k, :, :, lanes], orb_ref.at[k], sems.at[k])
        for k in range(orb_ref.shape[0])
    ]
    for copy in copies:
        copy.start()
    return copies


def rest_kernel(orb_hbm, edge_hbm, pass_ref, orb_ref, sems, pass_sem):
    copies = load_copies(orb_hbm, orb_ref, sems, LANES)
    copies.append(pltpu.make_async_copy(edge_hbm, pass_ref, pass_sem))
    copies[-1].start()
    for copy in copies:
        copy.wait()


def edge_kernel(per_block, orb_hbm, edge_ref, orb_ref, sems):
    local_k = orb_hbm.shape[0]
    copies = load_copies(orb_hbm, orb_ref, sems, 0)
    row = lax.broadcasted_iota(jnp.int32, (2 * per_block, 2 * LANES), 0)
    lane = lax.broadcasted_iota(jnp.int32, (2 * per_block, 2 * LANES), 1)
    column = jnp.where(row < per_block, row, row - per_block + LANES)
    chosen = jnp.where(lane == column, jnp.ones(row.shape, F32), jnp.zeros(row.shape, F32)).astype(BF16)
    group = ROWS // (2 * per_block)
    for g in range(local_k // group):
        rows = []
        for k in range(g * group, (g + 1) * group):
            copies[k].wait()
            both = jnp.concatenate([orb_ref[k, 0], orb_ref[k, 1]], axis=1)
            rows.append(dot(chosen, both, ((1,), (1,))))
        edge_ref[g * ROWS : (g + 1) * ROWS] = jnp.concatenate(rows, axis=0).astype(BF16)


def asked(shares):
    return [2, 1, *range(3, shares)]


def plane_of(shares):
    return lax.div(lax.axis_index("pts"), lax.axis_size("pts") // shares)


def tile_kernel(shares, per_share, per_block, *refs):
    blocks, (orb_ref, rest_ref, sel_ref, coulomb_ref) = refs[: shares * per_share], refs[shares * per_share :][:4]
    *outs, form_ref, wide, cells = refs[shares * per_share + 4 :]
    local_k, _, norb, _ = orb_ref.shape
    group = ROWS // (2 * per_block)
    share = per_share * per_block
    rows = 2 * share
    me, block = lax.axis_index("ka"), lax.axis_index("pts")
    plane = plane_of(shares)
    selector = sel_ref[jnp.bitwise_and(block, per_share - 1)]
    order = [0, *asked(shares)]
    for g in range(local_k // group):
        stacked = jnp.concatenate(
            [
                blocks[order.index(offset) * per_share + e][g * ROWS : (g + 1) * ROWS]
                for offset in range(shares)
                for e in range(per_share)
            ],
            axis=0,
        )
        chosen = dot(selector, stacked).astype(BF16)
        size = 2 * group * rows
        forms = [chosen[offset * size : (offset + 1) * size] for offset in range(shares)]
        for kk in range(group):
            k = g * group + kk
            left = [form[2 * kk * rows : (2 * kk + 1) * rows] for form in forms]
            right = [form[(2 * kk + 1) * rows : (2 * kk + 2) * rows] for form in forms]
            form = jnp.concatenate(
                [jnp.concatenate(left, axis=0), jnp.concatenate(right, axis=0)], axis=1
            )
            halves = [ref[k].reshape(2 * norb, ref.shape[3]) for ref in (orb_ref, rest_ref)]
            tile = dot(form, jnp.concatenate(halves, axis=1))
            for offset in range(shares):
                form_ref[lax.rem(plane + shares - offset, shares), k] = form[offset * rows : (offset + 1) * rows]
                for part in range(2):
                    low = offset * rows + part * share
                    start = offset * share * 2 * local_k + 2 * k + part
                    spread(wide, start, 2 * local_k, tile[low : low + share])
    size = share * 2 * local_k
    cells[...] = coulomb_ref[...].astype(F32)
    for s in range(shares):
        owned = jnp.bitwise_xor(jnp.bitwise_xor(me, s), plane)
        offset = lax.rem(plane + shares - owned, shares)
        outs[s][:size] = take(wide, pl.multiple_of(offset * size, size), size).astype(BF16)
        start = pl.multiple_of(owned * share, share)
        pieces = [cells[r, pl.ds(start, share), :] for r in range(local_k)]
        outs[s][size:] = jnp.concatenate(pieces, axis=0).astype(BF16)


def transform_kernel(shares, total, share, *refs):
    tiles, (fwd_ref, bwd_ref) = refs[:shares][::-1], refs[shares : shares + 2]
    outs, (gathered, weight, wide) = refs[shares + 2 : 2 * shares + 2], refs[2 * shares + 2 :]
    local_k = total // shares
    size = 2 * local_k * share
    me = lax.axis_index("ka")
    for s in range(shares):
        src = jnp.bitwise_xor(me, s)
        gathered[src] = tiles[s][:size].astype(gathered.dtype)
        cells = tiles[s][size:].astype(F32)
        for r in range(local_k):
            spread(weight, src * local_k + r, total, cells[r * share : (r + 1) * share])
    rows = 2 * local_k
    columns = []
    for c in range(share):
        columns.append(
            jnp.concatenate([gathered[a, c * rows : (c + 1) * rows] for a in range(shares)], axis=0).astype(BF16)
        )
    values = jnp.concatenate(columns, axis=1)
    cells = dot(fwd_ref[...], jnp.concatenate([values, values], axis=0))
    scale = jnp.concatenate([take(weight, c * total, total) for c in range(share)], axis=1)
    cells = (cells * jnp.concatenate([scale, scale], axis=0)).astype(BF16)
    kernel = dot(bwd_ref[...], jnp.concatenate([cells, cells], axis=0))
    points = kernel.shape[1] // share
    for c in range(share):
        spread(wide, c, share, kernel[:, c * points : (c + 1) * points])
    for s in range(shares):
        dest = jnp.bitwise_xor(me, s)
        outs[s][...] = take(wide, pl.multiple_of(dest * size, size), size).astype(BF16)


def weight_operands(pieces, right_ref, gathered):
    shares = len(pieces)
    groups, lanes, depth = right_ref.shape
    me, plane = lax.axis_index("ka"), plane_of(shares)
    for s in range(shares):
        gathered[jnp.bitwise_xor(jnp.bitwise_xor(me, s), plane)] = pieces[s][...]
    group = depth // (2 * gathered.shape[2])
    half = gathered.shape[1] // (groups * group) // 2
    for g in range(groups):
        right = []
        for kk in range(group):
            k = g * group + kk
            first, second = [], []
            for a in range(shares):
                piece = gathered[a, k * 2 * half : (k + 1) * 2 * half].astype(F32)
                first.append(piece)
                second.extend([piece[half:], -piece[:half]])
            first = jnp.concatenate(first, axis=0).astype(BF16)
            second = jnp.concatenate(second, axis=0).astype(BF16)
            parts = [jnp.zeros_like(first)] * (2 * group)
            parts[2 * kk], parts[2 * kk + 1] = first, second
            right.append(jnp.concatenate(parts, axis=1))
        right_ref[g] = jnp.concatenate(right, axis=0)


def weight_rows(offsets, flip, out_rows, right_ref, orb_ref, rest_ref, out_ref):
    groups, lanes, _ = right_ref.shape
    local_k, _, norb, _ = orb_ref.shape
    group = local_k // groups
    block = lax.axis_index("pts")
    core = jnp.bitwise_xor(jnp.bitwise_and(block, 1), flip)
    z = lax.shift_right_logical(block, 1)
    chunks = norb // out_rows // 2
    for g in range(groups):
        rows = []
        for offset in offsets:
            start = pl.multiple_of((2 * lax.rem(z + offset, chunks) + core) * out_rows, out_rows)
            parts = [
                ref[k, part, pl.ds(start, out_rows), :]
                for k in range(g * group, (g + 1) * group)
                for part in range(2)
                for ref in (orb_ref, rest_ref)
            ]
            rows.append(jnp.concatenate(parts, axis=1))
        result = dot(jnp.concatenate(rows, axis=0), right_ref[g], ((1,), (1,))).astype(out_ref.dtype)
        for i in range(len(offsets)):
            out_ref[i, :, g * lanes : (g + 1) * lanes] = result[i * out_rows : (i + 1) * out_rows]


def first_weight_kernel(shares, offsets, out_rows, *refs):
    pieces, (orb_ref, rest_ref, out_ref, right_ref, gathered) = refs[:shares][::-1], refs[shares:]
    weight_operands(pieces, right_ref, gathered)
    weight_rows(offsets, 1, out_rows, right_ref, orb_ref, rest_ref, out_ref)


def next_weight_kernel(offsets, flip, out_rows, right_ref, orb_ref, rest_ref, *refs):
    weight_rows(offsets, flip, out_rows, right_ref, orb_ref, rest_ref, refs[-1])


def pair_kernel(many, keep_ref, came_ref, *refs):
    for i, out_ref in enumerate(refs[-many:]):
        out_ref[...] = (keep_ref[i] + came_ref[i].astype(F32)).astype(out_ref.dtype)


def exchange_kernel(chunks, scale, *refs):
    pieces, (form_ref, out_hbm, wide, out_ref, sems) = refs[:chunks][::-1], refs[chunks:]
    shares, local_k, part_lanes, twice = form_ref.shape
    lanes = shares * part_lanes
    norb = twice // 2
    spans = norb // LANES
    out_rows = pieces[0].shape[0]
    total = pieces[0][...]
    for s in range(1, chunks):
        total = total + pieces[s][...].astype(F32)
    total = total * scale
    high = total.astype(BF16)
    low = (total - high.astype(F32)).astype(BF16)
    group = max(1, LANES // lanes)
    width = group * lanes
    lane = lax.broadcasted_iota(jnp.int32, (out_rows, width), 1)
    zero = jnp.zeros((out_rows, width), BF16)
    copies = []
    for g in range(local_k // group):
        high_g = high[:, g * width : (g + 1) * width]
        low_g = low[:, g * width : (g + 1) * width]
        left = []
        for kk in range(group):
            keep = (lane >= kk * lanes) & (lane < (kk + 1) * lanes)
            left.append(
                jnp.concatenate([jnp.where(keep, high_g, zero), jnp.where(keep, low_g, zero)], axis=1)
            )
        forms = [form_ref[d, g * group + kk] for kk in range(group) for d in range(shares)]
        result = dot(jnp.concatenate(left, axis=0), jnp.concatenate(forms + forms, axis=0))
        for kk in range(group):
            for part in range(2):
                for t in range(spans):
                    lane_start = part * norb + t * LANES
                    value = result[kk * out_rows : (kk + 1) * out_rows, lane_start : lane_start + LANES]
                    start = (kk * spans + t) * 2 + part
                    wide[g, pl.ds(start, out_rows, stride=2 * spans * group), :] = value
        out_ref[g] = wide[g].astype(BF16).reshape(out_ref.shape[1:])
        copies.append(pltpu.make_async_copy(out_ref.at[g], out_hbm.at[:, g], sems.at[g]))
        copies[-1].start()
    for copy in copies:
        copy.wait()


def swap(value, axis, mask):
    size = lax.axis_size(axis)
    return lax.ppermute(value, axis, [(i, i ^ mask) for i in range(size)])


def trade(pieces, axis, step):
    return [swap(pieces[s], axis, s * step) for s in reversed(range(1, len(pieces)))] + [pieces[0]]


def shift_along(pieces):
    chunks = len(pieces)
    came = []
    for s in range(1, chunks):
        pairs = [(2 * z + core, 2 * ((z - s) % chunks) + core) for z in range(chunks) for core in range(2)]
        came.append(lax.ppermute(pieces[s], "pts", pairs))
    return came[::-1] + [pieces[0]]


def body(orbitals, coulomb):
    shares, blocks = lax.axis_size("ka"), lax.axis_size("pts")
    local_k, _, norb, points = orbitals.shape
    columns = coulomb.shape[1]
    per_block = columns // blocks
    share = columns // shares
    total = local_k * shares
    out_rows = norb // blocks
    chunks = blocks // 2
    group = ROWS // (2 * per_block)
    shape = jax.ShapeDtypeStruct

    edge, first = call(
        functools.partial(edge_kernel, per_block),
        [
            shape((local_k * 2 * per_block, norb), BF16),
            shape((local_k, 2, norb, LANES), BF16),
        ],
        0,
        [pltpu.SemaphoreType.DMA((local_k,))],
        limit=50,
        size=4 * MIB,
        unread=1,
    )(orbitals)
    passed_edge, rest = call(
        rest_kernel,
        [shape(edge.shape, BF16), shape((local_k, 2, norb, points - LANES), BF16)],
        0,
        [pltpu.SemaphoreType.DMA((local_k,)), pltpu.SemaphoreType.DMA],
        limit=49,
        size=4 * MIB,
        unread=2,
    )(orbitals, edge)
    per_share = blocks // shares
    partner = swap(passed_edge, "pts", 1)
    came = [edge, partner] + [swap(edge, "pts", 2 * e + c) for e in range(1, per_share // 2) for c in range(2)]
    came = {0: came}
    for offset in asked(shares):
        came[offset] = []
        for e in range(per_share // 2):
            pairs = [(i, (i + offset * per_share) % blocks ^ (2 * e)) for i in range(blocks)]
            block = lax.ppermute(edge, "pts", pairs)
            came[offset] += [block, swap(block, "pts", 1)]
    table = column_selector(group, per_share, per_block, 1).reshape(-1, per_share, ROWS)
    places = [[place ^ e for e in range(per_share)] for place in range(per_share)]
    tables = [table[:, place].reshape(table.shape[0], -1).astype(np.float32) for place in places]
    selector = jnp.asarray(np.stack([np.kron(np.eye(shares, dtype=np.float32), t) for t in tables]), BF16)
    piece = shape((share * 2 * local_k, points), BF16)
    both = shape((share * 3 * local_k, points), BF16)
    *tiles, forms = call(
        functools.partial(tile_kernel, shares, per_share, per_block),
        [both] * shares + [shape((shares, local_k, 2 * share, 2 * norb), BF16)],
        blocks + 4,
        [
            tiled(shares * share * 2 * local_k, points),
            pltpu.VMEM(coulomb.shape, F32),
        ],
        size=6 * MIB,
    )(*[block for offset in [0, *asked(shares)] for block in came[offset]], first, rest, selector, coulomb)
    tiles = trade(tiles, "ka", 1)

    forward, backward = phase_tables(total)
    kernels = call(
        functools.partial(transform_kernel, shares, total, share),
        [piece] * shares,
        shares + 2,
        [
            pltpu.VMEM((shares, share * 2 * local_k, points), BF16 if local_k % 8 == 0 else F32),
            tiled(share * total, points),
            tiled(2 * total * share, points),
        ],
        size=2 * MIB,
    )(*tiles, jnp.asarray(forward), jnp.asarray(backward))
    kernels = trade(kernels, "ka", 1)

    lanes = local_k * 2 * columns
    pair = max(1, LANES // (2 * columns))
    early, late = list(reversed(range(1, chunks))), [0]
    sent, right = call(
        functools.partial(first_weight_kernel, shares, early, out_rows),
        [
            shape((len(early), out_rows, lanes), BF16),
            shape((local_k // pair, pair * 2 * columns, pair * 2 * points), BF16),
        ],
        shares + 2,
        [pltpu.VMEM((shares, share * 2 * local_k, points), BF16)],
    )(*kernels, first, rest)

    def rows_of(offsets, flip, kind, before):
        return call(
            functools.partial(next_weight_kernel, offsets, flip, out_rows),
            shape((len(offsets), out_rows, lanes), kind),
            3,
            unread=1,
        )(right, first, rest, before)

    def summed(offsets, keep, came, *before):
        kinds = [shape((out_rows, lanes), BF16 if offset else F32) for offset in offsets]
        kernel = functools.partial(pair_kernel, len(offsets))
        return call(kernel, kinds, 2, unread=len(before))(keep, came, *before)

    kept = rows_of(early, 0, F32, sent)
    sent_late = rows_of(late, 1, BF16, kept)
    kept_late = rows_of(late, 0, F32, sent_late)
    early_sums = summed(early, kept, swap(sent, "pts", 1), kept_late)
    late_sums = summed(late, kept_late, swap(sent_late, "pts", 1))
    sums = [*late_sums, *early_sums]
    sums = shift_along(sums)
    spans = norb // LANES
    rows = pair * spans * 2
    result = call(
        functools.partial(exchange_kernel, chunks, 1.0 / math.sqrt(points * blocks)),
        shape((out_rows, local_k // pair, rows, LANES), BF16),
        chunks + 1,
        [
            pltpu.VMEM((local_k // pair, out_rows * rows, LANES), F32),
            pltpu.VMEM((local_k // pair, out_rows, rows, LANES), BF16),
            pltpu.SemaphoreType.DMA((local_k // pair,)),
        ],
        size=4 * MIB,
        result=pltpu.HBM,
    )(*sums, forms)
    result = result.reshape(out_rows, local_k, spans, 2, LANES)
    return result.transpose(0, 1, 3, 2, 4).reshape(out_rows, local_k, 2, norb)


def solution(mesh):
    in_specs = (P("ka", None, None, "pts"), P("ka", None, "pts"))
    out_specs = P("pts", "ka", None, None)
    return jax.shard_map(body, mesh=mesh, in_specs=in_specs, out_specs=out_specs, check_vma=False)
```

```python
import functools
import math

import jax
import jax.numpy as jnp
import ml_dtypes
import numpy as np
from jax import lax
from jax.experimental import pallas as pl
from jax.experimental.pallas import tpu as pltpu
from jax.sharding import PartitionSpec as P

BF16 = jnp.bfloat16
F32 = jnp.float32
LANES = 128
ROWS = 16
MIB = 1 << 20


def split_terms(table):
    high = table.astype(ml_dtypes.bfloat16)
    low = (table - high.astype(np.float64)).astype(ml_dtypes.bfloat16)
    return np.concatenate([high, low], axis=1)


def phase_tables(total):
    index = np.arange(total)
    angles = (index[:, None] * index[None, :] % total) * (2.0 * math.pi / total)
    cosine, sine = np.cos(angles), np.sin(angles)
    forward = np.zeros((2, total, total, 2))
    forward[0, :, :, 0] = cosine
    forward[0, :, :, 1] = -sine
    forward[1, :, :, 0] = sine
    forward[1, :, :, 1] = cosine
    backward = np.zeros((total, 2, 2, total))
    backward[:, 0, 0] = cosine
    backward[:, 0, 1] = sine
    backward[:, 1, 1] = cosine
    backward[:, 1, 0] = -sine
    size = 2 * total
    return (
        split_terms(forward.reshape(size, size)),
        split_terms(backward.reshape(size, size) / total),
    )


def column_selector(group, blocks, per_block, shares):
    total = blocks * per_block
    share = total // shares
    table = np.zeros((group, 2, shares, 2, share, blocks, group, 2, per_block), np.float32)
    for k in range(group):
        for col in range(total):
            d, c = divmod(col, share)
            b, j = divmod(col, per_block)
            table[k, 0, d, 0, c, b, k, 0, j] = 1.0
            table[k, 0, d, 1, c, b, k, 1, j] = -1.0
            table[k, 1, d, 0, c, b, k, 1, j] = 1.0
            table[k, 1, d, 1, c, b, k, 0, j] = 1.0
    return table.reshape(group * 4 * total, blocks * group * 2 * per_block).astype(ml_dtypes.bfloat16)


def dot(left, right, dims=((1,), (0,))):
    return lax.dot_general(left, right, (dims, ((), ())), preferred_element_type=F32)


def spread(wide, start, stride, value):
    for t in range(wide.shape[0]):
        wide[t, pl.ds(start, value.shape[0], stride=stride), :] = value[:, t * LANES : (t + 1) * LANES]


def take(wide, start, size):
    return jnp.concatenate([wide[t, pl.ds(start, size), :] for t in range(wide.shape[0])], axis=1)


def tiled(rows, lanes):
    return pltpu.VMEM((lanes // LANES, rows, LANES), F32)


def call(kernel, out_shape, n_in, scratch=(), limit=24, flops=0, size=0, unread=0, result=pltpu.VMEM):
    whole = pl.BlockSpec(memory_space=pltpu.VMEM)
    return pl.pallas_call(
        kernel,
        out_shape=out_shape,
        in_specs=[whole] * n_in + [pl.BlockSpec(memory_space=pl.ANY)] * unread,
        out_specs=jax.tree.map(lambda _: pl.BlockSpec(memory_space=result), out_shape),
        scratch_shapes=list(scratch),
        compiler_params=pltpu.CompilerParams(vmem_limit_bytes=limit * MIB),
        cost_estimate=pl.CostEstimate(flops=flops, bytes_accessed=size, transcendentals=0),
    )


def load_copies(orb_hbm, orb_ref, sems, start):
    lanes = pl.ds(start, orb_ref.shape[3])
    copies = [
        pltpu.make_async_copy(orb_hbm.at[k, :, :, lanes], orb_ref.at[k], sems.at[k])
        for k in range(orb_ref.shape[0])
    ]
    for copy in copies:
        copy.start()
    return copies


def rest_kernel(orb_hbm, edge_hbm, pass_ref, orb_ref, sems, pass_sem):
    copies = load_copies(orb_hbm, orb_ref, sems, LANES)
    copies.append(pltpu.make_async_copy(edge_hbm, pass_ref, pass_sem))
    copies[-1].start()
    for copy in copies:
        copy.wait()


def edge_kernel(per_block, orb_hbm, edge_ref, orb_ref, sems):
    local_k = orb_hbm.shape[0]
    copies = load_copies(orb_hbm, orb_ref, sems, 0)
    row = lax.broadcasted_iota(jnp.int32, (2 * per_block, 2 * LANES), 0)
    lane = lax.broadcasted_iota(jnp.int32, (2 * per_block, 2 * LANES), 1)
    column = jnp.where(row < per_block, row, row - per_block + LANES)
    chosen = jnp.where(lane == column, jnp.ones(row.shape, F32), jnp.zeros(row.shape, F32)).astype(BF16)
    group = ROWS // (2 * per_block)
    for g in range(local_k // group):
        rows = []
        for k in range(g * group, (g + 1) * group):
            copies[k].wait()
            both = jnp.concatenate([orb_ref[k, 0], orb_ref[k, 1]], axis=1)
            rows.append(dot(chosen, both, ((1,), (1,))))
        edge_ref[g * ROWS : (g + 1) * ROWS] = jnp.concatenate(rows, axis=0).astype(BF16)


def asked(shares):
    return [2, 1, *range(3, shares)]


def plane_of(shares):
    return lax.div(lax.axis_index("pts"), lax.axis_size("pts") // shares)


def tile_kernel(shares, per_share, per_block, *refs):
    blocks, (orb_ref, rest_ref, sel_ref, coulomb_ref) = refs[: shares * per_share], refs[shares * per_share :][:4]
    *outs, form_ref, wide, cells = refs[shares * per_share + 4 :]
    local_k, _, norb, _ = orb_ref.shape
    group = ROWS // (2 * per_block)
    share = per_share * per_block
    rows = 2 * share
    me, block = lax.axis_index("ka"), lax.axis_index("pts")
    plane = plane_of(shares)
    selector = sel_ref[jnp.bitwise_and(block, per_share - 1)]
    order = [0, *asked(shares)]
    for g in range(local_k // group):
        stacked = jnp.concatenate(
            [
                blocks[order.index(offset) * per_share + e][g * ROWS : (g + 1) * ROWS]
                for offset in range(shares)
                for e in range(per_share)
            ],
            axis=0,
        )
        chosen = dot(selector, stacked).astype(BF16)
        size = 2 * group * rows
        forms = [chosen[offset * size : (offset + 1) * size] for offset in range(shares)]
        for kk in range(group):
            k = g * group + kk
            left = [form[2 * kk * rows : (2 * kk + 1) * rows] for form in forms]
            right = [form[(2 * kk + 1) * rows : (2 * kk + 2) * rows] for form in forms]
            form = jnp.concatenate(
                [jnp.concatenate(left, axis=0), jnp.concatenate(right, axis=0)], axis=1
            )
            halves = [ref[k].reshape(2 * norb, ref.shape[3]) for ref in (orb_ref, rest_ref)]
            tile = dot(form, jnp.concatenate(halves, axis=1))
            for offset in range(shares):
                form_ref[jnp.bitwise_xor(plane, offset), k] = form[offset * rows : (offset + 1) * rows]
                for part in range(2):
                    low = offset * rows + part * share
                    start = offset * share * 2 * local_k + 2 * k + part
                    spread(wide, start, 2 * local_k, tile[low : low + share])
    size = share * 2 * local_k
    cells[...] = coulomb_ref[...].astype(F32)
    for s in range(shares):
        offset = jnp.bitwise_xor(me, s)
        outs[s][:size] = take(wide, pl.multiple_of(offset * size, size), size).astype(BF16)
        start = pl.multiple_of(jnp.bitwise_xor(offset, plane) * share, share)
        pieces = [cells[r, pl.ds(start, share), :] for r in range(local_k)]
        outs[s][size:] = jnp.concatenate(pieces, axis=0).astype(BF16)


def transform_kernel(shares, total, share, *refs):
    tiles, (fwd_ref, bwd_ref) = refs[:shares][::-1], refs[shares : shares + 2]
    outs, (gathered, weight, wide) = refs[shares + 2 : 2 * shares + 2], refs[2 * shares + 2 :]
    local_k = total // shares
    size = 2 * local_k * share
    me = lax.axis_index("ka")
    for s in range(shares):
        src = jnp.bitwise_xor(me, s)
        gathered[src] = tiles[s][:size].astype(gathered.dtype)
        cells = tiles[s][size:].astype(F32)
        for r in range(local_k):
            spread(weight, src * local_k + r, total, cells[r * share : (r + 1) * share])
    rows = 2 * local_k
    columns = []
    for c in range(share):
        columns.append(
            jnp.concatenate([gathered[a, c * rows : (c + 1) * rows] for a in range(shares)], axis=0).astype(BF16)
        )
    values = jnp.concatenate(columns, axis=1)
    cells = dot(fwd_ref[...], jnp.concatenate([values, values], axis=0))
    scale = jnp.concatenate([take(weight, c * total, total) for c in range(share)], axis=1)
    cells = (cells * jnp.concatenate([scale, scale], axis=0)).astype(BF16)
    kernel = dot(bwd_ref[...], jnp.concatenate([cells, cells], axis=0))
    points = kernel.shape[1] // share
    for c in range(share):
        spread(wide, c, share, kernel[:, c * points : (c + 1) * points])
    for s in range(shares):
        dest = jnp.bitwise_xor(me, s)
        outs[s][...] = take(wide, pl.multiple_of(dest * size, size), size).astype(BF16)


def weight_operands(pieces, right_ref, gathered):
    shares = len(pieces)
    groups, lanes, depth = right_ref.shape
    me, plane = lax.axis_index("ka"), plane_of(shares)
    for s in range(shares):
        gathered[jnp.bitwise_xor(jnp.bitwise_xor(me, s), plane)] = pieces[s][...]
    group = depth // (2 * gathered.shape[2])
    half = gathered.shape[1] // (groups * group) // 2
    for g in range(groups):
        right = []
        for kk in range(group):
            k = g * group + kk
            first, second = [], []
            for a in range(shares):
                piece = gathered[a, k * 2 * half : (k + 1) * 2 * half].astype(F32)
                first.append(piece)
                second.extend([piece[half:], -piece[:half]])
            first = jnp.concatenate(first, axis=0).astype(BF16)
            second = jnp.concatenate(second, axis=0).astype(BF16)
            parts = [jnp.zeros_like(first)] * (2 * group)
            parts[2 * kk], parts[2 * kk + 1] = first, second
            right.append(jnp.concatenate(parts, axis=1))
        right_ref[g] = jnp.concatenate(right, axis=0)


def weight_rows(offsets, flip, out_rows, right_ref, orb_ref, rest_ref, out_ref):
    groups, lanes, _ = right_ref.shape
    local_k, _, norb, _ = orb_ref.shape
    group = local_k // groups
    block = lax.axis_index("pts")
    core = jnp.bitwise_xor(jnp.bitwise_and(block, 1), flip)
    z = lax.shift_right_logical(block, 1)
    chunks = norb // out_rows // 2
    for g in range(groups):
        rows = []
        for offset in offsets:
            start = pl.multiple_of((2 * lax.rem(z + offset, chunks) + core) * out_rows, out_rows)
            parts = [
                ref[k, part, pl.ds(start, out_rows), :]
                for k in range(g * group, (g + 1) * group)
                for part in range(2)
                for ref in (orb_ref, rest_ref)
            ]
            rows.append(jnp.concatenate(parts, axis=1))
        result = dot(jnp.concatenate(rows, axis=0), right_ref[g], ((1,), (1,))).astype(out_ref.dtype)
        for i in range(len(offsets)):
            out_ref[i, :, g * lanes : (g + 1) * lanes] = result[i * out_rows : (i + 1) * out_rows]


def first_weight_kernel(shares, offsets, out_rows, *refs):
    pieces, (orb_ref, rest_ref, out_ref, right_ref, gathered) = refs[:shares][::-1], refs[shares:]
    weight_operands(pieces, right_ref, gathered)
    weight_rows(offsets, 1, out_rows, right_ref, orb_ref, rest_ref, out_ref)


def next_weight_kernel(offsets, flip, out_rows, right_ref, orb_ref, rest_ref, *refs):
    weight_rows(offsets, flip, out_rows, right_ref, orb_ref, rest_ref, refs[-1])


def pair_kernel(keep_ref, came_ref, *outs):
    for i, out_ref in enumerate(outs):
        out_ref[...] = (keep_ref[i] + came_ref[i].astype(F32)).astype(out_ref.dtype)


def exchange_kernel(chunks, scale, *refs):
    pieces, (form_ref, out_hbm, wide, out_ref, sems) = refs[:chunks][::-1], refs[chunks:]
    shares, local_k, part_lanes, twice = form_ref.shape
    lanes = shares * part_lanes
    norb = twice // 2
    spans = norb // LANES
    out_rows = pieces[0].shape[0]
    total = pieces[0][...]
    for s in range(1, chunks):
        total = total + pieces[s][...].astype(F32)
    total = total * scale
    high = total.astype(BF16)
    low = (total - high.astype(F32)).astype(BF16)
    group = max(1, LANES // lanes)
    width = group * lanes
    lane = lax.broadcasted_iota(jnp.int32, (out_rows, width), 1)
    zero = jnp.zeros((out_rows, width), BF16)
    copies = []
    for g in range(local_k // group):
        high_g = high[:, g * width : (g + 1) * width]
        low_g = low[:, g * width : (g + 1) * width]
        left = []
        for kk in range(group):
            keep = (lane >= kk * lanes) & (lane < (kk + 1) * lanes)
            left.append(
                jnp.concatenate([jnp.where(keep, high_g, zero), jnp.where(keep, low_g, zero)], axis=1)
            )
        forms = [form_ref[d, g * group + kk] for kk in range(group) for d in range(shares)]
        result = dot(jnp.concatenate(left, axis=0), jnp.concatenate(forms + forms, axis=0))
        for kk in range(group):
            for part in range(2):
                for t in range(spans):
                    lane_start = part * norb + t * LANES
                    value = result[kk * out_rows : (kk + 1) * out_rows, lane_start : lane_start + LANES]
                    start = (kk * spans + t) * 2 + part
                    wide[g, pl.ds(start, out_rows, stride=2 * spans * group), :] = value
        out_ref[g] = wide[g].astype(BF16).reshape(out_ref.shape[1:])
        copies.append(pltpu.make_async_copy(out_ref.at[g], out_hbm.at[:, g], sems.at[g]))
        copies[-1].start()
    for copy in copies:
        copy.wait()


def swap(value, axis, mask):
    size = lax.axis_size(axis)
    return lax.ppermute(value, axis, [(i, i ^ mask) for i in range(size)])


def trade(pieces, axis, step):
    return [swap(pieces[s], axis, s * step) for s in reversed(range(1, len(pieces)))] + [pieces[0]]


def shift_along(pieces):
    chunks = len(pieces)
    inner = range(chunks // 4, chunks - chunks // 4)
    came = []
    for s in range(1, chunks):
        sources = [range(chunks)]
        if 2 * s == chunks:
            sources = [inner, [z for z in range(chunks) if z not in inner]]
        for chosen in sources:
            pairs = [(2 * z + core, 2 * ((z - s) % chunks) + core) for z in chosen for core in range(2)]
            came.append(lax.ppermute(pieces[s], "pts", pairs))
    return came[::-1] + [pieces[0]]


def body(orbitals, coulomb):
    shares, blocks = lax.axis_size("ka"), lax.axis_size("pts")
    local_k, _, norb, points = orbitals.shape
    columns = coulomb.shape[1]
    per_block = columns // blocks
    share = columns // shares
    total = local_k * shares
    out_rows = norb // blocks
    chunks = blocks // 2
    group = ROWS // (2 * per_block)
    shape = jax.ShapeDtypeStruct

    edge, first = call(
        functools.partial(edge_kernel, per_block),
        [
            shape((local_k * 2 * per_block, norb), BF16),
            shape((local_k, 2, norb, LANES), BF16),
        ],
        0,
        [pltpu.SemaphoreType.DMA((local_k,))],
        limit=50,
        size=4 * MIB,
        unread=1,
    )(orbitals)
    passed_edge, rest = call(
        rest_kernel,
        [shape(edge.shape, BF16), shape((local_k, 2, norb, points - LANES), BF16)],
        0,
        [pltpu.SemaphoreType.DMA((local_k,)), pltpu.SemaphoreType.DMA],
        limit=49,
        size=4 * MIB,
        unread=2,
    )(orbitals, edge)
    per_share = blocks // shares
    partner = swap(passed_edge, "pts", 1)
    came = [edge, partner] + [swap(edge, "pts", 2 * e + c) for e in range(1, per_share // 2) for c in range(2)]
    came = {0: came}
    for offset in asked(shares):
        came[offset] = []
        for e in range(per_share // 2):
            block = swap(edge, "pts", offset * per_share + 2 * e)
            came[offset] += [block, swap(block, "pts", 1)]
    table = column_selector(group, per_share, per_block, 1).reshape(-1, per_share, ROWS)
    places = [[place ^ e for e in range(per_share)] for place in range(per_share)]
    tables = [table[:, place].reshape(table.shape[0], -1).astype(np.float32) for place in places]
    selector = jnp.asarray(np.stack([np.kron(np.eye(shares, dtype=np.float32), t) for t in tables]), BF16)
    piece = shape((share * 2 * local_k, points), BF16)
    both = shape((share * 3 * local_k, points), BF16)
    *tiles, forms = call(
        functools.partial(tile_kernel, shares, per_share, per_block),
        [both] * shares + [shape((shares, local_k, 2 * share, 2 * norb), BF16)],
        blocks + 4,
        [
            tiled(shares * share * 2 * local_k, points),
            pltpu.VMEM(coulomb.shape, F32),
        ],
        size=6 * MIB,
    )(*[block for offset in [0, *asked(shares)] for block in came[offset]], first, rest, selector, coulomb)
    tiles = trade(tiles, "ka", 1)

    forward, backward = phase_tables(total)
    kernels = call(
        functools.partial(transform_kernel, shares, total, share),
        [piece] * shares,
        shares + 2,
        [
            pltpu.VMEM((shares, share * 2 * local_k, points), BF16 if local_k % 8 == 0 else F32),
            tiled(share * total, points),
            tiled(2 * total * share, points),
        ],
        size=2 * MIB,
    )(*tiles, jnp.asarray(forward), jnp.asarray(backward))
    kernels = trade(kernels, "ka", 1)

    lanes = local_k * 2 * columns
    pair = max(1, LANES // (2 * columns))
    early, late = list(reversed(range(1, chunks))), [0]
    sent, right = call(
        functools.partial(first_weight_kernel, shares, early, out_rows),
        [
            shape((len(early), out_rows, lanes), BF16),
            shape((local_k // pair, pair * 2 * columns, pair * 2 * points), BF16),
        ],
        shares + 2,
        [pltpu.VMEM((shares, share * 2 * local_k, points), BF16)],
    )(*kernels, first, rest)

    def rows_of(offsets, flip, kind, before):
        return call(
            functools.partial(next_weight_kernel, offsets, flip, out_rows),
            shape((len(offsets), out_rows, lanes), kind),
            3,
            unread=1,
        )(right, first, rest, before)

    def summed(offsets, keep, came):
        kinds = [shape((out_rows, lanes), BF16 if offset else F32) for offset in offsets]
        return call(pair_kernel, kinds, 2)(keep, came)

    sent_late = rows_of(late, 1, BF16, sent)
    early_sums = summed(early, rows_of(early, 0, F32, sent_late), swap(sent, "pts", 1))
    late_sums = summed(late, rows_of(late, 0, F32, early_sums[0]), swap(sent_late, "pts", 1))
    sums = [*late_sums, *early_sums]
    sums = shift_along(sums)
    spans = norb // LANES
    rows = pair * spans * 2
    result = call(
        functools.partial(exchange_kernel, len(sums), 1.0 / math.sqrt(points * blocks)),
        shape((out_rows, local_k // pair, rows, LANES), BF16),
        len(sums) + 1,
        [
            pltpu.VMEM((local_k // pair, out_rows * rows, LANES), F32),
            pltpu.VMEM((local_k // pair, out_rows, rows, LANES), BF16),
            pltpu.SemaphoreType.DMA((local_k // pair,)),
        ],
        size=4 * MIB,
        result=pltpu.HBM,
    )(*sums, forms)
    result = result.reshape(out_rows, local_k, spans, 2, LANES)
    return result.transpose(0, 1, 3, 2, 4).reshape(out_rows, local_k, 2, norb)


def solution(mesh):
    in_specs = (P("ka", None, None, "pts"), P("ka", None, "pts"))
    out_specs = P("pts", "ka", None, None)
    return jax.shard_map(body, mesh=mesh, in_specs=in_specs, out_specs=out_specs, check_vma=False)
```

```python
import functools
import math

import jax
import jax.numpy as jnp
import ml_dtypes
import numpy as np
from jax import lax
from jax.experimental import pallas as pl
from jax.experimental.pallas import tpu as pltpu
from jax.sharding import PartitionSpec as P

BF16 = jnp.bfloat16
F32 = jnp.float32
LANES = 128
ROWS = 16
MIB = 1 << 20


def split_terms(table):
    high = table.astype(ml_dtypes.bfloat16)
    low = (table - high.astype(np.float64)).astype(ml_dtypes.bfloat16)
    return np.concatenate([high, low], axis=1)


def phase_tables(total):
    index = np.arange(total)
    angles = (index[:, None] * index[None, :] % total) * (2.0 * math.pi / total)
    cosine, sine = np.cos(angles), np.sin(angles)
    forward = np.zeros((2, total, total, 2))
    forward[0, :, :, 0] = cosine
    forward[0, :, :, 1] = -sine
    forward[1, :, :, 0] = sine
    forward[1, :, :, 1] = cosine
    backward = np.zeros((total, 2, 2, total))
    backward[:, 0, 0] = cosine
    backward[:, 0, 1] = sine
    backward[:, 1, 1] = cosine
    backward[:, 1, 0] = -sine
    size = 2 * total
    return (
        split_terms(forward.reshape(size, size)),
        split_terms(backward.reshape(size, size) / total),
    )


def column_selector(group, blocks, per_block, shares):
    total = blocks * per_block
    share = total // shares
    table = np.zeros((group, 2, shares, 2, share, blocks, group, 2, per_block), np.float32)
    for k in range(group):
        for col in range(total):
            d, c = divmod(col, share)
            b, j = divmod(col, per_block)
            table[k, 0, d, 0, c, b, k, 0, j] = 1.0
            table[k, 0, d, 1, c, b, k, 1, j] = -1.0
            table[k, 1, d, 0, c, b, k, 1, j] = 1.0
            table[k, 1, d, 1, c, b, k, 0, j] = 1.0
    return table.reshape(group * 4 * total, blocks * group * 2 * per_block).astype(ml_dtypes.bfloat16)


def dot(left, right, dims=((1,), (0,))):
    return lax.dot_general(left, right, (dims, ((), ())), preferred_element_type=F32)


def spread(wide, start, stride, value):
    for t in range(wide.shape[0]):
        wide[t, pl.ds(start, value.shape[0], stride=stride), :] = value[:, t * LANES : (t + 1) * LANES]


def take(wide, start, size):
    return jnp.concatenate([wide[t, pl.ds(start, size), :] for t in range(wide.shape[0])], axis=1)


def tiled(rows, lanes):
    return pltpu.VMEM((lanes // LANES, rows, LANES), F32)


def call(kernel, out_shape, n_in, scratch=(), limit=24, flops=0, size=0, unread=0, result=pltpu.VMEM):
    whole = pl.BlockSpec(memory_space=pltpu.VMEM)
    return pl.pallas_call(
        kernel,
        out_shape=out_shape,
        in_specs=[whole] * n_in + [pl.BlockSpec(memory_space=pl.ANY)] * unread,
        out_specs=jax.tree.map(lambda _: pl.BlockSpec(memory_space=result), out_shape),
        scratch_shapes=list(scratch),
        compiler_params=pltpu.CompilerParams(vmem_limit_bytes=limit * MIB),
        cost_estimate=pl.CostEstimate(flops=flops, bytes_accessed=size, transcendentals=0),
    )


def load_copies(orb_hbm, orb_ref, sems, start):
    lanes = pl.ds(start, orb_ref.shape[3])
    copies = [
        pltpu.make_async_copy(orb_hbm.at[k, :, :, lanes], orb_ref.at[k], sems.at[k])
        for k in range(orb_ref.shape[0])
    ]
    for copy in copies:
        copy.start()
    return copies


def rest_kernel(orb_hbm, edge_hbm, pass_ref, orb_ref, sems, pass_sem):
    copies = load_copies(orb_hbm, orb_ref, sems, LANES)
    copies.append(pltpu.make_async_copy(edge_hbm, pass_ref, pass_sem))
    copies[-1].start()
    for copy in copies:
        copy.wait()


def edge_kernel(per_block, orb_hbm, edge_ref, orb_ref, sems):
    local_k = orb_hbm.shape[0]
    copies = load_copies(orb_hbm, orb_ref, sems, 0)
    row = lax.broadcasted_iota(jnp.int32, (2 * per_block, 2 * LANES), 0)
    lane = lax.broadcasted_iota(jnp.int32, (2 * per_block, 2 * LANES), 1)
    column = jnp.where(row < per_block, row, row - per_block + LANES)
    chosen = jnp.where(lane == column, jnp.ones(row.shape, F32), jnp.zeros(row.shape, F32)).astype(BF16)
    group = ROWS // (2 * per_block)
    for g in range(local_k // group):
        rows = []
        for k in range(g * group, (g + 1) * group):
            copies[k].wait()
            both = jnp.concatenate([orb_ref[k, 0], orb_ref[k, 1]], axis=1)
            rows.append(dot(chosen, both, ((1,), (1,))))
        edge_ref[g * ROWS : (g + 1) * ROWS] = jnp.concatenate(rows, axis=0).astype(BF16)


def asked(shares):
    return [2, 1, *range(3, shares)]


def plane_of(shares):
    return lax.div(lax.axis_index("pts"), lax.axis_size("pts") // shares)


def tile_kernel(shares, per_share, per_block, *refs):
    blocks, (orb_ref, rest_ref, sel_ref, coulomb_ref) = refs[: shares * per_share], refs[shares * per_share :][:4]
    *outs, form_ref, wide, cells = refs[shares * per_share + 4 :]
    local_k, _, norb, _ = orb_ref.shape
    group = ROWS // (2 * per_block)
    share = per_share * per_block
    rows = 2 * share
    me, block = lax.axis_index("ka"), lax.axis_index("pts")
    plane = plane_of(shares)
    selector = sel_ref[jnp.bitwise_and(block, per_share - 1)]
    order = [0, *asked(shares)]
    for g in range(local_k // group):
        stacked = jnp.concatenate(
            [
                blocks[order.index(offset) * per_share + e][g * ROWS : (g + 1) * ROWS]
                for offset in range(shares)
                for e in range(per_share)
            ],
            axis=0,
        )
        chosen = dot(selector, stacked).astype(BF16)
        size = 2 * group * rows
        forms = [chosen[offset * size : (offset + 1) * size] for offset in range(shares)]
        for kk in range(group):
            k = g * group + kk
            left = [form[2 * kk * rows : (2 * kk + 1) * rows] for form in forms]
            right = [form[(2 * kk + 1) * rows : (2 * kk + 2) * rows] for form in forms]
            form = jnp.concatenate(
                [jnp.concatenate(left, axis=0), jnp.concatenate(right, axis=0)], axis=1
            )
            halves = [ref[k].reshape(2 * norb, ref.shape[3]) for ref in (orb_ref, rest_ref)]
            tile = dot(form, jnp.concatenate(halves, axis=1))
            for offset in range(shares):
                form_ref[jnp.bitwise_xor(plane, offset), k] = form[offset * rows : (offset + 1) * rows]
                for part in range(2):
                    low = offset * rows + part * share
                    start = offset * share * 2 * local_k + 2 * k + part
                    spread(wide, start, 2 * local_k, tile[low : low + share])
    size = share * 2 * local_k
    cells[...] = coulomb_ref[...].astype(F32)
    for s in range(shares):
        offset = jnp.bitwise_xor(me, s)
        outs[s][:size] = take(wide, pl.multiple_of(offset * size, size), size).astype(BF16)
        start = pl.multiple_of(jnp.bitwise_xor(offset, plane) * share, share)
        pieces = [cells[r, pl.ds(start, share), :] for r in range(local_k)]
        outs[s][size:] = jnp.concatenate(pieces, axis=0).astype(BF16)


def own_first(refs):
    return [refs[-1], *refs[:-1]]


def transform_kernel(shares, total, share, *refs):
    tiles, (fwd_ref, bwd_ref) = own_first(refs[:shares]), refs[shares : shares + 2]
    outs, (gathered, weight, wide) = refs[shares + 2 : 2 * shares + 2], refs[2 * shares + 2 :]
    local_k = total // shares
    size = 2 * local_k * share
    me = lax.axis_index("ka")
    for s in range(shares):
        src = jnp.bitwise_xor(me, s)
        gathered[src] = tiles[s][:size].astype(gathered.dtype)
        cells = tiles[s][size:].astype(F32)
        for r in range(local_k):
            spread(weight, src * local_k + r, total, cells[r * share : (r + 1) * share])
    rows = 2 * local_k
    columns = []
    for c in range(share):
        columns.append(
            jnp.concatenate([gathered[a, c * rows : (c + 1) * rows] for a in range(shares)], axis=0).astype(BF16)
        )
    values = jnp.concatenate(columns, axis=1)
    cells = dot(fwd_ref[...], jnp.concatenate([values, values], axis=0))
    scale = jnp.concatenate([take(weight, c * total, total) for c in range(share)], axis=1)
    cells = (cells * jnp.concatenate([scale, scale], axis=0)).astype(BF16)
    kernel = dot(bwd_ref[...], jnp.concatenate([cells, cells], axis=0))
    points = kernel.shape[1] // share
    for c in range(share):
        spread(wide, c, share, kernel[:, c * points : (c + 1) * points])
    for s in range(shares):
        dest = jnp.bitwise_xor(me, s)
        outs[s][...] = take(wide, pl.multiple_of(dest * size, size), size).astype(BF16)


def weight_operands(pieces, right_ref, gathered):
    shares = len(pieces)
    groups, lanes, depth = right_ref.shape
    me, plane = lax.axis_index("ka"), plane_of(shares)
    for s in range(shares):
        gathered[jnp.bitwise_xor(jnp.bitwise_xor(me, s), plane)] = pieces[s][...]
    group = depth // (2 * gathered.shape[2])
    half = gathered.shape[1] // (groups * group) // 2
    for g in range(groups):
        right = []
        for kk in range(group):
            k = g * group + kk
            first, second = [], []
            for a in range(shares):
                piece = gathered[a, k * 2 * half : (k + 1) * 2 * half].astype(F32)
                first.append(piece)
                second.extend([piece[half:], -piece[:half]])
            first = jnp.concatenate(first, axis=0).astype(BF16)
            second = jnp.concatenate(second, axis=0).astype(BF16)
            parts = [jnp.zeros_like(first)] * (2 * group)
            parts[2 * kk], parts[2 * kk + 1] = first, second
            right.append(jnp.concatenate(parts, axis=1))
        right_ref[g] = jnp.concatenate(right, axis=0)


def weight_rows(offsets, flip, out_rows, right_ref, orb_ref, rest_ref, out_ref):
    groups, lanes, _ = right_ref.shape
    local_k, _, norb, _ = orb_ref.shape
    group = local_k // groups
    block = lax.axis_index("pts")
    core = jnp.bitwise_xor(jnp.bitwise_and(block, 1), flip)
    z = lax.shift_right_logical(block, 1)
    chunks = norb // out_rows // 2
    for g in range(groups):
        rows = []
        for offset in offsets:
            start = pl.multiple_of((2 * lax.rem(z + offset, chunks) + core) * out_rows, out_rows)
            parts = [
                ref[k, part, pl.ds(start, out_rows), :]
                for k in range(g * group, (g + 1) * group)
                for part in range(2)
                for ref in (orb_ref, rest_ref)
            ]
            rows.append(jnp.concatenate(parts, axis=1))
        result = dot(jnp.concatenate(rows, axis=0), right_ref[g], ((1,), (1,))).astype(out_ref.dtype)
        for i in range(len(offsets)):
            out_ref[i, :, g * lanes : (g + 1) * lanes] = result[i * out_rows : (i + 1) * out_rows]


def first_weight_kernel(shares, offsets, out_rows, *refs):
    pieces, (orb_ref, rest_ref, out_ref, right_ref, gathered) = own_first(refs[:shares]), refs[shares:]
    weight_operands(pieces, right_ref, gathered)
    weight_rows(offsets, 1, out_rows, right_ref, orb_ref, rest_ref, out_ref)


def next_weight_kernel(offsets, flip, out_rows, right_ref, orb_ref, rest_ref, *refs):
    weight_rows(offsets, flip, out_rows, right_ref, orb_ref, rest_ref, refs[-1])


def pair_kernel(keep_ref, came_ref, *outs):
    for i, out_ref in enumerate(outs):
        out_ref[...] = (keep_ref[i] + came_ref[i].astype(F32)).astype(out_ref.dtype)


def exchange_kernel(chunks, scale, *refs):
    pieces, (form_ref, out_hbm, wide, out_ref, sems) = refs[:chunks][::-1], refs[chunks:]
    shares, local_k, part_lanes, twice = form_ref.shape
    lanes = shares * part_lanes
    norb = twice // 2
    spans = norb // LANES
    out_rows = pieces[0].shape[0]
    total = pieces[0][...]
    for s in range(1, chunks):
        total = total + pieces[s][...].astype(F32)
    total = total * scale
    high = total.astype(BF16)
    low = (total - high.astype(F32)).astype(BF16)
    group = max(1, LANES // lanes)
    width = group * lanes
    lane = lax.broadcasted_iota(jnp.int32, (out_rows, width), 1)
    zero = jnp.zeros((out_rows, width), BF16)
    copies = []
    for g in range(local_k // group):
        high_g = high[:, g * width : (g + 1) * width]
        low_g = low[:, g * width : (g + 1) * width]
        left = []
        for kk in range(group):
            keep = (lane >= kk * lanes) & (lane < (kk + 1) * lanes)
            left.append(
                jnp.concatenate([jnp.where(keep, high_g, zero), jnp.where(keep, low_g, zero)], axis=1)
            )
        forms = [form_ref[d, g * group + kk] for kk in range(group) for d in range(shares)]
        result = dot(jnp.concatenate(left, axis=0), jnp.concatenate(forms + forms, axis=0))
        for kk in range(group):
            for part in range(2):
                for t in range(spans):
                    lane_start = part * norb + t * LANES
                    value = result[kk * out_rows : (kk + 1) * out_rows, lane_start : lane_start + LANES]
                    start = (kk * spans + t) * 2 + part
                    wide[g, pl.ds(start, out_rows, stride=2 * spans * group), :] = value
        out_ref[g] = wide[g].astype(BF16).reshape(out_ref.shape[1:])
        copies.append(pltpu.make_async_copy(out_ref.at[g], out_hbm.at[:, g], sems.at[g]))
        copies[-1].start()
    for copy in copies:
        copy.wait()


def swap(value, axis, mask):
    size = lax.axis_size(axis)
    return lax.ppermute(value, axis, [(i, i ^ mask) for i in range(size)])


def trade(pieces, axis, step):
    return [swap(pieces[s], axis, s * step) for s in range(1, len(pieces))] + [pieces[0]]


def shift_along(pieces):
    chunks = len(pieces)
    came = []
    for s in range(1, chunks):
        pairs = [(2 * z + core, 2 * ((z - s) % chunks) + core) for z in range(chunks) for core in range(2)]
        came.append(lax.ppermute(pieces[s], "pts", pairs))
    return came[::-1] + [pieces[0]]


def body(orbitals, coulomb):
    shares, blocks = lax.axis_size("ka"), lax.axis_size("pts")
    local_k, _, norb, points = orbitals.shape
    columns = coulomb.shape[1]
    per_block = columns // blocks
    share = columns // shares
    total = local_k * shares
    out_rows = norb // blocks
    chunks = blocks // 2
    group = ROWS // (2 * per_block)
    shape = jax.ShapeDtypeStruct

    edge, first = call(
        functools.partial(edge_kernel, per_block),
        [
            shape((local_k * 2 * per_block, norb), BF16),
            shape((local_k, 2, norb, LANES), BF16),
        ],
        0,
        [pltpu.SemaphoreType.DMA((local_k,))],
        limit=50,
        size=4 * MIB,
        unread=1,
    )(orbitals)
    passed_edge, rest = call(
        rest_kernel,
        [shape(edge.shape, BF16), shape((local_k, 2, norb, points - LANES), BF16)],
        0,
        [pltpu.SemaphoreType.DMA((local_k,)), pltpu.SemaphoreType.DMA],
        limit=49,
        size=4 * MIB,
        unread=2,
    )(orbitals, edge)
    per_share = blocks // shares
    partner = swap(passed_edge, "pts", 1)
    came = [edge, partner] + [swap(edge, "pts", 2 * e + c) for e in range(1, per_share // 2) for c in range(2)]
    came = {0: came}
    for offset in asked(shares):
        came[offset] = []
        for e in range(per_share // 2):
            block = swap(edge, "pts", offset * per_share + 2 * e)
            came[offset] += [block, swap(block, "pts", 1)]
    table = column_selector(group, per_share, per_block, 1).reshape(-1, per_share, ROWS)
    places = [[place ^ e for e in range(per_share)] for place in range(per_share)]
    tables = [table[:, place].reshape(table.shape[0], -1).astype(np.float32) for place in places]
    selector = jnp.asarray(np.stack([np.kron(np.eye(shares, dtype=np.float32), t) for t in tables]), BF16)
    piece = shape((share * 2 * local_k, points), BF16)
    both = shape((share * 3 * local_k, points), BF16)
    *tiles, forms = call(
        functools.partial(tile_kernel, shares, per_share, per_block),
        [both] * shares + [shape((shares, local_k, 2 * share, 2 * norb), BF16)],
        blocks + 4,
        [
            tiled(shares * share * 2 * local_k, points),
            pltpu.VMEM(coulomb.shape, F32),
        ],
        size=6 * MIB,
    )(*[block for offset in [0, *asked(shares)] for block in came[offset]], first, rest, selector, coulomb)
    tiles = trade(tiles, "ka", 1)

    forward, backward = phase_tables(total)
    kernels = call(
        functools.partial(transform_kernel, shares, total, share),
        [piece] * shares,
        shares + 2,
        [
            pltpu.VMEM((shares, share * 2 * local_k, points), BF16 if local_k % 8 == 0 else F32),
            tiled(share * total, points),
            tiled(2 * total * share, points),
        ],
        size=2 * MIB,
    )(*tiles, jnp.asarray(forward), jnp.asarray(backward))
    kernels = trade(kernels, "ka", 1)

    lanes = local_k * 2 * columns
    pair = max(1, LANES // (2 * columns))
    early, late = list(reversed(range(1, chunks))), [0]
    sent, right = call(
        functools.partial(first_weight_kernel, shares, early, out_rows),
        [
            shape((len(early), out_rows, lanes), BF16),
            shape((local_k // pair, pair * 2 * columns, pair * 2 * points), BF16),
        ],
        shares + 2,
        [pltpu.VMEM((shares, share * 2 * local_k, points), BF16)],
    )(*kernels, first, rest)

    def rows_of(offsets, flip, kind, before):
        return call(
            functools.partial(next_weight_kernel, offsets, flip, out_rows),
            shape((len(offsets), out_rows, lanes), kind),
            3,
            unread=1,
        )(right, first, rest, before)

    def summed(offsets, keep, came):
        kinds = [shape((out_rows, lanes), BF16 if offset else F32) for offset in offsets]
        return call(pair_kernel, kinds, 2)(keep, came)

    sent_late = rows_of(late, 1, BF16, sent)
    early_sums = summed(early, rows_of(early, 0, F32, sent_late), swap(sent, "pts", 1))
    late_sums = summed(late, rows_of(late, 0, F32, early_sums[0]), swap(sent_late, "pts", 1))
    sums = [*late_sums, *early_sums]
    sums = shift_along(sums)
    spans = norb // LANES
    rows = pair * spans * 2
    result = call(
        functools.partial(exchange_kernel, chunks, 1.0 / math.sqrt(points * blocks)),
        shape((out_rows, local_k // pair, rows, LANES), BF16),
        chunks + 1,
        [
            pltpu.VMEM((local_k // pair, out_rows * rows, LANES), F32),
            pltpu.VMEM((local_k // pair, out_rows, rows, LANES), BF16),
            pltpu.SemaphoreType.DMA((local_k // pair,)),
        ],
        size=4 * MIB,
        result=pltpu.HBM,
    )(*sums, forms)
    result = result.reshape(out_rows, local_k, spans, 2, LANES)
    return result.transpose(0, 1, 3, 2, 4).reshape(out_rows, local_k, 2, norb)


def solution(mesh):
    in_specs = (P("ka", None, None, "pts"), P("ka", None, "pts"))
    out_specs = P("pts", "ka", None, None)
    return jax.shard_map(body, mesh=mesh, in_specs=in_specs, out_specs=out_specs, check_vma=False)
```

```python
import functools
import math

import jax
import jax.numpy as jnp
import ml_dtypes
import numpy as np
from jax import lax
from jax.experimental import pallas as pl
from jax.experimental.pallas import tpu as pltpu
from jax.sharding import PartitionSpec as P

BF16 = jnp.bfloat16
F32 = jnp.float32
LANES = 128
ROWS = 16
MIB = 1 << 20


def split_terms(table):
    high = table.astype(ml_dtypes.bfloat16)
    low = (table - high.astype(np.float64)).astype(ml_dtypes.bfloat16)
    return np.concatenate([high, low], axis=1)


def phase_tables(total):
    index = np.arange(total)
    angles = (index[:, None] * index[None, :] % total) * (2.0 * math.pi / total)
    cosine, sine = np.cos(angles), np.sin(angles)
    forward = np.zeros((2, total, total, 2))
    forward[0, :, :, 0] = cosine
    forward[0, :, :, 1] = -sine
    forward[1, :, :, 0] = sine
    forward[1, :, :, 1] = cosine
    backward = np.zeros((total, 2, 2, total))
    backward[:, 0, 0] = cosine
    backward[:, 0, 1] = sine
    backward[:, 1, 1] = cosine
    backward[:, 1, 0] = -sine
    size = 2 * total
    return (
        split_terms(forward.reshape(size, size)),
        split_terms(backward.reshape(size, size) / total),
    )


def column_selector(group, blocks, per_block, shares):
    total = blocks * per_block
    share = total // shares
    table = np.zeros((group, 2, shares, 2, share, blocks, group, 2, per_block), np.float32)
    for k in range(group):
        for col in range(total):
            d, c = divmod(col, share)
            b, j = divmod(col, per_block)
            table[k, 0, d, 0, c, b, k, 0, j] = 1.0
            table[k, 0, d, 1, c, b, k, 1, j] = -1.0
            table[k, 1, d, 0, c, b, k, 1, j] = 1.0
            table[k, 1, d, 1, c, b, k, 0, j] = 1.0
    return table.reshape(group * 4 * total, blocks * group * 2 * per_block).astype(ml_dtypes.bfloat16)


def dot(left, right, dims=((1,), (0,))):
    return lax.dot_general(left, right, (dims, ((), ())), preferred_element_type=F32)


def spread(wide, start, stride, value):
    for t in range(wide.shape[0]):
        wide[t, pl.ds(start, value.shape[0], stride=stride), :] = value[:, t * LANES : (t + 1) * LANES]


def take(wide, start, size):
    return jnp.concatenate([wide[t, pl.ds(start, size), :] for t in range(wide.shape[0])], axis=1)


def tiled(rows, lanes, stride):
    return pltpu.VMEM((lanes // LANES, rows + stride, LANES), F32)


def call(kernel, out_shape, n_in, scratch=(), limit=24, flops=0, size=0, unread=0, result=pltpu.VMEM):
    whole = pl.BlockSpec(memory_space=pltpu.VMEM)
    return pl.pallas_call(
        kernel,
        out_shape=out_shape,
        in_specs=[whole] * n_in + [pl.BlockSpec(memory_space=pl.ANY)] * unread,
        out_specs=jax.tree.map(lambda _: pl.BlockSpec(memory_space=result), out_shape),
        scratch_shapes=list(scratch),
        compiler_params=pltpu.CompilerParams(vmem_limit_bytes=limit * MIB),
        cost_estimate=pl.CostEstimate(flops=flops, bytes_accessed=size, transcendentals=0),
    )


def load_copies(orb_hbm, orb_ref, sems, start):
    lanes = pl.ds(start, orb_ref.shape[3])
    copies = [
        pltpu.make_async_copy(orb_hbm.at[k, :, :, lanes], orb_ref.at[k], sems.at[k])
        for k in range(orb_ref.shape[0])
    ]
    for copy in copies:
        copy.start()
    return copies


def rest_kernel(orb_hbm, edge_hbm, pass_ref, orb_ref, sems, pass_sem):
    copies = load_copies(orb_hbm, orb_ref, sems, LANES)
    copies.append(pltpu.make_async_copy(edge_hbm, pass_ref, pass_sem))
    copies[-1].start()
    for copy in copies:
        copy.wait()


def edge_kernel(per_block, orb_hbm, edge_ref, orb_ref, sems):
    local_k = orb_hbm.shape[0]
    copies = load_copies(orb_hbm, orb_ref, sems, 0)
    row = lax.broadcasted_iota(jnp.int32, (2 * per_block, 2 * LANES), 0)
    lane = lax.broadcasted_iota(jnp.int32, (2 * per_block, 2 * LANES), 1)
    column = jnp.where(row < per_block, row, row - per_block + LANES)
    chosen = jnp.where(lane == column, jnp.ones(row.shape, F32), jnp.zeros(row.shape, F32)).astype(BF16)
    group = ROWS // (2 * per_block)
    for g in range(local_k // group):
        rows = []
        for k in range(g * group, (g + 1) * group):
            copies[k].wait()
            both = jnp.concatenate([orb_ref[k, 0], orb_ref[k, 1]], axis=1)
            rows.append(dot(chosen, both, ((1,), (1,))))
        edge_ref[g * ROWS : (g + 1) * ROWS] = jnp.concatenate(rows, axis=0).astype(BF16)


def asked(shares):
    return [2, 1, *range(3, shares)]


def plane_of(shares):
    return lax.div(lax.axis_index("pts"), lax.axis_size("pts") // shares)


def tile_kernel(shares, per_share, per_block, *refs):
    blocks, (orb_ref, rest_ref, sel_ref, coulomb_ref) = refs[: shares * per_share], refs[shares * per_share :][:4]
    *outs, form_ref, wide, cells = refs[shares * per_share + 4 :]
    local_k, _, norb, _ = orb_ref.shape
    group = ROWS // (2 * per_block)
    share = per_share * per_block
    rows = 2 * share
    me, block = lax.axis_index("ka"), lax.axis_index("pts")
    plane = plane_of(shares)
    selector = sel_ref[jnp.bitwise_and(block, per_share - 1)]
    order = [0, *asked(shares)]
    for g in range(local_k // group):
        stacked = jnp.concatenate(
            [
                blocks[order.index(offset) * per_share + e][g * ROWS : (g + 1) * ROWS]
                for offset in range(shares)
                for e in range(per_share)
            ],
            axis=0,
        )
        chosen = dot(selector, stacked).astype(BF16)
        size = 2 * group * rows
        forms = [chosen[offset * size : (offset + 1) * size] for offset in range(shares)]
        for kk in range(group):
            k = g * group + kk
            left = [form[2 * kk * rows : (2 * kk + 1) * rows] for form in forms]
            right = [form[(2 * kk + 1) * rows : (2 * kk + 2) * rows] for form in forms]
            form = jnp.concatenate(
                [jnp.concatenate(left, axis=0), jnp.concatenate(right, axis=0)], axis=1
            )
            halves = [ref[k].reshape(2 * norb, ref.shape[3]) for ref in (orb_ref, rest_ref)]
            tile = dot(form, jnp.concatenate(halves, axis=1))
            for offset in range(shares):
                form_ref[jnp.bitwise_xor(plane, offset), k] = form[offset * rows : (offset + 1) * rows]
                for part in range(2):
                    low = offset * rows + part * share
                    start = offset * share * 2 * local_k + 2 * k + part
                    spread(wide, start, 2 * local_k, tile[low : low + share])
    size = share * 2 * local_k
    cells[...] = coulomb_ref[...].astype(F32)
    for s in range(shares):
        offset = jnp.bitwise_xor(me, s)
        outs[s][:size] = take(wide, pl.multiple_of(offset * size, size), size).astype(BF16)
        start = pl.multiple_of(jnp.bitwise_xor(offset, plane) * share, share)
        pieces = [cells[r, pl.ds(start, share), :] for r in range(local_k)]
        outs[s][size:] = jnp.concatenate(pieces, axis=0).astype(BF16)


def transform_kernel(shares, total, share, *refs):
    tiles, (fwd_ref, bwd_ref) = refs[:shares][::-1], refs[shares : shares + 2]
    outs, (gathered, weight, wide) = refs[shares + 2 : 2 * shares + 2], refs[2 * shares + 2 :]
    local_k = total // shares
    size = 2 * local_k * share
    me = lax.axis_index("ka")
    for s in range(shares):
        src = jnp.bitwise_xor(me, s)
        gathered[src] = tiles[s][:size].astype(gathered.dtype)
        cells = tiles[s][size:].astype(F32)
        for r in range(local_k):
            spread(weight, src * local_k + r, total, cells[r * share : (r + 1) * share])
    rows = 2 * local_k
    columns = []
    for c in range(share):
        columns.append(
            jnp.concatenate([gathered[a, c * rows : (c + 1) * rows] for a in range(shares)], axis=0).astype(BF16)
        )
    values = jnp.concatenate(columns, axis=1)
    cells = dot(fwd_ref[...], jnp.concatenate([values, values], axis=0))
    scale = jnp.concatenate([take(weight, c * total, total) for c in range(share)], axis=1)
    cells = (cells * jnp.concatenate([scale, scale], axis=0)).astype(BF16)
    kernel = dot(bwd_ref[...], jnp.concatenate([cells, cells], axis=0))
    points = kernel.shape[1] // share
    for c in range(share):
        spread(wide, c, share, kernel[:, c * points : (c + 1) * points])
    for s in range(shares):
        dest = jnp.bitwise_xor(me, s)
        outs[s][...] = take(wide, pl.multiple_of(dest * size, size), size).astype(BF16)


def weight_operands(pieces, right_ref, gathered):
    shares = len(pieces)
    groups, lanes, depth = right_ref.shape
    me, plane = lax.axis_index("ka"), plane_of(shares)
    for s in range(shares):
        gathered[jnp.bitwise_xor(jnp.bitwise_xor(me, s), plane)] = pieces[s][...]
    group = depth // (2 * gathered.shape[2])
    half = gathered.shape[1] // (groups * group) // 2
    for g in range(groups):
        right = []
        for kk in range(group):
            k = g * group + kk
            first, second = [], []
            for a in range(shares):
                piece = gathered[a, k * 2 * half : (k + 1) * 2 * half].astype(F32)
                first.append(piece)
                second.extend([piece[half:], -piece[:half]])
            first = jnp.concatenate(first, axis=0).astype(BF16)
            second = jnp.concatenate(second, axis=0).astype(BF16)
            parts = [jnp.zeros_like(first)] * (2 * group)
            parts[2 * kk], parts[2 * kk + 1] = first, second
            right.append(jnp.concatenate(parts, axis=1))
        right_ref[g] = jnp.concatenate(right, axis=0)


def weight_rows(offsets, flip, out_rows, right_ref, orb_ref, rest_ref, out_ref):
    groups, lanes, _ = right_ref.shape
    local_k, _, norb, _ = orb_ref.shape
    group = local_k // groups
    block = lax.axis_index("pts")
    core = jnp.bitwise_xor(jnp.bitwise_and(block, 1), flip)
    z = lax.shift_right_logical(block, 1)
    chunks = norb // out_rows // 2
    for g in range(groups):
        rows = []
        for offset in offsets:
            start = pl.multiple_of((2 * lax.rem(z + offset, chunks) + core) * out_rows, out_rows)
            parts = [
                ref[k, part, pl.ds(start, out_rows), :]
                for k in range(g * group, (g + 1) * group)
                for part in range(2)
                for ref in (orb_ref, rest_ref)
            ]
            rows.append(jnp.concatenate(parts, axis=1))
        result = dot(jnp.concatenate(rows, axis=0), right_ref[g], ((1,), (1,))).astype(out_ref.dtype)
        for i in range(len(offsets)):
            out_ref[i, :, g * lanes : (g + 1) * lanes] = result[i * out_rows : (i + 1) * out_rows]


def first_weight_kernel(shares, offsets, out_rows, *refs):
    pieces, (orb_ref, rest_ref, out_ref, right_ref, gathered) = refs[:shares][::-1], refs[shares:]
    weight_operands(pieces, right_ref, gathered)
    weight_rows(offsets, 1, out_rows, right_ref, orb_ref, rest_ref, out_ref)


def next_weight_kernel(offsets, flip, out_rows, right_ref, orb_ref, rest_ref, *refs):
    weight_rows(offsets, flip, out_rows, right_ref, orb_ref, rest_ref, refs[-1])


def pair_kernel(keep_ref, came_ref, *outs):
    for i, out_ref in enumerate(outs):
        out_ref[...] = (keep_ref[i] + came_ref[i].astype(F32)).astype(out_ref.dtype)


def exchange_kernel(chunks, scale, *refs):
    pieces, (form_ref, out_hbm, wide, out_ref, sems) = refs[:chunks][::-1], refs[chunks:]
    shares, local_k, part_lanes, twice = form_ref.shape
    lanes = shares * part_lanes
    norb = twice // 2
    spans = norb // LANES
    out_rows = pieces[0].shape[0]
    total = pieces[0][...]
    for s in range(1, chunks):
        total = total + pieces[s][...].astype(F32)
    total = total * scale
    high = total.astype(BF16)
    low = (total - high.astype(F32)).astype(BF16)
    group = max(1, LANES // lanes)
    width = group * lanes
    lane = lax.broadcasted_iota(jnp.int32, (out_rows, width), 1)
    zero = jnp.zeros((out_rows, width), BF16)
    copies = []
    for g in range(local_k // group):
        high_g = high[:, g * width : (g + 1) * width]
        low_g = low[:, g * width : (g + 1) * width]
        left = []
        for kk in range(group):
            keep = (lane >= kk * lanes) & (lane < (kk + 1) * lanes)
            left.append(
                jnp.concatenate([jnp.where(keep, high_g, zero), jnp.where(keep, low_g, zero)], axis=1)
            )
        forms = [form_ref[d, g * group + kk] for kk in range(group) for d in range(shares)]
        result = dot(jnp.concatenate(left, axis=0), jnp.concatenate(forms + forms, axis=0))
        for kk in range(group):
            for part in range(2):
                for t in range(spans):
                    lane_start = part * norb + t * LANES
                    value = result[kk * out_rows : (kk + 1) * out_rows, lane_start : lane_start + LANES]
                    start = (kk * spans + t) * 2 + part
                    wide[g, pl.ds(start, out_rows, stride=2 * spans * group), :] = value
        rows = out_ref.shape[1] * out_ref.shape[2]
        out_ref[g] = wide[g, :rows].astype(BF16).reshape(out_ref.shape[1:])
        copies.append(pltpu.make_async_copy(out_ref.at[g], out_hbm.at[:, g], sems.at[g]))
        copies[-1].start()
    for copy in copies:
        copy.wait()


def swap(value, axis, mask):
    size = lax.axis_size(axis)
    return lax.ppermute(value, axis, [(i, i ^ mask) for i in range(size)])


def trade(pieces, axis, step):
    return [swap(pieces[s], axis, s * step) for s in reversed(range(1, len(pieces)))] + [pieces[0]]


def shift_along(pieces):
    chunks = len(pieces)
    came = []
    for s in range(1, chunks):
        pairs = [(2 * z + core, 2 * ((z - s) % chunks) + core) for z in range(chunks) for core in range(2)]
        came.append(lax.ppermute(pieces[s], "pts", pairs))
    return came[::-1] + [pieces[0]]


def body(orbitals, coulomb):
    shares, blocks = lax.axis_size("ka"), lax.axis_size("pts")
    local_k, _, norb, points = orbitals.shape
    columns = coulomb.shape[1]
    per_block = columns // blocks
    share = columns // shares
    total = local_k * shares
    out_rows = norb // blocks
    chunks = blocks // 2
    group = ROWS // (2 * per_block)
    shape = jax.ShapeDtypeStruct

    edge, first = call(
        functools.partial(edge_kernel, per_block),
        [
            shape((local_k * 2 * per_block, norb), BF16),
            shape((local_k, 2, norb, LANES), BF16),
        ],
        0,
        [pltpu.SemaphoreType.DMA((local_k,))],
        limit=50,
        size=4 * MIB,
        unread=1,
    )(orbitals)
    passed_edge, rest = call(
        rest_kernel,
        [shape(edge.shape, BF16), shape((local_k, 2, norb, points - LANES), BF16)],
        0,
        [pltpu.SemaphoreType.DMA((local_k,)), pltpu.SemaphoreType.DMA],
        limit=49,
        size=4 * MIB,
        unread=2,
    )(orbitals, edge)
    per_share = blocks // shares
    partner = swap(passed_edge, "pts", 1)
    came = [edge, partner] + [swap(edge, "pts", 2 * e + c) for e in range(1, per_share // 2) for c in range(2)]
    came = {0: came}
    for offset in asked(shares):
        came[offset] = []
        for e in range(per_share // 2):
            block = swap(edge, "pts", offset * per_share + 2 * e)
            came[offset] += [block, swap(block, "pts", 1)]
    table = column_selector(group, per_share, per_block, 1).reshape(-1, per_share, ROWS)
    places = [[place ^ e for e in range(per_share)] for place in range(per_share)]
    tables = [table[:, place].reshape(table.shape[0], -1).astype(np.float32) for place in places]
    selector = jnp.asarray(np.stack([np.kron(np.eye(shares, dtype=np.float32), t) for t in tables]), BF16)
    piece = shape((share * 2 * local_k, points), BF16)
    both = shape((share * 3 * local_k, points), BF16)
    *tiles, forms = call(
        functools.partial(tile_kernel, shares, per_share, per_block),
        [both] * shares + [shape((shares, local_k, 2 * share, 2 * norb), BF16)],
        blocks + 4,
        [
            tiled(shares * share * 2 * local_k, points, 2 * local_k),
            pltpu.VMEM(coulomb.shape, F32),
        ],
        size=6 * MIB,
    )(*[block for offset in [0, *asked(shares)] for block in came[offset]], first, rest, selector, coulomb)
    tiles = trade(tiles, "ka", 1)

    forward, backward = phase_tables(total)
    kernels = call(
        functools.partial(transform_kernel, shares, total, share),
        [piece] * shares,
        shares + 2,
        [
            pltpu.VMEM((shares, share * 2 * local_k, points), BF16 if local_k % 8 == 0 else F32),
            tiled(share * total, points, total),
            tiled(2 * total * share, points, share),
        ],
        size=2 * MIB,
    )(*tiles, jnp.asarray(forward), jnp.asarray(backward))
    kernels = trade(kernels, "ka", 1)

    lanes = local_k * 2 * columns
    pair = max(1, LANES // (2 * columns))
    early, late = list(reversed(range(1, chunks))), [0]
    sent, right = call(
        functools.partial(first_weight_kernel, shares, early, out_rows),
        [
            shape((len(early), out_rows, lanes), BF16),
            shape((local_k // pair, pair * 2 * columns, pair * 2 * points), BF16),
        ],
        shares + 2,
        [pltpu.VMEM((shares, share * 2 * local_k, points), BF16)],
    )(*kernels, first, rest)

    def rows_of(offsets, flip, kind, before):
        return call(
            functools.partial(next_weight_kernel, offsets, flip, out_rows),
            shape((len(offsets), out_rows, lanes), kind),
            3,
            unread=1,
        )(right, first, rest, before)

    def summed(offsets, keep, came):
        kinds = [shape((out_rows, lanes), BF16 if offset else F32) for offset in offsets]
        return call(pair_kernel, kinds, 2)(keep, came)

    sent_late = rows_of(late, 1, BF16, sent)
    early_sums = summed(early, rows_of(early, 0, F32, sent_late), swap(sent, "pts", 1))
    late_sums = summed(late, rows_of(late, 0, F32, early_sums[0]), swap(sent_late, "pts", 1))
    sums = [*late_sums, *early_sums]
    sums = shift_along(sums)
    spans = norb // LANES
    rows = pair * spans * 2
    result = call(
        functools.partial(exchange_kernel, chunks, 1.0 / math.sqrt(points * blocks)),
        shape((out_rows, local_k // pair, rows, LANES), BF16),
        chunks + 1,
        [
            pltpu.VMEM((local_k // pair, (out_rows + 1) * rows, LANES), F32),
            pltpu.VMEM((local_k // pair, out_rows, rows, LANES), BF16),
            pltpu.SemaphoreType.DMA((local_k // pair,)),
        ],
        size=4 * MIB,
        result=pltpu.HBM,
    )(*sums, forms)
    result = result.reshape(out_rows, local_k, spans, 2, LANES)
    return result.transpose(0, 1, 3, 2, 4).reshape(out_rows, local_k, 2, norb)


def solution(mesh):
    in_specs = (P("ka", None, None, "pts"), P("ka", None, "pts"))
    out_specs = P("pts", "ka", None, None)
    return jax.shard_map(body, mesh=mesh, in_specs=in_specs, out_specs=out_specs, check_vma=False)
```

```python
import functools
import math

import jax
import jax.numpy as jnp
import ml_dtypes
import numpy as np
from jax import lax
from jax.experimental import pallas as pl
from jax.experimental.pallas import tpu as pltpu
from jax.sharding import PartitionSpec as P

BF16 = jnp.bfloat16
F32 = jnp.float32
LANES = 128
ROWS = 16
MIB = 1 << 20


def split_terms(table):
    high = table.astype(ml_dtypes.bfloat16)
    low = (table - high.astype(np.float64)).astype(ml_dtypes.bfloat16)
    return np.concatenate([high, low], axis=1)


def phase_tables(total):
    index = np.arange(total)
    angles = (index[:, None] * index[None, :] % total) * (2.0 * math.pi / total)
    cosine, sine = np.cos(angles), np.sin(angles)
    forward = np.zeros((2, total, total, 2))
    forward[0, :, :, 0] = cosine
    forward[0, :, :, 1] = -sine
    forward[1, :, :, 0] = sine
    forward[1, :, :, 1] = cosine
    backward = np.zeros((total, 2, 2, total))
    backward[:, 0, 0] = cosine
    backward[:, 0, 1] = sine
    backward[:, 1, 1] = cosine
    backward[:, 1, 0] = -sine
    size = 2 * total
    return (
        split_terms(forward.reshape(size, size)),
        split_terms(backward.reshape(size, size) / total),
    )


def column_selector(group, blocks, per_block, shares):
    total = blocks * per_block
    share = total // shares
    table = np.zeros((group, 2, shares, 2, share, blocks, group, 2, per_block), np.float32)
    for k in range(group):
        for col in range(total):
            d, c = divmod(col, share)
            b, j = divmod(col, per_block)
            table[k, 0, d, 0, c, b, k, 0, j] = 1.0
            table[k, 0, d, 1, c, b, k, 1, j] = -1.0
            table[k, 1, d, 0, c, b, k, 1, j] = 1.0
            table[k, 1, d, 1, c, b, k, 0, j] = 1.0
    return table.reshape(group * 4 * total, blocks * group * 2 * per_block).astype(ml_dtypes.bfloat16)


def dot(left, right, dims=((1,), (0,))):
    return lax.dot_general(left, right, (dims, ((), ())), preferred_element_type=F32)


def spread(wide, start, stride, value):
    for t in range(wide.shape[0]):
        wide[t, pl.ds(start, value.shape[0], stride=stride), :] = value[:, t * LANES : (t + 1) * LANES]


def take(wide, start, size):
    return jnp.concatenate([wide[t, pl.ds(start, size), :] for t in range(wide.shape[0])], axis=1)


def tiled(rows, lanes):
    return pltpu.VMEM((lanes // LANES, rows, LANES), F32)


def call(kernel, out_shape, n_in, scratch=(), limit=24, flops=0, size=0, unread=0, result=pltpu.VMEM):
    whole = pl.BlockSpec(memory_space=pltpu.VMEM)
    return pl.pallas_call(
        kernel,
        out_shape=out_shape,
        in_specs=[whole] * n_in + [pl.BlockSpec(memory_space=pl.ANY)] * unread,
        out_specs=jax.tree.map(lambda _: pl.BlockSpec(memory_space=result), out_shape),
        scratch_shapes=list(scratch),
        compiler_params=pltpu.CompilerParams(vmem_limit_bytes=limit * MIB),
        cost_estimate=pl.CostEstimate(flops=flops, bytes_accessed=size, transcendentals=0),
    )


def load_copies(orb_hbm, orb_ref, sems, start):
    lanes = pl.ds(start, orb_ref.shape[3])
    copies = [
        pltpu.make_async_copy(orb_hbm.at[k, :, :, lanes], orb_ref.at[k], sems.at[k])
        for k in range(orb_ref.shape[0])
    ]
    for copy in copies:
        copy.start()
    return copies


def rest_kernel(shares, coulomb_ref, orb_hbm, edge_hbm, pass_ref, orb_ref, cell_ref, wide, sems, pass_sem):
    copies = load_copies(orb_hbm, orb_ref, sems, LANES)
    copies.append(pltpu.make_async_copy(edge_hbm, pass_ref, pass_sem))
    copies[-1].start()
    share = coulomb_ref.shape[1] // shares
    me, plane = lax.axis_index("ka"), plane_of(shares)
    wide[...] = coulomb_ref[...].astype(F32)
    for s in range(shares):
        owned = jnp.bitwise_xor(jnp.bitwise_xor(me, s), plane)
        start = pl.multiple_of(owned * share, share)
        pieces = [wide[r, pl.ds(start, share), :] for r in range(wide.shape[0])]
        cell_ref[s] = jnp.concatenate(pieces, axis=0).astype(BF16)
    for copy in copies:
        copy.wait()


def edge_kernel(per_block, orb_hbm, edge_ref, orb_ref, sems):
    local_k = orb_hbm.shape[0]
    copies = load_copies(orb_hbm, orb_ref, sems, 0)
    row = lax.broadcasted_iota(jnp.int32, (2 * per_block, 2 * LANES), 0)
    lane = lax.broadcasted_iota(jnp.int32, (2 * per_block, 2 * LANES), 1)
    column = jnp.where(row < per_block, row, row - per_block + LANES)
    chosen = jnp.where(lane == column, jnp.ones(row.shape, F32), jnp.zeros(row.shape, F32)).astype(BF16)
    group = ROWS // (2 * per_block)
    for g in range(local_k // group):
        rows = []
        for k in range(g * group, (g + 1) * group):
            copies[k].wait()
            both = jnp.concatenate([orb_ref[k, 0], orb_ref[k, 1]], axis=1)
            rows.append(dot(chosen, both, ((1,), (1,))))
        edge_ref[g * ROWS : (g + 1) * ROWS] = jnp.concatenate(rows, axis=0).astype(BF16)


def asked(shares):
    return [2, 1, *range(3, shares)]


def plane_of(shares):
    return lax.div(lax.axis_index("pts"), lax.axis_size("pts") // shares)


def tile_kernel(shares, per_share, per_block, *refs):
    blocks, (orb_ref, rest_ref, sel_ref, cell_ref) = refs[: shares * per_share], refs[shares * per_share :][:4]
    *outs, form_ref, wide = refs[shares * per_share + 4 :]
    local_k, _, norb, _ = orb_ref.shape
    group = ROWS // (2 * per_block)
    share = per_share * per_block
    rows = 2 * share
    me, block = lax.axis_index("ka"), lax.axis_index("pts")
    plane = plane_of(shares)
    selector = sel_ref[jnp.bitwise_and(block, per_share - 1)]
    order = [0, *asked(shares)]
    for g in range(local_k // group):
        stacked = jnp.concatenate(
            [
                blocks[order.index(offset) * per_share + e][g * ROWS : (g + 1) * ROWS]
                for offset in range(shares)
                for e in range(per_share)
            ],
            axis=0,
        )
        chosen = dot(selector, stacked).astype(BF16)
        size = 2 * group * rows
        forms = [chosen[offset * size : (offset + 1) * size] for offset in range(shares)]
        for kk in range(group):
            k = g * group + kk
            left = [form[2 * kk * rows : (2 * kk + 1) * rows] for form in forms]
            right = [form[(2 * kk + 1) * rows : (2 * kk + 2) * rows] for form in forms]
            form = jnp.concatenate(
                [jnp.concatenate(left, axis=0), jnp.concatenate(right, axis=0)], axis=1
            )
            halves = [ref[k].reshape(2 * norb, ref.shape[3]) for ref in (orb_ref, rest_ref)]
            tile = dot(form, jnp.concatenate(halves, axis=1))
            for offset in range(shares):
                form_ref[jnp.bitwise_xor(plane, offset), k] = form[offset * rows : (offset + 1) * rows]
                for part in range(2):
                    low = offset * rows + part * share
                    start = offset * share * 2 * local_k + 2 * k + part
                    spread(wide, start, 2 * local_k, tile[low : low + share])
    size = share * 2 * local_k
    for s in range(shares):
        offset = jnp.bitwise_xor(me, s)
        outs[s][:size] = take(wide, pl.multiple_of(offset * size, size), size).astype(BF16)
        outs[s][size:] = cell_ref[s]


def transform_kernel(shares, total, share, *refs):
    tiles, (fwd_ref, bwd_ref) = refs[:shares][::-1], refs[shares : shares + 2]
    outs, (gathered, weight, wide) = refs[shares + 2 : 2 * shares + 2], refs[2 * shares + 2 :]
    local_k = total // shares
    size = 2 * local_k * share
    me = lax.axis_index("ka")
    for s in range(shares):
        src = jnp.bitwise_xor(me, s)
        gathered[src] = tiles[s][:size].astype(gathered.dtype)
        cells = tiles[s][size:].astype(F32)
        for r in range(local_k):
            spread(weight, src * local_k + r, total, cells[r * share : (r + 1) * share])
    rows = 2 * local_k
    columns = []
    for c in range(share):
        columns.append(
            jnp.concatenate([gathered[a, c * rows : (c + 1) * rows] for a in range(shares)], axis=0).astype(BF16)
        )
    values = jnp.concatenate(columns, axis=1)
    cells = dot(fwd_ref[...], jnp.concatenate([values, values], axis=0))
    scale = jnp.concatenate([take(weight, c * total, total) for c in range(share)], axis=1)
    cells = (cells * jnp.concatenate([scale, scale], axis=0)).astype(BF16)
    kernel = dot(bwd_ref[...], jnp.concatenate([cells, cells], axis=0))
    points = kernel.shape[1] // share
    for c in range(share):
        spread(wide, c, share, kernel[:, c * points : (c + 1) * points])
    for s in range(shares):
        dest = jnp.bitwise_xor(me, s)
        outs[s][...] = take(wide, pl.multiple_of(dest * size, size), size).astype(BF16)


def weight_operands(pieces, right_ref, gathered):
    shares = len(pieces)
    groups, lanes, depth = right_ref.shape
    me, plane = lax.axis_index("ka"), plane_of(shares)
    for s in range(shares):
        gathered[jnp.bitwise_xor(jnp.bitwise_xor(me, s), plane)] = pieces[s][...]
    group = depth // (2 * gathered.shape[2])
    half = gathered.shape[1] // (groups * group) // 2
    for g in range(groups):
        right = []
        for kk in range(group):
            k = g * group + kk
            first, second = [], []
            for a in range(shares):
                piece = gathered[a, k * 2 * half : (k + 1) * 2 * half].astype(F32)
                first.append(piece)
                second.extend([piece[half:], -piece[:half]])
            first = jnp.concatenate(first, axis=0).astype(BF16)
            second = jnp.concatenate(second, axis=0).astype(BF16)
            parts = [jnp.zeros_like(first)] * (2 * group)
            parts[2 * kk], parts[2 * kk + 1] = first, second
            right.append(jnp.concatenate(parts, axis=1))
        right_ref[g] = jnp.concatenate(right, axis=0)


def weight_rows(offsets, flip, out_rows, right_ref, orb_ref, rest_ref, out_ref):
    groups, lanes, _ = right_ref.shape
    local_k, _, norb, _ = orb_ref.shape
    group = local_k // groups
    block = lax.axis_index("pts")
    core = jnp.bitwise_xor(jnp.bitwise_and(block, 1), flip)
    z = lax.shift_right_logical(block, 1)
    chunks = norb // out_rows // 2
    for g in range(groups):
        rows = []
        for offset in offsets:
            start = pl.multiple_of((2 * lax.rem(z + offset, chunks) + core) * out_rows, out_rows)
            parts = [
                ref[k, part, pl.ds(start, out_rows), :]
                for k in range(g * group, (g + 1) * group)
                for part in range(2)
                for ref in (orb_ref, rest_ref)
            ]
            rows.append(jnp.concatenate(parts, axis=1))
        result = dot(jnp.concatenate(rows, axis=0), right_ref[g], ((1,), (1,))).astype(out_ref.dtype)
        for i in range(len(offsets)):
            out_ref[i, :, g * lanes : (g + 1) * lanes] = result[i * out_rows : (i + 1) * out_rows]


def first_weight_kernel(shares, offsets, out_rows, *refs):
    pieces, (orb_ref, rest_ref, out_ref, right_ref, gathered) = refs[:shares][::-1], refs[shares:]
    weight_operands(pieces, right_ref, gathered)
    weight_rows(offsets, 1, out_rows, right_ref, orb_ref, rest_ref, out_ref)


def next_weight_kernel(offsets, flip, out_rows, right_ref, orb_ref, rest_ref, *refs):
    weight_rows(offsets, flip, out_rows, right_ref, orb_ref, rest_ref, refs[-1])


def pair_kernel(keep_ref, came_ref, *outs):
    for i, out_ref in enumerate(outs):
        out_ref[...] = (keep_ref[i] + came_ref[i].astype(F32)).astype(out_ref.dtype)


def exchange_kernel(chunks, scale, *refs):
    pieces, (form_ref, out_hbm, wide, out_ref, sems) = refs[:chunks][::-1], refs[chunks:]
    shares, local_k, part_lanes, twice = form_ref.shape
    lanes = shares * part_lanes
    norb = twice // 2
    spans = norb // LANES
    out_rows = pieces[0].shape[0]
    total = pieces[0][...]
    for s in range(1, chunks):
        total = total + pieces[s][...].astype(F32)
    total = total * scale
    high = total.astype(BF16)
    low = (total - high.astype(F32)).astype(BF16)
    group = max(1, LANES // lanes)
    width = group * lanes
    lane = lax.broadcasted_iota(jnp.int32, (out_rows, width), 1)
    zero = jnp.zeros((out_rows, width), BF16)
    copies = []
    for g in range(local_k // group):
        high_g = high[:, g * width : (g + 1) * width]
        low_g = low[:, g * width : (g + 1) * width]
        left = []
        for kk in range(group):
            keep = (lane >= kk * lanes) & (lane < (kk + 1) * lanes)
            left.append(
                jnp.concatenate([jnp.where(keep, high_g, zero), jnp.where(keep, low_g, zero)], axis=1)
            )
        forms = [form_ref[d, g * group + kk] for kk in range(group) for d in range(shares)]
        result = dot(jnp.concatenate(left, axis=0), jnp.concatenate(forms + forms, axis=0))
        for kk in range(group):
            for part in range(2):
                for t in range(spans):
                    lane_start = part * norb + t * LANES
                    value = result[kk * out_rows : (kk + 1) * out_rows, lane_start : lane_start + LANES]
                    start = (kk * spans + t) * 2 + part
                    wide[g, pl.ds(start, out_rows, stride=2 * spans * group), :] = value
        out_ref[g] = wide[g].astype(BF16).reshape(out_ref.shape[1:])
        copies.append(pltpu.make_async_copy(out_ref.at[g], out_hbm.at[:, g], sems.at[g]))
        copies[-1].start()
    for copy in copies:
        copy.wait()


def swap(value, axis, mask):
    size = lax.axis_size(axis)
    return lax.ppermute(value, axis, [(i, i ^ mask) for i in range(size)])


def trade(pieces, axis, step):
    return [swap(pieces[s], axis, s * step) for s in reversed(range(1, len(pieces)))] + [pieces[0]]


def shift_along(pieces):
    chunks = len(pieces)
    came = []
    for s in range(1, chunks):
        pairs = [(2 * z + core, 2 * ((z - s) % chunks) + core) for z in range(chunks) for core in range(2)]
        came.append(lax.ppermute(pieces[s], "pts", pairs))
    return came[::-1] + [pieces[0]]


def body(orbitals, coulomb):
    shares, blocks = lax.axis_size("ka"), lax.axis_size("pts")
    local_k, _, norb, points = orbitals.shape
    columns = coulomb.shape[1]
    per_block = columns // blocks
    share = columns // shares
    total = local_k * shares
    out_rows = norb // blocks
    chunks = blocks // 2
    group = ROWS // (2 * per_block)
    shape = jax.ShapeDtypeStruct

    edge, first = call(
        functools.partial(edge_kernel, per_block),
        [
            shape((local_k * 2 * per_block, norb), BF16),
            shape((local_k, 2, norb, LANES), BF16),
        ],
        0,
        [pltpu.SemaphoreType.DMA((local_k,))],
        limit=50,
        size=4 * MIB,
        unread=1,
    )(orbitals)
    passed_edge, rest, cells = call(
        functools.partial(rest_kernel, shares),
        [
            shape(edge.shape, BF16),
            shape((local_k, 2, norb, points - LANES), BF16),
            shape((shares, local_k * share, points), BF16),
        ],
        1,
        [pltpu.VMEM(coulomb.shape, F32), pltpu.SemaphoreType.DMA((local_k,)), pltpu.SemaphoreType.DMA],
        limit=49,
        size=4 * MIB,
        unread=2,
    )(coulomb, orbitals, edge)
    per_share = blocks // shares
    partner = swap(passed_edge, "pts", 1)
    came = [edge, partner] + [swap(edge, "pts", 2 * e + c) for e in range(1, per_share // 2) for c in range(2)]
    came = {0: came}
    for offset in asked(shares):
        came[offset] = []
        for e in range(per_share // 2):
            block = swap(edge, "pts", offset * per_share + 2 * e)
            came[offset] += [block, swap(block, "pts", 1)]
    table = column_selector(group, per_share, per_block, 1).reshape(-1, per_share, ROWS)
    places = [[place ^ e for e in range(per_share)] for place in range(per_share)]
    tables = [table[:, place].reshape(table.shape[0], -1).astype(np.float32) for place in places]
    selector = jnp.asarray(np.stack([np.kron(np.eye(shares, dtype=np.float32), t) for t in tables]), BF16)
    piece = shape((share * 2 * local_k, points), BF16)
    both = shape((share * 3 * local_k, points), BF16)
    *tiles, forms = call(
        functools.partial(tile_kernel, shares, per_share, per_block),
        [both] * shares + [shape((shares, local_k, 2 * share, 2 * norb), BF16)],
        blocks + 4,
        [
            tiled(shares * share * 2 * local_k, points),
        ],
        size=6 * MIB,
    )(*[block for offset in [0, *asked(shares)] for block in came[offset]], first, rest, selector, cells)
    tiles = trade(tiles, "ka", 1)

    forward, backward = phase_tables(total)
    kernels = call(
        functools.partial(transform_kernel, shares, total, share),
        [piece] * shares,
        shares + 2,
        [
            pltpu.VMEM((shares, share * 2 * local_k, points), BF16 if local_k % 8 == 0 else F32),
            tiled(share * total, points),
            tiled(2 * total * share, points),
        ],
        size=2 * MIB,
    )(*tiles, jnp.asarray(forward), jnp.asarray(backward))
    kernels = trade(kernels, "ka", 1)

    lanes = local_k * 2 * columns
    pair = max(1, LANES // (2 * columns))
    early, late = list(reversed(range(1, chunks))), [0]
    sent, right = call(
        functools.partial(first_weight_kernel, shares, early, out_rows),
        [
            shape((len(early), out_rows, lanes), BF16),
            shape((local_k // pair, pair * 2 * columns, pair * 2 * points), BF16),
        ],
        shares + 2,
        [pltpu.VMEM((shares, share * 2 * local_k, points), BF16)],
    )(*kernels, first, rest)

    def rows_of(offsets, flip, kind, before):
        return call(
            functools.partial(next_weight_kernel, offsets, flip, out_rows),
            shape((len(offsets), out_rows, lanes), kind),
            3,
            unread=1,
        )(right, first, rest, before)

    def summed(offsets, keep, came):
        kinds = [shape((out_rows, lanes), BF16 if offset else F32) for offset in offsets]
        return call(pair_kernel, kinds, 2)(keep, came)

    sent_late = rows_of(late, 1, BF16, sent)
    early_sums = summed(early, rows_of(early, 0, F32, sent_late), swap(sent, "pts", 1))
    late_sums = summed(late, rows_of(late, 0, F32, early_sums[0]), swap(sent_late, "pts", 1))
    sums = [*late_sums, *early_sums]
    sums = shift_along(sums)
    spans = norb // LANES
    rows = pair * spans * 2
    result = call(
        functools.partial(exchange_kernel, chunks, 1.0 / math.sqrt(points * blocks)),
        shape((out_rows, local_k // pair, rows, LANES), BF16),
        chunks + 1,
        [
            pltpu.VMEM((local_k // pair, out_rows * rows, LANES), F32),
            pltpu.VMEM((local_k // pair, out_rows, rows, LANES), BF16),
            pltpu.SemaphoreType.DMA((local_k // pair,)),
        ],
        size=4 * MIB,
        result=pltpu.HBM,
    )(*sums, forms)
    result = result.reshape(out_rows, local_k, spans, 2, LANES)
    return result.transpose(0, 1, 3, 2, 4).reshape(out_rows, local_k, 2, norb)


def solution(mesh):
    in_specs = (P("ka", None, None, "pts"), P("ka", None, "pts"))
    out_specs = P("pts", "ka", None, None)
    return jax.shard_map(body, mesh=mesh, in_specs=in_specs, out_specs=out_specs, check_vma=False)
```

```python
import functools
import math

import jax
import jax.numpy as jnp
import ml_dtypes
import numpy as np
from jax import lax
from jax.experimental import pallas as pl
from jax.experimental.pallas import tpu as pltpu
from jax.sharding import PartitionSpec as P

BF16 = jnp.bfloat16
F32 = jnp.float32
LANES = 128
ROWS = 16
MIB = 1 << 20


def split_terms(table):
    high = table.astype(ml_dtypes.bfloat16)
    low = (table - high.astype(np.float64)).astype(ml_dtypes.bfloat16)
    return np.concatenate([high, low], axis=1)


def phase_tables(total):
    index = np.arange(total)
    angles = (index[:, None] * index[None, :] % total) * (2.0 * math.pi / total)
    cosine, sine = np.cos(angles), np.sin(angles)
    forward = np.zeros((2, total, total, 2))
    forward[0, :, :, 0] = cosine
    forward[0, :, :, 1] = -sine
    forward[1, :, :, 0] = sine
    forward[1, :, :, 1] = cosine
    backward = np.zeros((total, 2, 2, total))
    backward[:, 0, 0] = cosine
    backward[:, 0, 1] = sine
    backward[:, 1, 1] = cosine
    backward[:, 1, 0] = -sine
    size = 2 * total
    return (
        split_terms(forward.reshape(size, size)),
        split_terms(backward.reshape(size, size) / total),
    )


def column_selector(group, blocks, per_block, shares):
    total = blocks * per_block
    share = total // shares
    table = np.zeros((group, 2, shares, 2, share, blocks, group, 2, per_block), np.float32)
    for k in range(group):
        for col in range(total):
            d, c = divmod(col, share)
            b, j = divmod(col, per_block)
            table[k, 0, d, 0, c, b, k, 0, j] = 1.0
            table[k, 0, d, 1, c, b, k, 1, j] = -1.0
            table[k, 1, d, 0, c, b, k, 1, j] = 1.0
            table[k, 1, d, 1, c, b, k, 0, j] = 1.0
    return table.reshape(group * 4 * total, blocks * group * 2 * per_block).astype(ml_dtypes.bfloat16)


def dot(left, right, dims=((1,), (0,))):
    return lax.dot_general(left, right, (dims, ((), ())), preferred_element_type=F32)


def spread(wide, start, stride, value):
    for t in range(wide.shape[0]):
        wide[t, pl.ds(start, value.shape[0], stride=stride), :] = value[:, t * LANES : (t + 1) * LANES]


def take(wide, start, size):
    return jnp.concatenate([wide[t, pl.ds(start, size), :] for t in range(wide.shape[0])], axis=1)


def tiled(rows, lanes):
    return pltpu.VMEM((lanes // LANES, rows, LANES), F32)


def call(kernel, out_shape, n_in, scratch=(), limit=24, flops=0, size=0, unread=0, result=pltpu.VMEM):
    whole = pl.BlockSpec(memory_space=pltpu.VMEM)
    return pl.pallas_call(
        kernel,
        out_shape=out_shape,
        in_specs=[whole] * n_in + [pl.BlockSpec(memory_space=pl.ANY)] * unread,
        out_specs=jax.tree.map(lambda _: pl.BlockSpec(memory_space=result), out_shape),
        scratch_shapes=list(scratch),
        compiler_params=pltpu.CompilerParams(vmem_limit_bytes=limit * MIB),
        cost_estimate=pl.CostEstimate(flops=flops, bytes_accessed=size, transcendentals=0),
    )


def load_copies(orb_hbm, orb_ref, sems, start):
    lanes = pl.ds(start, orb_ref.shape[3])
    count = sems.shape[0]
    step = orb_ref.shape[0] // count
    copies = [
        pltpu.make_async_copy(
            orb_hbm.at[pl.ds(i * step, step), :, :, lanes], orb_ref.at[pl.ds(i * step, step)], sems.at[i]
        )
        for i in range(count)
    ]
    for copy in copies:
        copy.start()
    return copies


def rest_kernel(orb_hbm, edge_hbm, pass_ref, orb_ref, sems, pass_sem):
    copies = load_copies(orb_hbm, orb_ref, sems, LANES)
    copies.append(pltpu.make_async_copy(edge_hbm, pass_ref, pass_sem))
    copies[-1].start()
    for copy in copies:
        copy.wait()


def edge_kernel(per_block, orb_hbm, edge_ref, orb_ref, sems):
    local_k = orb_hbm.shape[0]
    copies = load_copies(orb_hbm, orb_ref, sems, 0)
    row = lax.broadcasted_iota(jnp.int32, (2 * per_block, 2 * LANES), 0)
    lane = lax.broadcasted_iota(jnp.int32, (2 * per_block, 2 * LANES), 1)
    column = jnp.where(row < per_block, row, row - per_block + LANES)
    chosen = jnp.where(lane == column, jnp.ones(row.shape, F32), jnp.zeros(row.shape, F32)).astype(BF16)
    group = ROWS // (2 * per_block)
    for g in range(local_k // group):
        rows = []
        copies[g].wait()
        for k in range(g * group, (g + 1) * group):
            both = jnp.concatenate([orb_ref[k, 0], orb_ref[k, 1]], axis=1)
            rows.append(dot(chosen, both, ((1,), (1,))))
        edge_ref[g * ROWS : (g + 1) * ROWS] = jnp.concatenate(rows, axis=0).astype(BF16)


def asked(shares):
    return [2, 1, *range(3, shares)]


def plane_of(shares):
    return lax.div(lax.axis_index("pts"), lax.axis_size("pts") // shares)


def tile_kernel(shares, per_share, per_block, *refs):
    blocks, (orb_ref, rest_ref, sel_ref, coulomb_ref) = refs[: shares * per_share], refs[shares * per_share :][:4]
    *outs, form_ref, wide, cells = refs[shares * per_share + 4 :]
    local_k, _, norb, _ = orb_ref.shape
    group = ROWS // (2 * per_block)
    share = per_share * per_block
    rows = 2 * share
    me, block = lax.axis_index("ka"), lax.axis_index("pts")
    plane = plane_of(shares)
    selector = sel_ref[jnp.bitwise_and(block, per_share - 1)]
    order = [0, *asked(shares)]
    for g in range(local_k // group):
        stacked = jnp.concatenate(
            [
                blocks[order.index(offset) * per_share + e][g * ROWS : (g + 1) * ROWS]
                for offset in range(shares)
                for e in range(per_share)
            ],
            axis=0,
        )
        chosen = dot(selector, stacked).astype(BF16)
        size = 2 * group * rows
        forms = [chosen[offset * size : (offset + 1) * size] for offset in range(shares)]
        for kk in range(group):
            k = g * group + kk
            left = [form[2 * kk * rows : (2 * kk + 1) * rows] for form in forms]
            right = [form[(2 * kk + 1) * rows : (2 * kk + 2) * rows] for form in forms]
            form = jnp.concatenate(
                [jnp.concatenate(left, axis=0), jnp.concatenate(right, axis=0)], axis=1
            )
            halves = [ref[k].reshape(2 * norb, ref.shape[3]) for ref in (orb_ref, rest_ref)]
            tile = dot(form, jnp.concatenate(halves, axis=1))
            for offset in range(shares):
                form_ref[jnp.bitwise_xor(plane, offset), k] = form[offset * rows : (offset + 1) * rows]
                for part in range(2):
                    low = offset * rows + part * share
                    start = offset * share * 2 * local_k + 2 * k + part
                    spread(wide, start, 2 * local_k, tile[low : low + share])
    size = share * 2 * local_k
    cells[...] = coulomb_ref[...].astype(F32)
    for s in range(shares):
        offset = jnp.bitwise_xor(me, s)
        outs[s][:size] = take(wide, pl.multiple_of(offset * size, size), size).astype(BF16)
        start = pl.multiple_of(jnp.bitwise_xor(offset, plane) * share, share)
        pieces = [cells[r, pl.ds(start, share), :] for r in range(local_k)]
        outs[s][size:] = jnp.concatenate(pieces, axis=0).astype(BF16)


def transform_kernel(shares, total, share, *refs):
    tiles, (fwd_ref, bwd_ref) = refs[:shares][::-1], refs[shares : shares + 2]
    outs, (gathered, weight, wide) = refs[shares + 2 : 2 * shares + 2], refs[2 * shares + 2 :]
    local_k = total // shares
    size = 2 * local_k * share
    me = lax.axis_index("ka")
    for s in range(shares):
        src = jnp.bitwise_xor(me, s)
        gathered[src] = tiles[s][:size].astype(gathered.dtype)
        cells = tiles[s][size:].astype(F32)
        for r in range(local_k):
            spread(weight, src * local_k + r, total, cells[r * share : (r + 1) * share])
    rows = 2 * local_k
    columns = []
    for c in range(share):
        columns.append(
            jnp.concatenate([gathered[a, c * rows : (c + 1) * rows] for a in range(shares)], axis=0).astype(BF16)
        )
    values = jnp.concatenate(columns, axis=1)
    cells = dot(fwd_ref[...], jnp.concatenate([values, values], axis=0))
    scale = jnp.concatenate([take(weight, c * total, total) for c in range(share)], axis=1)
    cells = (cells * jnp.concatenate([scale, scale], axis=0)).astype(BF16)
    kernel = dot(bwd_ref[...], jnp.concatenate([cells, cells], axis=0))
    points = kernel.shape[1] // share
    for c in range(share):
        spread(wide, c, share, kernel[:, c * points : (c + 1) * points])
    for s in range(shares):
        dest = jnp.bitwise_xor(me, s)
        outs[s][...] = take(wide, pl.multiple_of(dest * size, size), size).astype(BF16)


def weight_operands(pieces, right_ref, gathered):
    shares = len(pieces)
    groups, lanes, depth = right_ref.shape
    me, plane = lax.axis_index("ka"), plane_of(shares)
    for s in range(shares):
        gathered[jnp.bitwise_xor(jnp.bitwise_xor(me, s), plane)] = pieces[s][...]
    group = depth // (2 * gathered.shape[2])
    half = gathered.shape[1] // (groups * group) // 2
    for g in range(groups):
        right = []
        for kk in range(group):
            k = g * group + kk
            first, second = [], []
            for a in range(shares):
                piece = gathered[a, k * 2 * half : (k + 1) * 2 * half].astype(F32)
                first.append(piece)
                second.extend([piece[half:], -piece[:half]])
            first = jnp.concatenate(first, axis=0).astype(BF16)
            second = jnp.concatenate(second, axis=0).astype(BF16)
            parts = [jnp.zeros_like(first)] * (2 * group)
            parts[2 * kk], parts[2 * kk + 1] = first, second
            right.append(jnp.concatenate(parts, axis=1))
        right_ref[g] = jnp.concatenate(right, axis=0)


def weight_rows(offsets, flip, out_rows, right_ref, orb_ref, rest_ref, out_ref):
    groups, lanes, _ = right_ref.shape
    local_k, _, norb, _ = orb_ref.shape
    group = local_k // groups
    block = lax.axis_index("pts")
    core = jnp.bitwise_xor(jnp.bitwise_and(block, 1), flip)
    z = lax.shift_right_logical(block, 1)
    chunks = norb // out_rows // 2
    for g in range(groups):
        rows = []
        for offset in offsets:
            start = pl.multiple_of((2 * lax.rem(z + offset, chunks) + core) * out_rows, out_rows)
            parts = [
                ref[k, part, pl.ds(start, out_rows), :]
                for k in range(g * group, (g + 1) * group)
                for part in range(2)
                for ref in (orb_ref, rest_ref)
            ]
            rows.append(jnp.concatenate(parts, axis=1))
        result = dot(jnp.concatenate(rows, axis=0), right_ref[g], ((1,), (1,))).astype(out_ref.dtype)
        for i in range(len(offsets)):
            out_ref[i, :, g * lanes : (g + 1) * lanes] = result[i * out_rows : (i + 1) * out_rows]


def first_weight_kernel(shares, offsets, out_rows, *refs):
    pieces, (orb_ref, rest_ref, out_ref, right_ref, gathered) = refs[:shares][::-1], refs[shares:]
    weight_operands(pieces, right_ref, gathered)
    weight_rows(offsets, 1, out_rows, right_ref, orb_ref, rest_ref, out_ref)


def next_weight_kernel(offsets, flip, out_rows, right_ref, orb_ref, rest_ref, *refs):
    weight_rows(offsets, flip, out_rows, right_ref, orb_ref, rest_ref, refs[-1])


def pair_kernel(keep_ref, came_ref, *outs):
    for i, out_ref in enumerate(outs):
        out_ref[...] = (keep_ref[i] + came_ref[i].astype(F32)).astype(out_ref.dtype)


def exchange_kernel(chunks, scale, *refs):
    pieces, (form_ref, out_hbm, wide, out_ref, sems) = refs[:chunks][::-1], refs[chunks:]
    shares, local_k, part_lanes, twice = form_ref.shape
    lanes = shares * part_lanes
    norb = twice // 2
    spans = norb // LANES
    out_rows = pieces[0].shape[0]
    total = pieces[0][...]
    for s in range(1, chunks):
        total = total + pieces[s][...].astype(F32)
    total = total * scale
    high = total.astype(BF16)
    low = (total - high.astype(F32)).astype(BF16)
    group = max(1, LANES // lanes)
    width = group * lanes
    lane = lax.broadcasted_iota(jnp.int32, (out_rows, width), 1)
    zero = jnp.zeros((out_rows, width), BF16)
    copies = []
    for g in range(local_k // group):
        high_g = high[:, g * width : (g + 1) * width]
        low_g = low[:, g * width : (g + 1) * width]
        left = []
        for kk in range(group):
            keep = (lane >= kk * lanes) & (lane < (kk + 1) * lanes)
            left.append(
                jnp.concatenate([jnp.where(keep, high_g, zero), jnp.where(keep, low_g, zero)], axis=1)
            )
        forms = [form_ref[d, g * group + kk] for kk in range(group) for d in range(shares)]
        result = dot(jnp.concatenate(left, axis=0), jnp.concatenate(forms + forms, axis=0))
        for kk in range(group):
            for part in range(2):
                for t in range(spans):
                    lane_start = part * norb + t * LANES
                    value = result[kk * out_rows : (kk + 1) * out_rows, lane_start : lane_start + LANES]
                    start = (kk * spans + t) * 2 + part
                    wide[g, pl.ds(start, out_rows, stride=2 * spans * group), :] = value
        out_ref[g] = wide[g].astype(BF16).reshape(out_ref.shape[1:])
        copies.append(pltpu.make_async_copy(out_ref.at[g], out_hbm.at[:, g], sems.at[g]))
        copies[-1].start()
    for copy in copies:
        copy.wait()


def swap(value, axis, mask):
    size = lax.axis_size(axis)
    return lax.ppermute(value, axis, [(i, i ^ mask) for i in range(size)])


def trade(pieces, axis, step):
    return [swap(pieces[s], axis, s * step) for s in reversed(range(1, len(pieces)))] + [pieces[0]]


def shift_along(pieces):
    chunks = len(pieces)
    came = []
    for s in range(1, chunks):
        pairs = [(2 * z + core, 2 * ((z - s) % chunks) + core) for z in range(chunks) for core in range(2)]
        came.append(lax.ppermute(pieces[s], "pts", pairs))
    return came[::-1] + [pieces[0]]


def body(orbitals, coulomb):
    shares, blocks = lax.axis_size("ka"), lax.axis_size("pts")
    local_k, _, norb, points = orbitals.shape
    columns = coulomb.shape[1]
    per_block = columns // blocks
    share = columns // shares
    total = local_k * shares
    out_rows = norb // blocks
    chunks = blocks // 2
    group = ROWS // (2 * per_block)
    shape = jax.ShapeDtypeStruct

    edge, first = call(
        functools.partial(edge_kernel, per_block),
        [
            shape((local_k * 2 * per_block, norb), BF16),
            shape((local_k, 2, norb, LANES), BF16),
        ],
        0,
        [pltpu.SemaphoreType.DMA((local_k // group,))],
        limit=50,
        size=4 * MIB,
        unread=1,
    )(orbitals)
    passed_edge, rest = call(
        rest_kernel,
        [shape(edge.shape, BF16), shape((local_k, 2, norb, points - LANES), BF16)],
        0,
        [pltpu.SemaphoreType.DMA((local_k // group,)), pltpu.SemaphoreType.DMA],
        limit=49,
        size=4 * MIB,
        unread=2,
    )(orbitals, edge)
    per_share = blocks // shares
    partner = swap(passed_edge, "pts", 1)
    came = [edge, partner] + [swap(edge, "pts", 2 * e + c) for e in range(1, per_share // 2) for c in range(2)]
    came = {0: came}
    for offset in asked(shares):
        came[offset] = []
        for e in range(per_share // 2):
            block = swap(edge, "pts", offset * per_share + 2 * e)
            came[offset] += [block, swap(block, "pts", 1)]
    table = column_selector(group, per_share, per_block, 1).reshape(-1, per_share, ROWS)
    places = [[place ^ e for e in range(per_share)] for place in range(per_share)]
    tables = [table[:, place].reshape(table.shape[0], -1).astype(np.float32) for place in places]
    selector = jnp.asarray(np.stack([np.kron(np.eye(shares, dtype=np.float32), t) for t in tables]), BF16)
    piece = shape((share * 2 * local_k, points), BF16)
    both = shape((share * 3 * local_k, points), BF16)
    *tiles, forms = call(
        functools.partial(tile_kernel, shares, per_share, per_block),
        [both] * shares + [shape((shares, local_k, 2 * share, 2 * norb), BF16)],
        blocks + 4,
        [
            tiled(shares * share * 2 * local_k, points),
            pltpu.VMEM(coulomb.shape, F32),
        ],
        size=6 * MIB,
    )(*[block for offset in [0, *asked(shares)] for block in came[offset]], first, rest, selector, coulomb)
    tiles = trade(tiles, "ka", 1)

    forward, backward = phase_tables(total)
    kernels = call(
        functools.partial(transform_kernel, shares, total, share),
        [piece] * shares,
        shares + 2,
        [
            pltpu.VMEM((shares, share * 2 * local_k, points), BF16 if local_k % 8 == 0 else F32),
            tiled(share * total, points),
            tiled(2 * total * share, points),
        ],
        size=2 * MIB,
    )(*tiles, jnp.asarray(forward), jnp.asarray(backward))
    kernels = trade(kernels, "ka", 1)

    lanes = local_k * 2 * columns
    pair = max(1, LANES // (2 * columns))
    early, late = list(reversed(range(1, chunks))), [0]
    sent, right = call(
        functools.partial(first_weight_kernel, shares, early, out_rows),
        [
            shape((len(early), out_rows, lanes), BF16),
            shape((local_k // pair, pair * 2 * columns, pair * 2 * points), BF16),
        ],
        shares + 2,
        [pltpu.VMEM((shares, share * 2 * local_k, points), BF16)],
    )(*kernels, first, rest)

    def rows_of(offsets, flip, kind, before):
        return call(
            functools.partial(next_weight_kernel, offsets, flip, out_rows),
            shape((len(offsets), out_rows, lanes), kind),
            3,
            unread=1,
        )(right, first, rest, before)

    def summed(offsets, keep, came):
        kinds = [shape((out_rows, lanes), BF16 if offset else F32) for offset in offsets]
        return call(pair_kernel, kinds, 2)(keep, came)

    sent_late = rows_of(late, 1, BF16, sent)
    early_sums = summed(early, rows_of(early, 0, F32, sent_late), swap(sent, "pts", 1))
    late_sums = summed(late, rows_of(late, 0, F32, early_sums[0]), swap(sent_late, "pts", 1))
    sums = [*late_sums, *early_sums]
    sums = shift_along(sums)
    spans = norb // LANES
    rows = pair * spans * 2
    result = call(
        functools.partial(exchange_kernel, chunks, 1.0 / math.sqrt(points * blocks)),
        shape((out_rows, local_k // pair, rows, LANES), BF16),
        chunks + 1,
        [
            pltpu.VMEM((local_k // pair, out_rows * rows, LANES), F32),
            pltpu.VMEM((local_k // pair, out_rows, rows, LANES), BF16),
            pltpu.SemaphoreType.DMA((local_k // pair,)),
        ],
        size=4 * MIB,
        result=pltpu.HBM,
    )(*sums, forms)
    result = result.reshape(out_rows, local_k, spans, 2, LANES)
    return result.transpose(0, 1, 3, 2, 4).reshape(out_rows, local_k, 2, norb)


def solution(mesh):
    in_specs = (P("ka", None, None, "pts"), P("ka", None, "pts"))
    out_specs = P("pts", "ka", None, None)
    return jax.shard_map(body, mesh=mesh, in_specs=in_specs, out_specs=out_specs, check_vma=False)
```
